32 devices in a mesh: batch: 4 (over y, x), seq: 8 (over z, core).
Axes of the slice: x: 2, y: 2, z: 4, core: 2. Of those that a mesh axis runs over, the one named last changes fastest.
Arguments:
- inputs: bfloat16 [4, 2048, 1024], P('batch', 'seq'), may hold values from -6 to 6
- out_grad: bfloat16 [4, 2048, 1024], P('batch', 'seq'), may hold values from -6 to 6
- row_lengths: int32 [4, 5], P('batch'), may hold values from 32 to 1920, as said below
- norm_gain: bfloat16 [1024], P('seq'), may hold values from 0.5 to 1.5
- w_gate: bfloat16 [1024, 1536], P('seq'), may hold values from -0.1875 to 0.1875
- w_in: bfloat16 [1024, 1536], P('seq'), may hold values from -0.1875 to 0.1875
- conv_w: bfloat16 [4, 1536], P(None, 'seq'), may hold values from -3 to 3
- conv_b: bfloat16 [1536], P('seq'), may hold values from -2 to 2
- w_rgate: bfloat16 [1536, 128], P('seq'), may hold values from -0.5 to 0.5
- b_rgate: bfloat16 [1536], P('seq'), may hold values from -4 to 4
- w_igate: bfloat16 [1536, 128], P('seq'), may hold values from -0.5 to 0.5
- b_igate: bfloat16 [1536], P('seq'), may hold values from -4 to 4
- lam: bfloat16 [1536], P('seq'), may hold values from 4 to 16
- w_out: bfloat16 [1536, 1024], P('seq'), may hold values from -0.4375 to 0.4375
- mlp_gain: bfloat16 [1024], P('seq'), may hold values from 0.5 to 1.5
- w_mlp_gate: bfloat16 [1024, 3072], P('seq'), may hold values from -0.1875 to 0.1875
- w_mlp_up: bfloat16 [1024, 3072], P('seq'), may hold values from -0.1875 to 0.1875
- w_mlp_down: bfloat16 [3072, 1024], P('seq'), may hold values from -0.21875 to 0.21875
Outputs:
- block_out: bfloat16 [4, 2048, 1024], P('batch', 'seq')
- input_grad: float32 [4, 2048, 1024], P('batch', 'seq')
- grad_norm_gain: float32 [1024], P('seq')
- grad_w_gate: float32 [1024, 1536], P('seq')
- grad_w_in: float32 [1024, 1536], P('seq')
- grad_conv_w: float32 [4, 1536], P(None, 'seq')
- grad_conv_b: float32 [1536], P('seq')
- grad_w_rgate: float32 [1536, 128], P('seq')
- grad_b_rgate: float32 [1536], P('seq')
- grad_w_igate: float32 [1536, 128], P('seq')
- grad_b_igate: float32 [1536], P('seq')
- grad_lam: float32 [1536], P('seq')
- grad_w_out: float32 [1536, 1024], P('seq')
- grad_mlp_gain: float32 [1024], P('seq')
- grad_w_mlp_gate: float32 [1024, 3072], P('seq')
- grad_w_mlp_up: float32 [1024, 3072], P('seq')
- grad_w_mlp_down: float32 [3072, 1024], P('seq')
- gate_mean: float32 [4, 5, 1536], P('batch')
The draws below stay inside these ranges and needn't reach their ends.
Inputs may be any that keep to these rules, and one draw needn't show every extreme that they name: `row_lengths`: in each bucket rows 0, 1, 3 and 4 hold 32 to 96 tokens each and row 2 holds the rest of the 2048 positions; in one bucket rows 0, 1, 3 and 4 hold exactly 32 tokens each.
All inputs are finite; a program needn't handle non-finite values.
Results may differ from the reference program's by a relative error of at most 0.015.
Values may be sent and summed in bfloat16 or wider, within the bound.
A program may use at most 256 MiB of HBM per device.

```python
import jax
import jax.numpy as jnp
from jax import lax

D = 1024
DR = 1536
FF = 3072
BLOCK = 128
KERNEL = 4
ROWS = 5
GROUP = 256
NBLK = 12
BUCKETS = 4
LENGTH = 2048


def draw_row_lengths(key, part):
    key = jax.random.fold_in(key, 11)
    rows_key, pick_key = jax.random.split(key, 2)
    edge_rows = jax.random.randint(rows_key, (BUCKETS, 4), GROUP // 8, 3 * GROUP // 8 + 1, dtype=jnp.int32)
    chosen = jax.random.randint(pick_key, (), 0, BUCKETS, dtype=jnp.int32)
    bucket_ids = jnp.arange(BUCKETS, dtype=jnp.int32)[:, None]
    edge_rows = jnp.where(bucket_ids == chosen, jnp.int32(GROUP // 8), edge_rows).astype(jnp.int32)
    spanning = (LENGTH - jnp.sum(edge_rows, axis=1, keepdims=True)).astype(jnp.int32)
    return jnp.concatenate([edge_rows[:, :2], spanning, edge_rows[:, 2:]], axis=1).astype(jnp.int32)


def draw_lam(key, part):
    key = jax.random.fold_in(key, 23)
    pick_key, slow_key, fast_key = jax.random.split(key, 3)
    slow_share = 0.5
    picked = jax.random.uniform(pick_key, (DR,), jnp.float32) < slow_share
    slow_rate = jnp.exp(jax.random.uniform(slow_key, (DR,), jnp.float32, jnp.log(0.2), jnp.log(2.0))) / (4.0 * LENGTH)
    fast_rate = jnp.exp(jax.random.uniform(fast_key, (DR,), jnp.float32, jnp.log(1.0 / 200.0), jnp.log(1.0 / 120.0)))
    rate = jnp.where(picked, slow_rate, fast_rate)
    return (-jnp.log(jnp.expm1(rate))).astype(jnp.bfloat16)


def steps_of(own_key, dims, cuts, least, top_value):
    gain = 1.0
    for axis_at, parts in cuts:
        draws = jax.random.uniform(jax.random.fold_in(jax.random.fold_in(own_key, 6), axis_at), (parts,), jnp.float32, least / len(cuts), top_value / len(cuts))
        gain = gain * jnp.repeat(jnp.exp(draws), dims[axis_at] // parts).reshape((-1,) + (1,) * (len(dims) - 1 - axis_at))
    return gain


def gaussian(key, shape, spread, reach, cuts=(), kind=jnp.bfloat16):
    factor_of = steps_of(key, shape, cuts, -0.22, 0.18) if cuts else 1.0
    values = jax.random.normal(key, shape, jnp.float32) * spread * factor_of
    return jnp.minimum(jnp.maximum(values, -reach), reach).astype(kind)


def setup_inputs(seed: int = 0) -> dict:
    streams_of = jax.random.split(jax.random.key(seed), 19)
    inputs = gaussian(streams_of[0], (BUCKETS, LENGTH, D), 1.0, 6.0, ((0, 4), (1, 8)))
    out_grad = gaussian(streams_of[1], (BUCKETS, LENGTH, D), 1.0, 6.0, ((0, 4), (1, 8)))
    row_lengths = draw_row_lengths(jax.random.fold_in(streams_of[18], 71), 0)
    norm_gain = jnp.clip(1.0 + 0.1 * jax.random.normal(streams_of[3], (D,), jnp.float32), 0.5, 1.5).astype(jnp.bfloat16)
    w_gate = gaussian(streams_of[4], (D, DR), D ** -0.5, 0.1875, ((0, 8),))
    w_in = gaussian(streams_of[5], (D, DR), D ** -0.5, 0.1875, ((0, 8),))
    conv_w = gaussian(streams_of[6], (KERNEL, DR), 0.5, 3.0, ((1, 8),))
    conv_b = gaussian(streams_of[7], (DR,), 0.3, 2.0, ((0, 8),))
    w_rgate = gaussian(streams_of[8], (DR, BLOCK), BLOCK ** -0.5, 0.5, ((0, 8),))
    b_rgate = gaussian(streams_of[9], (DR,), 1.0, 4.0, ((0, 8),))
    w_igate = gaussian(streams_of[10], (DR, BLOCK), BLOCK ** -0.5, 0.5, ((0, 8),))
    b_igate = gaussian(streams_of[11], (DR,), 1.0, 4.0, ((0, 8),))
    lam = draw_lam(jax.random.fold_in(streams_of[18], 71), 0)
    w_out = gaussian(streams_of[13], (DR, D), (DR // 8) ** -0.5, 0.4375, ((0, 8),))
    mlp_gain = jnp.clip(1.0 + 0.1 * jax.random.normal(streams_of[14], (D,), jnp.float32), 0.5, 1.5).astype(jnp.bfloat16)
    w_mlp_gate = gaussian(streams_of[15], (D, FF), D ** -0.5, 0.1875, ((0, 8),))
    w_mlp_up = gaussian(streams_of[16], (D, FF), D ** -0.5, 0.1875, ((0, 8),))
    w_mlp_down = gaussian(streams_of[17], (FF, D), (FF // 4) ** -0.5, 0.21875, ((0, 8),))
    return dict(inputs=inputs, out_grad=out_grad, row_lengths=row_lengths, norm_gain=norm_gain, w_gate=w_gate, w_in=w_in, conv_w=conv_w, conv_b=conv_b, w_rgate=w_rgate, b_rgate=b_rgate, w_igate=w_igate, b_igate=b_igate, lam=lam, w_out=w_out, mlp_gain=mlp_gain, w_mlp_gate=w_mlp_gate, w_mlp_up=w_mlp_up, w_mlp_down=w_mlp_down)


NORM_EPS = 1e-06
DECAY_SCALE = 8.0

@jax.custom_vjp
def low(v):
    return lax.optimization_barrier(v.astype(jnp.bfloat16)).astype(jnp.float32)

@jax.custom_vjp
def low_back(v):
    return v

def low_keep(v):
    return (low(v), None)

def low_pass(kept, grad):
    return (grad,)

def back_keep(v):
    return (v, None)

def back_low(kept, grad):
    return (low(grad),)
low.defvjp(low_keep, low_pass)
low_back.defvjp(back_keep, back_low)

def rms_scale(values):
    return values * lax.rsqrt(lax.optimization_barrier(jnp.mean(values * values, axis=-1, keepdims=True)) + NORM_EPS)

def gelu_tanh(values):
    return jax.nn.gelu(values, approximate=True)

def block_product(values, weight):
    count = values.shape[0]
    shaped = values.reshape(count, NBLK, BLOCK)
    result = jnp.einsum('lni,nij->lnj', shaped, weight.reshape(NBLK, BLOCK, BLOCK), precision=lax.Precision.HIGHEST)
    return result.reshape(count, DR)

def token_step(carry, pair):
    following = pair[0] * carry + pair[1]
    return (following, following)

def block_recur(state, pieces):
    return lax.scan(token_step, state, pieces)

def recur(carried, drive):
    initial = jnp.zeros((DR,), jnp.float32)
    final, states = lax.scan(jax.checkpoint(block_recur), initial, (carried.reshape(-1, GROUP, DR), drive.reshape(-1, GROUP, DR)))
    return states.reshape(-1, DR)

def mix_block(tokens, weights, restart, conv_ok, members):
    norm_gain, w_gate, w_in, conv_w, conv_b, w_rgate, b_rgate, w_igate, b_igate, lam, w_out, mlp_gain, w_mlp_gate, w_mlp_up, w_mlp_down = weights
    count = tokens.shape[0]
    normed = low(rms_scale(tokens) * norm_gain)
    gate_branch = gelu_tanh(low_back(jnp.dot(normed, w_gate, precision=lax.Precision.HIGHEST)))
    inner = low(low_back(jnp.dot(normed, w_in, precision=lax.Precision.HIGHEST)))
    padded = jnp.concatenate([jnp.zeros((KERNEL - 1, DR), jnp.float32), inner], axis=0)
    conv_sum = conv_b + jnp.zeros((count, DR), jnp.float32)
    for tap in range(KERNEL):
        conv_sum = conv_sum + conv_w[tap] * padded[KERNEL - 1 - tap:KERNEL - 1 - tap + count] * conv_ok[tap][:, None]
    conv = low(conv_sum)
    r_pre = low_back(block_product(conv, w_rgate) + b_rgate)
    i_pre = low_back(block_product(conv, w_igate) + b_igate)
    log_a = -DECAY_SCALE * jax.nn.sigmoid(r_pre) * jax.nn.softplus(-lam)
    decays = jnp.exp(log_a)
    factor = jnp.where(restart[:, None] > 0, 1.0, jnp.sqrt(-jnp.expm1(2.0 * log_a)))
    drive = factor * jax.nn.sigmoid(i_pre) * conv
    carried = decays * (1.0 - restart[:, None])
    states = recur(carried, drive)
    mixed = low(states * gate_branch)
    residual = tokens + low_back(jnp.dot(mixed, w_out, precision=lax.Precision.HIGHEST))
    normed2 = low(rms_scale(residual) * mlp_gain)
    up_gate = low_back(jnp.dot(normed2, w_mlp_gate, precision=lax.Precision.HIGHEST))
    up_lin = low_back(jnp.dot(normed2, w_mlp_up, precision=lax.Precision.HIGHEST))
    hidden = low(gelu_tanh(up_gate) * up_lin)
    result = residual + jnp.dot(hidden, w_mlp_down, precision=lax.Precision.HIGHEST)
    row_sums = jnp.dot(members.T, decays, precision=lax.Precision.HIGHEST)
    return (result, row_sums)

def reference(inputs, out_grad, row_lengths, norm_gain, w_gate, w_in, conv_w, conv_b, w_rgate, b_rgate, w_igate, b_igate, lam, w_out, mlp_gain, w_mlp_gate, w_mlp_up, w_mlp_down):
    params = (norm_gain, w_gate, w_in, conv_w, conv_b, w_rgate, b_rgate, w_igate, b_igate, lam, w_out, mlp_gain, w_mlp_gate, w_mlp_up, w_mlp_down)
    params = tuple((item.astype(jnp.float32) for item in params))
    positions = jnp.arange(LENGTH, dtype=jnp.int32)
    row_numbers = jnp.arange(ROWS, dtype=jnp.int32)

    def tables(lengths):
        row_ends = jnp.cumsum(lengths).astype(jnp.int32)
        row_starts = (row_ends - lengths).astype(jnp.int32)
        started = positions[:, None] >= row_starts[None, :]
        row_index = lax.optimization_barrier(jnp.sum(started.astype(jnp.int32), axis=1)).astype(jnp.int32) - 1
        row_first = lax.optimization_barrier(jnp.max(jnp.where(started, row_starts[None, :], 0), axis=1)).astype(jnp.int32)
        offset = positions - row_first
        restart = (offset == 0).astype(jnp.float32)
        conv_ok = jnp.stack([(offset >= tap).astype(jnp.float32) for tap in range(KERNEL)])
        members = (row_index[:, None] == row_numbers[None, :]).astype(jnp.float32)
        return (restart, conv_ok, members)
    restarts, conv_oks, member_sets = jax.vmap(tables)(row_lengths)

    def forward(tokens_all, *weights):

        def per_bucket(carry, item):
            tokens, restart, conv_ok, members = item
            result, row_sums = jax.checkpoint(mix_block)(tokens, weights, restart, conv_ok, members)
            return (carry, (result, row_sums))
        unused, (results, sums) = lax.scan(per_bucket, jnp.zeros((), jnp.float32), (tokens_all, restarts, conv_oks, member_sets))
        return (results, sums)
    results, pullback, sums = jax.vjp(forward, inputs.astype(jnp.float32), *params, has_aux=True)
    grad_x, grad_gain, grad_gate, grad_inw, grad_cw, grad_cb, grad_rw, grad_rb, grad_iw, grad_ib, grad_lambda, grad_outw, grad_mgain, grad_mgate, grad_mup, grad_mdown = pullback(out_grad.astype(jnp.float32))
    gate_mean = sums / row_lengths.astype(jnp.float32)[:, :, None]
    return (results.astype(jnp.bfloat16), grad_x, grad_gain, grad_gate, grad_inw, grad_cw, grad_cb, grad_rw, grad_rb, grad_iw, grad_ib, grad_lambda, grad_outw, grad_mgain, grad_mgate, grad_mup, grad_mdown, gate_mean)
```

```python
import functools
import types

import jax
import jax.numpy as jnp
from jax import lax
from jax.experimental import pallas as pl
from jax.experimental.pallas import tpu as pltpu
from jax.sharding import PartitionSpec as P

NORM_EPS = 1e-06
DECAY_SCALE = 8.0
BF = jnp.bfloat16
F32 = jnp.float32
GELU_SCALE = 0.7978845608028654
GELU_CUBE = 0.044715
TILE = 64
NN = (((1,), (0,)), ((), ()))
NT = (((1,), (1,)), ((), ()))
TN = (((0,), (0,)), ((), ()))


def dot(left, right, dims=NN):
    return lax.dot_general(left, right, dims, preferred_element_type=F32)


def loop(count, body):
    def step(i, carry):
        body(i)
        return carry

    lax.fori_loop(0, count, step, 0)


class Net:
    def __init__(self, send, recv):
        self.send, self.recv, self.count = send, recv, 0
        self.pending = []
        self.p = lax.axis_index("batch")
        self.q = lax.axis_index("seq")
        self.z = lax.div(self.q, 2)
        self.c = lax.rem(self.q, 2)
        self.o = 1 - self.c
        p = self.p
        self.near = (p, p + 1 - 2 * lax.rem(p, 2), lax.rem(p + 2, 4), 3 - p)

    def plane(self, k, core):
        return {"batch": self.near[k], "seq": self.z * 2 + core}

    def line(self, z, core):
        return {"batch": self.p, "seq": z * 2 + core}

    def up(self, k):
        return lax.rem(self.z + k, 4)

    def down(self, k):
        return lax.rem(self.z + 4 - k, 4)

    def slot(self, k, core):
        return self.near[k] * 2 + core

    def greet(self):
        barrier = pltpu.get_barrier_semaphore()
        partners = [self.plane(k, core) for k in (1, 2, 3) for core in (0, 1)]
        partners += [self.line(self.up(k), core) for k in (1, 2, 3) for core in (0, 1)]
        partners += [self.line(self.z, self.o)]
        for partner in partners:
            pl.semaphore_signal(barrier, inc=1, device_id=partner, device_id_type=pl.DeviceIdType.MESH)
        pl.semaphore_wait(barrier, len(partners))

    def reserve(self, count):
        first = self.count
        self.count += count
        return first

    def describe(self, src, dst, device, send_at, recv_at):
        return pltpu.make_async_remote_copy(
            src_ref=src,
            dst_ref=dst,
            send_sem=self.send.at[send_at],
            recv_sem=self.recv.at[recv_at],
            device_id=device,
            device_id_type=pl.DeviceIdType.MESH,
        )

    def copy(self, src, dst, device):
        at = self.reserve(1)
        made = self.describe(src, dst, device, at, at)
        made.start()
        self.pending.append(made)
        return made

    def drain(self):
        for made in self.pending:
            made.wait_send()
        self.pending = []


class Gather:
    def __init__(self, net, own, everything):
        self.net, self.own, self.all = net, own, everything
        self.half = own.shape[0] // 2

    def part(self, slot, h):
        return self.all.at[slot, pl.ds(h * self.half, self.half)]

    def start(self):
        net = self.net
        mine = net.slot(0, net.c)
        low, high = self.own.at[pl.ds(0, self.half)], self.own.at[pl.ds(self.half, self.half)]
        self.x0 = net.copy(low, self.part(mine, 0), net.plane(1, net.c))
        self.y1 = net.copy(high, self.part(mine, 1), net.plane(2, net.c))
        self.x1 = net.copy(high, self.part(mine, 1), net.plane(1, net.c))
        self.y0 = net.copy(low, self.part(mine, 0), net.plane(2, net.c))
        self.s = [net.copy(self.own, self.all.at[mine], net.plane(0, net.o))]

    def forward(self):
        net = self.net
        self.x0.wait_recv()
        mine = self.part(net.slot(1, net.c), 0)
        self.d0 = net.copy(mine, mine, net.plane(2, net.c))
        self.y1.wait_recv()
        mine = self.part(net.slot(2, net.c), 1)
        self.d1 = net.copy(mine, mine, net.plane(1, net.c))

    def across(self, k):
        net = self.net
        mine = self.all.at[net.slot(k, net.c)]
        self.s.append(net.copy(mine, mine, net.plane(0, net.o)))

    def middle(self):
        self.x1.wait_recv()
        self.across(1)
        self.y0.wait_recv()
        self.across(2)

    def last(self):
        self.d0.wait_recv()
        self.d1.wait_recv()
        self.across(3)

    def sibling(self, k):
        self.s[k].wait_recv()


class Reduce:
    def __init__(self, net, r):
        self.net = net
        self.keep, self.out, self.into = r.rs_keep, r.rs_out, r.rs_in
        self.xs, self.ys, self.xr, self.yr = r.rs_xs, r.rs_ys, r.rs_xr, r.rs_yr
        self.rows = self.keep.shape[1]
        self.half = self.rows // 2
        self.cross = [None] * 4

    def put_own(self, k, value):
        self.keep[k] = value

    def put_other(self, k, value):
        net = self.net
        self.out[k] = value.astype(BF)
        self.cross[k] = net.copy(self.out.at[k], self.into.at[k], net.plane(0, net.o))

    def merge(self, k):
        self.cross[k].wait_recv()
        step = 32

        def body(i):
            rows = pl.ds(pl.multiple_of(i * step, step), step)
            self.keep[k, rows, :] = self.keep[k, rows, :] + self.into[k, rows, :].astype(F32)

        loop(self.rows // step, body)

    def low(self, dst, j, k, h, extra=None):
        step = 32

        def body(i):
            rows = pl.ds(pl.multiple_of(i * step, step), step)
            source = pl.ds(pl.multiple_of(h * self.half + i * step, step), step)
            value = self.keep[k, source, :]
            if extra is not None:
                value = value + extra[0, rows, :].astype(F32)
            dst[j, rows, :] = value.astype(BF)

        loop(self.half // step, body)

    def send(self, src, dst, j, k):
        net = self.net
        return net.copy(src.at[j], dst.at[j], net.plane(k, net.c))

    def far(self):
        self.merge(3)
        self.low(self.xs, 0, 3, 0)
        self.x0 = self.send(self.xs, self.xr, 0, 1)
        self.low(self.ys, 0, 3, 1)
        self.y0 = self.send(self.ys, self.yr, 0, 2)

    def near_x(self):
        self.merge(1)
        self.low(self.xs, 1, 1, 0)
        self.x1 = self.send(self.xs, self.xr, 1, 1)

    def near_y(self):
        self.merge(2)
        self.low(self.ys, 1, 2, 1)
        self.y1 = self.send(self.ys, self.yr, 1, 2)

    def relay(self):
        self.x0.wait_recv()
        self.low(self.ys, 2, 2, 0, self.xr)
        self.y2 = self.send(self.ys, self.yr, 2, 2)
        self.y0.wait_recv()
        self.low(self.xs, 2, 1, 1, self.yr)
        self.x2 = self.send(self.xs, self.xr, 2, 1)

    def finish(self):
        self.merge(0)
        for made in (self.x1, self.y1, self.x2, self.y2):
            made.wait_recv()

    def total(self, h, i, step):
        rows = pl.ds(pl.multiple_of(i * step, step), step)
        source = pl.ds(pl.multiple_of(h * self.half + i * step, step), step)
        first, second = (self.xr, self.yr) if h == 0 else (self.yr, self.xr)
        return (
            self.keep[0, source, :] + first[1, rows, :].astype(F32) + second[2, rows, :].astype(F32)
        )


def reduce_scratch(rows, width):
    half = rows // 2
    return dict(
        rs_keep=pltpu.VMEM((4, rows, width), F32),
        rs_out=pltpu.VMEM((4, rows, width), BF),
        rs_in=pltpu.VMEM((4, rows, width), BF),
        rs_xs=pltpu.VMEM((3, half, width), BF),
        rs_ys=pltpu.VMEM((3, half, width), BF),
        rs_xr=pltpu.VMEM((3, half, width), BF),
        rs_yr=pltpu.VMEM((3, half, width), BF),
    )


def kernel_call(body, ins, outs, scratch, copies, cid):
    names = list(ins) + list(outs) + list(scratch)
    spec = pl.BlockSpec(memory_space=pltpu.VMEM)
    shapes = list(scratch.values())
    remote = copies > 0
    if remote:
        names += ["send", "recv"]
        shapes += [pltpu.SemaphoreType.DMA((copies,)), pltpu.SemaphoreType.DMA((copies,))]

    def kernel(*refs):
        body(types.SimpleNamespace(**dict(zip(names, refs))))

    params = dict(vmem_limit_bytes=61 * 2**20)
    if remote:
        params.update(collective_id=cid, has_side_effects=True)
    results = pl.pallas_call(
        kernel,
        out_shape=list(outs.values()),
        in_specs=[spec] * len(ins),
        out_specs=[spec] * len(outs),
        scratch_shapes=shapes,
        compiler_params=pltpu.CompilerParams(**params),
        name=body.__name__,
    )(*ins.values())
    return dict(zip(outs, results))


def array(*shape, dtype=F32):
    return jax.ShapeDtypeStruct(shape, dtype)


def gelu_parts(v):
    square = v * v
    t = jnp.tanh(GELU_SCALE * v * (1.0 + GELU_CUBE * square))
    half = 0.5 + 0.5 * t
    slope = half + 0.5 * v * (1.0 - t * t) * (GELU_SCALE * (1.0 + 3.0 * GELU_CUBE * square))
    return v * half, slope


def decay_parts(sr, rate):
    log_a = -DECAY_SCALE * sr * rate
    a = jnp.exp(log_a)
    y = 2.0 * log_a
    series = 1.0 + y * (1 / 6) * (1.0 + y * (1 / 7))
    for n in (5, 4, 3, 2):
        series = 1.0 + y * (1 / n) * series
    m2 = jnp.where(y > -0.35, -y * series, 1.0 - a * a)
    return a, jnp.maximum(m2, 1e-36)


def offsets(r, b, first_position, rows):
    starts = r.starts_all[b]
    at = lax.convert_element_type(first_position, F32) + lax.broadcasted_iota(
        jnp.int32, (rows, 128), 0
    ).astype(F32)
    first = jnp.zeros((rows, 128), F32)
    for row in range(5):
        start = starts[row : row + 1, :]
        first = jnp.maximum(first, jnp.where(at >= start, start, 0.0))
    return first, at - first


def roll_rows(value, by):
    return pltpu.roll(value, by, 0)


def combine_segments(p_end, s_end, reverse):
    row = lax.broadcasted_iota(jnp.int32, (8, 128), 0)
    for d in (1, 2, 4):
        by = 8 - d if reverse else d
        valid = row < 8 - d if reverse else row >= d
        p_sh, s_sh = roll_rows(p_end, by), roll_rows(s_end, by)
        s_end = jnp.where(valid, p_end * s_sh + s_end, s_end)
        p_end = jnp.where(valid, p_end * p_sh, p_end)
    edge = row == (7 if reverse else 0)
    by = 7 if reverse else 1
    enter_p = jnp.where(edge, 1.0, roll_rows(p_end, by))
    enter_s = jnp.where(edge, 0.0, roll_rows(s_end, by))
    last = 0 if reverse else 7
    return enter_p, enter_s, p_end[last : last + 1, :], s_end[last : last + 1, :]


def column_sum(value):
    return jnp.sum(value.reshape(-1, 8, 128), axis=0)


def scan_segments(decay, value, reverse):
    length = decay.shape[1] // 8

    def step(i, carry):
        j = length - 1 - i if reverse else i
        at = pl.ds(j, 8, stride=length)
        done = []
        for s in range(8):
            p, v = carry[s]
            d = decay[s, at, :]
            if reverse:
                v = v + value[s, at, :]
                value[s, at, :] = v
                decay[s, at, :] = p
                p, v = d * p, d * v
            else:
                p, v = d * p, d * v + value[s, at, :]
                value[s, at, :] = v
                decay[s, at, :] = p
            done.append((p, v))
        return tuple(done)

    start = tuple((jnp.ones((8, 128), F32), jnp.zeros((8, 128), F32)) for _ in range(8))
    return lax.fori_loop(0, length, step, start)


def entering_states(r, net, ends, reverse):
    z = net.z
    for s in range(8):
        ep, es, tp, ts = combine_segments(*ends[s], reverse)
        r.ent_p[s] = ep
        r.ent_s[s] = es
        r.tot[z, 0, s : s + 1, :] = tp
        r.tot[z, 1, s : s + 1, :] = ts
    copies = [net.copy(r.tot.at[z], r.tot.at[z], net.line(net.up(k), net.c)) for k in (1, 2, 3)]
    for made in copies:
        made.wait_recv()
    state = jnp.zeros((8, 128), F32)
    for i in range(4):
        at = 3 - i if reverse else i
        new = r.tot[at, 0] * state + r.tot[at, 1]
        state = jnp.where((at > z) if reverse else (at < z), new, state)
    r.inc[...] = state
    for s in range(8):
        r.ent_s[s] = r.ent_s[s] + r.ent_p[s] * r.inc[s : s + 1, :]


def tile_rows(i):
    return pl.ds(pl.multiple_of(i * TILE, TILE), TILE)


def recur_front(r):
    net = Net(r.send, r.recv)
    net.greet()
    p, z, c, o, q = net.p, net.z, net.c, net.o, net.q
    sibling = net.plane(0, o)
    tokens = Gather(net, r.x, r.x_all)
    tokens.start()
    mine = net.slot(0, c)
    r.small_all[q] = r.small[...]
    r.starts_all[p] = r.starts[...]
    small = [net.copy(r.small, r.small_all.at[q], net.line(net.up(k), core)) for k in (1, 2, 3) for core in (c, o)]
    small.append(net.copy(r.small, r.small_all.at[q], sibling))
    starts = [net.copy(r.starts, r.starts_all.at[p], net.plane(k, c)) for k in (1, 2, 3)]
    width = r.wg3.shape[2]
    first = pl.multiple_of(p * width, 128)
    chip = pl.ds(first, width)
    theirs = pl.ds(pl.multiple_of(o * 128, 128), 256)
    theirs_in = pl.ds(pl.multiple_of(first + o * 128, 128), 256)
    pairs = ((r.wg, r.wg3), (r.wi, r.wi3))
    from_line = [
        [net.copy(src.at[:, chip], dst.at[q], net.line(net.up(k), c)) for src, dst in pairs] for k in (1, 2, 3)
    ]
    across = [net.copy(src.at[:, theirs_in], dst.at[q, :, theirs], sibling) for src, dst in pairs]
    spread = []

    def spread_rows(src, dst):
        at = net.reserve(4)

        @pl.when(z == p)
        def _():
            dst[c] = src[...]
            for k in (1, 2, 3):
                net.describe(src, dst.at[c], net.line(net.up(k), c), at + k, at).start()

        spread.append((src, dst, at))

    def spread_over(entry):
        src, dst, at = entry

        @pl.when(z != p)
        def _():
            net.describe(src, dst.at[c], sibling, at, at).wait_recv()

        across.append(net.copy(dst.at[c], dst.at[c], sibling))

    def spread_end():
        for src, dst, at in spread:

            @pl.when(z == p)
            def _(src=src, dst=dst, at=at):
                for k in (1, 2, 3):
                    net.describe(src, dst.at[c], sibling, at + k, at).wait_send()

    spread_rows(r.wr, r.wr3)
    spread_rows(r.wv, r.wv3)
    for src, dst in pairs:
        dst[q] = src[:, chip]
    cols = r.wmg_out.shape[2]
    piece = cols // 4
    selects = []
    k_at = lax.broadcasted_iota(jnp.int32, (cols, cols), 0)
    j_at = lax.broadcasted_iota(jnp.int32, (cols, cols), 1)
    for part in range(4):
        inside = (j_at >= part * piece) & (j_at < (part + 1) * piece)
        chosen = inside & (k_at == j_at + (p - part) * piece)
        selects.append(jnp.where(chosen, 1.0, 0.0).astype(BF))
    for src, out in ((r.wmg, r.wmg_out), (r.wmu, r.wmu_out)):
        for core in (0, 1):
            picked = None
            for part in range(4):
                stretch = src[:, (part * 2 + core) * cols : (part * 2 + core + 1) * cols]
                term = dot(stretch, selects[part])
                picked = term if picked is None else picked + term
            out[core] = picked.astype(BF)
    for made in small + starts:
        made.wait_recv()
    low, high = r.small_all[2 * p], r.small_all[2 * p + 1]
    at_first = jnp.concatenate([low[:, :192], high[:, :64]], axis=1)
    at_second = jnp.concatenate([low[:, 128:192], high[:, :192]], axis=1)
    both = lax.select(c == 0, at_first, at_second)
    for n in range(2):
        r.chan[n] = both[:, n * 128 : (n + 1) * 128]
    gain = jnp.concatenate([r.small_all[i, 10:11, 0:128] for i in range(8)], axis=1)
    r.gain1[...] = gain
    r.gain2[...] = jnp.concatenate([r.small_all[i, 10:11, 128:256] for i in range(8)], axis=1)

    def normalise(slot):
        def body(i):
            rows = pl.ds(pl.multiple_of(i * 32, 32), 32)
            v = r.x_all[slot, rows, :].astype(F32)
            s = lax.rsqrt(jnp.mean(v * v, axis=-1, keepdims=True) + NORM_EPS)
            r.normed[slot, rows, :] = (v * s * gain).astype(BF)

        loop(8, body)

    r.x_all[mine] = r.x[...]
    normalise(mine)
    tokens.sibling(0)
    normalise(net.slot(0, o))
    tokens.forward()
    for k in (1, 2, 3):
        for (src, dst), made in zip(pairs, from_line[k - 1]):
            made.wait_recv()
            here = dst.at[net.down(k) * 2 + c, :, theirs]
            across.append(net.copy(here, here, sibling))
    tokens.middle()
    for k in (1, 2):
        normalise(net.slot(k, c))
    for k in (1, 2):
        tokens.sibling(k)
        normalise(net.slot(k, o))
    tokens.last()
    for entry in spread:
        spread_over(entry)
    for made in across:
        made.wait_recv()
    spread_rows(r.wout, r.wout3)
    feed = []
    for src, dst in ((r.wmg_out, r.wmg_all), (r.wmu_out, r.wmu_all)):
        dst[q] = src[c]
        for k in (1, 2, 3):
            for core in (c, o):
                feed.append(net.copy(src.at[core], dst.at[q], net.line(net.up(k), core)))
        feed.append(net.copy(src.at[o], dst.at[q], sibling))
    down = pl.ds(pl.multiple_of(p * piece, 16), piece)
    r.wmd_all[z] = r.wmd[down, :]
    for k in (1, 2, 3):
        feed.append(net.copy(r.wmd.at[down], r.wmd_all.at[z], net.line(net.up(k), c)))
    cots = Gather(net, r.g, r.g_all)
    cots.start()
    r.g_all[mine] = r.g[...]
    own_cols = pl.ds(pl.multiple_of(c * 128, 128), 256)
    for i in range(8):
        r.w2[i * 128 : (i + 1) * 128, 0:256] = r.wg3[i, :, own_cols]
        r.w2[i * 128 : (i + 1) * 128, 256:512] = r.wi3[i, :, own_cols]
    rows_of = r.wr3.shape[1]
    for n in range(2):
        for part, src in enumerate((r.wr3, r.wv3)):
            flat = jnp.concatenate([src[0], src[1]], axis=0)
            pick = lax.select(c == 0, flat[n * 128 : (n + 1) * 128], flat[(n + 1) * 128 : (n + 2) * 128])
            r.wri[n, :, part * 128 : (part + 1) * 128] = pick

    def project(slot):
        b, half = lax.div(slot, 2), lax.rem(slot, 2)
        at = pl.multiple_of(half * 256, 256)
        h = r.normed[slot]
        gate = dot(h, r.w2[:, 0:256])
        inner = dot(h, r.w2[:, 256:512]).astype(BF).astype(F32)
        for n in range(2):
            lanes = slice(n * 128, (n + 1) * 128)
            r.gp[b * 2 + n, pl.ds(at, 256), :] = gate[:, lanes]
            r.inner[b * 2 + n, pl.ds(at + 8, 256), :] = inner[:, lanes]

    for k in (0, 1, 2):
        project(net.slot(k, c))
        project(net.slot(k, o))
    normalise(net.slot(3, c))
    project(net.slot(3, c))
    tokens.sibling(3)
    normalise(net.slot(3, o))
    project(net.slot(3, o))
    edge = net.reserve(1)

    def edge_copy():
        return net.describe(
            r.inner.at[:, pl.ds(512, 8)], r.inner.at[:, pl.ds(0, 8)], net.line(net.up(1), c), edge, edge
        )

    @pl.when(z < 3)
    def _():
        edge_copy().start()

    @pl.when(z == 0)
    def _():
        r.inner[:, 0:8, :] = jnp.zeros((8, 8, 128), F32)

    cots.forward()

    def gelu_tile(i):
        s, rows = lax.div(i, 8), tile_rows(lax.rem(i, 8))
        v = r.gp[s, rows, :]
        t = jnp.tanh(GELU_SCALE * v * (1.0 + GELU_CUBE * v * v))
        r.gb[s, rows, :] = 0.5 * v * (1.0 + t)

    loop(64, gelu_tile)

    @pl.when(z > 0)
    def _():
        edge_copy().wait_recv()

    @pl.when(z < 3)
    def _():
        edge_copy().wait_send()

    def conv_tile(i):
        s, tile = lax.div(i, 8), lax.rem(i, 8)
        b, n = lax.div(s, 2), lax.rem(s, 2)
        rows = tile_rows(tile)
        _, offset = offsets(r, b, z * 512 + tile * TILE, TILE)
        window = r.inner[s, pl.ds(pl.multiple_of(tile * TILE, 8), TILE + 8), :]
        chan = r.chan[n]
        total = chan[4:5, :] + chan[0:1, :] * window[8:, :]
        for k in (1, 2, 3):
            total = total + chan[k : k + 1, :] * jnp.where(offset >= k, window[8 - k : TILE + 8 - k, :], 0.0)
        r.conv[s, rows, :] = total.astype(BF)

    loop(64, conv_tile)
    cots.middle()

    def gates(i):
        s, half = lax.div(i, 2), lax.rem(i, 2)
        n = lax.rem(s, 2)
        rows = pl.ds(pl.multiple_of(half * 256, 256), 256)
        pre = dot(r.conv[s, rows, :], r.wri[n])
        r.sr[s, rows, :] = pre[:, :128]
        r.si[s, rows, :] = pre[:, 128:]

    loop(16, gates)

    def terms(s):
        b, n = lax.div(s, 2), lax.rem(s, 2)
        chan = r.chan[n]
        starts_b = r.starts_all[b]

        def tile(i, sums):
            rows = tile_rows(i)
            first, offset = offsets(r, b, z * 512 + i * TILE, TILE)
            sr = jax.nn.sigmoid(r.sr[s, rows, :] + chan[5:6, :])
            si = jax.nn.sigmoid(r.si[s, rows, :] + chan[6:7, :])
            r.sr[s, rows, :] = sr
            r.si[s, rows, :] = si
            a, m2 = decay_parts(sr, chan[7:8, :])
            restart = offset == 0.0
            r.dec[s, rows, :] = jnp.where(restart, 0.0, a)
            m = jnp.where(restart, 1.0, jnp.sqrt(m2))
            r.drv[s, rows, :] = m * si * r.conv[s, rows, :].astype(F32)
            return tuple(
                sums[row] + column_sum(jnp.where(first == starts_b[row : row + 1, :], a, 0.0)) for row in range(5)
            )

        sums = lax.fori_loop(0, 512 // TILE, tile, tuple(jnp.zeros((8, 128), F32) for _ in range(5)))
        sums = [jnp.sum(part, axis=0, keepdims=True) for part in sums] + [jnp.zeros((3, 128), F32)]
        r.rs_all[z, s] = jnp.concatenate(sums, axis=0)

    loop(8, terms)
    spread_over(spread[-1])
    row_sums = [net.copy(r.rs_all.at[z], r.rs_all.at[z], net.line(net.up(k), c)) for k in (1, 2, 3)]
    ends = scan_segments(r.dec, r.drv, False)
    entering_states(r, net, ends, False)
    cots.last()
    across[-1].wait_recv()

    def own_rows(i):
        at = c * 128 + i * 64
        rows = pl.ds(pl.multiple_of(lax.rem(at, 192), 64), 64)
        value = r.wout3[lax.div(at, 192), rows, :]
        to = pl.ds(pl.multiple_of(i * 64, 64), 64)
        r.wo[to, :] = value
        r.wom[to, :] = value

    loop(4, own_rows)
    r.wom[pl.ds(pl.multiple_of(o * 192, 64), 64), :] = jnp.zeros((64, r.wom.shape[1]), BF)

    for n in range(2):
        for b in range(4):
            r.states[b * 2 + n, 7:8, :] = r.inc[b * 2 + n : b * 2 + n + 1, :]

    def mix_tile(i):
        s, tile = lax.div(i, 8), lax.rem(i, 8)
        b, n = lax.div(s, 2), lax.rem(s, 2)
        rows = tile_rows(tile)
        enter = r.ent_s[s, pl.ds(tile, 1), :]
        states = r.drv[s, rows, :] + r.dec[s, rows, :] * enter
        r.states[s, pl.ds(pl.multiple_of(tile * TILE + 8, 8), TILE), :] = states
        lanes = pl.ds(pl.multiple_of(n * 128, 128), 128)
        r.mixed[b * 2 + lax.div(tile, 4), tile_rows(lax.rem(tile, 4)), lanes] = (states * r.gb[s, rows, :]).astype(BF)

    loop(64, mix_tile)
    total = Reduce(net, r)
    for k in (3, 1, 2, 0):
        total.put_other(k, dot(r.mixed[net.slot(k, o)], r.wom[...]))
        total.put_own(k, dot(r.mixed[net.slot(k, c)], r.wom[...]))
    total.far()
    total.near_x()
    total.near_y()
    total.relay()
    for k in (1, 2, 3):
        cots.sibling(k)
    cots.sibling(0)
    total.finish()
    gain2 = r.gain2[...]
    for h in range(2):

        def body(i, h=h):
            rows = pl.ds(pl.multiple_of(h * 128 + i * 32, 32), 32)
            v = r.x[rows, :].astype(F32) + total.total(h, i, 32)
            r.residual[rows, :] = v
            s = lax.rsqrt(jnp.mean(v * v, axis=-1, keepdims=True) + NORM_EPS)
            r.n2[rows, :] = (v * s * gain2).astype(BF)

        loop(4, body)
    for made in feed + row_sums:
        made.wait_recv()
    r.rows_sum[...] = r.rs_all[0] + r.rs_all[1] + r.rs_all[2] + r.rs_all[3]
    spread_end()
    net.drain()


def feed_forward(r):
    net = Net(r.send, r.recv)
    net.greet()
    z, c, o = net.z, net.c, net.o
    acts = Gather(net, r.n2, r.n2_all)
    acts.start()
    mine = net.slot(0, c)
    r.n2_all[mine] = r.n2[...]
    width = r.wmg.shape[2]
    back = Reduce(net, r)

    def gate_up():
        return r.wmg[...].reshape(-1, width), r.wmu[...].reshape(-1, width)

    def down():
        return r.wmd[...].reshape(width, -1)

    def part(k, core):
        slot = net.slot(k, core)
        h = r.n2_all[slot]
        wmg, wmu = gate_up()
        r.ug[...] = dot(h, wmg)
        r.ul[...] = dot(h, wmu)
        r.dh[...] = dot(r.g_all[slot], down(), NT)

        def body(i):
            rows = pl.ds(pl.multiple_of(i * 32, 32), 32)
            gelu, slope = gelu_parts(r.ug[rows, :])
            ul, dh = r.ul[rows, :], r.dh[rows, :]
            r.hid[slot, rows, :] = (gelu * ul).astype(BF)
            r.dgu[slot, rows, 0:width] = (dh * ul * slope).astype(BF)
            r.dgu[slot, rows, width : 2 * width] = (dh * gelu).astype(BF)

        loop(8, body)
        wmg, wmu = gate_up()
        grad = dot(r.dgu[slot, :, 0:width], wmg, NT) + dot(r.dgu[slot, :, width : 2 * width], wmu, NT)
        if core is c:
            back.put_own(k, grad)
        else:
            back.put_other(k, grad)

    part(0, c)
    acts.sibling(0)
    part(0, o)
    acts.forward()
    acts.middle()
    part(1, c)
    part(2, c)
    acts.sibling(1)
    part(1, o)
    acts.sibling(2)
    part(2, o)
    acts.last()
    part(3, c)
    acts.sibling(3)
    part(3, o)
    back.far()
    back.near_x()
    back.near_y()
    back.relay()
    flat = r.dgu[...].reshape(-1, 2 * width)
    for i in range(4):
        rows = r.n2_all[:, :, i * 256 : (i + 1) * 256].reshape(-1, 256)
        r.gm[i] = dot(rows, flat, TN).astype(BF)
    hid = r.hid[...].reshape(-1, width)
    g_flat = r.g_all[...].reshape(hid.shape[0], -1)
    piece = width // 4
    for half in range(2):
        cols = slice(half * 512, half * 512 + 512)
        value = dot(hid, g_flat[:, cols], TN).astype(BF)
        for i in range(4):
            r.gd[i, :, cols] = value[i * piece : (i + 1) * piece, :]
    back.finish()
    gain2 = r.gain2[...]
    sums = jnp.zeros((8, r.n2.shape[1]), F32)
    for h in range(2):

        def body(i, sums, h=h):
            rows = pl.ds(pl.multiple_of(h * 128 + i * 32, 32), 32)
            v = r.residual[rows, :]
            dn = back.total(h, i, 32)
            s = lax.rsqrt(jnp.mean(v * v, axis=-1, keepdims=True) + NORM_EPS)
            u = dn * gain2
            pulled = s * u - v * (s * s * s * jnp.mean(u * v, axis=-1, keepdims=True))
            d_res = r.g[rows, :].astype(F32) + pulled
            r.d_res[rows, :] = d_res
            r.d_out[rows, :] = d_res.astype(BF)
            return sums + jnp.sum((dn * v * s).reshape(4, 8, -1), axis=0)

        sums = lax.fori_loop(0, 4, body, sums)
    r.gain2_sum[...] = sums
    for partner in (net.plane(0, o), net.plane(1, c), net.plane(2, c)):
        pl.semaphore_signal(r.free, inc=1, device_id=partner, device_id_type=pl.DeviceIdType.MESH)
    pl.semaphore_wait(r.free, 3)
    net.drain()
    out = Reduce(net, r)
    for k in (3, 1, 2, 0):
        out.put_other(k, dot(r.hid[net.slot(k, o)], down()))
        out.put_own(k, dot(r.hid[net.slot(k, c)], down()))
    out.far()
    out.near_x()
    out.near_y()
    out.relay()
    out.finish()
    for h in range(2):

        def body(i, h=h):
            rows = pl.ds(pl.multiple_of(h * 128 + i * 32, 32), 32)
            r.block_out[rows, :] = (r.residual[rows, :] + out.total(h, i, 32)).astype(BF)

        loop(4, body)
    net.drain()


def recur_back(r):
    net = Net(r.send, r.recv)
    net.greet()
    p, z, c, o, q = net.p, net.z, net.c, net.o, net.q
    sibling = net.plane(0, o)
    grads = Gather(net, r.d_out, r.do_all)
    grads.start()
    mine = net.slot(0, c)
    r.do_all[mine] = r.d_out[...]

    def line_sum_start(src, dst):
        return [net.copy(src.at[net.up(k)], dst.at[k - 1], net.line(net.up(k), c)) for k in (1, 2, 3)]

    def line_sum_end(copies, src, dst, out):
        for made in copies:
            made.wait_recv()
        rows = out.shape[0]
        step = 32

        def body(i):
            at = pl.ds(pl.multiple_of(i * step, step), step)
            value = src[z, at, :].astype(F32)
            for k in range(3):
                value = value + dst[k, at, :].astype(F32)
            out[at, :] = value.astype(BF)

        loop(rows // step, body)

    mlp_m = line_sum_start(r.gm, r.gm_in)
    mlp_d = line_sum_start(r.gd, r.gd_in)

    def back_out(slot):
        b, half = lax.div(slot, 2), lax.rem(slot, 2)
        dm = dot(r.do_all[slot], r.wo[...], NT)
        for n in range(2):
            r.dconv[b * 2 + n, pl.ds(pl.multiple_of(half * 256, 256), 256), :] = dm[:, n * 128 : (n + 1) * 128]

    back_out(mine)
    grads.sibling(0)
    back_out(net.slot(0, o))
    lane = lax.rem(lax.broadcasted_iota(jnp.int32, (32, 512), 1), 256)
    counted = (lane >= 64 * c) & (lane < 192 + 64 * c)

    def mask_rows(i):
        rows = pl.ds(pl.multiple_of(i * 32, 32), 32)
        r.w2m[rows, :] = jnp.where(counted, r.w2[rows, :].astype(F32), 0.0).astype(BF)

    loop(r.w2.shape[0] // 32, mask_rows)
    grads.forward()
    grads.middle()
    for k in (1, 2):
        back_out(net.slot(k, c))
    for k in (1, 2):
        grads.sibling(k)
        back_out(net.slot(k, o))
    grads.last()
    back_out(net.slot(3, c))
    grads.sibling(3)
    back_out(net.slot(3, o))

    def first_pass(i):
        s, tile = lax.div(i, 8), lax.rem(i, 8)
        b, n = lax.div(s, 2), lax.rem(s, 2)
        rows = tile_rows(tile)
        _, offset = offsets(r, b, z * 512 + tile * TILE, TILE)
        gelu, slope = gelu_parts(r.gp[s, rows, :])
        dm = r.dconv[s, rows, :]
        states = r.states[s, pl.ds(pl.multiple_of(tile * TILE + 8, 8), TILE), :]
        lanes = pl.ds(pl.multiple_of(n * 128, 128), 128)
        r.dgi[b * 2 + lax.div(tile, 4), tile_rows(lax.rem(tile, 4)), lanes] = (dm * states * slope).astype(BF)
        r.drv[s, rows, :] = dm * gelu
        a, _ = decay_parts(r.sr[s, rows, :], r.chan[n, 7:8, :])
        r.dec[s, rows, :] = jnp.where(offset == 0.0, 0.0, a)

    loop(64, first_pass)
    ends = scan_segments(r.dec, r.drv, True)
    entering_states(r, net, ends, True)
    r.vec[...] = jnp.zeros((2, 8, 8, 128), F32)

    def second_pass(s):
        b, n = lax.div(s, 2), lax.rem(s, 2)
        chan = r.chan[n]

        def tile(i, sums):
            rows = tile_rows(i)
            _, offset = offsets(r, b, z * 512 + i * TILE, TILE)
            live = offset != 0.0
            enter = r.ent_s[s, pl.ds(i, 1), :]
            ds = r.drv[s, rows, :] + r.dec[s, rows, :] * enter
            window = r.states[s, pl.ds(pl.multiple_of(i * TILE, 8), TILE + 8), :]
            before = window[7 : TILE + 7, :]
            sr, si = r.sr[s, rows, :], r.si[s, rows, :]
            cv = r.conv[s, rows, :].astype(F32)
            a, m2 = decay_parts(sr, chan[7:8, :])
            inv = lax.rsqrt(m2)
            m = jnp.where(live, m2 * inv, 1.0)
            dsi = ds * si
            d_log = jnp.where(live, a * (ds * before - dsi * cv * a * inv), 0.0)
            lam_term = d_log * sr
            d_r = (-DECAY_SCALE) * chan[7:8, :] * lam_term * (1.0 - sr)
            dm_i = dsi * m
            d_i = dm_i * cv * (1.0 - si)
            d_r, d_i = d_r.astype(BF), d_i.astype(BF)
            r.dri[s, rows, 0:128] = d_r
            r.dri[s, rows, 128:256] = d_i
            r.dconv[s, rows, :] = dm_i
            return (
                sums[0] + column_sum(d_r.astype(F32)),
                sums[1] + column_sum(d_i.astype(F32)),
                sums[2] + column_sum(lam_term),
            )

        zero = jnp.zeros((8, 128), F32)
        sums = lax.fori_loop(0, 512 // TILE, tile, (zero, zero, zero))
        r.vec[n, 5] = r.vec[n, 5] + sums[0]
        r.vec[n, 6] = r.vec[n, 6] + sums[1]
        r.vec[n, 7] = r.vec[n, 7] + sums[2]

    loop(8, second_pass)

    def gate_back(i):
        s, half = lax.div(i, 2), lax.rem(i, 2)
        n = lax.rem(s, 2)
        rows = pl.ds(pl.multiple_of(half * 256, 256), 256)
        r.dconv[s, rows, :] = r.dconv[s, rows, :] + dot(r.dri[s, rows, :], r.wri[n], NT)

    loop(16, gate_back)
    edge = net.reserve(1)

    def edge_copy():
        return net.describe(
            r.dconv.at[:, pl.ds(0, 8)], r.dconv.at[:, pl.ds(512, 8)], net.line(net.down(1), c), edge, edge
        )

    @pl.when(z > 0)
    def _():
        edge_copy().start()

    @pl.when(z == 3)
    def _():
        r.dconv[:, 512:520, :] = jnp.zeros((8, 8, 128), F32)

    for n in range(2):
        total = None
        for b in range(4):
            term = dot(r.conv[b * 2 + n], r.dri[b * 2 + n], TN)
            total = term if total is None else total + term
        r.go[n * 128 : (n + 1) * 128, 1024:1280] = total.astype(BF)
    mixed = r.mixed[...].reshape(-1, 256)
    for half in range(2):
        cols = slice(half * 512, half * 512 + 512)
        r.go[:, cols] = dot(mixed, r.do_all[:, :, cols].reshape(-1, 512), TN).astype(BF)
    go_rows = r.go_in.shape[1]
    own_rows = pl.ds(pl.multiple_of(c * 64, 16), go_rows)
    go_at = net.reserve(3)

    def go_copy(k):
        return net.describe(r.go.at[own_rows], r.go_in.at[k - 1], net.line(p, c), go_at + k - 1, go_at + k - 1)

    for k in (1, 2, 3):

        @pl.when(lax.rem(z + 4 - p, 4) == k)
        def _(k=k):
            go_copy(k).start()

    line_sum_end(mlp_m, r.gm, r.gm_in, r.gm_sum)
    line_sum_end(mlp_d, r.gd, r.gd_in, r.gd_sum)
    owners = []
    half_rows = r.gm_sum.shape[0] // 2
    slot_mine = p * 2 + c

    def to_owners(src, dst):
        for k in (1, 2, 3):
            for core in (c, o):
                rows = pl.ds(pl.multiple_of(core * half_rows, 16), half_rows)
                owners.append(net.copy(src.at[rows], dst.at[slot_mine], net.plane(k, core)))
        theirs = src.at[pl.ds(pl.multiple_of(o * half_rows, 16), half_rows)]
        owners.append(net.copy(theirs, dst.at[slot_mine], sibling))
        dst[slot_mine] = src[pl.ds(pl.multiple_of(c * half_rows, 16), half_rows), :]

    to_owners(r.gm_sum, r.fm)
    r.fd[p] = r.gd_sum[...]
    for k in (1, 2, 3):
        owners.append(net.copy(r.gd_sum, r.fd.at[p], net.plane(k, c)))
    for k in (1, 2, 3):
        for core in (c, o):
            owners.append(
                net.copy(r.rows_sum.at[pl.ds(net.near[k] * 2, 2)], r.fr.at[slot_mine], net.plane(k, core))
            )
    owners.append(net.copy(r.rows_sum.at[pl.ds(p * 2, 2)], r.fr.at[slot_mine], sibling))
    r.fr[slot_mine] = r.rows_sum[pl.ds(p * 2, 2)]

    @pl.when(z < 3)
    def _():
        edge_copy().wait_recv()

    @pl.when(z > 0)
    def _():
        edge_copy().wait_send()

    def conv_back(s):
        b, n = lax.div(s, 2), lax.rem(s, 2)
        chan = r.chan[n]
        lanes = pl.ds(pl.multiple_of(256 + n * 128, 128), 128)

        def tile(i, sums):
            _, offset = offsets(r, b, z * 512 + i * TILE, TILE + 8)
            window = r.dconv[s, pl.ds(pl.multiple_of(i * TILE, 8), TILE + 8), :]
            inner = r.inner[s, pl.ds(pl.multiple_of(i * TILE, 8), TILE + 8), :]
            total = chan[0:1, :] * window[:TILE, :]
            out = [sums[0] + column_sum(window[:TILE, :] * inner[8:, :])]
            for k in (1, 2, 3):
                masked = jnp.where(offset >= k, window, 0.0)
                total = total + chan[k : k + 1, :] * masked[k : TILE + k, :]
                out.append(sums[k] + column_sum(masked[:TILE, :] * inner[8 - k : TILE + 8 - k, :]))
            out.append(sums[4] + column_sum(window[:TILE, :]))
            r.dgi[b * 2 + lax.div(i, 4), tile_rows(lax.rem(i, 4)), lanes] = total.astype(BF)
            return tuple(out)

        sums = lax.fori_loop(0, 512 // TILE, tile, tuple(jnp.zeros((8, 128), F32) for _ in range(5)))
        for j in range(5):
            r.vec[n, j] = r.vec[n, j] + sums[j]

    loop(8, conv_back)
    back = Reduce(net, r)
    for k in (3, 1, 2, 0):
        back.put_other(k, dot(r.dgi[net.slot(k, o)], r.w2m[...], NT))
        back.put_own(k, dot(r.dgi[net.slot(k, c)], r.w2m[...], NT))
    back.far()
    back.near_x()
    back.near_y()
    back.relay()
    flat = r.dgi[...].reshape(-1, 512)
    half_c = pl.ds(pl.multiple_of(c * 128, 128), 128)
    for i in range(4):
        value = dot(r.normed[:, :, i * 256 : (i + 1) * 256].reshape(-1, 256), flat, TN)
        for j in range(2):
            n0, n1 = value[:, j * 256 : j * 256 + 128], value[:, j * 256 + 128 : j * 256 + 256]
            r.ga[i, :, j * 128 : (j + 1) * 128] = lax.select(c == 0, n0, n1).astype(BF)
            shared = lax.select(c == 0, n1, n0)
            mine_rows = lax.select(c == 0, shared[0:128], shared[128:256])
            r.gb2[i, :, j * 128 : (j + 1) * 128] = mine_rows.astype(BF)
    sum_a = line_sum_start(r.ga, r.ga_in)
    sum_b = line_sum_start(r.gb2, r.gb2_in)
    for n in range(2):
        sums = [jnp.sum(r.vec[n, j], axis=0, keepdims=True) for j in range(8)]
        sums[7] = sums[7] * (DECAY_SCALE * r.chan[n, 8:9, :])
        r.vsum[z, :, n * 128 : (n + 1) * 128] = jnp.concatenate(sums, axis=0)
    vec = [net.copy(r.vsum.at[z], r.vsum.at[z], net.line(net.up(k), c)) for k in (1, 2, 3)]
    back.finish()
    gain = r.gain1[...]
    sums = jnp.zeros((8, r.x.shape[1]), F32)
    for h in range(2):

        def body(i, sums, h=h):
            rows = pl.ds(pl.multiple_of(h * 128 + i * 32, 32), 32)
            v = r.x[rows, :].astype(F32)
            dn = back.total(h, i, 32)
            s = lax.rsqrt(jnp.mean(v * v, axis=-1, keepdims=True) + NORM_EPS)
            u = dn * gain
            r.d_in[rows, :] = r.d_res[rows, :] + (
                s * u - v * (s * s * s * jnp.mean(u * v, axis=-1, keepdims=True))
            )
            return sums + jnp.sum((dn * v * s).reshape(4, 8, -1), axis=0)

        sums = lax.fori_loop(0, 4, body, sums)
    gains = jnp.concatenate(
        [
            jnp.sum(sums, axis=0, keepdims=True),
            jnp.sum(r.gain2_sum[...], axis=0, keepdims=True),
            jnp.zeros((6, sums.shape[1]), F32),
        ],
        axis=0,
    )
    for i in range(8):
        r.gsum[i] = gains[:, i * 128 : (i + 1) * 128]
    r.gline[q] = r.gsum[q]
    gain_line = [
        net.copy(r.gsum.at[net.up(k) * 2 + core], r.gline.at[q], net.line(net.up(k), core))
        for k in (1, 2, 3)
        for core in (c, o)
    ]
    gain_line.append(net.copy(r.gsum.at[z * 2 + o], r.gline.at[q], sibling))
    for made in vec:
        made.wait_recv()
    r.vout[p] = r.vsum[0] + r.vsum[1] + r.vsum[2] + r.vsum[3]
    fo_at = net.reserve(6)

    def owner_copies(partners):
        made = []
        for k in partners:
            made.append(net.describe(r.vout.at[p], r.vout.at[p], net.plane(k, c), fo_at + k - 1, fo_at))
            made.append(net.describe(r.fo.at[0], r.fo.at[0], net.plane(k, c), fo_at + 2 + k, fo_at + 3))
        return made

    @pl.when(z == p)
    def _():
        for k in (1, 2, 3):
            go_copy(k).wait_recv()

        def body(i):
            at = pl.ds(pl.multiple_of(i * 16, 16), 16)
            value = r.go[pl.ds(pl.multiple_of(c * 64 + i * 16, 16), 16), :].astype(F32)
            for k in range(3):
                value = value + r.go_in[k, at, :].astype(F32)
            r.fo[0, at, :] = value.astype(BF)

        loop(go_rows // 16, body)
        for made in owner_copies((1, 2, 3)):
            made.start()

    for k in (1, 2, 3):

        @pl.when(lax.rem(z + 4 - p, 4) == k)
        def _(k=k):
            go_copy(k).wait_send()

    line_sum_end(sum_a, r.ga, r.ga_in, r.ga_sum)
    to_owners(r.ga_sum, r.fa)
    line_sum_end(sum_b, r.gb2, r.gb2_in, r.gb2_sum)
    r.fb[p] = r.gb2_sum[...]
    for k in (1, 2, 3):
        owners.append(net.copy(r.gb2_sum, r.fb.at[p], net.plane(k, c)))
    for made in gain_line:
        made.wait_recv()
    total = r.gline[0]
    for i in range(1, 8):
        total = total + r.gline[i]
    r.gplane[p] = total
    gain_plane = [net.copy(r.gplane.at[p], r.gplane.at[p], net.plane(k, c)) for k in (1, 2, 3)]

    @pl.when(z != p)
    def _():
        for made in owner_copies((1,)):
            made.wait_recv()

    @pl.when(z == p)
    def _():
        for made in owner_copies((1, 2, 3)):
            made.wait_send()

    for made in owners + gain_plane:
        made.wait_recv()
    r.gain_out[...] = r.gplane[0] + r.gplane[1] + r.gplane[2] + r.gplane[3]
    r.vec_out[...] = r.vout[z]
    net.drain()


def assemble(r):
    c = lax.rem(lax.axis_index("seq"), 2)
    for chip in range(4):
        for j, out in enumerate((r.o_gate, r.o_in)):
            lanes = slice(j * 128, (j + 1) * 128)
            at = chip * 384
            out[:, at : at + 128] = r.fa[chip * 2, :, lanes].astype(F32)
            out[:, at + 128 : at + 256] = r.fb[chip, :, lanes].astype(F32)
            out[:, at + 256 : at + 384] = r.fa[chip * 2 + 1, :, lanes].astype(F32)
    cols = r.fm.shape[2] // 2
    piece = cols // 4
    for j, out in enumerate((r.o_mgate, r.o_mup)):
        for part in range(4):
            for core in range(2):
                at = (part * 2 + core) * cols
                lanes = slice(j * cols + part * piece, j * cols + (part + 1) * piece)
                out[:, at : at + cols] = jnp.concatenate(
                    [r.fm[chip * 2 + core, :, lanes].astype(F32) for chip in range(4)], axis=1
                )
    for chip in range(4):
        r.o_mdown[chip * piece : (chip + 1) * piece, :] = r.fd[chip].astype(F32)
    r.o_out[...] = r.fo[0, :, 0:1024].astype(F32)
    r.o_r[...] = r.fo[0, :, 1024:1152].astype(F32)
    r.o_i[...] = r.fo[0, :, 1152:1280].astype(F32)
    vec = r.vec_in[...]
    r.o_vec[...] = lax.select(c == 0, vec[:, 0:192], vec[:, 64:256])
    counts = r.starts[...]
    for chip in range(4):
        for half, (slot, n) in enumerate(((chip * 2, 0), (chip * 2, 1), (chip * 2 + 1, 1))):
            at = chip * 384 + half * 128
            r.o_mean[:, at : at + 128] = r.fr[slot, n] / counts[8:16, :]


def shifted(value, axis, by):
    count = lax.axis_size(axis)
    pairs = [(i, i + by) for i in range(count) if 0 <= i + by < count]
    return lax.ppermute(value, axis, pairs)


def entering(value, axis, combine, identity, reverse):
    count, place = (lax.axis_size(axis), lax.axis_index(axis))
    everything = jax.tree.map(lambda part: lax.all_gather(part, axis), value)
    start = jax.tree.map(
        lambda part, zero: jnp.broadcast_to(jnp.asarray(zero, part.dtype), part.shape),
        value,
        identity,
    )

    def step(k, before):
        at = count - 1 - k if reverse else k
        reached = at > place if reverse else at < place
        new = combine(before, jax.tree.map(lambda part: part[at], everything))
        return jax.tree.map(lambda a, b: jnp.where(reached, a, b), new, before)

    return lax.fori_loop(0, count, step, start)


def rms_scale(values):
    return values * lax.rsqrt(jnp.mean(values * values, axis=-1, keepdims=True) + NORM_EPS)


def gelu_tanh(values):
    return jax.nn.gelu(values, approximate=True)


def link(earlier, later):
    return (earlier[0] * later[0], later[0] * earlier[1] + later[1])


def block_product(values, weight):
    count, channels = values.shape
    block_size = weight.shape[1]
    shaped = values.reshape(count, channels // block_size, block_size)
    result = jnp.einsum(
        "lni,nij->lnj",
        shaped,
        weight.reshape(channels // block_size, block_size, block_size),
        preferred_element_type=jnp.float32,
    )
    return result.reshape(count, channels)


def block_back(grads, weight):
    count, channels = grads.shape
    block_size = weight.shape[1]
    shaped = grads.reshape(count, channels // block_size, block_size)
    result = jnp.einsum(
        "lnj,nij->lni",
        shaped,
        weight.reshape(channels // block_size, block_size, block_size),
        preferred_element_type=jnp.float32,
    )
    return result.reshape(count, channels)


def block_weight_grad(values, grads, block_size):
    count, channels = values.shape
    left = values.reshape(count, channels // block_size, block_size)
    right = grads.reshape(count, channels // block_size, block_size)
    return jnp.einsum("lni,lnj->nij", left, right, preferred_element_type=jnp.float32).reshape(
        channels, block_size
    )


def recurrence_terms(conv_in, r_in, i_in, lam_in, restart):
    log_a = -DECAY_SCALE * jax.nn.sigmoid(r_in) * jax.nn.softplus(-lam_in)
    decays = jnp.exp(log_a)
    factor = jnp.where(restart[:, None] > 0, 1.0, jnp.sqrt(-jnp.expm1(2.0 * log_a)))
    return (decays * (1.0 - restart[:, None]), factor * jax.nn.sigmoid(i_in) * conv_in, decays)


def shards(
    inputs,
    out_grad,
    row_lengths,
    norm_gain,
    w_gate,
    w_in,
    conv_w,
    conv_b,
    w_rgate,
    b_rgate,
    w_igate,
    b_igate,
    lam,
    w_out,
    mlp_gain,
    w_mlp_gate,
    w_mlp_up,
    w_mlp_down,
):
    gathered = (
        lax.all_gather(norm_gain, "seq", axis=0, tiled=True),
        lax.all_gather(w_gate, "seq", axis=0, tiled=True),
        lax.all_gather(w_in, "seq", axis=0, tiled=True),
        lax.all_gather(conv_w, "seq", axis=1, tiled=True),
        lax.all_gather(conv_b, "seq", axis=0, tiled=True),
        lax.all_gather(w_rgate, "seq", axis=0, tiled=True),
        lax.all_gather(b_rgate, "seq", axis=0, tiled=True),
        lax.all_gather(w_igate, "seq", axis=0, tiled=True),
        lax.all_gather(b_igate, "seq", axis=0, tiled=True),
        lax.all_gather(lam, "seq", axis=0, tiled=True),
        lax.all_gather(w_out, "seq", axis=0, tiled=True),
        lax.all_gather(mlp_gain, "seq", axis=0, tiled=True),
        lax.all_gather(w_mlp_gate, "seq", axis=0, tiled=True),
        lax.all_gather(w_mlp_up, "seq", axis=0, tiled=True),
        lax.all_gather(w_mlp_down, "seq", axis=0, tiled=True),
    )
    gain_first = gathered[0].astype(jnp.float32)
    conv_taps = gathered[3].astype(jnp.float32)
    conv_bias = gathered[4].astype(jnp.float32)
    lam_value = gathered[9].astype(jnp.float32)
    gain_second = gathered[11].astype(jnp.float32)
    tokens = inputs[0].astype(jnp.float32)
    local_len = tokens.shape[0]
    channels = gathered[2].shape[1]
    block_size = gathered[5].shape[1]
    kernel_taps = conv_taps.shape[0]
    lengths = row_lengths[0]
    row_ends = jnp.cumsum(lengths)
    row_starts = row_ends - lengths
    positions = lax.axis_index("seq") * local_len + jnp.arange(local_len, dtype=jnp.int32)
    started = positions[:, None] >= row_starts[None, :]
    row_index = jnp.sum(started.astype(jnp.int32), axis=1) - 1
    row_first = jnp.max(jnp.where(started, row_starts[None, :], 0), axis=1)
    offset = positions - row_first
    restart = (offset == 0).astype(jnp.float32)
    members = (row_index[:, None] == jnp.arange(lengths.shape[0], dtype=jnp.int32)[None, :]).astype(
        jnp.float32
    )
    tap_masks = [(offset >= tap).astype(jnp.float32)[:, None] for tap in range(kernel_taps)]
    scaled, norm_pull = jax.vjp(rms_scale, tokens)
    normed = (scaled * gain_first).astype(jnp.bfloat16)
    gate_pre = jnp.dot(normed, gathered[1], preferred_element_type=jnp.float32)
    gate_branch, gate_pull = jax.vjp(gelu_tanh, gate_pre)
    inner = jnp.dot(normed, gathered[2], preferred_element_type=jnp.float32).astype(jnp.bfloat16)
    edge_rows = shifted(inner[local_len - kernel_taps + 1 :], "seq", 1)
    extended = jnp.concatenate([edge_rows, inner], axis=0).astype(jnp.float32)
    conv_sum = conv_bias + jnp.zeros((local_len, channels), jnp.float32)
    for tap in range(kernel_taps):
        start_row = kernel_taps - 1 - tap
        conv_sum = (
            conv_sum + conv_taps[tap] * extended[start_row : start_row + local_len] * tap_masks[tap]
        )
    conv_low = conv_sum.astype(jnp.bfloat16)
    conv_value = conv_low.astype(jnp.float32)
    r_pre = block_product(conv_low, gathered[5]) + gathered[6].astype(jnp.float32)
    i_pre = block_product(conv_low, gathered[7]) + gathered[8].astype(jnp.float32)

    def local_terms(conv_in, r_in, i_in, lam_in):
        return recurrence_terms(conv_in, r_in, i_in, lam_in, restart)

    (carried, drive_term, decays), recur_pull = jax.vjp(
        local_terms, conv_value, r_pre, i_pre, lam_value
    )
    prefix_decay, local_state = lax.associative_scan(link, (carried, drive_term), axis=0)
    identity = (jnp.ones((channels,), jnp.float32), jnp.zeros((channels,), jnp.float32))
    incoming = entering((prefix_decay[-1], local_state[-1]), "seq", link, identity, False)[1]
    states = local_state + prefix_decay * incoming
    mixed_low = (states * gate_branch).astype(jnp.bfloat16)
    residual = tokens + jnp.dot(mixed_low, gathered[10], preferred_element_type=jnp.float32)
    scaled_two, norm_pull_two = jax.vjp(rms_scale, residual)
    normed_two = (scaled_two * gain_second).astype(jnp.bfloat16)
    up_gate = jnp.dot(normed_two, gathered[12], preferred_element_type=jnp.float32)
    up_lin = jnp.dot(normed_two, gathered[13], preferred_element_type=jnp.float32)
    gelu_up, up_pull = jax.vjp(gelu_tanh, up_gate)
    hidden = (gelu_up * up_lin).astype(jnp.bfloat16)
    block_out = (
        residual + jnp.dot(hidden, gathered[14], preferred_element_type=jnp.float32)
    ).astype(jnp.bfloat16)
    row_sums = lax.psum(jnp.dot(members.T, decays, precision=lax.Precision.HIGHEST), "seq")
    gate_mean = row_sums / lengths.astype(jnp.float32)[:, None]
    grad_top = out_grad[0]
    grad_mdown = jnp.einsum("tf,td->fd", hidden, grad_top, preferred_element_type=jnp.float32)
    d_hidden = jnp.einsum("td,fd->tf", grad_top, gathered[14], preferred_element_type=jnp.float32)
    d_upgate = up_pull(d_hidden * up_lin)[0].astype(jnp.bfloat16)
    d_uplin = (d_hidden * gelu_up).astype(jnp.bfloat16)
    grad_mgate = jnp.einsum("td,tf->df", normed_two, d_upgate, preferred_element_type=jnp.float32)
    grad_mup = jnp.einsum("td,tf->df", normed_two, d_uplin, preferred_element_type=jnp.float32)
    d_normed_two = jnp.einsum(
        "tf,df->td", d_upgate, gathered[12], preferred_element_type=jnp.float32
    )
    d_normed_two = d_normed_two + jnp.einsum(
        "tf,df->td", d_uplin, gathered[13], preferred_element_type=jnp.float32
    )
    grad_mgain = jnp.sum(d_normed_two * scaled_two, axis=0)
    d_residual = grad_top.astype(jnp.float32) + norm_pull_two(d_normed_two * gain_second)[0]
    d_outlow = d_residual.astype(jnp.bfloat16)
    grad_outw = jnp.einsum("tr,td->rd", mixed_low, d_outlow, preferred_element_type=jnp.float32)
    d_mixed = jnp.einsum("td,rd->tr", d_outlow, gathered[10], preferred_element_type=jnp.float32)
    direct = d_mixed * gate_branch
    d_gatelow = gate_pull(d_mixed * states)[0].astype(jnp.bfloat16)
    grad_gatew = jnp.einsum("td,tr->dr", normed, d_gatelow, preferred_element_type=jnp.float32)
    next_decay = jnp.concatenate([carried[1:], jnp.ones((1, channels), jnp.float32)], axis=0)
    suffix_decay, local_grad = lax.associative_scan(
        link, (next_decay, direct), axis=0, reverse=True
    )
    arriving = entering(
        (carried[0] * suffix_decay[0], carried[0] * local_grad[0]), "seq", link, identity, True
    )[1]
    d_states = local_grad + suffix_decay * arriving
    previous = jnp.concatenate([incoming[None, :], states[:-1]], axis=0)
    grad_convval, d_rpre, d_ipre, grad_lambda = recur_pull(
        (d_states * previous, d_states, jnp.zeros_like(decays))
    )
    d_rlow = d_rpre.astype(jnp.bfloat16)
    d_ilow = d_ipre.astype(jnp.bfloat16)
    grad_rw = block_weight_grad(conv_low, d_rlow, block_size)
    grad_rb = jnp.sum(d_rlow.astype(jnp.float32), axis=0)
    grad_iw = block_weight_grad(conv_low, d_ilow, block_size)
    grad_ib = jnp.sum(d_ilow.astype(jnp.float32), axis=0)
    grad_convsum = grad_convval + block_back(d_rlow, gathered[5]) + block_back(d_ilow, gathered[7])
    grad_cb = jnp.sum(grad_convsum, axis=0)
    conv_again = gathered[3].astype(jnp.float32)
    grad_extended = jnp.zeros((local_len + kernel_taps - 1, channels), jnp.float32)
    tap_grads = []
    for tap in range(kernel_taps):
        start_row = kernel_taps - 1 - tap
        masked = grad_convsum * tap_masks[tap]
        tap_grads.append(jnp.sum(masked * extended[start_row : start_row + local_len], axis=0))
        grad_extended = grad_extended + jnp.pad(
            masked * conv_again[tap], ((start_row, tap), (0, 0))
        )
    grad_cw = jnp.stack(tap_grads)
    edge_grads = shifted(grad_extended[: kernel_taps - 1], "seq", -1)
    d_inner = (
        grad_extended[kernel_taps - 1 :]
        + jnp.pad(edge_grads, ((local_len - kernel_taps + 1, 0), (0, 0)))
    ).astype(jnp.bfloat16)
    grad_inw = jnp.einsum("td,tr->dr", normed, d_inner, preferred_element_type=jnp.float32)
    d_normed = jnp.einsum("tr,dr->td", d_gatelow, gathered[1], preferred_element_type=jnp.float32)
    d_normed = d_normed + jnp.einsum(
        "tr,dr->td", d_inner, gathered[2], preferred_element_type=jnp.float32
    )
    grad_gain = jnp.sum(d_normed * scaled, axis=0)
    d_tokens = d_residual + norm_pull(d_normed * gain_first)[0]
    shares = (
        lax.psum_scatter(grad_gain, "seq", scatter_dimension=0, tiled=True),
        lax.psum_scatter(grad_gatew, "seq", scatter_dimension=0, tiled=True),
        lax.psum_scatter(grad_inw, "seq", scatter_dimension=0, tiled=True),
        lax.psum_scatter(grad_cw, "seq", scatter_dimension=1, tiled=True),
        lax.psum_scatter(grad_cb, "seq", scatter_dimension=0, tiled=True),
        lax.psum_scatter(grad_rw, "seq", scatter_dimension=0, tiled=True),
        lax.psum_scatter(grad_rb, "seq", scatter_dimension=0, tiled=True),
        lax.psum_scatter(grad_iw, "seq", scatter_dimension=0, tiled=True),
        lax.psum_scatter(grad_ib, "seq", scatter_dimension=0, tiled=True),
        lax.psum_scatter(grad_lambda, "seq", scatter_dimension=0, tiled=True),
        lax.psum_scatter(grad_outw, "seq", scatter_dimension=0, tiled=True),
        lax.psum_scatter(grad_mgain, "seq", scatter_dimension=0, tiled=True),
        lax.psum_scatter(grad_mgate, "seq", scatter_dimension=0, tiled=True),
        lax.psum_scatter(grad_mup, "seq", scatter_dimension=0, tiled=True),
        lax.psum_scatter(grad_mdown, "seq", scatter_dimension=0, tiled=True),
    )
    totals = (
        lax.psum(shares[0].astype(jnp.bfloat16), "batch").astype(jnp.float32),
        lax.psum(shares[1].astype(jnp.bfloat16), "batch").astype(jnp.float32),
        lax.psum(shares[2].astype(jnp.bfloat16), "batch").astype(jnp.float32),
        lax.psum(shares[3].astype(jnp.bfloat16), "batch").astype(jnp.float32),
        lax.psum(shares[4].astype(jnp.bfloat16), "batch").astype(jnp.float32),
        lax.psum(shares[5].astype(jnp.bfloat16), "batch").astype(jnp.float32),
        lax.psum(shares[6].astype(jnp.bfloat16), "batch").astype(jnp.float32),
        lax.psum(shares[7].astype(jnp.bfloat16), "batch").astype(jnp.float32),
        lax.psum(shares[8].astype(jnp.bfloat16), "batch").astype(jnp.float32),
        lax.psum(shares[9].astype(jnp.bfloat16), "batch").astype(jnp.float32),
        lax.psum(shares[10].astype(jnp.bfloat16), "batch").astype(jnp.float32),
        lax.psum(shares[11].astype(jnp.bfloat16), "batch").astype(jnp.float32),
        lax.psum(shares[12].astype(jnp.bfloat16), "batch").astype(jnp.float32),
        lax.psum(shares[13].astype(jnp.bfloat16), "batch").astype(jnp.float32),
        lax.psum(shares[14].astype(jnp.bfloat16), "batch").astype(jnp.float32),
    )
    return (
        block_out[None],
        d_tokens[None],
        totals[0],
        totals[1],
        totals[2],
        totals[3],
        totals[4],
        totals[5],
        totals[6],
        totals[7],
        totals[8],
        totals[9],
        totals[10],
        totals[11],
        totals[12],
        totals[13],
        totals[14],
        gate_mean[None],
    )


def pack(row_lengths, norm_gain, conv_w, conv_b, b_rgate, b_igate, lam, mlp_gain):
    lengths = row_lengths[0]
    starts = jnp.cumsum(lengths) - lengths
    column = jnp.concatenate(
        [starts.astype(F32), jnp.zeros((3,), F32), lengths.astype(F32), jnp.ones((3,), F32)]
    )
    lam = lam.astype(F32)
    rows = jnp.concatenate(
        [
            conv_w.astype(F32),
            conv_b.astype(F32)[None],
            b_rgate.astype(F32)[None],
            b_igate.astype(F32)[None],
            jax.nn.softplus(-lam)[None],
            jax.nn.sigmoid(-lam)[None],
        ],
        axis=0,
    )
    rows = jnp.pad(rows, ((0, 1), (0, 64)))
    gains = jnp.concatenate([norm_gain.astype(F32), mlp_gain.astype(F32)])[None]
    small = jnp.concatenate([rows, gains, jnp.zeros((5, 256), F32)], axis=0)
    return small, jnp.broadcast_to(column[:, None], (16, 128))


def planes(
    inputs,
    out_grad,
    row_lengths,
    norm_gain,
    w_gate,
    w_in,
    conv_w,
    conv_b,
    w_rgate,
    b_rgate,
    w_igate,
    b_igate,
    lam,
    w_out,
    mlp_gain,
    w_mlp_gate,
    w_mlp_up,
    w_mlp_down,
):
    small, starts = pack(row_lengths, norm_gain, conv_w, conv_b, b_rgate, b_igate, lam, mlp_gain)
    x, g = inputs[0], out_grad[0]
    vmem = pltpu.VMEM
    front = kernel_call(
        recur_front,
        dict(
            x=x, g=g, small=small, starts=starts, wg=w_gate, wi=w_in, wr=w_rgate, wv=w_igate, wout=w_out,
            wmg=w_mlp_gate, wmu=w_mlp_up, wmd=w_mlp_down,
        ),
        dict(
            normed=array(8, 256, 1024, dtype=BF),
            g_all=array(8, 256, 1024, dtype=BF),
            w2=array(1024, 512, dtype=BF),
            wo=array(256, 1024, dtype=BF),
            wri=array(2, 128, 256, dtype=BF),
            wmg_all=array(8, 128, 384, dtype=BF),
            wmu_all=array(8, 128, 384, dtype=BF),
            wmd_all=array(4, 96, 1024, dtype=BF),
            gp=array(8, 512, 128),
            inner=array(8, 520, 128),
            conv=array(8, 512, 128, dtype=BF),
            sr=array(8, 512, 128),
            si=array(8, 512, 128),
            states=array(8, 520, 128),
            mixed=array(8, 256, 256, dtype=BF),
            residual=array(256, 1024),
            n2=array(256, 1024, dtype=BF),
            chan=array(2, 16, 128),
            starts_all=array(4, 16, 128),
            rows_sum=array(8, 8, 128),
            gain1=array(1, 1024),
            gain2=array(1, 1024),
        ),
        dict(
            x_all=vmem((8, 256, 1024), BF),
            small_all=vmem((8, 16, 256), F32),
            wg3=vmem((8, 128, 384), BF),
            wi3=vmem((8, 128, 384), BF),
            wr3=vmem((2, 192, 128), BF),
            wv3=vmem((2, 192, 128), BF),
            wout3=vmem((2, 192, 1024), BF),
            wom=vmem((256, 1024), BF),
            wmg_out=vmem((2, 128, 384), BF),
            wmu_out=vmem((2, 128, 384), BF),
            gb=vmem((8, 512, 128), F32),
            dec=vmem((8, 512, 128), F32),
            drv=vmem((8, 512, 128), F32),
            ent_p=vmem((8, 8, 128), F32),
            ent_s=vmem((8, 8, 128), F32),
            tot=vmem((4, 2, 8, 128), F32),
            inc=vmem((8, 128), F32),
            rs_all=vmem((4, 8, 8, 128), F32),
            **reduce_scratch(256, 1024),
        ),
        110,
        0,
    )
    feed = kernel_call(
        feed_forward,
        dict(
            n2=front["n2"], g=g, g_all=front["g_all"], residual=front["residual"], gain2=front["gain2"],
            wmg=front["wmg_all"], wmu=front["wmu_all"], wmd=front["wmd_all"],
        ),
        dict(
            block_out=array(256, 1024, dtype=BF),
            d_res=array(256, 1024),
            d_out=array(256, 1024, dtype=BF),
            gain2_sum=array(8, 1024),
            gm=array(4, 256, 768, dtype=BF),
            gd=array(4, 96, 1024, dtype=BF),
        ),
        dict(
            n2_all=vmem((8, 256, 1024), BF),
            ug=vmem((256, 384), F32),
            ul=vmem((256, 384), F32),
            dh=vmem((256, 384), F32),
            hid=vmem((8, 256, 384), BF),
            dgu=vmem((8, 256, 768), BF),
            free=pltpu.SemaphoreType.REGULAR,
            **reduce_scratch(256, 1024),
        ),
        40,
        1,
    )
    back = kernel_call(
        recur_back,
        dict(
            x=x, d_out=feed["d_out"], d_res=feed["d_res"], gain2_sum=feed["gain2_sum"], gm=feed["gm"], gd=feed["gd"],
            **{
                name: front[name]
                for name in (
                    "normed", "w2", "wo", "wri", "gp", "inner", "conv", "sr", "si", "states", "mixed", "chan",
                    "starts_all", "rows_sum", "gain1",
                )
            },
        ),
        dict(
            d_in=array(256, 1024),
            fm=array(8, 128, 768, dtype=BF),
            fd=array(4, 96, 1024, dtype=BF),
            fa=array(8, 128, 256, dtype=BF),
            fb=array(4, 128, 256, dtype=BF),
            fo=array(1, 192, 1280, dtype=BF),
            fr=array(8, 2, 8, 128),
            vec_out=array(8, 256),
            gain_out=array(8, 128),
        ),
        dict(
            do_all=vmem((8, 256, 1024), BF),
            gm_in=vmem((3, 256, 768), BF),
            gd_in=vmem((3, 96, 1024), BF),
            gm_sum=vmem((256, 768), BF),
            gd_sum=vmem((96, 1024), BF),
            w2m=vmem((1024, 512), BF),
            drv=vmem((8, 512, 128), F32),
            dec=vmem((8, 512, 128), F32),
            dri=vmem((8, 512, 256), BF),
            dconv=vmem((8, 520, 128), F32),
            dgi=vmem((8, 256, 512), BF),
            vec=vmem((2, 8, 8, 128), F32),
            vsum=vmem((4, 8, 256), F32),
            vout=vmem((4, 8, 256), F32),
            ent_p=vmem((8, 8, 128), F32),
            ent_s=vmem((8, 8, 128), F32),
            tot=vmem((4, 2, 8, 128), F32),
            inc=vmem((8, 128), F32),
            go=vmem((256, 1280), BF),
            go_in=vmem((3, 192, 1280), BF),
            ga=vmem((4, 256, 256), BF),
            ga_in=vmem((3, 256, 256), BF),
            ga_sum=vmem((256, 256), BF),
            gb2=vmem((4, 128, 256), BF),
            gb2_in=vmem((3, 128, 256), BF),
            gb2_sum=vmem((128, 256), BF),
            gsum=vmem((8, 8, 128), F32),
            gline=vmem((8, 8, 128), F32),
            gplane=vmem((4, 8, 128), F32),
            **reduce_scratch(256, 1024),
        ),
        110,
        2,
    )
    out = kernel_call(
        assemble,
        dict(
            fm=back["fm"], fd=back["fd"], fa=back["fa"], fb=back["fb"], fo=back["fo"], fr=back["fr"],
            vec_in=back["vec_out"], starts=starts,
        ),
        dict(
            o_gate=array(128, 1536),
            o_in=array(128, 1536),
            o_mgate=array(128, 3072),
            o_mup=array(128, 3072),
            o_mdown=array(384, 1024),
            o_out=array(192, 1024),
            o_r=array(192, 128),
            o_i=array(192, 128),
            o_vec=array(8, 192),
            o_mean=array(8, 1536),
        ),
        {},
        0,
        None,
    )
    vec, gains = out["o_vec"], back["gain_out"]
    return (
        feed["block_out"][None],
        back["d_in"][None],
        gains[0],
        out["o_gate"],
        out["o_in"],
        vec[0:4],
        vec[4],
        out["o_r"],
        vec[5],
        out["o_i"],
        vec[6],
        vec[7],
        out["o_out"],
        gains[1],
        out["o_mgate"],
        out["o_mup"],
        out["o_mdown"],
        out["o_mean"][None, 0:5],
    )


def solution(mesh):
    in_specs = (
        P("batch", "seq", None),
        P("batch", "seq", None),
        P("batch", None),
        P("seq"),
        P("seq", None),
        P("seq", None),
        P(None, "seq"),
        P("seq"),
        P("seq", None),
        P("seq"),
        P("seq", None),
        P("seq"),
        P("seq"),
        P("seq", None),
        P("seq"),
        P("seq", None),
        P("seq", None),
        P("seq", None),
    )
    out_specs = (
        P("batch", "seq", None),
        P("batch", "seq", None),
        P("seq"),
        P("seq", None),
        P("seq", None),
        P(None, "seq"),
        P("seq"),
        P("seq", None),
        P("seq"),
        P("seq", None),
        P("seq"),
        P("seq"),
        P("seq", None),
        P("seq"),
        P("seq", None),
        P("seq", None),
        P("seq", None),
        P("batch", None, None),
    )
    in_planes = mesh.shape["batch"] == 4 and mesh.shape["seq"] == 8
    body = planes if in_planes else shards
    return jax.shard_map(body, mesh=mesh, in_specs=in_specs, out_specs=out_specs, check_vma=False)
```

```python
import functools
import types

import jax
import jax.numpy as jnp
from jax import lax
from jax.experimental import pallas as pl
from jax.experimental.pallas import tpu as pltpu
from jax.sharding import PartitionSpec as P

NORM_EPS = 1e-06
DECAY_SCALE = 8.0
BF = jnp.bfloat16
F32 = jnp.float32
GELU_SCALE = 0.7978845608028654
GELU_CUBE = 0.044715
TILE = 64
NN = (((1,), (0,)), ((), ()))
NT = (((1,), (1,)), ((), ()))
TN = (((0,), (0,)), ((), ()))


def dot(left, right, dims=NN):
    return lax.dot_general(left, right, dims, preferred_element_type=F32)


def loop(count, body):
    def step(i, carry):
        body(i)
        return carry

    lax.fori_loop(0, count, step, 0)


class Net:
    def __init__(self, r):
        self.send, self.recv, self.count = r.send, r.recv, 0
        self.here, self.here_count = r.local, 0
        self.pending = []
        self.p = lax.axis_index("batch")
        self.q = lax.axis_index("seq")
        self.z = lax.div(self.q, 2)
        self.c = lax.rem(self.q, 2)
        self.o = 1 - self.c
        p = self.p
        self.near = (p, p + 1 - 2 * lax.rem(p, 2), lax.rem(p + 2, 4), 3 - p)

    def plane(self, k, core):
        return {"batch": self.near[k], "seq": self.z * 2 + core}

    def line(self, z, core):
        return {"batch": self.p, "seq": z * 2 + core}

    def up(self, k):
        return lax.rem(self.z + k, 4)

    def down(self, k):
        return lax.rem(self.z + 4 - k, 4)

    def slot(self, k, core):
        return self.near[k] * 2 + core

    def greet(self):
        barrier = pltpu.get_barrier_semaphore()
        partners = [self.plane(k, core) for k in (1, 2, 3) for core in (0, 1)]
        partners += [self.line(self.up(k), core) for k in (1, 2, 3) for core in (0, 1)]
        partners += [self.line(self.z, self.o)]
        for partner in partners:
            pl.semaphore_signal(barrier, inc=1, device_id=partner, device_id_type=pl.DeviceIdType.MESH)
        pl.semaphore_wait(barrier, len(partners))

    def reserve(self, count):
        first = self.count
        self.count += count
        return first

    def describe(self, src, dst, device, send_at, recv_at):
        return pltpu.make_async_remote_copy(
            src_ref=src,
            dst_ref=dst,
            send_sem=self.send.at[send_at],
            recv_sem=self.recv.at[recv_at],
            device_id=device,
            device_id_type=pl.DeviceIdType.MESH,
        )

    def copy(self, src, dst, device, sent=None):
        at = self.reserve(1)
        made = self.describe(src, dst, device, at, at)
        made.start()
        (self.pending if sent is None else sent).append(made)
        return made

    def local(self, src, dst):
        made = pltpu.make_async_copy(src, dst, self.here.at[self.here_count])
        self.here_count += 1
        made.start()
        return made

    def drain(self):
        assert (self.count, self.here_count) == (self.send.shape[0], self.here.shape[0]), (self.count, self.here_count)
        for made in self.pending:
            made.wait_send()
        self.pending = []


class Gather:
    def __init__(self, net, own, everything):
        self.net, self.own, self.all = net, own, everything
        self.sent = []
        self.half = everything.shape[1] // 2

    def part(self, slot, h):
        return self.all.at[slot, pl.ds(h * self.half, self.half)]

    def start(self):
        net = self.net
        mine = net.slot(0, net.c)
        low, high = self.own.at[pl.ds(0, self.half)], self.own.at[pl.ds(self.half, self.half)]
        self.s = []
        self.x0 = net.copy(low, self.part(mine, 0), net.plane(1, net.c), self.sent)
        self.y1 = net.copy(high, self.part(mine, 1), net.plane(2, net.c), self.sent)
        self.x1 = net.copy(high, self.part(mine, 1), net.plane(1, net.c), self.sent)
        self.y0 = net.copy(low, self.part(mine, 0), net.plane(2, net.c), self.sent)
        self.s.append(net.copy(self.own, self.all.at[mine], net.plane(0, net.o), self.sent))

    def forward(self):
        net = self.net
        self.x0.wait_recv()
        mine = self.part(net.slot(1, net.c), 0)
        self.d0 = net.copy(mine, mine, net.plane(2, net.c), self.sent)
        self.y1.wait_recv()
        mine = self.part(net.slot(2, net.c), 1)
        self.d1 = net.copy(mine, mine, net.plane(1, net.c), self.sent)

    def across(self, k):
        net = self.net
        mine = self.all.at[net.slot(k, net.c)]
        self.s.append(net.copy(mine, mine, net.plane(0, net.o), self.sent))

    def middle(self):
        self.x1.wait_recv()
        self.across(1)
        self.y0.wait_recv()
        self.across(2)

    def last(self):
        self.d0.wait_recv()
        self.d1.wait_recv()
        self.across(3)

    def sibling(self, k):
        self.s[k].wait_recv()

    def release(self):
        for made in self.sent:
            made.wait_send()
        self.sent = []


class LineGather:
    def __init__(self, net, own, first, place):
        self.net, self.own, self.first, self.place = net, own, first, place
        self.at = net.reserve(4 * len(own))

    def made(self, k, j):
        net = self.net
        src, core = self.own[j]
        at = self.at + 4 * j + k - 1
        return net.describe(src, self.first(j), net.line(net.up(k), core), at, at)

    def handed(self, j):
        net = self.net
        far = 6 - 3 * net.z
        here = self.place(j, far)
        at = self.at + 4 * j
        return net.describe(here, here, net.line(3 - far, net.c), at + 3, at + 2 * net.z - 2)

    def direct(self, k, body):
        z = self.net.z
        if k == 2:
            body()
        else:
            pl.when(z != (0 if k == 3 else 3))(body)

    def start(self, k, items):
        def send():
            for j in items:
                self.made(k, j).start()

        self.direct(k, send)

    def inside(self, body):
        z = self.net.z
        pl.when((z == 1) | (z == 2))(body)

    def relay(self):
        @self.inside
        def _():
            for j in range(len(self.own)):
                self.made(2, j).wait_recv()
                self.handed(j).start()

    def end(self):
        z = self.net.z
        for k in (1, 3):
            for j in range(len(self.own)):
                self.made(k, j).wait_recv()

        @pl.when((z == 0) | (z == 3))
        def _():
            for j in range(len(self.own)):
                self.made(2, j).wait_recv()

    def drain(self):
        for k in (1, 2, 3):

            def wait(k=k):
                for j in range(len(self.own)):
                    self.made(k, j).wait_send()

            self.direct(k, wait)

        @self.inside
        def _():
            for j in range(len(self.own)):
                self.handed(j).wait_send()


class LineSum:
    def __init__(self, net, block, slot):
        self.net, self.block, self.slot = net, block, slot
        self.at = net.reserve(3)

    def made(self, k):
        net = self.net
        at = self.at + k - 1
        to = lax.rem(2 * net.z + 1, 5) if k == 2 else net.up(k)
        return net.describe(self.block(net.up(k)), self.slot(k), net.line(to, net.c), at, at)

    def start(self):
        z = self.net.z
        self.made(2).start()
        pl.when(z != 1)(lambda: self.made(1).start())
        pl.when(z != 2)(lambda: self.made(3).start())

    def relay(self, step=16):
        z = self.net.z

        @pl.when((z == 1) | (z == 2))
        def _():
            self.made(2).wait_recv()
            mine, extra = self.block(3 - z), self.slot(2)

            def body(i):
                rows = pl.ds(pl.multiple_of(i * step, step), step)
                mine[rows, :] = (mine[rows, :].astype(F32) + extra[rows, :].astype(F32)).astype(BF)

            loop(mine.shape[0] // step, body)

        pl.when(z == 1)(lambda: self.made(1).start())
        pl.when(z == 2)(lambda: self.made(3).start())

    def end(self, dst, step=16):
        z = self.net.z
        self.made(1).wait_recv()
        self.made(3).wait_recv()
        edge = (z == 0) | (z == 3)
        pl.when(edge)(lambda: self.made(2).wait_recv())
        share = jnp.where(edge, 1.0, 0.0)
        own = self.block(z)

        def body(i):
            rows = pl.ds(pl.multiple_of(i * step, step), step)
            value = own[rows, :].astype(F32) + share * self.slot(2)[rows, :].astype(F32)
            value = value + self.slot(1)[rows, :].astype(F32) + self.slot(3)[rows, :].astype(F32)
            dst[rows, :] = value.astype(BF)

        loop(dst.shape[0] // step, body)

    def drain(self):
        for k in (1, 2, 3):
            self.made(k).wait_send()


class Reduce:
    def __init__(self, net, r, value):
        self.net, self.value = net, value
        self.keep, self.out, self.into = r.rs_keep, r.rs_out, r.rs_in
        self.xs, self.ys, self.xr, self.yr = r.rs_xs, r.rs_ys, r.rs_xr, r.rs_yr
        self.half = self.keep.shape[1]
        self.cross = [None] * 4
        self.sent = []

    def other(self, k):
        net = self.net
        self.out[k] = self.value(k, net.o).astype(BF)
        self.cross[k] = net.copy(self.out.at[k], self.into.at[k], net.plane(0, net.o), self.sent)

    def mine(self, k):
        self.cross[k].wait_recv()
        value = self.value(k, self.net.c) + self.into[k].astype(F32)
        return value[: self.half], value[self.half :]

    def send(self, src, dst, j, k):
        net = self.net
        return net.copy(src.at[j], dst.at[j], net.plane(k, net.c), self.sent)

    def far(self):
        low, high = self.mine(3)
        self.xs[0] = low.astype(BF)
        self.x0 = self.send(self.xs, self.xr, 0, 1)
        self.ys[0] = high.astype(BF)
        self.y0 = self.send(self.ys, self.yr, 0, 2)

    def near(self):
        low, high = self.mine(1)
        self.xs[1] = low.astype(BF)
        self.x1 = self.send(self.xs, self.xr, 1, 1)
        self.keep[2] = high
        low, high = self.mine(2)
        self.ys[1] = high.astype(BF)
        self.y1 = self.send(self.ys, self.yr, 1, 2)
        self.keep[3] = low

    def relay(self):
        self.x0.wait_recv()
        self.ys[2] = (self.keep[3] + self.xr[0].astype(F32)).astype(BF)
        self.y2 = self.send(self.ys, self.yr, 2, 2)
        self.y0.wait_recv()
        self.xs[2] = (self.keep[2] + self.yr[0].astype(F32)).astype(BF)
        self.x2 = self.send(self.xs, self.xr, 2, 1)

    def own(self):
        self.keep[0], self.keep[1] = self.mine(0)

    def finish(self):
        for made in (self.x1, self.y1, self.x2, self.y2):
            made.wait_recv()
        for made in self.sent:
            made.wait_send()
        self.sent = []

    def total(self, h, i, step):
        rows = pl.ds(pl.multiple_of(i * step, step), step)
        first, second = (self.xr, self.yr) if h == 0 else (self.yr, self.xr)
        return self.keep[h, rows, :] + first[1, rows, :].astype(F32) + second[2, rows, :].astype(F32)


def reduce_scratch(rows, width):
    half = rows // 2
    return dict(
        rs_keep=pltpu.VMEM((4, half, width), F32),
        rs_out=pltpu.VMEM((4, rows, width), BF),
        rs_in=pltpu.VMEM((4, rows, width), BF),
        rs_xs=pltpu.VMEM((3, half, width), BF),
        rs_ys=pltpu.VMEM((3, half, width), BF),
        rs_xr=pltpu.VMEM((3, half, width), BF),
        rs_yr=pltpu.VMEM((3, half, width), BF),
    )


def kernel_call(body, ins, outs, scratch, copies, local, far):
    names = list(ins) + list(outs) + list(scratch)
    near = pl.BlockSpec(memory_space=pltpu.VMEM)
    away = pl.BlockSpec(memory_space=pl.ANY)
    shapes = list(scratch.values())
    if copies:
        names += ["send", "recv", "local"]
        shapes += [pltpu.SemaphoreType.DMA((n,)) for n in (copies, copies, local)]

    def kernel(*refs):
        body(types.SimpleNamespace(**dict(zip(names, refs))))

    params = dict(vmem_limit_bytes=62 * 2**20)
    if copies:
        params.update(collective_id=0, has_side_effects=True)
    results = pl.pallas_call(
        kernel,
        out_shape=list(outs.values()),
        in_specs=[away if name in far else near for name in ins],
        out_specs=[away if name in far else near for name in outs],
        scratch_shapes=shapes,
        compiler_params=pltpu.CompilerParams(**params),
        name=body.__name__,
    )(*ins.values())
    return dict(zip(outs, results))


def array(*shape, dtype=F32):
    return jax.ShapeDtypeStruct(shape, dtype)


def gelu_parts(v):
    square = v * v
    t = jnp.tanh(GELU_SCALE * v * (1.0 + GELU_CUBE * square))
    half = 0.5 + 0.5 * t
    slope = half + 0.5 * v * (1.0 - t * t) * (GELU_SCALE * (1.0 + 3.0 * GELU_CUBE * square))
    return v * half, slope


def decay_parts(sr, rate):
    log_a = -DECAY_SCALE * sr * rate
    a = jnp.exp(log_a)
    y = 2.0 * log_a
    series = 1.0 + y * (1 / 6) * (1.0 + y * (1 / 7))
    for n in (5, 4, 3, 2):
        series = 1.0 + y * (1 / n) * series
    m2 = jnp.where(y > -0.35, -y * series, 1.0 - a * a)
    return a, jnp.maximum(m2, 1e-36)


def column_sum(value):
    return jnp.sum(value.reshape(-1, 8, 128), axis=0)


def scan_slabs(decay, value, reverse):
    count = decay.shape[1] // 8
    row = lax.broadcasted_iota(jnp.int32, (8, 128), 0)

    def step(i, carry):
        t = count - 1 - i if reverse else i
        at = pl.ds(pl.multiple_of(t * 8, 8), 8)
        done = []
        for s in range(8):
            pc, vc = carry[s]
            p, own = decay[s, at, :], value[s, at, :]
            v = p * own if reverse else own
            for d in (1, 2, 4):
                by = 8 - d if reverse else d
                inside = row < 8 - d if reverse else row >= d
                v = v + p * jnp.where(inside, pltpu.roll(v, by, 0), 0.0)
                p = p * jnp.where(inside, pltpu.roll(p, by, 0), 1.0)
            v = v + p * vc
            p = p * pc
            if reverse:
                edge = row == 7
                value[s, at, :] = own + jnp.where(edge, vc, pltpu.roll(v, 7, 0))
                decay[s, at, :] = jnp.where(edge, pc, pltpu.roll(p, 7, 0))
                last = slice(0, 1)
            else:
                value[s, at, :] = v
                decay[s, at, :] = p
                last = slice(7, 8)
            done.append((jnp.broadcast_to(p[last], (8, 128)), jnp.broadcast_to(v[last], (8, 128))))
        return tuple(done)

    start = tuple((jnp.ones((8, 128), F32), jnp.zeros((8, 128), F32)) for _ in range(8))
    return lax.fori_loop(0, count, step, start)


def exchange_ends(r, net, ends, at):
    for s in range(8):
        r.tot[at, net.z, 0, s : s + 1, :] = ends[s][0][0:1, :]
        r.tot[at, net.z, 1, s : s + 1, :] = ends[s][1][0:1, :]
    mine = r.tot.at[at, net.z]
    return [net.copy(mine, mine, net.line(net.up(k), net.c)) for k in (1, 2, 3)]


def entering_states(r, net, copies, at, reverse):
    for made in copies:
        made.wait_recv()
    state = jnp.zeros((8, 128), F32)
    for i in range(4):
        z = 3 - i if reverse else i
        new = r.tot[at, z, 0] * state + r.tot[at, z, 1]
        state = jnp.where((z > net.z) if reverse else (z < net.z), new, state)
    r.inc[...] = state


def tile_rows(i):
    return pl.ds(pl.multiple_of(i * TILE, TILE), TILE)


def layer(r):
    r.do_all = r.x_all
    r.dconv = r.gb
    r.dgi = r.dgu
    r.ug, r.ul = r.d_res.at[:, 0:384], r.d_res.at[:, 384:768]
    r.ga = [r.hid.at[i, :, 0:256] for i in range(4)]
    r.gb2 = [r.hid.at[4 + i, 0:128, 0:256] for i in range(4)]
    net = Net(r)
    p, z, c, o, q = net.p, net.z, net.c, net.o, net.q
    sibling = net.plane(0, o)
    mine = net.slot(0, c)
    cols = r.wgu_out.shape[2]
    piece = cols // 4
    down = pl.ds(pl.multiple_of(p * piece, 16), piece)
    quarter = pl.ds(pl.multiple_of(p * 48, 16), 48)
    staged = []
    for j in range(8):
        lanes = pl.ds(j * cols, cols)
        staged.append(net.local(r.wmg.at[:, lanes], r.hid.at[j, pl.ds(0, 128)]))
        staged.append(net.local(r.wmu.at[:, lanes], r.hid.at[j, pl.ds(128, 128)]))
    width = 3 * 128
    first = pl.multiple_of(p * width, 128)
    chip = pl.ds(first, width)
    own_lanes = pl.ds(pl.multiple_of(c * width, 128), width)
    wi_rows, wg_rows = pl.ds(128, 128), pl.ds(0, 128)
    placed = [
        net.local(r.wg.at[:, chip], r.wgi3.at[z, wg_rows, own_lanes]),
        net.local(r.wi.at[:, chip], r.wgi3.at[z, wi_rows, own_lanes]),
        net.local(r.wmd.at[down], r.wmd_all.at[z]),
        net.local(r.wout.at[quarter], r.wq.at[z]),
        net.local(r.wr.at[quarter], r.gq.at[z, :, pl.ds(0, 128)]),
        net.local(r.wv.at[quarter], r.gq.at[z, :, pl.ds(128, 128)]),
        net.local(r.g, r.g_all.at[mine]),
    ]
    r.lens_out[0:1, 0:5] = r.lens[...].astype(F32)
    net.greet()
    r.small_all[q] = r.small[...]
    r.lens_all[p] = r.lens_out[...]
    small = [net.copy(r.small, r.small_all.at[q], net.line(net.up(k), core)) for k in (1, 2, 3) for core in (c, o)]
    small.append(net.copy(r.small, r.small_all.at[q], sibling))
    lens = [net.copy(r.lens_out, r.lens_all.at[p], net.plane(k, c)) for k in (1, 2, 3)]
    tokens = Gather(net, r.x, r.x_all)
    tokens.start()
    theirs = pl.ds(pl.multiple_of(c * width + o * 128, 128), 256)

    def along(ref, sent=None):
        return [net.copy(ref, ref, net.line(net.up(k), c), sent) for k in (1, 2, 3)]

    handed = []

    def heads_start(rows):
        here = r.wgi3.at[z, rows, theirs]
        return along(r.wgi3.at[z, rows, own_lanes], handed), [net.copy(here, here, sibling, handed)]

    for made in placed:
        made.wait()
    heads_in, heads_in_over = heads_start(wi_rows)
    gates_in = along(r.gq.at[z])

    def hand_over(copies, rows, over):
        for k in (1, 2, 3):
            copies[k - 1].wait_recv()
            here = r.wgi3.at[net.down(k), rows, theirs]
            over.append(net.copy(here, here, sibling, handed))

    def arrange(over, rows, lanes):
        for made in over:
            made.wait_recv()
        for core in range(2):
            cols_in = pl.ds(pl.multiple_of(core * width + c * 128, 128), 256)
            for at in range(4):
                to = slice((at * 2 + core) * 128, (at * 2 + core + 1) * 128)
                r.w2[to, lanes] = r.wgi3[at, rows, cols_in]

    def exchange(arrivals, src, dst):
        for made in arrivals:
            made.wait_recv()
        dst[c, quarter, :] = src[p]
        return [net.copy(src.at[net.near[k]], dst.at[c, quarter], net.plane(k, c)) for k in (1, 2, 3)]

    def share(copies, dst):
        for made in copies:
            made.wait_recv()
        return net.copy(dst.at[c], dst.at[c], sibling)

    selects = []
    k_at = lax.broadcasted_iota(jnp.int32, (cols, cols), 0)
    j_at = lax.broadcasted_iota(jnp.int32, (cols, cols), 1)
    for part in range(4):
        inside = (j_at >= part * piece) & (j_at < (part + 1) * piece)
        chosen = inside & (k_at == j_at + (p - part) * piece)
        selects.append(jnp.where(chosen, 1.0, 0.0).astype(BF))
    for made in staged:
        made.wait()
    for which in range(2):
        rows = slice(which * 128, (which + 1) * 128)
        for core in (0, 1):
            picked = None
            for part in range(4):
                term = dot(r.hid[part * 2 + core, rows, :], selects[part])
                picked = term if picked is None else picked + term
            r.wgu_out[core, rows, :] = picked.astype(BF)
    for made in small + lens:
        made.wait_recv()
    low, high = r.small_all[2 * p].astype(F32), r.small_all[2 * p + 1].astype(F32)
    at_first = jnp.concatenate([low[:, :192], high[:, :64]], axis=1)
    at_second = jnp.concatenate([low[:, 128:192], high[:, :192]], axis=1)
    both = lax.select(c == 0, at_first, at_second)
    for n in range(2):
        r.chan[n] = both[:, n * 128 : (n + 1) * 128]
        lam = -r.chan[n, 7:8, :]
        e = jnp.exp(-jnp.abs(lam))
        series = 1.0 - e * (6 / 7)
        for k in (6, 5, 4, 3, 2):
            series = 1.0 - e * ((k - 1) / k) * series
        rate = jnp.maximum(lam, 0.0) + jnp.where(e < 0.05, e * series, jnp.log(1.0 + e))
        r.chan[n, 7:8, :] = rate
        r.chan[n, 8:9, :] = jax.nn.sigmoid(lam)
    for i in range(8):
        gains = r.small_all[i].astype(F32)[10:11, :]
        r.gain[0:1, i * 128 : (i + 1) * 128] = gains[:, 0:128]
        r.gain[1:2, i * 128 : (i + 1) * 128] = gains[:, 128:256]
    gain = r.gain[0:1, :]
    for b in range(4):
        start = jnp.zeros((1, 128), F32)
        for row in range(5):
            r.starts_all[b, row : row + 1, :] = start
            start = start + jnp.broadcast_to(r.lens_all[b, 0:1, row : row + 1], (1, 128))


    def offset_rows(i):
        b, tile = lax.div(i, 13), lax.rem(i, 13)
        starts = r.starts_all[b]
        at = lax.convert_element_type(z * 512 + tile * 40, F32)
        at = at + lax.broadcasted_iota(jnp.int32, (40, 128), 0).astype(F32)
        begun = jnp.zeros((40, 128), F32)
        for row in range(1, 5):
            start = starts[row : row + 1, :]
            begun = jnp.where(at >= start, start, begun)
        r.off[b, pl.ds(pl.multiple_of(tile * 40, 8), 40), :] = at - begun

    loop(52, offset_rows)

    def normalise(slot):
        def body(i):
            rows = pl.ds(pl.multiple_of(i * 32, 32), 32)
            v = r.x_all[slot, rows, :].astype(F32)
            s = lax.rsqrt(jnp.mean(v * v, axis=-1, keepdims=True) + NORM_EPS)
            r.normed[slot, rows, :] = (v * s * gain).astype(BF)

        loop(8, body)

    r.x_all[mine] = r.x[...]
    normalise(mine)
    tokens.sibling(0)
    normalise(net.slot(0, o))
    tokens.forward()
    out_in = along(r.wq.at[z])
    heads_gate, heads_gate_over = heads_start(wg_rows)
    hand_over(heads_in, wi_rows, heads_in_over)
    tokens.middle()
    gates_out = exchange(gates_in, r.gq, r.g3)
    for k in (1, 2):
        normalise(net.slot(k, c))
    for k in (1, 2):
        tokens.sibling(k)
        normalise(net.slot(k, o))
    arrange(heads_in_over, slice(128, 256), slice(256, 512))

    def project_inner(slot):
        b, half = lax.div(slot, 2), lax.rem(slot, 2)
        at = pl.multiple_of(half * 256, 256)
        inner = dot(r.normed[slot], r.w2[:, 256:512]).astype(BF).astype(F32)
        for n in range(2):
            r.inner[b * 2 + n, pl.ds(at + 8, 256), :] = inner[:, n * 128 : (n + 1) * 128]

    def project_gate(slot):
        b, half = lax.div(slot, 2), lax.rem(slot, 2)
        at = pl.multiple_of(half * 256, 256)
        gate = dot(r.normed[slot], r.w2[:, 0:256])
        for n in range(2):
            r.gp[b * 2 + n, pl.ds(at, 256), :] = gate[:, n * 128 : (n + 1) * 128]

    for k in (0, 1, 2):
        project_inner(net.slot(k, c))
        project_inner(net.slot(k, o))
    tokens.last()
    normalise(net.slot(3, c))
    project_inner(net.slot(3, c))
    tokens.sibling(3)
    normalise(net.slot(3, o))
    project_inner(net.slot(3, o))
    edge = net.reserve(1)

    def edge_copy():
        return net.describe(
            r.inner.at[:, pl.ds(512, 8)], r.inner.at[:, pl.ds(0, 8)], net.line(net.up(1), c), edge, edge
        )

    @pl.when(z < 3)
    def _():
        edge_copy().start()

    @pl.when(z == 0)
    def _():
        r.inner[:, 0:8, :] = jnp.zeros((8, 8, 128), F32)

    gates_over = share(gates_out, r.g3)
    stored = net.local(r.normed, r.normed_far)
    tokens.release()
    gates_over.wait_recv()
    for i in range(4):
        at = c * 128 + i * 64
        value = r.g3[lax.div(at, 192), pl.ds(pl.multiple_of(lax.rem(at, 192), 64), 64), :]
        r.wri[i // 2, (i % 2) * 64 : (i % 2 + 1) * 64, :] = value

    @pl.when(z > 0)
    def _():
        edge_copy().wait_recv()


    def conv_tile(i):
        b, tile = lax.div(i, 8), lax.rem(i, 8)
        rows = tile_rows(tile)
        offset = r.off[b, rows, :]
        for n in range(2):
            s = b * 2 + n
            window = r.inner[s, pl.ds(pl.multiple_of(tile * TILE, 8), TILE + 8), :]
            chan = r.chan[n]
            total = chan[4:5, :] + chan[0:1, :] * window[8:, :]
            for k in (1, 2, 3):
                total = total + chan[k : k + 1, :] * jnp.where(offset >= k, window[8 - k : TILE + 8 - k, :], 0.0)
            r.conv[s, rows, :] = total.astype(BF)

    loop(32, conv_tile)
    feed = LineGather(
        net,
        [(r.wgu_out.at[core], core) for core in (c, o)],
        lambda j: r.wgu_all.at[q],
        lambda j, at: r.wgu_all.at[at * 2 + (c, o)[j]],
    )
    feed_down = LineGather(net, [(r.wmd.at[down], c)], lambda j: r.wmd_all.at[z], lambda j, at: r.wmd_all.at[at])
    feed.start(2, (0,))
    out_rows_in = exchange(out_in, r.wq, r.w3)
    cots = Gather(net, r.g_all.at[mine], r.g_all)
    cots.start()

    def gate_products(i):
        s, half = lax.div(i, 2), lax.rem(i, 2)
        n = lax.rem(s, 2)
        rows = pl.ds(pl.multiple_of(half * 256, 256), 256)
        pre = dot(r.conv[s, rows, :], r.wri[n])
        r.sr[s, rows, :] = pre[:, :128]
        r.si[s, rows, :] = pre[:, 128:]

    loop(16, gate_products)

    def terms(b):
        starts_b = r.starts_all[b]

        def tile(i, sums):
            rows = tile_rows(i)
            offset = r.off[b, rows, :]
            at = lax.convert_element_type(z * 512 + i * TILE, F32)
            begun = at + lax.broadcasted_iota(jnp.int32, (TILE, 128), 0).astype(F32) - offset
            restart = offset == 0.0
            added = []
            for n in range(2):
                s = b * 2 + n
                chan = r.chan[n]
                sr = jax.nn.sigmoid(r.sr[s, rows, :] + chan[5:6, :])
                si = jax.nn.sigmoid(r.si[s, rows, :] + chan[6:7, :])
                r.sr[s, rows, :] = sr
                r.si[s, rows, :] = si
                a, m2 = decay_parts(sr, chan[7:8, :])
                r.dec[s, rows, :] = jnp.where(restart, 0.0, a)
                m = jnp.where(restart, 1.0, jnp.sqrt(m2))
                r.drv[s, rows, :] = m * si * r.conv[s, rows, :].astype(F32)
                for row in range(5):
                    inside = jnp.where(begun == starts_b[row : row + 1, :], a, 0.0)
                    added.append(sums[n * 5 + row] + column_sum(inside))
            return tuple(added)

        sums = lax.fori_loop(0, 512 // TILE, tile, tuple(jnp.zeros((8, 128), F32) for _ in range(10)))
        for n in range(2):
            rows = [jnp.sum(part, axis=0, keepdims=True) for part in sums[n * 5 : n * 5 + 5]]
            r.rs_all[z, b * 2 + n] = jnp.concatenate(rows + [jnp.zeros((3, 128), F32)], axis=0)

    loop(4, terms)
    ends = scan_slabs(r.dec, r.drv, False)
    ends = exchange_ends(r, net, ends, 0)
    feed.start(2, (1,))
    feed.start(1, (0, 1))
    feed.start(3, (0, 1))
    r.wgu_all[q] = r.wgu_out[c]
    feed_over = net.copy(r.wgu_out.at[o], r.wgu_all.at[q], sibling)
    hand_over(heads_gate, wg_rows, heads_gate_over)
    cots.forward()
    arrange(heads_gate_over, slice(0, 128), slice(0, 256))
    for made in handed:
        made.wait_send()
    for k in (2, 1, 3):
        feed_down.start(k, (0,))
    for slot in range(8):
        project_gate(slot)

    def gelu_tile(i):
        s, rows = lax.div(i, 8), tile_rows(lax.rem(i, 8))
        v = r.gp[s, rows, :]
        t = jnp.tanh(GELU_SCALE * v * (1.0 + GELU_CUBE * v * v))
        r.gb[s, rows, :] = 0.5 * v * (1.0 + t)

    loop(64, gelu_tile)
    out_over = share(out_rows_in, r.w3)
    entering_states(r, net, ends, 0, False)
    row_sums = [net.copy(r.rs_all.at[z], r.rs_all.at[z], net.line(net.up(k), c)) for k in (1, 2, 3)]
    out_over.wait_recv()

    def own_rows(i):
        at = c * 128 + i * 64
        value = r.w3[lax.div(at, 192), pl.ds(pl.multiple_of(lax.rem(at, 192), 64), 64), :]
        r.wo[pl.ds(pl.multiple_of(i * 64, 64), 64), :] = value

    loop(4, own_rows)
    for s in range(8):
        r.states[s, 7:8, :] = r.inc[s : s + 1, :]

    def mix_tile(i):
        s, tile = lax.div(i, 8), lax.rem(i, 8)
        b, n = lax.div(s, 2), lax.rem(s, 2)
        rows = tile_rows(tile)
        states = r.drv[s, rows, :] + r.dec[s, rows, :] * r.inc[pl.ds(s, 1), :]
        r.states[s, pl.ds(pl.multiple_of(tile * TILE + 8, 8), TILE), :] = states
        lanes = pl.ds(pl.multiple_of(n * 128, 128), 128)
        r.mixed[b * 2 + lax.div(tile, 4), tile_rows(lax.rem(tile, 4)), lanes] = (states * r.gb[s, rows, :]).astype(BF)

    loop(64, mix_tile)
    stored.wait()
    lane = lax.broadcasted_iota(jnp.int32, (1, 256), 1)
    counted = jnp.where((lane >= 64 * c) & (lane < 192 + 64 * c), 1.0, 0.0)
    counted_two = jnp.concatenate([counted, counted], axis=1)

    def masked(value, mask):
        return (value.astype(F32) * mask).astype(BF)

    total = Reduce(
        net, r, lambda k, core: dot(masked(r.mixed[net.slot(k, core)], counted), r.wo[...])
    )
    for k in (3, 1, 2, 0):
        total.other(k)
    total.far()
    total.near()
    cots.middle()
    total.own()
    cots.last()
    for k in (0, 1, 2, 3):
        cots.sibling(k)
    cots.release()
    total.relay()
    feed_down.relay()
    feed.relay()
    def wmd():
        return r.wmd_all[...].reshape(cols, -1)

    total.finish()
    gain2 = r.gain[1:2, :]
    for h in range(2):

        def residual_rows(i, h=h):
            rows = pl.ds(pl.multiple_of(h * 128 + i * 32, 32), 32)
            v = r.x[rows, :].astype(F32) + total.total(h, i, 32)
            r.residual[rows, :] = v
            s = lax.rsqrt(jnp.mean(v * v, axis=-1, keepdims=True) + NORM_EPS)
            r.normed[mine, rows, :] = (v * s * gain2).astype(BF)

        loop(4, residual_rows)

    n2_all = r.normed
    acts = Gather(net, n2_all.at[mine], n2_all)
    acts.start()

    def gate_up(which):
        return r.wgu_all[:, which * 128 : (which + 1) * 128, :].reshape(-1, cols)

    def d_normed2(k, core):
        slot = net.slot(k, core)
        return dot(r.dgu[slot, :, 0:cols], gate_up(0), NT) + dot(r.dgu[slot, :, cols:], gate_up(1), NT)

    back = Reduce(net, r, d_normed2)

    def part(k, core):
        slot = net.slot(k, core)
        h = n2_all[slot]
        r.ug[...] = dot(h, gate_up(0))
        r.ul[...] = dot(h, gate_up(1))

        def body(i):
            rows = pl.ds(pl.multiple_of(i * 32, 32), 32)
            gelu, slope = gelu_parts(r.ug[rows, :])
            ul, dh = r.ul[rows, :], r.dgu[slot, rows, 0:cols].astype(F32)
            r.hid[slot, rows, :] = (gelu * ul).astype(BF)
            r.dgu[slot, rows, 0:cols] = (dh * ul * slope).astype(BF)
            r.dgu[slot, rows, cols:] = (dh * gelu).astype(BF)

        loop(8, body)

    feed_down.end()
    for slot in range(8):
        r.dgu[slot, :, 0:cols] = dot(r.g_all[slot], wmd(), NT).astype(BF)
    feed_over.wait_recv()
    feed.end()
    part(0, c)
    acts.sibling(0)
    part(0, o)
    back.other(0)
    acts.forward()
    acts.middle()
    part(1, c)
    part(2, c)
    acts.sibling(1)
    part(1, o)
    back.other(1)
    acts.sibling(2)
    part(2, o)
    back.other(2)
    acts.last()
    acts.sibling(3)
    part(3, o)
    back.other(3)
    part(3, c)
    back.far()
    back.near()
    back.relay()
    back.own()
    acts.release()
    for i in range(4):
        rows = n2_all[:, :, i * 256 : (i + 1) * 256].reshape(-1, 256)
        r.gm[i] = dot(rows, r.dgu[...].reshape(-1, 2 * cols), TN).astype(BF)

    def gm_in(k):
        return r.wgi3.at[k - 1]

    mlp_m = LineSum(net, lambda t: r.gm.at[t], gm_in)
    mlp_m.start()
    hid = r.hid[...].reshape(-1, cols)
    for half in range(2):
        lanes = slice(half * 512, half * 512 + 512)
        value = dot(hid, r.g_all[:, :, lanes].reshape(-1, 512), TN).astype(BF)
        for i in range(4):
            r.gd[i, :, lanes] = value[i * piece : (i + 1) * piece, :]
    mlp_d = LineSum(net, lambda t: r.gd.at[t], lambda k: r.gd_in.at[k - 1])
    mlp_d.start()
    back.finish()
    sums = jnp.zeros((8, r.x.shape[1]), F32)
    for h in range(2):

        def residual_back(i, sums, h=h):
            rows = pl.ds(pl.multiple_of(h * 128 + i * 32, 32), 32)
            v = r.residual[rows, :]
            dn = back.total(h, i, 32)
            s = lax.rsqrt(jnp.mean(v * v, axis=-1, keepdims=True) + NORM_EPS)
            u = dn * gain2
            pulled = s * u - v * (s * s * s * jnp.mean(u * v, axis=-1, keepdims=True))
            d_res = r.g_all[mine, rows, :].astype(F32) + pulled
            r.d_res[rows, :] = d_res
            r.do_all[mine, rows, :] = d_res.astype(BF)
            return sums + jnp.sum((dn * v * s).reshape(4, 8, -1), axis=0)

        sums = lax.fori_loop(0, 4, residual_back, sums)
    r.gain2_sum[...] = sums

    owners, returned = [], []

    def to_owners(src, dst):
        for k in (1, 2, 3):
            for core in (c, o):
                rows = pl.ds(pl.multiple_of(core * 128, 128), 128)
                owners.append(net.copy(src.at[rows], dst.at[mine], net.plane(k, core)))
        rows = pl.ds(pl.multiple_of(o * 128, 128), 128)
        owners.append(net.copy(src.at[rows], dst.at[mine], sibling))
        rows = pl.ds(pl.multiple_of(c * 128, 128), 128)
        returned.append(net.local(src.at[rows], dst.at[mine]))

    def to_chips(src, dst):
        for k in (1, 2, 3):
            owners.append(net.copy(src, dst.at[p], net.plane(k, c)))
        returned.append(net.local(src, dst.at[p]))

    fo_at = net.reserve(4)

    def vector_copy(k):
        return net.describe(r.vout.at[p], r.vout.at[p], net.plane(k, c), fo_at + k, fo_at)

    def mlp_sums():
        mlp_m.end(r.gm_sum)
        to_owners(r.gm_sum, r.fm)

    grads = Gather(net, r.do_all.at[mine], r.do_all)
    grads.start()

    def back_out(slot):
        b, half = lax.div(slot, 2), lax.rem(slot, 2)
        dm = dot(r.do_all[slot], r.wo[...], NT)
        for n in range(2):
            r.dconv[b * 2 + n, pl.ds(pl.multiple_of(half * 256, 256), 256), :] = dm[:, n * 128 : (n + 1) * 128]

    back_out(mine)
    grads.sibling(0)
    back_out(net.slot(0, o))
    out = Reduce(net, r, lambda k, core: dot(r.hid[net.slot(k, core)], wmd()))
    for k in (3, 1, 2, 0):
        out.other(k)
    mlp_m.relay()
    grads.forward()
    out.far()
    out.near()
    out.own()
    grads.middle()
    for k in (1, 2):
        back_out(net.slot(k, c))
    for k in (1, 2):
        grads.sibling(k)
        back_out(net.slot(k, o))
    grads.last()
    back_out(net.slot(3, c))
    grads.sibling(3)
    back_out(net.slot(3, o))

    def first_pass(i):
        b, tile = lax.div(i, 8), lax.rem(i, 8)
        rows = tile_rows(tile)
        live = r.off[b, rows, :] != 0.0
        for n in range(2):
            s = b * 2 + n
            gelu, slope = gelu_parts(r.gp[s, rows, :])
            dm = r.dconv[s, rows, :]
            states = r.states[s, pl.ds(pl.multiple_of(tile * TILE + 8, 8), TILE), :]
            lanes = slice(n * 128, (n + 1) * 128)
            r.dgi[b * 2 + lax.div(tile, 4), tile_rows(lax.rem(tile, 4)), lanes] = (dm * states * slope).astype(BF)
            r.drv[s, rows, :] = dm * gelu
            a = jnp.exp(-DECAY_SCALE * r.sr[s, rows, :] * r.chan[n, 7:8, :])
            r.dec[s, rows, :] = jnp.where(live, a, 0.0)

    loop(32, first_pass)
    ends = scan_slabs(r.dec, r.drv, True)
    ends = exchange_ends(r, net, ends, 1)
    out.relay()
    go_in, go_line_in = r.go_q, r.go_l
    mixed = r.mixed[...].reshape(-1, 256)
    for half in range(2):
        lanes = slice(half * 512, half * 512 + 512)
        r.go[:, lanes] = dot(mixed, r.do_all[:, :, lanes].reshape(-1, 512), TN).astype(BF)
    grads.release()
    fetched = net.local(r.normed_far, r.do_all)
    go_rows = [pl.ds(pl.multiple_of(c * 64 + near * 48, 16), 48) for near in net.near]

    def go_start(lanes):
        return [net.copy(r.go.at[go_rows[k], lanes], go_in.at[p, :, lanes], net.plane(k, c)) for k in (1, 2, 3)]

    go_out = go_start(pl.ds(0, 1024))
    mlp_sums()
    entering_states(r, net, ends, 1, True)
    mlp_d.relay()
    r.vec[...] = jnp.zeros((2, 8, 8, 128), F32)
    dri = r.normed

    def second_pass(s):
        b, n = lax.div(s, 2), lax.rem(s, 2)
        chan = r.chan[n]
        enter = r.inc[pl.ds(s, 1), :]
        lanes_r = pl.ds(pl.multiple_of(n * 256, 128), 128)
        lanes_i = pl.ds(pl.multiple_of(n * 256 + 128, 128), 128)

        def tile(i, sums):
            rows = tile_rows(i)
            live = r.off[b, rows, :] != 0.0
            ds = r.drv[s, rows, :] + r.dec[s, rows, :] * enter
            window = r.states[s, pl.ds(pl.multiple_of(i * TILE, 8), TILE + 8), :]
            before = window[7 : TILE + 7, :]
            sr, si = r.sr[s, rows, :], r.si[s, rows, :]
            cv = r.conv[s, rows, :].astype(F32)
            a, m2 = decay_parts(sr, chan[7:8, :])
            inv = lax.rsqrt(m2)
            m = jnp.where(live, m2 * inv, 1.0)
            dsi = ds * si
            d_log = jnp.where(live, a * (ds * before - dsi * cv * a * inv), 0.0)
            lam_term = d_log * sr
            d_r = (-DECAY_SCALE) * chan[7:8, :] * lam_term * (1.0 - sr)
            dm_i = dsi * m
            d_i = dm_i * cv * (1.0 - si)
            d_r, d_i = d_r.astype(BF), d_i.astype(BF)
            at = tile_rows(lax.rem(i, 4))
            dri[b * 2 + lax.div(i, 4), at, lanes_r] = d_r
            dri[b * 2 + lax.div(i, 4), at, lanes_i] = d_i
            r.dconv[s, rows, :] = dm_i
            return (
                sums[0] + column_sum(d_r.astype(F32)),
                sums[1] + column_sum(d_i.astype(F32)),
                sums[2] + column_sum(lam_term),
            )

        zero = jnp.zeros((8, 128), F32)
        sums = lax.fori_loop(0, 512 // TILE, tile, (zero, zero, zero))
        for j in range(3):
            r.vec[n, 5 + j] = r.vec[n, 5 + j] + sums[j]

    loop(8, second_pass)

    def gate_back(i):
        s, half = lax.div(i, 2), lax.rem(i, 2)
        b, n = lax.div(s, 2), lax.rem(s, 2)
        rows = pl.ds(pl.multiple_of(half * 256, 256), 256)
        lanes = pl.ds(pl.multiple_of(n * 256, 256), 256)
        r.dconv[s, rows, :] = r.dconv[s, rows, :] + dot(dri[b * 2 + half, :, lanes], r.wri[n], NT)

    loop(16, gate_back)
    edge_back = net.reserve(1)

    def edge_back_copy():
        return net.describe(
            r.dconv.at[:, pl.ds(0, 8)], r.dconv.at[:, pl.ds(512, 8)], net.line(net.down(1), c), edge_back, edge_back
        )

    @pl.when(z > 0)
    def _():
        edge_back_copy().start()

    @pl.when(z == 3)
    def _():
        r.dconv[:, 512:520, :] = jnp.zeros((8, 8, 128), F32)

    for n in range(2):
        total_ri = None
        for b in range(4):
            for half in range(2):
                term = dot(
                    r.conv[b * 2 + n, half * 256 : (half + 1) * 256, :],
                    dri[b * 2 + half, :, n * 256 : (n + 1) * 256],
                    TN,
                )
                total_ri = term if total_ri is None else total_ri + term
        r.go[n * 128 : (n + 1) * 128, 1024:1280] = total_ri.astype(BF)
    go_out += go_start(pl.ds(1024, 256))

    @pl.when(z < 3)
    def _():
        edge_back_copy().wait_recv()


    def conv_back(s):
        b, n = lax.div(s, 2), lax.rem(s, 2)
        chan = r.chan[n]
        lanes = pl.ds(pl.multiple_of(256 + n * 128, 128), 128)

        def tile(i, sums):
            offset = r.off[b, pl.ds(pl.multiple_of(i * TILE, 8), TILE + 8), :]
            window = r.dconv[s, pl.ds(pl.multiple_of(i * TILE, 8), TILE + 8), :]
            inner = r.inner[s, pl.ds(pl.multiple_of(i * TILE, 8), TILE + 8), :]
            value = chan[0:1, :] * window[:TILE, :]
            added = [sums[0] + column_sum(window[:TILE, :] * inner[8:, :])]
            for k in (1, 2, 3):
                held = jnp.where(offset >= k, window, 0.0)
                value = value + chan[k : k + 1, :] * held[k : TILE + k, :]
                added.append(sums[k] + column_sum(held[:TILE, :] * inner[8 - k : TILE + 8 - k, :]))
            added.append(sums[4] + column_sum(window[:TILE, :]))
            r.dgi[b * 2 + lax.div(i, 4), tile_rows(lax.rem(i, 4)), lanes] = value.astype(BF)
            return tuple(added)

        sums = lax.fori_loop(0, 512 // TILE, tile, tuple(jnp.zeros((8, 128), F32) for _ in range(5)))
        for j in range(5):
            r.vec[n, j] = r.vec[n, j] + sums[j]

    loop(8, conv_back)
    out.finish()
    for h in range(2):

        def out_rows(i, h=h):
            rows = pl.ds(pl.multiple_of(h * 128 + i * 32, 32), 32)
            value = (r.residual[rows, :] + out.total(h, i, 32)).astype(BF)
            for j in range(4):
                r.dgu[j, rows, 512:768] = value[:, j * 256 : (j + 1) * 256]

        loop(4, out_rows)
    for j in range(4):
        returned.append(net.local(r.dgu.at[j, :, pl.ds(512, 256)], r.block_out.at[:, pl.ds(j * 256, 256)]))
    for partner in (sibling, net.plane(1, c), net.plane(2, c)):
        pl.semaphore_signal(r.free, inc=1, device_id=partner, device_id_type=pl.DeviceIdType.MESH)
    for n in range(2):
        sums = [jnp.sum(r.vec[n, j], axis=0, keepdims=True) for j in range(8)]
        sums[7] = sums[7] * (DECAY_SCALE * r.chan[n, 8:9, :])
        r.vsum[z, :, n * 128 : (n + 1) * 128] = jnp.concatenate(sums, axis=0)
    vec = [net.copy(r.vsum.at[z], r.vsum.at[z], net.line(net.up(k), c)) for k in (1, 2, 3)]
    fetched.wait()
    flat = r.dgi[:, :, 0:512].reshape(-1, 512)
    for i in range(4):
        value = dot(r.do_all[:, :, i * 256 : (i + 1) * 256].reshape(-1, 256), flat, TN)
        for j in range(2):
            n0, n1 = value[:, j * 256 : j * 256 + 128], value[:, j * 256 + 128 : j * 256 + 256]
            r.ga[i][:, j * 128 : (j + 1) * 128] = lax.select(c == 0, n0, n1).astype(BF)
            shared = lax.select(c == 0, n1, n0)
            r.gb2[i][:, j * 128 : (j + 1) * 128] = lax.select(c == 0, shared[0:128], shared[128:256]).astype(BF)

    def ga_in(k):
        return r.g_all.at[7, :, pl.ds((k - 1) * 256, 256)]

    def gb_in(k):
        return r.g_all.at[3 + k, pl.ds(128, 128), pl.ds(0, 256)]

    sum_a = LineSum(net, lambda t: r.hid.at[t, :, 0:256], ga_in)
    sum_b = LineSum(net, lambda t: r.hid.at[4 + t, 0:128, 0:256], gb_in)
    sum_a.start()
    sum_b.start()
    first_back = Reduce(
        net,
        r,
        lambda k, core: dot(masked(r.dgi[net.slot(k, core), :, 0:512], counted_two), r.w2[...], NT),
    )
    pl.semaphore_wait(r.free, 3)
    for k in (3, 1, 2, 0):
        first_back.other(k)
    first_back.far()
    first_back.near()
    go_in[p] = r.go[go_rows[0], :]
    for made in go_out:
        made.wait_recv()
    go_line = LineSum(net, lambda t: go_in.at[t], lambda k: go_line_in.at[k - 1])
    go_line.start()
    first_back.relay()
    mlp_d.end(r.gd_sum)
    to_chips(r.gd_sum, r.fd)
    first_back.own()
    sum_a.relay()
    sum_b.relay()
    go_line.relay()
    first_back.finish()
    sums = jnp.zeros((8, r.x.shape[1]), F32)
    for h in range(2):

        def input_rows(i, sums, h=h):
            rows = pl.ds(pl.multiple_of(h * 128 + i * 32, 32), 32)
            v = r.x[rows, :].astype(F32)
            dn = first_back.total(h, i, 32)
            s = lax.rsqrt(jnp.mean(v * v, axis=-1, keepdims=True) + NORM_EPS)
            u = dn * r.gain[0:1, :]
            r.d_res[rows, :] = r.d_res[rows, :] + (
                s * u - v * (s * s * s * jnp.mean(u * v, axis=-1, keepdims=True))
            )
            return sums + jnp.sum((dn * v * s).reshape(4, 8, -1), axis=0)

        sums = lax.fori_loop(0, 4, input_rows, sums)
    returned.append(net.local(r.d_res, r.d_in))
    gains = jnp.concatenate(
        [
            jnp.sum(sums, axis=0, keepdims=True),
            jnp.sum(r.gain2_sum[...], axis=0, keepdims=True),
            jnp.zeros((6, sums.shape[1]), F32),
        ],
        axis=0,
    )
    for i in range(8):
        r.gsum[i] = gains[:, i * 128 : (i + 1) * 128]
    r.gline[q] = r.gsum[q]
    gain_line = [
        net.copy(r.gsum.at[net.up(k) * 2 + core], r.gline.at[q], net.line(net.up(k), core))
        for k in (1, 2, 3)
        for core in (c, o)
    ]
    gain_line.append(net.copy(r.gsum.at[z * 2 + o], r.gline.at[q], sibling))
    for made in row_sums:
        made.wait_recv()
    r.rows_sum[...] = r.rs_all[0] + r.rs_all[1] + r.rs_all[2] + r.rs_all[3]
    for k in (1, 2, 3):
        for core in (c, o):
            owners.append(net.copy(r.rows_sum.at[pl.ds(net.near[k] * 2, 2)], r.fr.at[mine], net.plane(k, core)))
    owners.append(net.copy(r.rows_sum.at[pl.ds(p * 2, 2)], r.fr.at[mine], sibling))
    returned.append(net.local(r.rows_sum.at[pl.ds(p * 2, 2)], r.fr.at[mine]))
    for made in vec:
        made.wait_recv()
    r.vout[p] = r.vsum[0] + r.vsum[1] + r.vsum[2] + r.vsum[3]

    @pl.when(z == p)
    def _():
        for k in (1, 2, 3):
            vector_copy(k).start()

    sum_a.end(r.ga_sum)
    to_owners(r.ga_sum, r.fa)
    sum_b.end(r.gb2_sum)
    to_chips(r.gb2_sum, r.fb)
    go_line.end(r.go_sum)
    to_chips(r.go_sum, r.fo)
    for made in gain_line:
        made.wait_recv()
    sums = r.gline[0]
    for i in range(1, 8):
        sums = sums + r.gline[i]
    r.gplane[p] = sums
    gain_plane = [net.copy(r.gplane.at[p], r.gplane.at[p], net.plane(k, c)) for k in (1, 2, 3)]

    @pl.when(z != p)
    def _():
        vector_copy(1).wait_recv()

    @pl.when(z == p)
    def _():
        for k in (1, 2, 3):
            vector_copy(k).wait_send()

    for made in owners + gain_plane:
        made.wait_recv()
    r.gain_out[...] = r.gplane[0] + r.gplane[1] + r.gplane[2] + r.gplane[3]
    r.vec_out[...] = r.vout[z]
    for made in returned:
        made.wait()
    @pl.when(z < 3)
    def _():
        edge_copy().wait_send()

    @pl.when(z > 0)
    def _():
        edge_back_copy().wait_send()

    feed.drain()
    feed_down.drain()
    for made in (mlp_m, mlp_d, go_line, sum_a, sum_b):
        made.drain()
    net.drain()


def assemble(r):
    c = lax.rem(lax.axis_index("seq"), 2)
    for chip in range(4):
        for j, out in enumerate((r.o_gate, r.o_in)):
            lanes = slice(j * 128, (j + 1) * 128)
            at = chip * 384
            out[:, at : at + 128] = r.fa[chip * 2, :, lanes].astype(F32)
            out[:, at + 128 : at + 256] = r.fb[chip, :, lanes].astype(F32)
            out[:, at + 256 : at + 384] = r.fa[chip * 2 + 1, :, lanes].astype(F32)
    cols = r.fm.shape[2] // 2
    piece = cols // 4
    for j, out in enumerate((r.o_mgate, r.o_mup)):
        for part in range(4):
            for core in range(2):
                at = (part * 2 + core) * cols
                lanes = slice(j * cols + part * piece, j * cols + (part + 1) * piece)
                out[:, at : at + cols] = jnp.concatenate(
                    [r.fm[chip * 2 + core, :, lanes].astype(F32) for chip in range(4)], axis=1
                )
    for chip in range(4):
        r.o_mdown[chip * piece : (chip + 1) * piece, :] = r.fd[chip].astype(F32)
    for chip in range(4):
        rows = slice(chip * 48, (chip + 1) * 48)
        r.o_out[rows, :] = r.fo[chip, :, 0:1024].astype(F32)
        r.o_r[rows, :] = r.fo[chip, :, 1024:1152].astype(F32)
        r.o_i[rows, :] = r.fo[chip, :, 1152:1280].astype(F32)
    vec = r.vec_in[...]
    vec = lax.select(c == 0, vec[:, 0:192], vec[:, 64:256])
    r.o_cw[...] = vec[0:4]
    for j, out in enumerate((r.o_cb, r.o_rb, r.o_ib, r.o_lam)):
        out[...] = vec[4 + j : 5 + j]
    r.o_ngain[...] = r.gains[0:1, :]
    r.o_mgain[...] = r.gains[1:2, :]
    counts = [jnp.broadcast_to(r.lens[0:1, row : row + 1].astype(F32), (1, 128)) for row in range(5)]
    for chip in range(4):
        for half, (slot, n) in enumerate(((chip * 2, 0), (chip * 2, 1), (chip * 2 + 1, 1))):
            at = chip * 384 + half * 128
            for row in range(5):
                r.o_mean[row, :, at : at + 128] = r.fr[slot, n, row : row + 1, :] / counts[row]


def shifted(value, axis, by):
    count = lax.axis_size(axis)
    pairs = [(i, i + by) for i in range(count) if 0 <= i + by < count]
    return lax.ppermute(value, axis, pairs)


def entering(value, axis, combine, identity, reverse):
    count, place = (lax.axis_size(axis), lax.axis_index(axis))
    everything = jax.tree.map(lambda part: lax.all_gather(part, axis), value)
    start = jax.tree.map(
        lambda part, zero: jnp.broadcast_to(jnp.asarray(zero, part.dtype), part.shape),
        value,
        identity,
    )

    def step(k, before):
        at = count - 1 - k if reverse else k
        reached = at > place if reverse else at < place
        new = combine(before, jax.tree.map(lambda part: part[at], everything))
        return jax.tree.map(lambda a, b: jnp.where(reached, a, b), new, before)

    return lax.fori_loop(0, count, step, start)


def rms_scale(values):
    return values * lax.rsqrt(jnp.mean(values * values, axis=-1, keepdims=True) + NORM_EPS)


def gelu_tanh(values):
    return jax.nn.gelu(values, approximate=True)


def link(earlier, later):
    return (earlier[0] * later[0], later[0] * earlier[1] + later[1])


def block_product(values, weight):
    count, channels = values.shape
    block_size = weight.shape[1]
    shaped = values.reshape(count, channels // block_size, block_size)
    result = jnp.einsum(
        "lni,nij->lnj",
        shaped,
        weight.reshape(channels // block_size, block_size, block_size),
        preferred_element_type=jnp.float32,
    )
    return result.reshape(count, channels)


def block_back(grads, weight):
    count, channels = grads.shape
    block_size = weight.shape[1]
    shaped = grads.reshape(count, channels // block_size, block_size)
    result = jnp.einsum(
        "lnj,nij->lni",
        shaped,
        weight.reshape(channels // block_size, block_size, block_size),
        preferred_element_type=jnp.float32,
    )
    return result.reshape(count, channels)


def block_weight_grad(values, grads, block_size):
    count, channels = values.shape
    left = values.reshape(count, channels // block_size, block_size)
    right = grads.reshape(count, channels // block_size, block_size)
    return jnp.einsum("lni,lnj->nij", left, right, preferred_element_type=jnp.float32).reshape(
        channels, block_size
    )


def recurrence_terms(conv_in, r_in, i_in, lam_in, restart):
    log_a = -DECAY_SCALE * jax.nn.sigmoid(r_in) * jax.nn.softplus(-lam_in)
    decays = jnp.exp(log_a)
    factor = jnp.where(restart[:, None] > 0, 1.0, jnp.sqrt(-jnp.expm1(2.0 * log_a)))
    return (decays * (1.0 - restart[:, None]), factor * jax.nn.sigmoid(i_in) * conv_in, decays)


def shards(
    inputs,
    out_grad,
    row_lengths,
    norm_gain,
    w_gate,
    w_in,
    conv_w,
    conv_b,
    w_rgate,
    b_rgate,
    w_igate,
    b_igate,
    lam,
    w_out,
    mlp_gain,
    w_mlp_gate,
    w_mlp_up,
    w_mlp_down,
):
    gathered = (
        lax.all_gather(norm_gain, "seq", axis=0, tiled=True),
        lax.all_gather(w_gate, "seq", axis=0, tiled=True),
        lax.all_gather(w_in, "seq", axis=0, tiled=True),
        lax.all_gather(conv_w, "seq", axis=1, tiled=True),
        lax.all_gather(conv_b, "seq", axis=0, tiled=True),
        lax.all_gather(w_rgate, "seq", axis=0, tiled=True),
        lax.all_gather(b_rgate, "seq", axis=0, tiled=True),
        lax.all_gather(w_igate, "seq", axis=0, tiled=True),
        lax.all_gather(b_igate, "seq", axis=0, tiled=True),
        lax.all_gather(lam, "seq", axis=0, tiled=True),
        lax.all_gather(w_out, "seq", axis=0, tiled=True),
        lax.all_gather(mlp_gain, "seq", axis=0, tiled=True),
        lax.all_gather(w_mlp_gate, "seq", axis=0, tiled=True),
        lax.all_gather(w_mlp_up, "seq", axis=0, tiled=True),
        lax.all_gather(w_mlp_down, "seq", axis=0, tiled=True),
    )
    gain_first = gathered[0].astype(jnp.float32)
    conv_taps = gathered[3].astype(jnp.float32)
    conv_bias = gathered[4].astype(jnp.float32)
    lam_value = gathered[9].astype(jnp.float32)
    gain_second = gathered[11].astype(jnp.float32)
    tokens = inputs[0].astype(jnp.float32)
    local_len = tokens.shape[0]
    channels = gathered[2].shape[1]
    block_size = gathered[5].shape[1]
    kernel_taps = conv_taps.shape[0]
    lengths = row_lengths[0]
    row_ends = jnp.cumsum(lengths)
    row_starts = row_ends - lengths
    positions = lax.axis_index("seq") * local_len + jnp.arange(local_len, dtype=jnp.int32)
    started = positions[:, None] >= row_starts[None, :]
    row_index = jnp.sum(started.astype(jnp.int32), axis=1) - 1
    row_first = jnp.max(jnp.where(started, row_starts[None, :], 0), axis=1)
    offset = positions - row_first
    restart = (offset == 0).astype(jnp.float32)
    members = (row_index[:, None] == jnp.arange(lengths.shape[0], dtype=jnp.int32)[None, :]).astype(
        jnp.float32
    )
    tap_masks = [(offset >= tap).astype(jnp.float32)[:, None] for tap in range(kernel_taps)]
    scaled, norm_pull = jax.vjp(rms_scale, tokens)
    normed = (scaled * gain_first).astype(jnp.bfloat16)
    gate_pre = jnp.dot(normed, gathered[1], preferred_element_type=jnp.float32)
    gate_branch, gate_pull = jax.vjp(gelu_tanh, gate_pre)
    inner = jnp.dot(normed, gathered[2], preferred_element_type=jnp.float32).astype(jnp.bfloat16)
    edge_rows = shifted(inner[local_len - kernel_taps + 1 :], "seq", 1)
    extended = jnp.concatenate([edge_rows, inner], axis=0).astype(jnp.float32)
    conv_sum = conv_bias + jnp.zeros((local_len, channels), jnp.float32)
    for tap in range(kernel_taps):
        start_row = kernel_taps - 1 - tap
        conv_sum = (
            conv_sum + conv_taps[tap] * extended[start_row : start_row + local_len] * tap_masks[tap]
        )
    conv_low = conv_sum.astype(jnp.bfloat16)
    conv_value = conv_low.astype(jnp.float32)
    r_pre = block_product(conv_low, gathered[5]) + gathered[6].astype(jnp.float32)
    i_pre = block_product(conv_low, gathered[7]) + gathered[8].astype(jnp.float32)

    def local_terms(conv_in, r_in, i_in, lam_in):
        return recurrence_terms(conv_in, r_in, i_in, lam_in, restart)

    (carried, drive_term, decays), recur_pull = jax.vjp(
        local_terms, conv_value, r_pre, i_pre, lam_value
    )
    prefix_decay, local_state = lax.associative_scan(link, (carried, drive_term), axis=0)
    identity = (jnp.ones((channels,), jnp.float32), jnp.zeros((channels,), jnp.float32))
    incoming = entering((prefix_decay[-1], local_state[-1]), "seq", link, identity, False)[1]
    states = local_state + prefix_decay * incoming
    mixed_low = (states * gate_branch).astype(jnp.bfloat16)
    residual = tokens + jnp.dot(mixed_low, gathered[10], preferred_element_type=jnp.float32)
    scaled_two, norm_pull_two = jax.vjp(rms_scale, residual)
    normed_two = (scaled_two * gain_second).astype(jnp.bfloat16)
    up_gate = jnp.dot(normed_two, gathered[12], preferred_element_type=jnp.float32)
    up_lin = jnp.dot(normed_two, gathered[13], preferred_element_type=jnp.float32)
    gelu_up, up_pull = jax.vjp(gelu_tanh, up_gate)
    hidden = (gelu_up * up_lin).astype(jnp.bfloat16)
    block_out = (
        residual + jnp.dot(hidden, gathered[14], preferred_element_type=jnp.float32)
    ).astype(jnp.bfloat16)
    row_sums = lax.psum(jnp.dot(members.T, decays, precision=lax.Precision.HIGHEST), "seq")
    gate_mean = row_sums / lengths.astype(jnp.float32)[:, None]
    grad_top = out_grad[0]
    grad_mdown = jnp.einsum("tf,td->fd", hidden, grad_top, preferred_element_type=jnp.float32)
    d_hidden = jnp.einsum("td,fd->tf", grad_top, gathered[14], preferred_element_type=jnp.float32)
    d_upgate = up_pull(d_hidden * up_lin)[0].astype(jnp.bfloat16)
    d_uplin = (d_hidden * gelu_up).astype(jnp.bfloat16)
    grad_mgate = jnp.einsum("td,tf->df", normed_two, d_upgate, preferred_element_type=jnp.float32)
    grad_mup = jnp.einsum("td,tf->df", normed_two, d_uplin, preferred_element_type=jnp.float32)
    d_normed_two = jnp.einsum(
        "tf,df->td", d_upgate, gathered[12], preferred_element_type=jnp.float32
    )
    d_normed_two = d_normed_two + jnp.einsum(
        "tf,df->td", d_uplin, gathered[13], preferred_element_type=jnp.float32
    )
    grad_mgain = jnp.sum(d_normed_two * scaled_two, axis=0)
    d_residual = grad_top.astype(jnp.float32) + norm_pull_two(d_normed_two * gain_second)[0]
    d_outlow = d_residual.astype(jnp.bfloat16)
    grad_outw = jnp.einsum("tr,td->rd", mixed_low, d_outlow, preferred_element_type=jnp.float32)
    d_mixed = jnp.einsum("td,rd->tr", d_outlow, gathered[10], preferred_element_type=jnp.float32)
    direct = d_mixed * gate_branch
    d_gatelow = gate_pull(d_mixed * states)[0].astype(jnp.bfloat16)
    grad_gatew = jnp.einsum("td,tr->dr", normed, d_gatelow, preferred_element_type=jnp.float32)
    next_decay = jnp.concatenate([carried[1:], jnp.ones((1, channels), jnp.float32)], axis=0)
    suffix_decay, local_grad = lax.associative_scan(
        link, (next_decay, direct), axis=0, reverse=True
    )
    arriving = entering(
        (carried[0] * suffix_decay[0], carried[0] * local_grad[0]), "seq", link, identity, True
    )[1]
    d_states = local_grad + suffix_decay * arriving
    previous = jnp.concatenate([incoming[None, :], states[:-1]], axis=0)
    grad_convval, d_rpre, d_ipre, grad_lambda = recur_pull(
        (d_states * previous, d_states, jnp.zeros_like(decays))
    )
    d_rlow = d_rpre.astype(jnp.bfloat16)
    d_ilow = d_ipre.astype(jnp.bfloat16)
    grad_rw = block_weight_grad(conv_low, d_rlow, block_size)
    grad_rb = jnp.sum(d_rlow.astype(jnp.float32), axis=0)
    grad_iw = block_weight_grad(conv_low, d_ilow, block_size)
    grad_ib = jnp.sum(d_ilow.astype(jnp.float32), axis=0)
    grad_convsum = grad_convval + block_back(d_rlow, gathered[5]) + block_back(d_ilow, gathered[7])
    grad_cb = jnp.sum(grad_convsum, axis=0)
    conv_again = gathered[3].astype(jnp.float32)
    grad_extended = jnp.zeros((local_len + kernel_taps - 1, channels), jnp.float32)
    tap_grads = []
    for tap in range(kernel_taps):
        start_row = kernel_taps - 1 - tap
        masked = grad_convsum * tap_masks[tap]
        tap_grads.append(jnp.sum(masked * extended[start_row : start_row + local_len], axis=0))
        grad_extended = grad_extended + jnp.pad(
            masked * conv_again[tap], ((start_row, tap), (0, 0))
        )
    grad_cw = jnp.stack(tap_grads)
    edge_grads = shifted(grad_extended[: kernel_taps - 1], "seq", -1)
    d_inner = (
        grad_extended[kernel_taps - 1 :]
        + jnp.pad(edge_grads, ((local_len - kernel_taps + 1, 0), (0, 0)))
    ).astype(jnp.bfloat16)
    grad_inw = jnp.einsum("td,tr->dr", normed, d_inner, preferred_element_type=jnp.float32)
    d_normed = jnp.einsum("tr,dr->td", d_gatelow, gathered[1], preferred_element_type=jnp.float32)
    d_normed = d_normed + jnp.einsum(
        "tr,dr->td", d_inner, gathered[2], preferred_element_type=jnp.float32
    )
    grad_gain = jnp.sum(d_normed * scaled, axis=0)
    d_tokens = d_residual + norm_pull(d_normed * gain_first)[0]
    shares = (
        lax.psum_scatter(grad_gain, "seq", scatter_dimension=0, tiled=True),
        lax.psum_scatter(grad_gatew, "seq", scatter_dimension=0, tiled=True),
        lax.psum_scatter(grad_inw, "seq", scatter_dimension=0, tiled=True),
        lax.psum_scatter(grad_cw, "seq", scatter_dimension=1, tiled=True),
        lax.psum_scatter(grad_cb, "seq", scatter_dimension=0, tiled=True),
        lax.psum_scatter(grad_rw, "seq", scatter_dimension=0, tiled=True),
        lax.psum_scatter(grad_rb, "seq", scatter_dimension=0, tiled=True),
        lax.psum_scatter(grad_iw, "seq", scatter_dimension=0, tiled=True),
        lax.psum_scatter(grad_ib, "seq", scatter_dimension=0, tiled=True),
        lax.psum_scatter(grad_lambda, "seq", scatter_dimension=0, tiled=True),
        lax.psum_scatter(grad_outw, "seq", scatter_dimension=0, tiled=True),
        lax.psum_scatter(grad_mgain, "seq", scatter_dimension=0, tiled=True),
        lax.psum_scatter(grad_mgate, "seq", scatter_dimension=0, tiled=True),
        lax.psum_scatter(grad_mup, "seq", scatter_dimension=0, tiled=True),
        lax.psum_scatter(grad_mdown, "seq", scatter_dimension=0, tiled=True),
    )
    totals = (
        lax.psum(shares[0].astype(jnp.bfloat16), "batch").astype(jnp.float32),
        lax.psum(shares[1].astype(jnp.bfloat16), "batch").astype(jnp.float32),
        lax.psum(shares[2].astype(jnp.bfloat16), "batch").astype(jnp.float32),
        lax.psum(shares[3].astype(jnp.bfloat16), "batch").astype(jnp.float32),
        lax.psum(shares[4].astype(jnp.bfloat16), "batch").astype(jnp.float32),
        lax.psum(shares[5].astype(jnp.bfloat16), "batch").astype(jnp.float32),
        lax.psum(shares[6].astype(jnp.bfloat16), "batch").astype(jnp.float32),
        lax.psum(shares[7].astype(jnp.bfloat16), "batch").astype(jnp.float32),
        lax.psum(shares[8].astype(jnp.bfloat16), "batch").astype(jnp.float32),
        lax.psum(shares[9].astype(jnp.bfloat16), "batch").astype(jnp.float32),
        lax.psum(shares[10].astype(jnp.bfloat16), "batch").astype(jnp.float32),
        lax.psum(shares[11].astype(jnp.bfloat16), "batch").astype(jnp.float32),
        lax.psum(shares[12].astype(jnp.bfloat16), "batch").astype(jnp.float32),
        lax.psum(shares[13].astype(jnp.bfloat16), "batch").astype(jnp.float32),
        lax.psum(shares[14].astype(jnp.bfloat16), "batch").astype(jnp.float32),
    )
    return (
        block_out[None],
        d_tokens[None],
        totals[0],
        totals[1],
        totals[2],
        totals[3],
        totals[4],
        totals[5],
        totals[6],
        totals[7],
        totals[8],
        totals[9],
        totals[10],
        totals[11],
        totals[12],
        totals[13],
        totals[14],
        gate_mean[None],
    )


def pack(conv_w, conv_b, b_rgate, b_igate, lam, norm_gain, mlp_gain):
    row = lax.broadcasted_iota(jnp.int32, (16, 256), 0)
    lane = lax.broadcasted_iota(jnp.int32, (16, 256), 1)
    small = jnp.pad(conv_w, ((0, 12), (0, 64)))
    for at, value in ((4, conv_b), (5, b_rgate), (6, b_igate), (7, lam)):
        spread = jnp.broadcast_to(jnp.pad(value, (0, 64)), (16, 256))
        small = jnp.where(row == at, spread, small)
    for first, value in ((0, norm_gain), (128, mlp_gain)):
        spread = jnp.broadcast_to(jnp.pad(value, (first, 128 - first)), (16, 256))
        small = jnp.where((row == 10) & (lane // 128 == first // 128), spread, small)
    return small


def planes(
    inputs,
    out_grad,
    row_lengths,
    norm_gain,
    w_gate,
    w_in,
    conv_w,
    conv_b,
    w_rgate,
    b_rgate,
    w_igate,
    b_igate,
    lam,
    w_out,
    mlp_gain,
    w_mlp_gate,
    w_mlp_up,
    w_mlp_down,
):
    small = pack(conv_w, conv_b, b_rgate, b_igate, lam, norm_gain, mlp_gain)
    vmem = pltpu.VMEM
    done = kernel_call(
        layer,
        dict(
            x=inputs[0], small=small, lens=row_lengths, g=out_grad[0], wg=w_gate, wi=w_in, wr=w_rgate, wv=w_igate, wout=w_out,
            wmg=w_mlp_gate, wmu=w_mlp_up, wmd=w_mlp_down,
        ),
        dict(
            block_out=array(256, 1024, dtype=BF),
            d_in=array(256, 1024),
            fm=array(8, 128, 768, dtype=BF),
            fd=array(4, 96, 1024, dtype=BF),
            fa=array(8, 128, 256, dtype=BF),
            fb=array(4, 128, 256, dtype=BF),
            fo=array(4, 48, 1280, dtype=BF),
            fr=array(8, 2, 8, 128),
            vec_out=array(8, 256),
            gain_out=array(8, 128),
            normed_far=array(8, 256, 1024, dtype=BF),
        ),
        dict(
            x_all=vmem((8, 256, 1024), BF),
            normed=vmem((8, 256, 1024), BF),
            g_all=vmem((8, 256, 1024), BF),
            small_all=vmem((8, 16, 256), BF),
            lens_out=vmem((8, 128), F32),
            lens_all=vmem((4, 8, 128), F32),
            off=vmem((4, 520, 128), F32),
            starts_all=vmem((4, 8, 128), F32),
            chan=vmem((2, 16, 128), F32),
            gain=vmem((8, 1024), F32),
            wgi3=vmem((4, 256, 768), BF),
            w2=vmem((1024, 512), BF),
            gq=vmem((4, 48, 256), BF),
            g3=vmem((2, 192, 256), BF),
            wq=vmem((4, 48, 1024), BF),
            wri=vmem((2, 128, 256), BF),
            w3=vmem((2, 192, 1024), BF),
            wo=vmem((256, 1024), BF),
            wgu_out=vmem((2, 256, 384), BF),
            wgu_all=vmem((8, 256, 384), BF),
            wmd_all=vmem((4, 96, 1024), BF),
            gp=vmem((8, 512, 128), F32),
            gb=vmem((8, 520, 128), F32),
            inner=vmem((8, 520, 128), F32),
            conv=vmem((8, 512, 128), BF),
            sr=vmem((8, 512, 128), F32),
            si=vmem((8, 512, 128), F32),
            dec=vmem((8, 512, 128), F32),
            drv=vmem((8, 512, 128), F32),
            states=vmem((8, 520, 128), F32),
            mixed=vmem((8, 256, 256), BF),
            tot=vmem((2, 4, 2, 8, 128), F32),
            inc=vmem((8, 128), F32),
            rs_all=vmem((4, 8, 8, 128), F32),
            rows_sum=vmem((8, 8, 128), F32),
            residual=vmem((256, 1024), F32),
            d_res=vmem((256, 1024), F32),
            hid=vmem((8, 256, 384), BF),
            dgu=vmem((8, 256, 768), BF),
            gm=vmem((4, 256, 768), BF),
            gm_sum=vmem((256, 768), BF),
            gd=vmem((4, 96, 1024), BF),
            gd_in=vmem((3, 96, 1024), BF),
            gd_sum=vmem((96, 1024), BF),
            go=vmem((256, 1280), BF),
            go_q=vmem((4, 48, 1280), BF),
            go_l=vmem((3, 48, 1280), BF),
            go_sum=vmem((48, 1280), BF),
            ga_sum=vmem((256, 256), BF),
            gb2_sum=vmem((128, 256), BF),
            gain2_sum=vmem((8, 1024), F32),
            vec=vmem((2, 8, 8, 128), F32),
            vsum=vmem((4, 8, 256), F32),
            vout=vmem((4, 8, 256), F32),
            gsum=vmem((8, 8, 128), F32),
            gline=vmem((8, 8, 128), F32),
            gplane=vmem((4, 8, 128), F32),
            free=pltpu.SemaphoreType.REGULAR,
            **reduce_scratch(256, 1024),
        ),
        210,
        36,
        (
            "g", "wg", "wi", "wr", "wv", "wout", "wmg", "wmu", "wmd", "d_in", "block_out", "fm", "fd", "fa", "fb", "fo",
            "fr", "normed_far",
        ),
    )
    out = kernel_call(
        assemble,
        dict(
            {name: done[name] for name in ("fm", "fd", "fa", "fb", "fo", "fr")},
            vec_in=done["vec_out"], gains=done["gain_out"], lens=row_lengths,
        ),
        dict(
            o_gate=array(128, 1536),
            o_in=array(128, 1536),
            o_mgate=array(128, 3072),
            o_mup=array(128, 3072),
            o_mdown=array(384, 1024),
            o_out=array(192, 1024),
            o_r=array(192, 128),
            o_i=array(192, 128),
            o_cw=array(4, 192),
            o_cb=array(1, 192),
            o_rb=array(1, 192),
            o_ib=array(1, 192),
            o_lam=array(1, 192),
            o_ngain=array(1, 128),
            o_mgain=array(1, 128),
            o_mean=array(5, 1, 1536),
        ),
        {},
        0,
        0,
        (),
    )
    return (
        done["block_out"][None],
        done["d_in"][None],
        out["o_ngain"][0],
        out["o_gate"],
        out["o_in"],
        out["o_cw"],
        out["o_cb"][0],
        out["o_r"],
        out["o_rb"][0],
        out["o_i"],
        out["o_ib"][0],
        out["o_lam"][0],
        out["o_out"],
        out["o_mgain"][0],
        out["o_mgate"],
        out["o_mup"],
        out["o_mdown"],
        jnp.transpose(out["o_mean"], (1, 0, 2)),
    )


def solution(mesh):
    in_specs = (
        P("batch", "seq", None),
        P("batch", "seq", None),
        P("batch", None),
        P("seq"),
        P("seq", None),
        P("seq", None),
        P(None, "seq"),
        P("seq"),
        P("seq", None),
        P("seq"),
        P("seq", None),
        P("seq"),
        P("seq"),
        P("seq", None),
        P("seq"),
        P("seq", None),
        P("seq", None),
        P("seq", None),
    )
    out_specs = (
        P("batch", "seq", None),
        P("batch", "seq", None),
        P("seq"),
        P("seq", None),
        P("seq", None),
        P(None, "seq"),
        P("seq"),
        P("seq", None),
        P("seq"),
        P("seq", None),
        P("seq"),
        P("seq"),
        P("seq", None),
        P("seq"),
        P("seq", None),
        P("seq", None),
        P("seq", None),
        P("batch", None, None),
    )
    in_planes = mesh.shape["batch"] == 4 and mesh.shape["seq"] == 8
    body = planes if in_planes else shards
    return jax.shard_map(body, mesh=mesh, in_specs=in_specs, out_specs=out_specs, check_vma=False)
```

```python
import functools
import types

import jax
import jax.numpy as jnp
from jax import lax
from jax.experimental import pallas as pl
from jax.experimental.pallas import tpu as pltpu
from jax.sharding import PartitionSpec as P

NORM_EPS = 1e-06
DECAY_SCALE = 8.0
BF = jnp.bfloat16
F32 = jnp.float32
GELU_SCALE = 0.7978845608028654
GELU_CUBE = 0.044715
TILE = 64
NN = (((1,), (0,)), ((), ()))
NT = (((1,), (1,)), ((), ()))
TN = (((0,), (0,)), ((), ()))


def dot(left, right, dims=NN):
    return lax.dot_general(left, right, dims, preferred_element_type=F32)


def loop(count, body):
    def step(i, carry):
        body(i)
        return carry

    lax.fori_loop(0, count, step, 0)


class Net:
    def __init__(self, r):
        self.send, self.recv, self.count = r.send, r.recv, 0
        self.here, self.here_count = r.local, 0
        self.pending = []
        self.p = lax.axis_index("batch")
        self.q = lax.axis_index("seq")
        self.z = lax.div(self.q, 2)
        self.c = lax.rem(self.q, 2)
        self.o = 1 - self.c
        p = self.p
        self.near = (p, p + 1 - 2 * lax.rem(p, 2), lax.rem(p + 2, 4), 3 - p)

    def plane(self, k, core):
        return {"batch": self.near[k], "seq": self.z * 2 + core}

    def line(self, z, core):
        return {"batch": self.p, "seq": z * 2 + core}

    def up(self, k):
        return lax.rem(self.z + k, 4)

    def down(self, k):
        return lax.rem(self.z + 4 - k, 4)

    def slot(self, k, core):
        return self.near[k] * 2 + core

    def greet(self):
        barrier = pltpu.get_barrier_semaphore()
        partners = [self.plane(k, core) for k in (1, 2, 3) for core in (0, 1)]
        partners += [self.line(self.up(k), core) for k in (1, 2, 3) for core in (0, 1)]
        partners += [self.line(self.z, self.o)]
        for partner in partners:
            pl.semaphore_signal(barrier, inc=1, device_id=partner, device_id_type=pl.DeviceIdType.MESH)
        pl.semaphore_wait(barrier, len(partners))

    def reserve(self, count):
        first = self.count
        self.count += count
        return first

    def describe(self, src, dst, device, send_at, recv_at):
        return pltpu.make_async_remote_copy(
            src_ref=src,
            dst_ref=dst,
            send_sem=self.send.at[send_at],
            recv_sem=self.recv.at[recv_at],
            device_id=device,
            device_id_type=pl.DeviceIdType.MESH,
        )

    def copy(self, src, dst, device, sent=None, at=None):
        at = self.reserve(1) if at is None else at
        made = self.describe(src, dst, device, at, at)
        made.start()
        (self.pending if sent is None else sent).append(made)
        return made

    def local(self, src, dst):
        made = pltpu.make_async_copy(src, dst, self.here.at[self.here_count])
        self.here_count += 1
        made.start()
        return made

    def drain(self):
        assert (self.count, self.here_count) == (self.send.shape[0], self.here.shape[0]), (self.count, self.here_count)
        for made in self.pending:
            made.wait_send()
        self.pending = []


class Gather:
    def __init__(self, net, own, everything, at=None):
        self.net, self.own, self.all = net, own, everything
        self.sent = []
        self.at = net.reserve(10) if at is None else at
        self.half = everything.shape[1] // 2

    def part(self, slot, h):
        return self.all.at[slot, pl.ds(h * self.half, self.half)]

    def start(self):
        net = self.net
        mine = net.slot(0, net.c)
        low, high = self.own.at[pl.ds(0, self.half)], self.own.at[pl.ds(self.half, self.half)]
        self.s = []
        self.x0 = net.copy(low, self.part(mine, 0), net.plane(1, net.c), self.sent, self.at + 0)
        self.y1 = net.copy(high, self.part(mine, 1), net.plane(2, net.c), self.sent, self.at + 1)
        self.x1 = net.copy(high, self.part(mine, 1), net.plane(1, net.c), self.sent, self.at + 2)
        self.y0 = net.copy(low, self.part(mine, 0), net.plane(2, net.c), self.sent, self.at + 3)
        self.s.append(net.copy(self.own, self.all.at[mine], net.plane(0, net.o), self.sent, self.at + 4))

    def forward(self):
        net = self.net
        self.x0.wait_recv()
        mine = self.part(net.slot(1, net.c), 0)
        self.d0 = net.copy(mine, mine, net.plane(2, net.c), self.sent, self.at + 5)
        self.y1.wait_recv()
        mine = self.part(net.slot(2, net.c), 1)
        self.d1 = net.copy(mine, mine, net.plane(1, net.c), self.sent, self.at + 6)

    def across(self, k):
        net = self.net
        mine = self.all.at[net.slot(k, net.c)]
        self.s.append(net.copy(mine, mine, net.plane(0, net.o), self.sent, self.at + 6 + k))

    def middle(self):
        self.x1.wait_recv()
        self.across(1)
        self.y0.wait_recv()
        self.across(2)

    def last(self):
        self.d0.wait_recv()
        self.d1.wait_recv()
        self.across(3)

    def sibling(self, k):
        self.s[k].wait_recv()

    def release(self):
        for made in self.sent:
            made.wait_send()
        self.sent = []


class LineGather:
    def __init__(self, net, own, first, place):
        self.net, self.own, self.first, self.place = net, own, first, place
        self.at = net.reserve(4 * len(own))

    def made(self, k, j):
        net = self.net
        src, core = self.own[j]
        at = self.at + 4 * j + k - 1
        return net.describe(src, self.first(j), net.line(net.up(k), core), at, at)

    def handed(self, j):
        net = self.net
        far = 6 - 3 * net.z
        here = self.place(j, far)
        at = self.at + 4 * j
        return net.describe(here, here, net.line(3 - far, net.c), at + 3, at + 2 * net.z - 2)

    def direct(self, k, body):
        z = self.net.z
        if k == 2:
            body()
        else:
            pl.when(z != (0 if k == 3 else 3))(body)

    def start(self, k, items):
        def send():
            for j in items:
                self.made(k, j).start()

        self.direct(k, send)

    def inside(self, body):
        z = self.net.z
        pl.when((z == 1) | (z == 2))(body)

    def relay(self):
        @self.inside
        def _():
            for j in range(len(self.own)):
                self.made(2, j).wait_recv()
                self.handed(j).start()

    def end(self):
        z = self.net.z
        for k in (1, 3):
            for j in range(len(self.own)):
                self.made(k, j).wait_recv()

        @pl.when((z == 0) | (z == 3))
        def _():
            for j in range(len(self.own)):
                self.made(2, j).wait_recv()

    def drain(self):
        for k in (1, 2, 3):

            def wait(k=k):
                for j in range(len(self.own)):
                    self.made(k, j).wait_send()

            self.direct(k, wait)

        @self.inside
        def _():
            for j in range(len(self.own)):
                self.handed(j).wait_send()


class LineSum:
    def __init__(self, net, block, slot):
        self.net, self.block, self.slot = net, block, slot
        self.at = net.reserve(3)

    def made(self, k):
        net = self.net
        at = self.at + k - 1
        to = lax.rem(2 * net.z + 1, 5) if k == 2 else net.up(k)
        return net.describe(self.block(net.up(k)), self.slot(k), net.line(to, net.c), at, at)

    def start(self):
        z = self.net.z
        self.made(2).start()
        pl.when(z != 1)(lambda: self.made(1).start())
        pl.when(z != 2)(lambda: self.made(3).start())

    def relay(self, step=16):
        z = self.net.z

        @pl.when((z == 1) | (z == 2))
        def _():
            self.made(2).wait_recv()
            mine, extra = self.block(3 - z), self.slot(2)

            def body(i):
                rows = pl.ds(pl.multiple_of(i * step, step), step)
                mine[rows, :] = (mine[rows, :].astype(F32) + extra[rows, :].astype(F32)).astype(BF)

            loop(mine.shape[0] // step, body)

        pl.when(z == 1)(lambda: self.made(1).start())
        pl.when(z == 2)(lambda: self.made(3).start())

    def end(self, dst, step=16):
        z = self.net.z
        self.made(1).wait_recv()
        self.made(3).wait_recv()
        edge = (z == 0) | (z == 3)
        pl.when(edge)(lambda: self.made(2).wait_recv())
        share = jnp.where(edge, 1.0, 0.0)
        own = self.block(z)

        def body(i):
            rows = pl.ds(pl.multiple_of(i * step, step), step)
            value = own[rows, :].astype(F32) + share * self.slot(2)[rows, :].astype(F32)
            value = value + self.slot(1)[rows, :].astype(F32) + self.slot(3)[rows, :].astype(F32)
            dst[rows, :] = value.astype(BF)

        loop(dst.shape[0] // step, body)

    def drain(self):
        for k in (1, 2, 3):
            self.made(k).wait_send()


class Reduce:
    def __init__(self, net, r, value, at=None):
        self.net, self.value = net, value
        self.at = net.reserve(10) if at is None else at
        self.keep, self.out, self.into = r.rs_keep, r.rs_out, r.rs_in
        self.xs, self.ys, self.xr, self.yr = r.rs_xs, r.rs_ys, r.rs_xr, r.rs_yr
        self.half = self.keep.shape[1]
        self.cross = [None] * 4
        self.sent = []

    def other(self, k):
        net = self.net
        self.out[k] = self.value(k, net.o).astype(BF)
        self.cross[k] = net.copy(self.out.at[k], self.into.at[k], net.plane(0, net.o), self.sent, self.at + k)

    def mine(self, k):
        self.cross[k].wait_recv()
        value = self.value(k, self.net.c) + self.into[k].astype(F32)
        return value[: self.half], value[self.half :]

    def send(self, src, dst, j, k):
        net = self.net
        at = self.at + 4 + j + (0 if src is self.xs else 3)
        return net.copy(src.at[j], dst.at[j], net.plane(k, net.c), self.sent, at)

    def far(self):
        low, high = self.mine(3)
        self.xs[0] = low.astype(BF)
        self.x0 = self.send(self.xs, self.xr, 0, 1)
        self.ys[0] = high.astype(BF)
        self.y0 = self.send(self.ys, self.yr, 0, 2)

    def near(self):
        low, high = self.mine(1)
        self.xs[1] = low.astype(BF)
        self.x1 = self.send(self.xs, self.xr, 1, 1)
        self.keep[2] = high
        low, high = self.mine(2)
        self.ys[1] = high.astype(BF)
        self.y1 = self.send(self.ys, self.yr, 1, 2)
        self.keep[3] = low

    def relay(self):
        self.x0.wait_recv()
        self.ys[2] = (self.keep[3] + self.xr[0].astype(F32)).astype(BF)
        self.y2 = self.send(self.ys, self.yr, 2, 2)
        self.y0.wait_recv()
        self.xs[2] = (self.keep[2] + self.yr[0].astype(F32)).astype(BF)
        self.x2 = self.send(self.xs, self.xr, 2, 1)

    def own(self):
        self.keep[0], self.keep[1] = self.mine(0)

    def finish(self):
        for made in (self.x1, self.y1, self.x2, self.y2):
            made.wait_recv()
        for made in self.sent:
            made.wait_send()
        self.sent = []

    def total(self, h, i, step):
        rows = pl.ds(pl.multiple_of(i * step, step), step)
        first, second = (self.xr, self.yr) if h == 0 else (self.yr, self.xr)
        return self.keep[h, rows, :] + first[1, rows, :].astype(F32) + second[2, rows, :].astype(F32)


def reduce_scratch(rows, width):
    half = rows // 2
    return dict(
        rs_keep=pltpu.VMEM((4, half, width), F32),
        rs_out=pltpu.VMEM((4, rows, width), BF),
        rs_in=pltpu.VMEM((4, rows, width), BF),
        rs_xs=pltpu.VMEM((3, half, width), BF),
        rs_ys=pltpu.VMEM((3, half, width), BF),
        rs_xr=pltpu.VMEM((3, half, width), BF),
        rs_yr=pltpu.VMEM((3, half, width), BF),
    )


def kernel_call(body, ins, outs, scratch, copies, local, far):
    names = list(ins) + list(outs) + list(scratch)
    near = pl.BlockSpec(memory_space=pltpu.VMEM)
    away = pl.BlockSpec(memory_space=pl.ANY)
    shapes = list(scratch.values())
    if copies:
        names += ["send", "recv"]
        shapes += [pltpu.SemaphoreType.DMA((copies,))] * 2
    if local:
        names.append("local")
        shapes.append(pltpu.SemaphoreType.DMA((local,)))

    def kernel(*refs):
        body(types.SimpleNamespace(**dict(zip(names, refs))))

    params = dict(vmem_limit_bytes=62 * 2**20)
    if copies:
        params.update(collective_id=0, has_side_effects=True)
    results = pl.pallas_call(
        kernel,
        out_shape=list(outs.values()),
        in_specs=[away if name in far else near for name in ins],
        out_specs=[away if name in far else near for name in outs],
        scratch_shapes=shapes,
        compiler_params=pltpu.CompilerParams(**params),
        name=body.__name__,
    )(*ins.values())
    return dict(zip(outs, results))


def array(*shape, dtype=F32):
    return jax.ShapeDtypeStruct(shape, dtype)


def gelu_parts(v):
    square = v * v
    t = jnp.tanh(GELU_SCALE * v * (1.0 + GELU_CUBE * square))
    half = 0.5 + 0.5 * t
    slope = half + 0.5 * v * (1.0 - t * t) * (GELU_SCALE * (1.0 + 3.0 * GELU_CUBE * square))
    return v * half, slope


def decay_parts(sr, rate):
    log_a = -DECAY_SCALE * sr * rate
    a = jnp.exp(log_a)
    y = 2.0 * log_a
    series = 1.0 + y * (1 / 6) * (1.0 + y * (1 / 7))
    for n in (5, 4, 3, 2):
        series = 1.0 + y * (1 / n) * series
    m2 = jnp.where(y > -0.35, -y * series, 1.0 - a * a)
    return a, jnp.maximum(m2, 1e-36)


def column_sum(value):
    return jnp.sum(value.reshape(-1, 8, 128), axis=0)


def scan_slabs(decay, value, reverse):
    count = decay.shape[1] // 8
    row = lax.broadcasted_iota(jnp.int32, (8, 128), 0)

    def step(i, carry):
        t = count - 1 - i if reverse else i
        at = pl.ds(pl.multiple_of(t * 8, 8), 8)
        done = []
        for s in range(8):
            pc, vc = carry[s]
            p, own = decay[s, at, :], value[s, at, :]
            v = p * own if reverse else own
            for d in (1, 2, 4):
                by = 8 - d if reverse else d
                inside = row < 8 - d if reverse else row >= d
                v = v + p * jnp.where(inside, pltpu.roll(v, by, 0), 0.0)
                p = p * jnp.where(inside, pltpu.roll(p, by, 0), 1.0)
            v = v + p * vc
            p = p * pc
            if reverse:
                edge = row == 7
                value[s, at, :] = own + jnp.where(edge, vc, pltpu.roll(v, 7, 0))
                decay[s, at, :] = jnp.where(edge, pc, pltpu.roll(p, 7, 0))
                last = slice(0, 1)
            else:
                value[s, at, :] = v
                decay[s, at, :] = p
                last = slice(7, 8)
            done.append((jnp.broadcast_to(p[last], (8, 128)), jnp.broadcast_to(v[last], (8, 128))))
        return tuple(done)

    start = tuple((jnp.ones((8, 128), F32), jnp.zeros((8, 128), F32)) for _ in range(8))
    return lax.fori_loop(0, count, step, start)


def exchange_ends(r, net, ends, at):
    for s in range(8):
        r.tot[at, net.z, 0, s : s + 1, :] = ends[s][0][0:1, :]
        r.tot[at, net.z, 1, s : s + 1, :] = ends[s][1][0:1, :]
    mine = r.tot.at[at, net.z]
    return [net.copy(mine, mine, net.line(net.up(k), net.c)) for k in (1, 2, 3)]


def entering_states(r, net, copies, at, reverse):
    for made in copies:
        made.wait_recv()
    state = jnp.zeros((8, 128), F32)
    for i in range(4):
        z = 3 - i if reverse else i
        new = r.tot[at, z, 0] * state + r.tot[at, z, 1]
        state = jnp.where((z > net.z) if reverse else (z < net.z), new, state)
    r.inc[...] = state


def tile_rows(i):
    return pl.ds(pl.multiple_of(i * TILE, TILE), TILE)


def layer(r):
    r.do_all = r.x_all
    r.dconv = r.gb
    r.dgi = r.dgu
    r.ug, r.ul = r.d_res.at[:, 0:384], r.d_res.at[:, 384:768]
    r.ga = [r.hid.at[i, :, 0:256] for i in range(4)]
    r.gb2 = [r.hid.at[4 + i, 0:128, 0:256] for i in range(4)]
    net = Net(r)
    p, z, c, o, q = net.p, net.z, net.c, net.o, net.q
    sibling = net.plane(0, o)
    mine = net.slot(0, c)
    cols = r.wgu_out.shape[2]
    piece = cols // 4
    down = pl.ds(pl.multiple_of(p * piece, 16), piece)
    quarter = pl.ds(pl.multiple_of(p * 48, 16), 48)
    staged = []
    for j in range(8):
        lanes = pl.ds(j * cols, cols)
        staged.append(net.local(r.wmg.at[:, lanes], r.hid.at[j, pl.ds(0, 128)]))
        staged.append(net.local(r.wmu.at[:, lanes], r.hid.at[j, pl.ds(128, 128)]))
    width = 3 * 128
    first = pl.multiple_of(p * width, 128)
    chip = pl.ds(first, width)
    own_lanes = pl.ds(pl.multiple_of(c * width, 128), width)
    wi_rows, wg_rows = pl.ds(128, 128), pl.ds(0, 128)
    placed = [
        net.local(r.wg.at[:, chip], r.wgi3.at[z, wg_rows, own_lanes]),
        net.local(r.wi.at[:, chip], r.wgi3.at[z, wi_rows, own_lanes]),
        net.local(r.wmd.at[down], r.wmd_all.at[z]),
        net.local(r.wout.at[quarter], r.wq.at[z]),
        net.local(r.wr.at[quarter], r.gq.at[z, :, pl.ds(0, 128)]),
        net.local(r.wv.at[quarter], r.gq.at[z, :, pl.ds(128, 128)]),
        net.local(r.g, r.g_all.at[mine]),
    ]
    r.lens_out[0:1, 0:5] = r.lens[...].astype(F32)
    r.small_rows[...] = jnp.zeros((16, 256), F32)
    r.small_rows[0:4, 0:192] = r.cw[...].astype(F32)
    for at, ref in ((4, r.cb), (5, r.br), (6, r.bi), (7, r.lam)):
        r.small_rows[at : at + 1, 0:192] = ref[...].astype(F32).reshape(1, 192)
    for at, ref in ((0, r.ngain), (128, r.mgain)):
        r.small_rows[10:11, at : at + 128] = ref[...].astype(F32).reshape(1, 128)
    r.small[...] = r.small_rows[...].astype(BF)
    net.greet()
    r.small_all[q] = r.small[...]
    r.lens_all[p] = r.lens_out[...]
    small = [net.copy(r.small, r.small_all.at[q], net.line(net.up(k), core)) for k in (1, 2, 3) for core in (c, o)]
    small.append(net.copy(r.small, r.small_all.at[q], sibling))
    lens = [net.copy(r.lens_out, r.lens_all.at[p], net.plane(k, c)) for k in (1, 2, 3)]
    tokens = Gather(net, r.x, r.x_all)
    tokens.start()
    theirs = pl.ds(pl.multiple_of(c * width + o * 128, 128), 256)

    def along(ref, sent=None):
        return [net.copy(ref, ref, net.line(net.up(k), c), sent) for k in (1, 2, 3)]

    handed = []

    def heads_start(rows):
        here = r.wgi3.at[z, rows, theirs]
        return along(r.wgi3.at[z, rows, own_lanes], handed), [net.copy(here, here, sibling, handed)]

    for made in placed:
        made.wait()
    heads_in, heads_in_over = heads_start(wi_rows)
    gates_in = along(r.gq.at[z])

    def hand_over(copies, rows, over):
        for k in (1, 2, 3):
            copies[k - 1].wait_recv()
            here = r.wgi3.at[net.down(k), rows, theirs]
            over.append(net.copy(here, here, sibling, handed))

    def arrange(over, rows, lanes):
        for made in over:
            made.wait_recv()
        for core in range(2):
            cols_in = pl.ds(pl.multiple_of(core * width + c * 128, 128), 256)
            for at in range(4):
                to = slice((at * 2 + core) * 128, (at * 2 + core + 1) * 128)
                r.w2[to, lanes] = r.wgi3[at, rows, cols_in]

    def exchange(arrivals, src, dst):
        for made in arrivals:
            made.wait_recv()
        dst[c, quarter, :] = src[p]
        return [net.copy(src.at[net.near[k]], dst.at[c, quarter], net.plane(k, c)) for k in (1, 2, 3)]

    def share(copies, dst):
        for made in copies:
            made.wait_recv()
        return net.copy(dst.at[c], dst.at[c], sibling)

    selects = []
    k_at = lax.broadcasted_iota(jnp.int32, (cols, cols), 0)
    j_at = lax.broadcasted_iota(jnp.int32, (cols, cols), 1)
    for part in range(4):
        inside = (j_at >= part * piece) & (j_at < (part + 1) * piece)
        chosen = inside & (k_at == j_at + (p - part) * piece)
        selects.append(jnp.where(chosen, 1.0, 0.0).astype(BF))
    for made in staged:
        made.wait()
    for which in range(2):
        rows = slice(which * 128, (which + 1) * 128)
        for core in (0, 1):
            picked = None
            for part in range(4):
                term = dot(r.hid[part * 2 + core, rows, :], selects[part])
                picked = term if picked is None else picked + term
            r.wgu_out[core, rows, :] = picked.astype(BF)
    for made in small + lens:
        made.wait_recv()
    low, high = r.small_all[2 * p].astype(F32), r.small_all[2 * p + 1].astype(F32)
    at_first = jnp.concatenate([low[:, :192], high[:, :64]], axis=1)
    at_second = jnp.concatenate([low[:, 128:192], high[:, :192]], axis=1)
    both = lax.select(c == 0, at_first, at_second)
    for n in range(2):
        r.chan[n] = both[:, n * 128 : (n + 1) * 128]
        lam = -r.chan[n, 7:8, :]
        e = jnp.exp(-jnp.abs(lam))
        series = 1.0 - e * (6 / 7)
        for k in (6, 5, 4, 3, 2):
            series = 1.0 - e * ((k - 1) / k) * series
        rate = jnp.maximum(lam, 0.0) + jnp.where(e < 0.05, e * series, jnp.log(1.0 + e))
        r.chan[n, 7:8, :] = rate
        r.chan[n, 8:9, :] = jax.nn.sigmoid(lam)
    for i in range(8):
        gains = r.small_all[i].astype(F32)[10:11, :]
        r.gain[0:1, i * 128 : (i + 1) * 128] = gains[:, 0:128]
        r.gain[1:2, i * 128 : (i + 1) * 128] = gains[:, 128:256]
    gain = r.gain[0:1, :]
    for b in range(4):
        start = jnp.zeros((1, 128), F32)
        for row in range(5):
            r.starts_all[b, row : row + 1, :] = start
            start = start + jnp.broadcast_to(r.lens_all[b, 0:1, row : row + 1], (1, 128))


    def offset_rows(i):
        b, tile = lax.div(i, 13), lax.rem(i, 13)
        starts = r.starts_all[b]
        at = lax.convert_element_type(z * 512 + tile * 40, F32)
        at = at + lax.broadcasted_iota(jnp.int32, (40, 128), 0).astype(F32)
        begun = jnp.zeros((40, 128), F32)
        for row in range(1, 5):
            start = starts[row : row + 1, :]
            begun = jnp.where(at >= start, start, begun)
        r.off[b, pl.ds(pl.multiple_of(tile * 40, 8), 40), :] = at - begun

    loop(52, offset_rows)

    def normalise(slot):
        def body(i):
            rows = pl.ds(pl.multiple_of(i * 32, 32), 32)
            v = r.x_all[slot, rows, :].astype(F32)
            s = lax.rsqrt(jnp.mean(v * v, axis=-1, keepdims=True) + NORM_EPS)
            r.normed[slot, rows, :] = (v * s * gain).astype(BF)

        loop(8, body)

    r.x_all[mine] = r.x[...]
    normalise(mine)
    tokens.sibling(0)
    normalise(net.slot(0, o))
    tokens.forward()
    out_in = along(r.wq.at[z])
    heads_gate, heads_gate_over = heads_start(wg_rows)
    hand_over(heads_in, wi_rows, heads_in_over)
    tokens.middle()
    for k in (1, 2):
        normalise(net.slot(k, c))
    for k in (1, 2):
        tokens.sibling(k)
        normalise(net.slot(k, o))
    arrange(heads_in_over, slice(128, 256), slice(256, 512))

    def project_inner(slot):
        b, half = lax.div(slot, 2), lax.rem(slot, 2)
        at = pl.multiple_of(half * 256, 256)
        inner = dot(r.normed[slot], r.w2[:, 256:512]).astype(BF).astype(F32)
        for n in range(2):
            r.inner[b * 2 + n, pl.ds(at + 8, 256), :] = inner[:, n * 128 : (n + 1) * 128]

    def project_gate(slot):
        b, half = lax.div(slot, 2), lax.rem(slot, 2)
        at = pl.multiple_of(half * 256, 256)
        gate = dot(r.normed[slot], r.w2[:, 0:256])
        for n in range(2):
            r.gp[b * 2 + n, pl.ds(at, 256), :] = gate[:, n * 128 : (n + 1) * 128]

    for k in (0, 1, 2):
        project_inner(net.slot(k, c))
        project_inner(net.slot(k, o))
    gates_out = exchange(gates_in, r.gq, r.g3)
    tokens.last()
    normalise(net.slot(3, c))
    project_inner(net.slot(3, c))
    tokens.sibling(3)
    normalise(net.slot(3, o))
    project_inner(net.slot(3, o))
    edge = net.reserve(1)

    def edge_copy():
        return net.describe(
            r.inner.at[:, pl.ds(512, 8)], r.inner.at[:, pl.ds(0, 8)], net.line(net.up(1), c), edge, edge
        )

    @pl.when(z < 3)
    def _():
        edge_copy().start()

    @pl.when(z == 0)
    def _():
        r.inner[:, 0:8, :] = jnp.zeros((8, 8, 128), F32)

    gates_over = share(gates_out, r.g3)
    stored = net.local(r.normed, r.normed_far)
    tokens.release()
    gates_over.wait_recv()
    for i in range(4):
        at = c * 128 + i * 64
        value = r.g3[lax.div(at, 192), pl.ds(pl.multiple_of(lax.rem(at, 192), 64), 64), :]
        r.wri[i // 2, (i % 2) * 64 : (i % 2 + 1) * 64, :] = value

    @pl.when(z > 0)
    def _():
        edge_copy().wait_recv()


    def conv_tile(i):
        b, tile = lax.div(i, 8), lax.rem(i, 8)
        rows = tile_rows(tile)
        offset = r.off[b, rows, :]
        for n in range(2):
            s = b * 2 + n
            window = r.inner[s, pl.ds(pl.multiple_of(tile * TILE, 8), TILE + 8), :]
            chan = r.chan[n]
            total = chan[4:5, :] + chan[0:1, :] * window[8:, :]
            for k in (1, 2, 3):
                total = total + chan[k : k + 1, :] * jnp.where(offset >= k, window[8 - k : TILE + 8 - k, :], 0.0)
            r.conv[s, rows, :] = total.astype(BF)

    loop(32, conv_tile)
    feed = LineGather(
        net,
        [(r.wgu_out.at[core], core) for core in (c, o)],
        lambda j: r.wgu_all.at[q],
        lambda j, at: r.wgu_all.at[at * 2 + (c, o)[j]],
    )
    feed_down = LineGather(net, [(r.wmd.at[down], c)], lambda j: r.wmd_all.at[z], lambda j, at: r.wmd_all.at[at])
    feed.start(2, (0,))
    out_rows_in = exchange(out_in, r.wq, r.w3)
    cots = Gather(net, r.g_all.at[mine], r.g_all)
    cots.start()

    def gate_products(i):
        s, half = lax.div(i, 2), lax.rem(i, 2)
        n = lax.rem(s, 2)
        rows = pl.ds(pl.multiple_of(half * 256, 256), 256)
        pre = dot(r.conv[s, rows, :], r.wri[n])
        r.sr[s, rows, :] = pre[:, :128]
        r.si[s, rows, :] = pre[:, 128:]

    loop(16, gate_products)

    def terms(b):
        starts_b = r.starts_all[b]

        def tile(i, sums):
            rows = tile_rows(i)
            offset = r.off[b, rows, :]
            at = lax.convert_element_type(z * 512 + i * TILE, F32)
            begun = at + lax.broadcasted_iota(jnp.int32, (TILE, 128), 0).astype(F32) - offset
            restart = offset == 0.0
            added = []
            for n in range(2):
                s = b * 2 + n
                chan = r.chan[n]
                sr = jax.nn.sigmoid(r.sr[s, rows, :] + chan[5:6, :])
                si = jax.nn.sigmoid(r.si[s, rows, :] + chan[6:7, :])
                r.sr[s, rows, :] = sr
                r.si[s, rows, :] = si
                a, m2 = decay_parts(sr, chan[7:8, :])
                r.dec[s, rows, :] = jnp.where(restart, 0.0, a)
                m = jnp.where(restart, 1.0, jnp.sqrt(m2))
                r.drv[s, rows, :] = m * si * r.conv[s, rows, :].astype(F32)
                for row in range(5):
                    inside = jnp.where(begun == starts_b[row : row + 1, :], a, 0.0)
                    added.append(sums[n * 5 + row] + column_sum(inside))
            return tuple(added)

        sums = lax.fori_loop(0, 512 // TILE, tile, tuple(jnp.zeros((8, 128), F32) for _ in range(10)))
        for n in range(2):
            rows = [jnp.sum(part, axis=0, keepdims=True) for part in sums[n * 5 : n * 5 + 5]]
            r.rs_all[z, b * 2 + n] = jnp.concatenate(rows + [jnp.zeros((3, 128), F32)], axis=0)

    loop(4, terms)
    ends = scan_slabs(r.dec, r.drv, False)
    ends = exchange_ends(r, net, ends, 0)
    feed.start(2, (1,))
    feed.start(1, (0, 1))
    feed.start(3, (0, 1))
    r.wgu_all[q] = r.wgu_out[c]
    feed_over = net.copy(r.wgu_out.at[o], r.wgu_all.at[q], sibling)
    hand_over(heads_gate, wg_rows, heads_gate_over)
    cots.forward()
    arrange(heads_gate_over, slice(0, 128), slice(0, 256))
    for made in handed:
        made.wait_send()
    for k in (2, 1, 3):
        feed_down.start(k, (0,))
    for slot in range(8):
        project_gate(slot)

    def gelu_tile(i):
        s, rows = lax.div(i, 8), tile_rows(lax.rem(i, 8))
        v = r.gp[s, rows, :]
        t = jnp.tanh(GELU_SCALE * v * (1.0 + GELU_CUBE * v * v))
        r.gb[s, rows, :] = 0.5 * v * (1.0 + t)

    loop(64, gelu_tile)
    out_over = share(out_rows_in, r.w3)
    entering_states(r, net, ends, 0, False)
    row_sums = [net.copy(r.rs_all.at[z], r.rs_all.at[z], net.line(net.up(k), c)) for k in (1, 2, 3)]
    out_over.wait_recv()

    def own_rows(i):
        at = c * 128 + i * 64
        value = r.w3[lax.div(at, 192), pl.ds(pl.multiple_of(lax.rem(at, 192), 64), 64), :]
        r.wo[pl.ds(pl.multiple_of(i * 64, 64), 64), :] = value

    loop(4, own_rows)
    for s in range(8):
        r.states[s, 7:8, :] = r.inc[s : s + 1, :]

    def mix_tile(i):
        s, tile = lax.div(i, 8), lax.rem(i, 8)
        b, n = lax.div(s, 2), lax.rem(s, 2)
        rows = tile_rows(tile)
        states = r.drv[s, rows, :] + r.dec[s, rows, :] * r.inc[pl.ds(s, 1), :]
        r.states[s, pl.ds(pl.multiple_of(tile * TILE + 8, 8), TILE), :] = states
        lanes = pl.ds(pl.multiple_of(n * 128, 128), 128)
        r.mixed[b * 2 + lax.div(tile, 4), tile_rows(lax.rem(tile, 4)), lanes] = (states * r.gb[s, rows, :]).astype(BF)

    loop(64, mix_tile)
    stored.wait()
    lane = lax.broadcasted_iota(jnp.int32, (1, 256), 1)
    counted = jnp.where((lane >= 64 * c) & (lane < 192 + 64 * c), 1.0, 0.0)
    counted_two = jnp.concatenate([counted, counted], axis=1)

    def masked(value, mask):
        return (value.astype(F32) * mask).astype(BF)

    total = Reduce(
        net, r, lambda k, core: dot(masked(r.mixed[net.slot(k, core)], counted), r.wo[...])
    )
    for k in (3, 1, 2, 0):
        total.other(k)
    total.far()
    total.near()
    cots.middle()
    total.own()
    cots.last()
    for k in (0, 1, 2, 3):
        cots.sibling(k)
    cots.release()
    total.relay()
    feed_down.relay()
    feed.relay()
    def wmd():
        return r.wmd_all[...].reshape(cols, -1)

    total.finish()
    gain2 = r.gain[1:2, :]
    for h in range(2):

        def residual_rows(i, h=h):
            rows = pl.ds(pl.multiple_of(h * 128 + i * 32, 32), 32)
            v = r.x[rows, :].astype(F32) + total.total(h, i, 32)
            r.residual[rows, :] = v
            s = lax.rsqrt(jnp.mean(v * v, axis=-1, keepdims=True) + NORM_EPS)
            r.normed[mine, rows, :] = (v * s * gain2).astype(BF)

        loop(4, residual_rows)

    n2_all = r.normed
    acts = Gather(net, n2_all.at[mine], n2_all, tokens.at)
    acts.start()

    def gate_up(which):
        return r.wgu_all[:, which * 128 : (which + 1) * 128, :].reshape(-1, cols)

    def d_normed2(k, core):
        slot = net.slot(k, core)
        return dot(r.dgu[slot, :, 0:cols], gate_up(0), NT) + dot(r.dgu[slot, :, cols:], gate_up(1), NT)

    back = Reduce(net, r, d_normed2, total.at)

    def part(k, core):
        slot = net.slot(k, core)
        h = n2_all[slot]
        r.ug[...] = dot(h, gate_up(0))
        r.ul[...] = dot(h, gate_up(1))

        def body(i):
            rows = pl.ds(pl.multiple_of(i * 32, 32), 32)
            gelu, slope = gelu_parts(r.ug[rows, :])
            ul, dh = r.ul[rows, :], r.dgu[slot, rows, 0:cols].astype(F32)
            r.hid[slot, rows, :] = (gelu * ul).astype(BF)
            r.dgu[slot, rows, 0:cols] = (dh * ul * slope).astype(BF)
            r.dgu[slot, rows, cols:] = (dh * gelu).astype(BF)

        loop(8, body)

    feed_down.end()
    for slot in range(8):
        r.dgu[slot, :, 0:cols] = dot(r.g_all[slot], wmd(), NT).astype(BF)
    feed_over.wait_recv()
    feed.end()
    part(0, c)
    acts.sibling(0)
    part(0, o)
    back.other(0)
    acts.forward()
    acts.middle()
    part(1, c)
    part(2, c)
    acts.sibling(1)
    part(1, o)
    back.other(1)
    acts.sibling(2)
    part(2, o)
    back.other(2)
    acts.last()
    acts.sibling(3)
    part(3, o)
    back.other(3)
    part(3, c)
    back.far()
    back.near()
    back.relay()
    back.own()
    acts.release()
    for i in range(4):
        rows = n2_all[:, :, i * 256 : (i + 1) * 256].reshape(-1, 256)
        r.gm[i] = dot(rows, r.dgu[...].reshape(-1, 2 * cols), TN).astype(BF)

    def gm_in(k):
        return r.wgi3.at[k - 1]

    mlp_m = LineSum(net, lambda t: r.gm.at[t], gm_in)
    mlp_m.start()
    hid = r.hid[...].reshape(-1, cols)
    for half in range(2):
        lanes = slice(half * 512, half * 512 + 512)
        value = dot(hid, r.g_all[:, :, lanes].reshape(-1, 512), TN).astype(BF)
        for i in range(4):
            r.gd[i, :, lanes] = value[i * piece : (i + 1) * piece, :]
    mlp_d = LineSum(net, lambda t: r.gd.at[t], lambda k: r.gd_in.at[k - 1])
    mlp_d.start()
    back.finish()
    sums = jnp.zeros((8, r.x.shape[1]), F32)
    for h in range(2):

        def residual_back(i, sums, h=h):
            rows = pl.ds(pl.multiple_of(h * 128 + i * 32, 32), 32)
            v = r.residual[rows, :]
            dn = back.total(h, i, 32)
            s = lax.rsqrt(jnp.mean(v * v, axis=-1, keepdims=True) + NORM_EPS)
            u = dn * gain2
            pulled = s * u - v * (s * s * s * jnp.mean(u * v, axis=-1, keepdims=True))
            d_res = r.g_all[mine, rows, :].astype(F32) + pulled
            r.d_res[rows, :] = d_res
            r.do_all[mine, rows, :] = d_res.astype(BF)
            return sums + jnp.sum((dn * v * s).reshape(4, 8, -1), axis=0)

        sums = lax.fori_loop(0, 4, residual_back, sums)
    r.gain2_sum[...] = sums

    owners, returned = [], []

    def to_owners(src, dst):
        for k in (1, 2, 3):
            for core in (c, o):
                rows = pl.ds(pl.multiple_of(core * 128, 128), 128)
                owners.append(net.copy(src.at[rows], dst.at[mine], net.plane(k, core)))
        rows = pl.ds(pl.multiple_of(o * 128, 128), 128)
        owners.append(net.copy(src.at[rows], dst.at[mine], sibling))
        rows = pl.ds(pl.multiple_of(c * 128, 128), 128)
        returned.append(net.local(src.at[rows], dst.at[mine]))

    def to_chips(src, dst):
        for k in (1, 2, 3):
            owners.append(net.copy(src, dst.at[p], net.plane(k, c)))
        returned.append(net.local(src, dst.at[p]))

    fo_at = net.reserve(4)

    def vector_copy(k):
        return net.describe(r.vout.at[p], r.vout.at[p], net.plane(k, c), fo_at + k, fo_at)

    def mlp_sums():
        mlp_m.end(r.gm_sum)
        to_owners(r.gm_sum, r.fm)

    grads = Gather(net, r.do_all.at[mine], r.do_all, cots.at)
    grads.start()

    def back_out(slot):
        b, half = lax.div(slot, 2), lax.rem(slot, 2)
        dm = dot(r.do_all[slot], r.wo[...], NT)
        for n in range(2):
            r.dconv[b * 2 + n, pl.ds(pl.multiple_of(half * 256, 256), 256), :] = dm[:, n * 128 : (n + 1) * 128]

    back_out(mine)
    grads.sibling(0)
    back_out(net.slot(0, o))
    out = Reduce(net, r, lambda k, core: dot(r.hid[net.slot(k, core)], wmd()), total.at)
    for k in (3, 1, 2, 0):
        out.other(k)
    mlp_m.relay()
    grads.forward()
    out.far()
    out.near()
    out.own()
    grads.middle()
    for k in (1, 2):
        back_out(net.slot(k, c))
    for k in (1, 2):
        grads.sibling(k)
        back_out(net.slot(k, o))
    grads.last()
    back_out(net.slot(3, c))
    grads.sibling(3)
    back_out(net.slot(3, o))

    def first_pass(i):
        b, tile = lax.div(i, 8), lax.rem(i, 8)
        rows = tile_rows(tile)
        live = r.off[b, rows, :] != 0.0
        for n in range(2):
            s = b * 2 + n
            gelu, slope = gelu_parts(r.gp[s, rows, :])
            dm = r.dconv[s, rows, :]
            states = r.states[s, pl.ds(pl.multiple_of(tile * TILE + 8, 8), TILE), :]
            lanes = slice(n * 128, (n + 1) * 128)
            r.dgi[b * 2 + lax.div(tile, 4), tile_rows(lax.rem(tile, 4)), lanes] = (dm * states * slope).astype(BF)
            r.drv[s, rows, :] = dm * gelu
            a = jnp.exp(-DECAY_SCALE * r.sr[s, rows, :] * r.chan[n, 7:8, :])
            r.dec[s, rows, :] = jnp.where(live, a, 0.0)

    loop(32, first_pass)
    ends = scan_slabs(r.dec, r.drv, True)
    ends = exchange_ends(r, net, ends, 1)
    out.relay()
    go_in, go_line_in = r.go_q, r.go_l
    mixed = r.mixed[...].reshape(-1, 256)
    for half in range(2):
        lanes = slice(half * 512, half * 512 + 512)
        r.go[:, lanes] = dot(mixed, r.do_all[:, :, lanes].reshape(-1, 512), TN).astype(BF)
    grads.release()
    fetched = net.local(r.normed_far, r.do_all)
    go_rows = [pl.ds(pl.multiple_of(c * 64 + near * 48, 16), 48) for near in net.near]

    def go_start(lanes):
        return [net.copy(r.go.at[go_rows[k], lanes], go_in.at[p, :, lanes], net.plane(k, c)) for k in (1, 2, 3)]

    go_out = go_start(pl.ds(0, 1024))
    mlp_sums()
    entering_states(r, net, ends, 1, True)
    mlp_d.relay()
    r.vec[...] = jnp.zeros((2, 8, 8, 128), F32)
    dri = r.normed

    def second_pass(s):
        b, n = lax.div(s, 2), lax.rem(s, 2)
        chan = r.chan[n]
        enter = r.inc[pl.ds(s, 1), :]
        lanes_r = pl.ds(pl.multiple_of(n * 256, 128), 128)
        lanes_i = pl.ds(pl.multiple_of(n * 256 + 128, 128), 128)

        def tile(i, sums):
            rows = tile_rows(i)
            live = r.off[b, rows, :] != 0.0
            ds = r.drv[s, rows, :] + r.dec[s, rows, :] * enter
            window = r.states[s, pl.ds(pl.multiple_of(i * TILE, 8), TILE + 8), :]
            before = window[7 : TILE + 7, :]
            sr, si = r.sr[s, rows, :], r.si[s, rows, :]
            cv = r.conv[s, rows, :].astype(F32)
            a, m2 = decay_parts(sr, chan[7:8, :])
            inv = lax.rsqrt(m2)
            m = jnp.where(live, m2 * inv, 1.0)
            dsi = ds * si
            d_log = jnp.where(live, a * (ds * before - dsi * cv * a * inv), 0.0)
            lam_term = d_log * sr
            d_r = (-DECAY_SCALE) * chan[7:8, :] * lam_term * (1.0 - sr)
            dm_i = dsi * m
            d_i = dm_i * cv * (1.0 - si)
            d_r, d_i = d_r.astype(BF), d_i.astype(BF)
            at = tile_rows(lax.rem(i, 4))
            dri[b * 2 + lax.div(i, 4), at, lanes_r] = d_r
            dri[b * 2 + lax.div(i, 4), at, lanes_i] = d_i
            r.dconv[s, rows, :] = dm_i
            return (
                sums[0] + column_sum(d_r.astype(F32)),
                sums[1] + column_sum(d_i.astype(F32)),
                sums[2] + column_sum(lam_term),
            )

        zero = jnp.zeros((8, 128), F32)
        sums = lax.fori_loop(0, 512 // TILE, tile, (zero, zero, zero))
        for j in range(3):
            r.vec[n, 5 + j] = r.vec[n, 5 + j] + sums[j]

    loop(8, second_pass)

    def gate_back(i):
        s, half = lax.div(i, 2), lax.rem(i, 2)
        b, n = lax.div(s, 2), lax.rem(s, 2)
        rows = pl.ds(pl.multiple_of(half * 256, 256), 256)
        lanes = pl.ds(pl.multiple_of(n * 256, 256), 256)
        r.dconv[s, rows, :] = r.dconv[s, rows, :] + dot(dri[b * 2 + half, :, lanes], r.wri[n], NT)

    loop(16, gate_back)
    edge_back = net.reserve(1)

    def edge_back_copy():
        return net.describe(
            r.dconv.at[:, pl.ds(0, 8)], r.dconv.at[:, pl.ds(512, 8)], net.line(net.down(1), c), edge_back, edge_back
        )

    @pl.when(z > 0)
    def _():
        edge_back_copy().start()

    @pl.when(z == 3)
    def _():
        r.dconv[:, 512:520, :] = jnp.zeros((8, 8, 128), F32)

    for n in range(2):
        total_ri = None
        for b in range(4):
            for half in range(2):
                term = dot(
                    r.conv[b * 2 + n, half * 256 : (half + 1) * 256, :],
                    dri[b * 2 + half, :, n * 256 : (n + 1) * 256],
                    TN,
                )
                total_ri = term if total_ri is None else total_ri + term
        r.go[n * 128 : (n + 1) * 128, 1024:1280] = total_ri.astype(BF)
    go_out += go_start(pl.ds(1024, 256))

    @pl.when(z < 3)
    def _():
        edge_back_copy().wait_recv()


    def conv_back(s):
        b, n = lax.div(s, 2), lax.rem(s, 2)
        chan = r.chan[n]
        lanes = pl.ds(pl.multiple_of(256 + n * 128, 128), 128)

        def tile(i, sums):
            offset = r.off[b, pl.ds(pl.multiple_of(i * TILE, 8), TILE + 8), :]
            window = r.dconv[s, pl.ds(pl.multiple_of(i * TILE, 8), TILE + 8), :]
            inner = r.inner[s, pl.ds(pl.multiple_of(i * TILE, 8), TILE + 8), :]
            value = chan[0:1, :] * window[:TILE, :]
            added = [sums[0] + column_sum(window[:TILE, :] * inner[8:, :])]
            for k in (1, 2, 3):
                held = jnp.where(offset >= k, window, 0.0)
                value = value + chan[k : k + 1, :] * held[k : TILE + k, :]
                added.append(sums[k] + column_sum(held[:TILE, :] * inner[8 - k : TILE + 8 - k, :]))
            added.append(sums[4] + column_sum(window[:TILE, :]))
            r.dgi[b * 2 + lax.div(i, 4), tile_rows(lax.rem(i, 4)), lanes] = value.astype(BF)
            return tuple(added)

        sums = lax.fori_loop(0, 512 // TILE, tile, tuple(jnp.zeros((8, 128), F32) for _ in range(5)))
        for j in range(5):
            r.vec[n, j] = r.vec[n, j] + sums[j]

    loop(8, conv_back)
    out.finish()
    for h in range(2):

        def out_rows(i, h=h):
            rows = pl.ds(pl.multiple_of(h * 128 + i * 32, 32), 32)
            value = (r.residual[rows, :] + out.total(h, i, 32)).astype(BF)
            for j in range(4):
                r.dgu[j, rows, 512:768] = value[:, j * 256 : (j + 1) * 256]

        loop(4, out_rows)
    for j in range(4):
        returned.append(net.local(r.dgu.at[j, :, pl.ds(512, 256)], r.block_out.at[:, pl.ds(j * 256, 256)]))
    for partner in (sibling, net.plane(1, c), net.plane(2, c)):
        pl.semaphore_signal(r.free, inc=1, device_id=partner, device_id_type=pl.DeviceIdType.MESH)
    for n in range(2):
        sums = [jnp.sum(r.vec[n, j], axis=0, keepdims=True) for j in range(8)]
        sums[7] = sums[7] * (DECAY_SCALE * r.chan[n, 8:9, :])
        r.vsum[z, :, n * 128 : (n + 1) * 128] = jnp.concatenate(sums, axis=0)
    vec = [net.copy(r.vsum.at[z], r.vsum.at[z], net.line(net.up(k), c)) for k in (1, 2, 3)]
    fetched.wait()
    flat = r.dgi[:, :, 0:512].reshape(-1, 512)
    for i in range(4):
        value = dot(r.do_all[:, :, i * 256 : (i + 1) * 256].reshape(-1, 256), flat, TN)
        for j in range(2):
            n0, n1 = value[:, j * 256 : j * 256 + 128], value[:, j * 256 + 128 : j * 256 + 256]
            r.ga[i][:, j * 128 : (j + 1) * 128] = lax.select(c == 0, n0, n1).astype(BF)
            shared = lax.select(c == 0, n1, n0)
            r.gb2[i][:, j * 128 : (j + 1) * 128] = lax.select(c == 0, shared[0:128], shared[128:256]).astype(BF)

    def ga_in(k):
        return r.g_all.at[7, :, pl.ds((k - 1) * 256, 256)]

    def gb_in(k):
        return r.g_all.at[3 + k, pl.ds(128, 128), pl.ds(0, 256)]

    sum_a = LineSum(net, lambda t: r.hid.at[t, :, 0:256], ga_in)
    sum_b = LineSum(net, lambda t: r.hid.at[4 + t, 0:128, 0:256], gb_in)
    sum_a.start()
    sum_b.start()
    first_back = Reduce(
        net,
        r,
        lambda k, core: dot(masked(r.dgi[net.slot(k, core), :, 0:512], counted_two), r.w2[...], NT),
        total.at,
    )
    pl.semaphore_wait(r.free, 3)
    for k in (3, 1, 2, 0):
        first_back.other(k)
    first_back.far()
    first_back.near()
    go_in[p] = r.go[go_rows[0], :]
    for made in go_out:
        made.wait_recv()
    go_line = LineSum(net, lambda t: go_in.at[t], lambda k: go_line_in.at[k - 1])
    go_line.start()
    first_back.relay()
    mlp_d.end(r.gd_sum)
    to_chips(r.gd_sum, r.fd)
    first_back.own()
    sum_a.relay()
    sum_b.relay()
    go_line.relay()
    first_back.finish()
    sums = jnp.zeros((8, r.x.shape[1]), F32)
    for h in range(2):

        def input_rows(i, sums, h=h):
            rows = pl.ds(pl.multiple_of(h * 128 + i * 32, 32), 32)
            v = r.x[rows, :].astype(F32)
            dn = first_back.total(h, i, 32)
            s = lax.rsqrt(jnp.mean(v * v, axis=-1, keepdims=True) + NORM_EPS)
            u = dn * r.gain[0:1, :]
            r.d_res[rows, :] = r.d_res[rows, :] + (
                s * u - v * (s * s * s * jnp.mean(u * v, axis=-1, keepdims=True))
            )
            return sums + jnp.sum((dn * v * s).reshape(4, 8, -1), axis=0)

        sums = lax.fori_loop(0, 4, input_rows, sums)
    returned.append(net.local(r.d_res, r.d_in))
    gains = jnp.concatenate(
        [
            jnp.sum(sums, axis=0, keepdims=True),
            jnp.sum(r.gain2_sum[...], axis=0, keepdims=True),
            jnp.zeros((6, sums.shape[1]), F32),
        ],
        axis=0,
    )
    for i in range(8):
        r.gsum[i] = gains[:, i * 128 : (i + 1) * 128]
    r.gline[q] = r.gsum[q]
    gain_line = [
        net.copy(r.gsum.at[net.up(k) * 2 + core], r.gline.at[q], net.line(net.up(k), core))
        for k in (1, 2, 3)
        for core in (c, o)
    ]
    gain_line.append(net.copy(r.gsum.at[z * 2 + o], r.gline.at[q], sibling))
    for made in row_sums:
        made.wait_recv()
    r.rows_sum[...] = r.rs_all[0] + r.rs_all[1] + r.rs_all[2] + r.rs_all[3]
    for k in (1, 2, 3):
        for core in (c, o):
            owners.append(net.copy(r.rows_sum.at[pl.ds(net.near[k] * 2, 2)], r.fr.at[mine], net.plane(k, core)))
    owners.append(net.copy(r.rows_sum.at[pl.ds(p * 2, 2)], r.fr.at[mine], sibling))
    returned.append(net.local(r.rows_sum.at[pl.ds(p * 2, 2)], r.fr.at[mine]))
    for made in vec:
        made.wait_recv()
    r.vout[p] = r.vsum[0] + r.vsum[1] + r.vsum[2] + r.vsum[3]

    @pl.when(z == p)
    def _():
        for k in (1, 2, 3):
            vector_copy(k).start()

    sum_a.end(r.ga_sum)
    to_owners(r.ga_sum, r.fa)
    sum_b.end(r.gb2_sum)
    to_chips(r.gb2_sum, r.fb)
    go_line.end(r.go_sum)
    to_chips(r.go_sum, r.fo)
    for made in gain_line:
        made.wait_recv()
    sums = r.gline[0]
    for i in range(1, 8):
        sums = sums + r.gline[i]
    r.gplane[p] = sums
    gain_plane = [net.copy(r.gplane.at[p], r.gplane.at[p], net.plane(k, c)) for k in (1, 2, 3)]

    @pl.when(z != p)
    def _():
        vector_copy(1).wait_recv()

    @pl.when(z == p)
    def _():
        for k in (1, 2, 3):
            vector_copy(k).wait_send()

    for made in owners + gain_plane:
        made.wait_recv()
    r.gain_out[...] = r.gplane[0] + r.gplane[1] + r.gplane[2] + r.gplane[3]
    r.vec_out[...] = r.vout[z]
    for made in returned:
        made.wait()
    @pl.when(z < 3)
    def _():
        edge_copy().wait_send()

    @pl.when(z > 0)
    def _():
        edge_back_copy().wait_send()

    feed.drain()
    feed_down.drain()
    for made in (mlp_m, mlp_d, go_line, sum_a, sum_b):
        made.drain()
    net.drain()


def assemble(r):
    c = lax.rem(lax.axis_index("seq"), 2)
    count = 0
    stores = []

    def start(src, dst):
        nonlocal count
        made = pltpu.make_async_copy(src, dst, r.local.at[count])
        count += 1
        made.start()
        return made

    loads = [start(*pair) for pair in ((r.fm, r.vm), (r.fa, r.va), (r.fb, r.vb), (r.fd, r.vd), (r.fo, r.vo))]
    passed = [start(r.d_in, r.v_din), start(r.block_out, r.v_block)]
    vec = r.vec_in[...]
    vec = lax.select(c == 0, vec[:, 0:192], vec[:, 64:256])
    r.o_cw[...] = vec[0:4]
    for j, out in enumerate((r.o_cb, r.o_rb, r.o_ib, r.o_lam)):
        out[...] = vec[4 + j : 5 + j]
    r.o_ngain[...] = r.gains[0:1, :]
    r.o_mgain[...] = r.gains[1:2, :]
    counts = [jnp.broadcast_to(r.lens[0:1, row : row + 1].astype(F32), (1, 128)) for row in range(5)]
    for chip in range(4):
        for half, (slot, n) in enumerate(((chip * 2, 0), (chip * 2, 1), (chip * 2 + 1, 1))):
            at = chip * 384 + half * 128
            for row in range(5):
                r.o_mean[row, :, at : at + 128] = r.fr[slot, n, row : row + 1, :] / counts[row]
    cols = r.fm.shape[2] // 2
    piece = cols // 4
    loads[0].wait()
    for j, (stage, out) in enumerate(((r.s_mgate, r.o_mgate), (r.s_mup, r.o_mup))):
        for part in range(4):
            for core in range(2):
                at = (part * 2 + core) * cols
                lanes = slice(j * cols + part * piece, j * cols + (part + 1) * piece)
                stage[:, at : at + cols] = jnp.concatenate(
                    [r.vm[chip * 2 + core, :, lanes].astype(F32) for chip in range(4)], axis=1
                )
            here = pl.ds(part * 2 * cols, 2 * cols)
            stores.append(start(stage.at[:, here], out.at[:, here]))
    for made, src, dst in zip(passed, (r.v_din, r.v_block), (r.o_din, r.o_block)):
        made.wait()
        stores.append(start(src, dst))
    loads[1].wait()
    loads[2].wait()
    for j, (stage, out) in enumerate(((r.s_gate, r.o_gate), (r.s_in, r.o_in))):
        lanes = slice(j * 128, (j + 1) * 128)
        for chip in range(4):
            at = chip * 384
            stage[:, at : at + 128] = r.va[chip * 2, :, lanes].astype(F32)
            stage[:, at + 128 : at + 256] = r.vb[chip, :, lanes].astype(F32)
            stage[:, at + 256 : at + 384] = r.va[chip * 2 + 1, :, lanes].astype(F32)
        stores.append(start(stage, out))
    loads[3].wait()
    for chip in range(4):
        r.s_down[chip * piece : (chip + 1) * piece, :] = r.vd[chip].astype(F32)
    stores.append(start(r.s_down, r.o_mdown))
    loads[4].wait()
    for chip in range(4):
        rows = slice(chip * 48, (chip + 1) * 48)
        r.s_out[rows, :] = r.vo[chip, :, 0:1024].astype(F32)
        r.o_r[rows, :] = r.vo[chip, :, 1024:1152].astype(F32)
        r.o_i[rows, :] = r.vo[chip, :, 1152:1280].astype(F32)
    stores.append(start(r.s_out, r.o_out))
    for made in stores:
        made.wait()


def shifted(value, axis, by):
    count = lax.axis_size(axis)
    pairs = [(i, i + by) for i in range(count) if 0 <= i + by < count]
    return lax.ppermute(value, axis, pairs)


def entering(value, axis, combine, identity, reverse):
    count, place = (lax.axis_size(axis), lax.axis_index(axis))
    everything = jax.tree.map(lambda part: lax.all_gather(part, axis), value)
    start = jax.tree.map(
        lambda part, zero: jnp.broadcast_to(jnp.asarray(zero, part.dtype), part.shape),
        value,
        identity,
    )

    def step(k, before):
        at = count - 1 - k if reverse else k
        reached = at > place if reverse else at < place
        new = combine(before, jax.tree.map(lambda part: part[at], everything))
        return jax.tree.map(lambda a, b: jnp.where(reached, a, b), new, before)

    return lax.fori_loop(0, count, step, start)


def rms_scale(values):
    return values * lax.rsqrt(jnp.mean(values * values, axis=-1, keepdims=True) + NORM_EPS)


def gelu_tanh(values):
    return jax.nn.gelu(values, approximate=True)


def link(earlier, later):
    return (earlier[0] * later[0], later[0] * earlier[1] + later[1])


def block_product(values, weight):
    count, channels = values.shape
    block_size = weight.shape[1]
    shaped = values.reshape(count, channels // block_size, block_size)
    result = jnp.einsum(
        "lni,nij->lnj",
        shaped,
        weight.reshape(channels // block_size, block_size, block_size),
        preferred_element_type=jnp.float32,
    )
    return result.reshape(count, channels)


def block_back(grads, weight):
    count, channels = grads.shape
    block_size = weight.shape[1]
    shaped = grads.reshape(count, channels // block_size, block_size)
    result = jnp.einsum(
        "lnj,nij->lni",
        shaped,
        weight.reshape(channels // block_size, block_size, block_size),
        preferred_element_type=jnp.float32,
    )
    return result.reshape(count, channels)


def block_weight_grad(values, grads, block_size):
    count, channels = values.shape
    left = values.reshape(count, channels // block_size, block_size)
    right = grads.reshape(count, channels // block_size, block_size)
    return jnp.einsum("lni,lnj->nij", left, right, preferred_element_type=jnp.float32).reshape(
        channels, block_size
    )


def recurrence_terms(conv_in, r_in, i_in, lam_in, restart):
    log_a = -DECAY_SCALE * jax.nn.sigmoid(r_in) * jax.nn.softplus(-lam_in)
    decays = jnp.exp(log_a)
    factor = jnp.where(restart[:, None] > 0, 1.0, jnp.sqrt(-jnp.expm1(2.0 * log_a)))
    return (decays * (1.0 - restart[:, None]), factor * jax.nn.sigmoid(i_in) * conv_in, decays)


def shards(
    inputs,
    out_grad,
    row_lengths,
    norm_gain,
    w_gate,
    w_in,
    conv_w,
    conv_b,
    w_rgate,
    b_rgate,
    w_igate,
    b_igate,
    lam,
    w_out,
    mlp_gain,
    w_mlp_gate,
    w_mlp_up,
    w_mlp_down,
):
    gathered = (
        lax.all_gather(norm_gain, "seq", axis=0, tiled=True),
        lax.all_gather(w_gate, "seq", axis=0, tiled=True),
        lax.all_gather(w_in, "seq", axis=0, tiled=True),
        lax.all_gather(conv_w, "seq", axis=1, tiled=True),
        lax.all_gather(conv_b, "seq", axis=0, tiled=True),
        lax.all_gather(w_rgate, "seq", axis=0, tiled=True),
        lax.all_gather(b_rgate, "seq", axis=0, tiled=True),
        lax.all_gather(w_igate, "seq", axis=0, tiled=True),
        lax.all_gather(b_igate, "seq", axis=0, tiled=True),
        lax.all_gather(lam, "seq", axis=0, tiled=True),
        lax.all_gather(w_out, "seq", axis=0, tiled=True),
        lax.all_gather(mlp_gain, "seq", axis=0, tiled=True),
        lax.all_gather(w_mlp_gate, "seq", axis=0, tiled=True),
        lax.all_gather(w_mlp_up, "seq", axis=0, tiled=True),
        lax.all_gather(w_mlp_down, "seq", axis=0, tiled=True),
    )
    gain_first = gathered[0].astype(jnp.float32)
    conv_taps = gathered[3].astype(jnp.float32)
    conv_bias = gathered[4].astype(jnp.float32)
    lam_value = gathered[9].astype(jnp.float32)
    gain_second = gathered[11].astype(jnp.float32)
    tokens = inputs[0].astype(jnp.float32)
    local_len = tokens.shape[0]
    channels = gathered[2].shape[1]
    block_size = gathered[5].shape[1]
    kernel_taps = conv_taps.shape[0]
    lengths = row_lengths[0]
    row_ends = jnp.cumsum(lengths)
    row_starts = row_ends - lengths
    positions = lax.axis_index("seq") * local_len + jnp.arange(local_len, dtype=jnp.int32)
    started = positions[:, None] >= row_starts[None, :]
    row_index = jnp.sum(started.astype(jnp.int32), axis=1) - 1
    row_first = jnp.max(jnp.where(started, row_starts[None, :], 0), axis=1)
    offset = positions - row_first
    restart = (offset == 0).astype(jnp.float32)
    members = (row_index[:, None] == jnp.arange(lengths.shape[0], dtype=jnp.int32)[None, :]).astype(
        jnp.float32
    )
    tap_masks = [(offset >= tap).astype(jnp.float32)[:, None] for tap in range(kernel_taps)]
    scaled, norm_pull = jax.vjp(rms_scale, tokens)
    normed = (scaled * gain_first).astype(jnp.bfloat16)
    gate_pre = jnp.dot(normed, gathered[1], preferred_element_type=jnp.float32)
    gate_branch, gate_pull = jax.vjp(gelu_tanh, gate_pre)
    inner = jnp.dot(normed, gathered[2], preferred_element_type=jnp.float32).astype(jnp.bfloat16)
    edge_rows = shifted(inner[local_len - kernel_taps + 1 :], "seq", 1)
    extended = jnp.concatenate([edge_rows, inner], axis=0).astype(jnp.float32)
    conv_sum = conv_bias + jnp.zeros((local_len, channels), jnp.float32)
    for tap in range(kernel_taps):
        start_row = kernel_taps - 1 - tap
        conv_sum = (
            conv_sum + conv_taps[tap] * extended[start_row : start_row + local_len] * tap_masks[tap]
        )
    conv_low = conv_sum.astype(jnp.bfloat16)
    conv_value = conv_low.astype(jnp.float32)
    r_pre = block_product(conv_low, gathered[5]) + gathered[6].astype(jnp.float32)
    i_pre = block_product(conv_low, gathered[7]) + gathered[8].astype(jnp.float32)

    def local_terms(conv_in, r_in, i_in, lam_in):
        return recurrence_terms(conv_in, r_in, i_in, lam_in, restart)

    (carried, drive_term, decays), recur_pull = jax.vjp(
        local_terms, conv_value, r_pre, i_pre, lam_value
    )
    prefix_decay, local_state = lax.associative_scan(link, (carried, drive_term), axis=0)
    identity = (jnp.ones((channels,), jnp.float32), jnp.zeros((channels,), jnp.float32))
    incoming = entering((prefix_decay[-1], local_state[-1]), "seq", link, identity, False)[1]
    states = local_state + prefix_decay * incoming
    mixed_low = (states * gate_branch).astype(jnp.bfloat16)
    residual = tokens + jnp.dot(mixed_low, gathered[10], preferred_element_type=jnp.float32)
    scaled_two, norm_pull_two = jax.vjp(rms_scale, residual)
    normed_two = (scaled_two * gain_second).astype(jnp.bfloat16)
    up_gate = jnp.dot(normed_two, gathered[12], preferred_element_type=jnp.float32)
    up_lin = jnp.dot(normed_two, gathered[13], preferred_element_type=jnp.float32)
    gelu_up, up_pull = jax.vjp(gelu_tanh, up_gate)
    hidden = (gelu_up * up_lin).astype(jnp.bfloat16)
    block_out = (
        residual + jnp.dot(hidden, gathered[14], preferred_element_type=jnp.float32)
    ).astype(jnp.bfloat16)
    row_sums = lax.psum(jnp.dot(members.T, decays, precision=lax.Precision.HIGHEST), "seq")
    gate_mean = row_sums / lengths.astype(jnp.float32)[:, None]
    grad_top = out_grad[0]
    grad_mdown = jnp.einsum("tf,td->fd", hidden, grad_top, preferred_element_type=jnp.float32)
    d_hidden = jnp.einsum("td,fd->tf", grad_top, gathered[14], preferred_element_type=jnp.float32)
    d_upgate = up_pull(d_hidden * up_lin)[0].astype(jnp.bfloat16)
    d_uplin = (d_hidden * gelu_up).astype(jnp.bfloat16)
    grad_mgate = jnp.einsum("td,tf->df", normed_two, d_upgate, preferred_element_type=jnp.float32)
    grad_mup = jnp.einsum("td,tf->df", normed_two, d_uplin, preferred_element_type=jnp.float32)
    d_normed_two = jnp.einsum(
        "tf,df->td", d_upgate, gathered[12], preferred_element_type=jnp.float32
    )
    d_normed_two = d_normed_two + jnp.einsum(
        "tf,df->td", d_uplin, gathered[13], preferred_element_type=jnp.float32
    )
    grad_mgain = jnp.sum(d_normed_two * scaled_two, axis=0)
    d_residual = grad_top.astype(jnp.float32) + norm_pull_two(d_normed_two * gain_second)[0]
    d_outlow = d_residual.astype(jnp.bfloat16)
    grad_outw = jnp.einsum("tr,td->rd", mixed_low, d_outlow, preferred_element_type=jnp.float32)
    d_mixed = jnp.einsum("td,rd->tr", d_outlow, gathered[10], preferred_element_type=jnp.float32)
    direct = d_mixed * gate_branch
    d_gatelow = gate_pull(d_mixed * states)[0].astype(jnp.bfloat16)
    grad_gatew = jnp.einsum("td,tr->dr", normed, d_gatelow, preferred_element_type=jnp.float32)
    next_decay = jnp.concatenate([carried[1:], jnp.ones((1, channels), jnp.float32)], axis=0)
    suffix_decay, local_grad = lax.associative_scan(
        link, (next_decay, direct), axis=0, reverse=True
    )
    arriving = entering(
        (carried[0] * suffix_decay[0], carried[0] * local_grad[0]), "seq", link, identity, True
    )[1]
    d_states = local_grad + suffix_decay * arriving
    previous = jnp.concatenate([incoming[None, :], states[:-1]], axis=0)
    grad_convval, d_rpre, d_ipre, grad_lambda = recur_pull(
        (d_states * previous, d_states, jnp.zeros_like(decays))
    )
    d_rlow = d_rpre.astype(jnp.bfloat16)
    d_ilow = d_ipre.astype(jnp.bfloat16)
    grad_rw = block_weight_grad(conv_low, d_rlow, block_size)
    grad_rb = jnp.sum(d_rlow.astype(jnp.float32), axis=0)
    grad_iw = block_weight_grad(conv_low, d_ilow, block_size)
    grad_ib = jnp.sum(d_ilow.astype(jnp.float32), axis=0)
    grad_convsum = grad_convval + block_back(d_rlow, gathered[5]) + block_back(d_ilow, gathered[7])
    grad_cb = jnp.sum(grad_convsum, axis=0)
    conv_again = gathered[3].astype(jnp.float32)
    grad_extended = jnp.zeros((local_len + kernel_taps - 1, channels), jnp.float32)
    tap_grads = []
    for tap in range(kernel_taps):
        start_row = kernel_taps - 1 - tap
        masked = grad_convsum * tap_masks[tap]
        tap_grads.append(jnp.sum(masked * extended[start_row : start_row + local_len], axis=0))
        grad_extended = grad_extended + jnp.pad(
            masked * conv_again[tap], ((start_row, tap), (0, 0))
        )
    grad_cw = jnp.stack(tap_grads)
    edge_grads = shifted(grad_extended[: kernel_taps - 1], "seq", -1)
    d_inner = (
        grad_extended[kernel_taps - 1 :]
        + jnp.pad(edge_grads, ((local_len - kernel_taps + 1, 0), (0, 0)))
    ).astype(jnp.bfloat16)
    grad_inw = jnp.einsum("td,tr->dr", normed, d_inner, preferred_element_type=jnp.float32)
    d_normed = jnp.einsum("tr,dr->td", d_gatelow, gathered[1], preferred_element_type=jnp.float32)
    d_normed = d_normed + jnp.einsum(
        "tr,dr->td", d_inner, gathered[2], preferred_element_type=jnp.float32
    )
    grad_gain = jnp.sum(d_normed * scaled, axis=0)
    d_tokens = d_residual + norm_pull(d_normed * gain_first)[0]
    shares = (
        lax.psum_scatter(grad_gain, "seq", scatter_dimension=0, tiled=True),
        lax.psum_scatter(grad_gatew, "seq", scatter_dimension=0, tiled=True),
        lax.psum_scatter(grad_inw, "seq", scatter_dimension=0, tiled=True),
        lax.psum_scatter(grad_cw, "seq", scatter_dimension=1, tiled=True),
        lax.psum_scatter(grad_cb, "seq", scatter_dimension=0, tiled=True),
        lax.psum_scatter(grad_rw, "seq", scatter_dimension=0, tiled=True),
        lax.psum_scatter(grad_rb, "seq", scatter_dimension=0, tiled=True),
        lax.psum_scatter(grad_iw, "seq", scatter_dimension=0, tiled=True),
        lax.psum_scatter(grad_ib, "seq", scatter_dimension=0, tiled=True),
        lax.psum_scatter(grad_lambda, "seq", scatter_dimension=0, tiled=True),
        lax.psum_scatter(grad_outw, "seq", scatter_dimension=0, tiled=True),
        lax.psum_scatter(grad_mgain, "seq", scatter_dimension=0, tiled=True),
        lax.psum_scatter(grad_mgate, "seq", scatter_dimension=0, tiled=True),
        lax.psum_scatter(grad_mup, "seq", scatter_dimension=0, tiled=True),
        lax.psum_scatter(grad_mdown, "seq", scatter_dimension=0, tiled=True),
    )
    totals = (
        lax.psum(shares[0].astype(jnp.bfloat16), "batch").astype(jnp.float32),
        lax.psum(shares[1].astype(jnp.bfloat16), "batch").astype(jnp.float32),
        lax.psum(shares[2].astype(jnp.bfloat16), "batch").astype(jnp.float32),
        lax.psum(shares[3].astype(jnp.bfloat16), "batch").astype(jnp.float32),
        lax.psum(shares[4].astype(jnp.bfloat16), "batch").astype(jnp.float32),
        lax.psum(shares[5].astype(jnp.bfloat16), "batch").astype(jnp.float32),
        lax.psum(shares[6].astype(jnp.bfloat16), "batch").astype(jnp.float32),
        lax.psum(shares[7].astype(jnp.bfloat16), "batch").astype(jnp.float32),
        lax.psum(shares[8].astype(jnp.bfloat16), "batch").astype(jnp.float32),
        lax.psum(shares[9].astype(jnp.bfloat16), "batch").astype(jnp.float32),
        lax.psum(shares[10].astype(jnp.bfloat16), "batch").astype(jnp.float32),
        lax.psum(shares[11].astype(jnp.bfloat16), "batch").astype(jnp.float32),
        lax.psum(shares[12].astype(jnp.bfloat16), "batch").astype(jnp.float32),
        lax.psum(shares[13].astype(jnp.bfloat16), "batch").astype(jnp.float32),
        lax.psum(shares[14].astype(jnp.bfloat16), "batch").astype(jnp.float32),
    )
    return (
        block_out[None],
        d_tokens[None],
        totals[0],
        totals[1],
        totals[2],
        totals[3],
        totals[4],
        totals[5],
        totals[6],
        totals[7],
        totals[8],
        totals[9],
        totals[10],
        totals[11],
        totals[12],
        totals[13],
        totals[14],
        gate_mean[None],
    )


def planes(
    inputs,
    out_grad,
    row_lengths,
    norm_gain,
    w_gate,
    w_in,
    conv_w,
    conv_b,
    w_rgate,
    b_rgate,
    w_igate,
    b_igate,
    lam,
    w_out,
    mlp_gain,
    w_mlp_gate,
    w_mlp_up,
    w_mlp_down,
):
    vmem = pltpu.VMEM
    done = kernel_call(
        layer,
        dict(
            x=inputs[0], cw=conv_w, cb=conv_b, br=b_rgate, bi=b_igate, lam=lam, ngain=norm_gain, mgain=mlp_gain,
            lens=row_lengths, g=out_grad[0], wg=w_gate, wi=w_in, wr=w_rgate, wv=w_igate, wout=w_out,
            wmg=w_mlp_gate, wmu=w_mlp_up, wmd=w_mlp_down,
        ),
        dict(
            block_out=array(256, 1024, dtype=BF),
            d_in=array(256, 1024),
            fm=array(8, 128, 768, dtype=BF),
            fd=array(4, 96, 1024, dtype=BF),
            fa=array(8, 128, 256, dtype=BF),
            fb=array(4, 128, 256, dtype=BF),
            fo=array(4, 48, 1280, dtype=BF),
            fr=array(8, 2, 8, 128),
            vec_out=array(8, 256),
            gain_out=array(8, 128),
            normed_far=array(8, 256, 1024, dtype=BF),
        ),
        dict(
            x_all=vmem((8, 256, 1024), BF),
            normed=vmem((8, 256, 1024), BF),
            g_all=vmem((8, 256, 1024), BF),
            small_rows=vmem((16, 256), F32),
            small=vmem((16, 256), BF),
            small_all=vmem((8, 16, 256), BF),
            lens_out=vmem((8, 128), F32),
            lens_all=vmem((4, 8, 128), F32),
            off=vmem((4, 520, 128), F32),
            starts_all=vmem((4, 8, 128), F32),
            chan=vmem((2, 16, 128), F32),
            gain=vmem((8, 1024), F32),
            wgi3=vmem((4, 256, 768), BF),
            w2=vmem((1024, 512), BF),
            gq=vmem((4, 48, 256), BF),
            g3=vmem((2, 192, 256), BF),
            wq=vmem((4, 48, 1024), BF),
            wri=vmem((2, 128, 256), BF),
            w3=vmem((2, 192, 1024), BF),
            wo=vmem((256, 1024), BF),
            wgu_out=vmem((2, 256, 384), BF),
            wgu_all=vmem((8, 256, 384), BF),
            wmd_all=vmem((4, 96, 1024), BF),
            gp=vmem((8, 512, 128), F32),
            gb=vmem((8, 520, 128), F32),
            inner=vmem((8, 520, 128), F32),
            conv=vmem((8, 512, 128), BF),
            sr=vmem((8, 512, 128), F32),
            si=vmem((8, 512, 128), F32),
            dec=vmem((8, 512, 128), F32),
            drv=vmem((8, 512, 128), F32),
            states=vmem((8, 520, 128), F32),
            mixed=vmem((8, 256, 256), BF),
            tot=vmem((2, 4, 2, 8, 128), F32),
            inc=vmem((8, 128), F32),
            rs_all=vmem((4, 8, 8, 128), F32),
            rows_sum=vmem((8, 8, 128), F32),
            residual=vmem((256, 1024), F32),
            d_res=vmem((256, 1024), F32),
            hid=vmem((8, 256, 384), BF),
            dgu=vmem((8, 256, 768), BF),
            gm=vmem((4, 256, 768), BF),
            gm_sum=vmem((256, 768), BF),
            gd=vmem((4, 96, 1024), BF),
            gd_in=vmem((3, 96, 1024), BF),
            gd_sum=vmem((96, 1024), BF),
            go=vmem((256, 1280), BF),
            go_q=vmem((4, 48, 1280), BF),
            go_l=vmem((3, 48, 1280), BF),
            go_sum=vmem((48, 1280), BF),
            ga_sum=vmem((256, 256), BF),
            gb2_sum=vmem((128, 256), BF),
            gain2_sum=vmem((8, 1024), F32),
            vec=vmem((2, 8, 8, 128), F32),
            vsum=vmem((4, 8, 256), F32),
            vout=vmem((4, 8, 256), F32),
            gsum=vmem((8, 8, 128), F32),
            gline=vmem((8, 8, 128), F32),
            gplane=vmem((4, 8, 128), F32),
            free=pltpu.SemaphoreType.REGULAR,
            **reduce_scratch(256, 1024),
        ),
        160,
        36,
        (
            "g", "wg", "wi", "wr", "wv", "wout", "wmg", "wmu", "wmd", "d_in", "block_out", "fm", "fd", "fa", "fb", "fo",
            "fr", "normed_far",
        ),
    )
    out = kernel_call(
        assemble,
        dict(
            {name: done[name] for name in ("d_in", "block_out", "fm", "fd", "fa", "fb", "fo", "fr")},
            vec_in=done["vec_out"], gains=done["gain_out"], lens=row_lengths,
        ),
        dict(
            o_din=array(256, 1024),
            o_block=array(256, 1024, dtype=BF),
            o_gate=array(128, 1536),
            o_in=array(128, 1536),
            o_mgate=array(128, 3072),
            o_mup=array(128, 3072),
            o_mdown=array(384, 1024),
            o_out=array(192, 1024),
            o_r=array(192, 128),
            o_i=array(192, 128),
            o_cw=array(4, 192),
            o_cb=array(1, 192),
            o_rb=array(1, 192),
            o_ib=array(1, 192),
            o_lam=array(1, 192),
            o_ngain=array(1, 128),
            o_mgain=array(1, 128),
            o_mean=array(5, 1, 1536),
        ),
        dict(
            v_din=vmem((256, 1024), F32),
            v_block=vmem((256, 1024), BF),
            vm=vmem((8, 128, 768), BF),
            va=vmem((8, 128, 256), BF),
            vb=vmem((4, 128, 256), BF),
            vd=vmem((4, 96, 1024), BF),
            vo=vmem((4, 48, 1280), BF),
            s_mgate=vmem((128, 3072), F32),
            s_mup=vmem((128, 3072), F32),
            s_gate=vmem((128, 1536), F32),
            s_in=vmem((128, 1536), F32),
            s_down=vmem((384, 1024), F32),
            s_out=vmem((192, 1024), F32),
        ),
        0,
        21,
        (
            "d_in", "block_out", "fm", "fd", "fa", "fb", "fo", "o_din", "o_block", "o_gate", "o_in", "o_mgate", "o_mup",
            "o_mdown", "o_out",
        ),
    )
    return (
        out["o_block"][None],
        out["o_din"][None],
        out["o_ngain"][0],
        out["o_gate"],
        out["o_in"],
        out["o_cw"],
        out["o_cb"][0],
        out["o_r"],
        out["o_rb"][0],
        out["o_i"],
        out["o_ib"][0],
        out["o_lam"][0],
        out["o_out"],
        out["o_mgain"][0],
        out["o_mgate"],
        out["o_mup"],
        out["o_mdown"],
        jnp.transpose(out["o_mean"], (1, 0, 2)),
    )


def solution(mesh):
    in_specs = (
        P("batch", "seq", None),
        P("batch", "seq", None),
        P("batch", None),
        P("seq"),
        P("seq", None),
        P("seq", None),
        P(None, "seq"),
        P("seq"),
        P("seq", None),
        P("seq"),
        P("seq", None),
        P("seq"),
        P("seq"),
        P("seq", None),
        P("seq"),
        P("seq", None),
        P("seq", None),
        P("seq", None),
    )
    out_specs = (
        P("batch", "seq", None),
        P("batch", "seq", None),
        P("seq"),
        P("seq", None),
        P("seq", None),
        P(None, "seq"),
        P("seq"),
        P("seq", None),
        P("seq"),
        P("seq", None),
        P("seq"),
        P("seq"),
        P("seq", None),
        P("seq"),
        P("seq", None),
        P("seq", None),
        P("seq", None),
        P("batch", None, None),
    )
    in_planes = mesh.shape["batch"] == 4 and mesh.shape["seq"] == 8
    body = planes if in_planes else shards
    return jax.shard_map(body, mesh=mesh, in_specs=in_specs, out_specs=out_specs, check_vma=False)
```

```python
import functools
import types

import jax
import jax.numpy as jnp
from jax import lax
from jax.experimental import pallas as pl
from jax.experimental.pallas import tpu as pltpu
from jax.sharding import PartitionSpec as P

NORM_EPS = 1e-06
DECAY_SCALE = 8.0
BF = jnp.bfloat16
F32 = jnp.float32
GELU_SCALE = 0.7978845608028654
GELU_CUBE = 0.044715
TILE = 64
NN = (((1,), (0,)), ((), ()))
NT = (((1,), (1,)), ((), ()))
TN = (((0,), (0,)), ((), ()))


def dot(left, right, dims=NN):
    return lax.dot_general(left, right, dims, preferred_element_type=F32)


def loop(count, body):
    def step(i, carry):
        body(i)
        return carry

    lax.fori_loop(0, count, step, 0)


class Net:
    def __init__(self, r):
        self.send, self.recv, self.count = r.send, r.recv, 0
        self.here, self.here_count = r.local, 0
        self.pending = []
        self.p = lax.axis_index("batch")
        self.q = lax.axis_index("seq")
        self.z = lax.div(self.q, 2)
        self.c = lax.rem(self.q, 2)
        self.o = 1 - self.c
        p = self.p
        self.near = (p, p + 1 - 2 * lax.rem(p, 2), lax.rem(p + 2, 4), 3 - p)

    def plane(self, k, core):
        return {"batch": self.near[k], "seq": self.z * 2 + core}

    def line(self, z, core):
        return {"batch": self.p, "seq": z * 2 + core}

    def up(self, k):
        return lax.rem(self.z + k, 4)

    def down(self, k):
        return lax.rem(self.z + 4 - k, 4)

    def slot(self, k, core):
        return self.near[k] * 2 + core

    def greet(self):
        barrier = pltpu.get_barrier_semaphore()
        partners = [self.plane(k, core) for k in (1, 2, 3) for core in (0, 1)]
        partners += [self.line(self.up(k), core) for k in (1, 2, 3) for core in (0, 1)]
        partners += [self.line(self.z, self.o)]
        for partner in partners:
            pl.semaphore_signal(barrier, inc=1, device_id=partner, device_id_type=pl.DeviceIdType.MESH)
        pl.semaphore_wait(barrier, len(partners))

    def reserve(self, count):
        first = self.count
        self.count += count
        return first

    def describe(self, src, dst, device, send_at, recv_at):
        return pltpu.make_async_remote_copy(
            src_ref=src,
            dst_ref=dst,
            send_sem=self.send.at[send_at],
            recv_sem=self.recv.at[recv_at],
            device_id=device,
            device_id_type=pl.DeviceIdType.MESH,
        )

    def copy(self, src, dst, device, sent=None, at=None):
        at = self.reserve(1) if at is None else at
        made = self.describe(src, dst, device, at, at)
        made.start()
        (self.pending if sent is None else sent).append(made)
        return made

    def local(self, src, dst):
        made = pltpu.make_async_copy(src, dst, self.here.at[self.here_count])
        self.here_count += 1
        made.start()
        return made

    def drain(self):
        assert (self.count, self.here_count) == (self.send.shape[0], self.here.shape[0]), (self.count, self.here_count)
        for made in self.pending:
            made.wait_send()
        self.pending = []


class Gather:
    def __init__(self, net, own, everything, at=None):
        self.net, self.own, self.all = net, own, everything
        self.sent = []
        self.at = net.reserve(10) if at is None else at
        self.half = everything.shape[1] // 2

    def part(self, slot, h):
        return self.all.at[slot, pl.ds(h * self.half, self.half)]

    def start(self):
        net = self.net
        mine = net.slot(0, net.c)
        low, high = self.own.at[pl.ds(0, self.half)], self.own.at[pl.ds(self.half, self.half)]
        self.s = []
        self.x0 = net.copy(low, self.part(mine, 0), net.plane(1, net.c), self.sent, self.at + 0)
        self.y1 = net.copy(high, self.part(mine, 1), net.plane(2, net.c), self.sent, self.at + 1)
        self.x1 = net.copy(high, self.part(mine, 1), net.plane(1, net.c), self.sent, self.at + 2)
        self.y0 = net.copy(low, self.part(mine, 0), net.plane(2, net.c), self.sent, self.at + 3)
        self.s.append(net.copy(self.own, self.all.at[mine], net.plane(0, net.o), self.sent, self.at + 4))

    def forward(self):
        net = self.net
        self.x0.wait_recv()
        mine = self.part(net.slot(1, net.c), 0)
        self.d0 = net.copy(mine, mine, net.plane(2, net.c), self.sent, self.at + 5)
        self.y1.wait_recv()
        mine = self.part(net.slot(2, net.c), 1)
        self.d1 = net.copy(mine, mine, net.plane(1, net.c), self.sent, self.at + 6)

    def across(self, k):
        net = self.net
        mine = self.all.at[net.slot(k, net.c)]
        self.s.append(net.copy(mine, mine, net.plane(0, net.o), self.sent, self.at + 6 + k))

    def middle(self):
        self.x1.wait_recv()
        self.across(1)
        self.y0.wait_recv()
        self.across(2)

    def last(self):
        self.d0.wait_recv()
        self.d1.wait_recv()
        self.across(3)

    def sibling(self, k):
        self.s[k].wait_recv()

    def release(self):
        for made in self.sent:
            made.wait_send()
        self.sent = []


class Owners:
    def __init__(self, net, own, everything, extra=None):
        self.net, self.own, self.all, self.extra = net, own, everything, extra
        self.half = everything.shape[1] // 2
        self.s = [None] * 4

    def part(self, k, h):
        return self.all.at[self.net.near[k], pl.ds(h * self.half, self.half)]

    def across(self, k, block):
        if self.extra is not None:
            net = self.net
            rows = pl.ds(pl.multiple_of(net.o * self.half, 16), self.half)
            self.s[k] = net.copy(block.at[rows], self.extra.at[net.near[k]], net.plane(0, net.o))

    def start(self):
        net = self.net
        low, high = self.own.at[pl.ds(0, self.half)], self.own.at[pl.ds(self.half, self.half)]
        self.x0 = net.copy(low, self.part(0, 0), net.plane(1, net.c))
        self.y1 = net.copy(high, self.part(0, 1), net.plane(2, net.c))
        self.x1 = net.copy(high, self.part(0, 1), net.plane(1, net.c))
        self.y0 = net.copy(low, self.part(0, 0), net.plane(2, net.c))
        self.across(0, self.own)
        self.kept = net.local(self.own, self.all.at[net.p])

    def forward(self):
        net = self.net
        self.x0.wait_recv()
        self.d0 = net.copy(self.part(1, 0), self.part(1, 0), net.plane(2, net.c))
        self.y1.wait_recv()
        self.d1 = net.copy(self.part(2, 1), self.part(2, 1), net.plane(1, net.c))

    def middle(self):
        self.x1.wait_recv()
        self.across(1, self.all.at[self.net.near[1]])
        self.y0.wait_recv()
        self.across(2, self.all.at[self.net.near[2]])

    def last(self):
        self.d0.wait_recv()
        self.d1.wait_recv()
        self.across(3, self.all.at[self.net.near[3]])

    def end(self):
        if self.extra is not None:
            for made in self.s:
                made.wait_recv()
        self.kept.wait()


class LineGather:
    def __init__(self, net, own, first, place):
        self.net, self.own, self.first, self.place = net, own, first, place
        self.at = net.reserve(4 * len(own))

    def made(self, k, j):
        net = self.net
        src, core = self.own[j]
        at = self.at + 4 * j + k - 1
        return net.describe(src, self.first(j), net.line(net.up(k), core), at, at)

    def handed(self, j):
        net = self.net
        far = 6 - 3 * net.z
        here = self.place(j, far)
        at = self.at + 4 * j
        return net.describe(here, here, net.line(3 - far, net.c), at + 3, at + 2 * net.z - 2)

    def direct(self, k, body):
        z = self.net.z
        if k == 2:
            body()
        else:
            pl.when(z != (0 if k == 3 else 3))(body)

    def start(self, k, items):
        def send():
            for j in items:
                self.made(k, j).start()

        self.direct(k, send)

    def inside(self, body):
        z = self.net.z
        pl.when((z == 1) | (z == 2))(body)

    def relay(self):
        @self.inside
        def _():
            for j in range(len(self.own)):
                self.made(2, j).wait_recv()
                self.handed(j).start()

    def end(self):
        z = self.net.z
        for k in (1, 3):
            for j in range(len(self.own)):
                self.made(k, j).wait_recv()

        @pl.when((z == 0) | (z == 3))
        def _():
            for j in range(len(self.own)):
                self.made(2, j).wait_recv()

    def drain(self):
        for k in (1, 2, 3):

            def wait(k=k):
                for j in range(len(self.own)):
                    self.made(k, j).wait_send()

            self.direct(k, wait)

        @self.inside
        def _():
            for j in range(len(self.own)):
                self.handed(j).wait_send()


class LineSum:
    def __init__(self, net, block, slot):
        self.net, self.block, self.slot = net, block, slot
        self.at = net.reserve(3)

    def made(self, k):
        net = self.net
        at = self.at + k - 1
        to = lax.rem(2 * net.z + 1, 5) if k == 2 else net.up(k)
        return net.describe(self.block(net.up(k)), self.slot(k), net.line(to, net.c), at, at)

    def start(self):
        z = self.net.z
        self.made(2).start()
        pl.when(z != 1)(lambda: self.made(1).start())
        pl.when(z != 2)(lambda: self.made(3).start())

    def relay(self, step=16):
        z = self.net.z

        @pl.when((z == 1) | (z == 2))
        def _():
            self.made(2).wait_recv()
            mine, extra = self.block(3 - z), self.slot(2)

            def body(i):
                rows = pl.ds(pl.multiple_of(i * step, step), step)
                mine[rows, :] = (mine[rows, :].astype(F32) + extra[rows, :].astype(F32)).astype(BF)

            loop(mine.shape[0] // step, body)

        pl.when(z == 1)(lambda: self.made(1).start())
        pl.when(z == 2)(lambda: self.made(3).start())

    def end(self, dst, step=16):
        z = self.net.z
        self.made(1).wait_recv()
        self.made(3).wait_recv()
        edge = (z == 0) | (z == 3)
        pl.when(edge)(lambda: self.made(2).wait_recv())
        share = jnp.where(edge, 1.0, 0.0)
        own = self.block(z)

        def body(i):
            rows = pl.ds(pl.multiple_of(i * step, step), step)
            value = own[rows, :].astype(F32) + share * self.slot(2)[rows, :].astype(F32)
            value = value + self.slot(1)[rows, :].astype(F32) + self.slot(3)[rows, :].astype(F32)
            dst[rows, :] = value.astype(BF)

        loop(dst.shape[0] // step, body)

    def drain(self):
        for k in (1, 2, 3):
            self.made(k).wait_send()


class Reduce:
    def __init__(self, net, r, value, at=None):
        self.net, self.value = net, value
        self.at = net.reserve(10) if at is None else at
        self.keep, self.out, self.into = r.rs_keep, r.rs_out, r.rs_in
        self.xs, self.ys, self.xr, self.yr = r.rs_xs, r.rs_ys, r.rs_xr, r.rs_yr
        self.half = self.keep.shape[1]
        self.cross = [None] * 4
        self.sent = []

    def other(self, k):
        net = self.net
        self.out[k] = self.value(k, net.o).astype(BF)
        self.cross[k] = net.copy(self.out.at[k], self.into.at[k], net.plane(0, net.o), self.sent, self.at + k)

    def mine(self, k):
        self.cross[k].wait_recv()
        value = self.value(k, self.net.c) + self.into[k].astype(F32)
        return value[: self.half], value[self.half :]

    def send(self, src, dst, j, k):
        net = self.net
        at = self.at + 4 + j + (0 if src is self.xs else 3)
        return net.copy(src.at[j], dst.at[j], net.plane(k, net.c), self.sent, at)

    def far(self):
        low, high = self.mine(3)
        self.xs[0] = low.astype(BF)
        self.x0 = self.send(self.xs, self.xr, 0, 1)
        self.ys[0] = high.astype(BF)
        self.y0 = self.send(self.ys, self.yr, 0, 2)

    def near(self):
        low, high = self.mine(1)
        self.xs[1] = low.astype(BF)
        self.x1 = self.send(self.xs, self.xr, 1, 1)
        self.keep[2] = high
        low, high = self.mine(2)
        self.ys[1] = high.astype(BF)
        self.y1 = self.send(self.ys, self.yr, 1, 2)
        self.keep[3] = low

    def relay(self):
        self.x0.wait_recv()
        self.ys[2] = (self.keep[3] + self.xr[0].astype(F32)).astype(BF)
        self.y2 = self.send(self.ys, self.yr, 2, 2)
        self.y0.wait_recv()
        self.xs[2] = (self.keep[2] + self.yr[0].astype(F32)).astype(BF)
        self.x2 = self.send(self.xs, self.xr, 2, 1)

    def own(self):
        self.keep[0], self.keep[1] = self.mine(0)

    def finish(self):
        for made in (self.x1, self.y1, self.x2, self.y2):
            made.wait_recv()
        for made in self.sent:
            made.wait_send()
        self.sent = []

    def total(self, h, i, step):
        rows = pl.ds(pl.multiple_of(i * step, step), step)
        first, second = (self.xr, self.yr) if h == 0 else (self.yr, self.xr)
        return self.keep[h, rows, :] + first[1, rows, :].astype(F32) + second[2, rows, :].astype(F32)


def reduce_scratch(rows, width):
    half = rows // 2
    return dict(
        rs_keep=pltpu.VMEM((4, half, width), F32),
        rs_out=pltpu.VMEM((4, rows, width), BF),
        rs_in=pltpu.VMEM((4, rows, width), BF),
        rs_xs=pltpu.VMEM((3, half, width), BF),
        rs_ys=pltpu.VMEM((3, half, width), BF),
        rs_xr=pltpu.VMEM((3, half, width), BF),
        rs_yr=pltpu.VMEM((3, half, width), BF),
    )


def kernel_call(body, ins, outs, scratch, copies, local, far):
    names = list(ins) + list(outs) + list(scratch)
    near = pl.BlockSpec(memory_space=pltpu.VMEM)
    away = pl.BlockSpec(memory_space=pl.ANY)
    shapes = list(scratch.values())
    if copies:
        names += ["send", "recv"]
        shapes += [pltpu.SemaphoreType.DMA((copies,))] * 2
    if local:
        names.append("local")
        shapes.append(pltpu.SemaphoreType.DMA((local,)))

    def kernel(*refs):
        body(types.SimpleNamespace(**dict(zip(names, refs))))

    params = dict(vmem_limit_bytes=62 * 2**20)
    if copies:
        params.update(collective_id=0, has_side_effects=True)
    results = pl.pallas_call(
        kernel,
        out_shape=list(outs.values()),
        in_specs=[away if name in far else near for name in ins],
        out_specs=[away if name in far else near for name in outs],
        scratch_shapes=shapes,
        compiler_params=pltpu.CompilerParams(**params),
        name=body.__name__,
    )(*ins.values())
    return dict(zip(outs, results))


def array(*shape, dtype=F32):
    return jax.ShapeDtypeStruct(shape, dtype)


def gelu_parts(v):
    square = v * v
    t = jnp.tanh(GELU_SCALE * v * (1.0 + GELU_CUBE * square))
    half = 0.5 + 0.5 * t
    slope = half + 0.5 * v * (1.0 - t * t) * (GELU_SCALE * (1.0 + 3.0 * GELU_CUBE * square))
    return v * half, slope


def decay_parts(sr, rate):
    log_a = -DECAY_SCALE * sr * rate
    a = jnp.exp(log_a)
    y = 2.0 * log_a
    series = 1.0 + y * (1 / 6) * (1.0 + y * (1 / 7))
    for n in (5, 4, 3, 2):
        series = 1.0 + y * (1 / n) * series
    m2 = jnp.where(y > -0.35, -y * series, 1.0 - a * a)
    return a, jnp.maximum(m2, 1e-36)


def column_sum(value):
    return jnp.sum(value.reshape(-1, 8, 128), axis=0)


def scan_slabs(decay, value, reverse):
    count = decay.shape[1] // 8
    row = lax.broadcasted_iota(jnp.int32, (8, 128), 0)

    def step(i, carry):
        t = count - 1 - i if reverse else i
        at = pl.ds(pl.multiple_of(t * 8, 8), 8)
        done = []
        for s in range(8):
            pc, vc = carry[s]
            p, own = decay[s, at, :], value[s, at, :]
            v = p * own if reverse else own
            for d in (1, 2, 4):
                by = 8 - d if reverse else d
                inside = row < 8 - d if reverse else row >= d
                v = v + p * jnp.where(inside, pltpu.roll(v, by, 0), 0.0)
                p = p * jnp.where(inside, pltpu.roll(p, by, 0), 1.0)
            v = v + p * vc
            p = p * pc
            if reverse:
                edge = row == 7
                value[s, at, :] = own + jnp.where(edge, vc, pltpu.roll(v, 7, 0))
                decay[s, at, :] = jnp.where(edge, pc, pltpu.roll(p, 7, 0))
                last = slice(0, 1)
            else:
                value[s, at, :] = v
                decay[s, at, :] = p
                last = slice(7, 8)
            done.append((jnp.broadcast_to(p[last], (8, 128)), jnp.broadcast_to(v[last], (8, 128))))
        return tuple(done)

    start = tuple((jnp.ones((8, 128), F32), jnp.zeros((8, 128), F32)) for _ in range(8))
    return lax.fori_loop(0, count, step, start)


def exchange_ends(r, net, ends, at):
    for s in range(8):
        r.tot[at, net.z, 0, s : s + 1, :] = ends[s][0][0:1, :]
        r.tot[at, net.z, 1, s : s + 1, :] = ends[s][1][0:1, :]
    mine = r.tot.at[at, net.z]
    return [net.copy(mine, mine, net.line(net.up(k), net.c)) for k in (1, 2, 3)]


def entering_states(r, net, copies, at, reverse):
    for made in copies:
        made.wait_recv()
    state = jnp.zeros((8, 128), F32)
    for i in range(4):
        z = 3 - i if reverse else i
        new = r.tot[at, z, 0] * state + r.tot[at, z, 1]
        state = jnp.where((z > net.z) if reverse else (z < net.z), new, state)
    r.inc[...] = state


def tile_rows(i):
    return pl.ds(pl.multiple_of(i * TILE, TILE), TILE)


def layer(r):
    r.do_all = r.x_all
    r.dconv = r.gb
    r.dgi = r.dgu
    r.ug, r.ul = r.d_res.at[:, 0:384], r.d_res.at[:, 384:768]
    r.ga = [r.hid.at[i, :, 0:256] for i in range(4)]
    r.gb2 = [r.hid.at[4 + i, 0:128, 0:256] for i in range(4)]
    net = Net(r)
    p, z, c, o, q = net.p, net.z, net.c, net.o, net.q
    sibling = net.plane(0, o)
    mine = net.slot(0, c)
    cols = r.wgu_out.shape[2]
    piece = cols // 4
    down = pl.ds(pl.multiple_of(p * piece, 16), piece)
    quarter = pl.ds(pl.multiple_of(p * 48, 16), 48)
    staged = []
    for j in range(8):
        lanes = pl.ds(j * cols, cols)
        staged.append(net.local(r.wmg.at[:, lanes], r.hid.at[j, pl.ds(0, 128)]))
        staged.append(net.local(r.wmu.at[:, lanes], r.hid.at[j, pl.ds(128, 128)]))
    width = 3 * 128
    first = pl.multiple_of(p * width, 128)
    chip = pl.ds(first, width)
    own_lanes = pl.ds(pl.multiple_of(c * width, 128), width)
    wi_rows, wg_rows = pl.ds(128, 128), pl.ds(0, 128)
    placed = [
        net.local(r.wg.at[:, chip], r.wgi3.at[z, wg_rows, own_lanes]),
        net.local(r.wi.at[:, chip], r.wgi3.at[z, wi_rows, own_lanes]),
        net.local(r.wmd.at[down], r.wmd_all.at[z]),
        net.local(r.wout.at[quarter], r.wq.at[z]),
        net.local(r.wr.at[quarter], r.gq.at[z, :, pl.ds(0, 128)]),
        net.local(r.wv.at[quarter], r.gq.at[z, :, pl.ds(128, 128)]),
        net.local(r.g, r.g_all.at[mine]),
    ]
    r.lens_out[0:1, 0:5] = r.lens[...].astype(F32)
    r.small_rows[...] = jnp.zeros((16, 256), F32)
    r.small_rows[0:4, 0:192] = r.cw[...].astype(F32)
    for at, ref in ((4, r.cb), (5, r.br), (6, r.bi), (7, r.lam)):
        r.small_rows[at : at + 1, 0:192] = ref[...].astype(F32).reshape(1, 192)
    for at, ref in ((0, r.ngain), (128, r.mgain)):
        r.small_rows[10:11, at : at + 128] = ref[...].astype(F32).reshape(1, 128)
    r.small[...] = r.small_rows[...].astype(BF)
    net.greet()
    r.small_all[q] = r.small[...]
    r.lens_all[p] = r.lens_out[...]
    small = [net.copy(r.small, r.small_all.at[q], net.line(net.up(k), core)) for k in (1, 2, 3) for core in (c, o)]
    small.append(net.copy(r.small, r.small_all.at[q], sibling))
    lens = [net.copy(r.lens_out, r.lens_all.at[p], net.plane(k, c)) for k in (1, 2, 3)]
    tokens = Gather(net, r.x, r.x_all)
    tokens.start()
    theirs = pl.ds(pl.multiple_of(c * width + o * 128, 128), 256)

    def along(place):
        made = LineGather(net, [(place(z), c)], lambda j: place(z), lambda j, at: place(at))
        for k in (2, 1, 3):
            made.start(k, (0,))
        return made

    handed = []

    def heads_start(rows):
        here = r.wgi3.at[z, rows, theirs]
        made = along(lambda at: r.wgi3.at[at, rows, own_lanes])
        return made, [net.copy(here, here, sibling, handed)]

    for made in placed:
        made.wait()
    heads_in, heads_in_over = heads_start(wi_rows)
    gates_in = along(lambda at: r.gq.at[at])

    def hand_over(arrivals, rows, over):
        arrivals.end()
        for k in (1, 2, 3):
            here = r.wgi3.at[net.down(k), rows, theirs]
            over.append(net.copy(here, here, sibling, handed))

    def arrange(over, rows, lanes):
        for made in over:
            made.wait_recv()
        for core in range(2):
            cols_in = pl.ds(pl.multiple_of(core * width + c * 128, 128), 256)
            for at in range(4):
                to = slice((at * 2 + core) * 128, (at * 2 + core + 1) * 128)
                r.w2[to, lanes] = r.wgi3[at, rows, cols_in]

    def exchange(arrivals, src, dst):
        arrivals.end()
        dst[c, quarter, :] = src[p]
        return [net.copy(src.at[net.near[k]], dst.at[c, quarter], net.plane(k, c)) for k in (1, 2, 3)]

    def share(copies, dst):
        for made in copies:
            made.wait_recv()
        return net.copy(dst.at[c], dst.at[c], sibling)

    selects = []
    k_at = lax.broadcasted_iota(jnp.int32, (cols, cols), 0)
    j_at = lax.broadcasted_iota(jnp.int32, (cols, cols), 1)
    for part in range(4):
        inside = (j_at >= part * piece) & (j_at < (part + 1) * piece)
        chosen = inside & (k_at == j_at + (p - part) * piece)
        selects.append(jnp.where(chosen, 1.0, 0.0).astype(BF))
    for made in staged:
        made.wait()
    for which in range(2):
        rows = slice(which * 128, (which + 1) * 128)
        for core in (0, 1):
            picked = None
            for part in range(4):
                term = dot(r.hid[part * 2 + core, rows, :], selects[part])
                picked = term if picked is None else picked + term
            r.wgu_out[core, rows, :] = picked.astype(BF)
    for made in small + lens:
        made.wait_recv()
    low, high = r.small_all[2 * p].astype(F32), r.small_all[2 * p + 1].astype(F32)
    at_first = jnp.concatenate([low[:, :192], high[:, :64]], axis=1)
    at_second = jnp.concatenate([low[:, 128:192], high[:, :192]], axis=1)
    both = lax.select(c == 0, at_first, at_second)
    for n in range(2):
        r.chan[n] = both[:, n * 128 : (n + 1) * 128]
        lam = -r.chan[n, 7:8, :]
        e = jnp.exp(-jnp.abs(lam))
        series = 1.0 - e * (6 / 7)
        for k in (6, 5, 4, 3, 2):
            series = 1.0 - e * ((k - 1) / k) * series
        rate = jnp.maximum(lam, 0.0) + jnp.where(e < 0.05, e * series, jnp.log(1.0 + e))
        r.chan[n, 7:8, :] = rate
        r.chan[n, 8:9, :] = jax.nn.sigmoid(lam)
    for i in range(8):
        gains = r.small_all[i].astype(F32)[10:11, :]
        r.gain[0:1, i * 128 : (i + 1) * 128] = gains[:, 0:128]
        r.gain[1:2, i * 128 : (i + 1) * 128] = gains[:, 128:256]
    gain = r.gain[0:1, :]
    for b in range(4):
        start = jnp.zeros((1, 128), F32)
        for row in range(5):
            r.starts_all[b, row : row + 1, :] = start
            start = start + jnp.broadcast_to(r.lens_all[b, 0:1, row : row + 1], (1, 128))


    def offset_rows(i):
        b, tile = lax.div(i, 13), lax.rem(i, 13)
        starts = r.starts_all[b]
        at = lax.convert_element_type(z * 512 + tile * 40, F32)
        at = at + lax.broadcasted_iota(jnp.int32, (40, 128), 0).astype(F32)
        begun = jnp.zeros((40, 128), F32)
        for row in range(1, 5):
            start = starts[row : row + 1, :]
            begun = jnp.where(at >= start, start, begun)
        r.off[b, pl.ds(pl.multiple_of(tile * 40, 8), 40), :] = at - begun

    loop(52, offset_rows)

    def normalise(slot):
        def body(i):
            rows = pl.ds(pl.multiple_of(i * 32, 32), 32)
            v = r.x_all[slot, rows, :].astype(F32)
            s = lax.rsqrt(jnp.mean(v * v, axis=-1, keepdims=True) + NORM_EPS)
            r.normed[slot, rows, :] = (v * s * gain).astype(BF)

        loop(8, body)

    r.x_all[mine] = r.x[...]
    normalise(mine)
    tokens.sibling(0)
    normalise(net.slot(0, o))
    tokens.forward()
    heads_in.relay()
    gates_in.relay()
    out_in = along(lambda at: r.wq.at[at])
    feed = LineGather(
        net,
        [(r.wgu_out.at[core], core) for core in (c, o)],
        lambda j: r.wgu_all.at[q],
        lambda j, at: r.wgu_all.at[at * 2 + (c, o)[j]],
    )
    feed_down = LineGather(net, [(r.wmd.at[down], c)], lambda j: r.wmd_all.at[z], lambda j, at: r.wmd_all.at[at])
    hand_over(heads_in, wi_rows, heads_in_over)
    tokens.middle()
    gates_out = exchange(gates_in, r.gq, r.g3)
    for k in (1, 2):
        normalise(net.slot(k, c))
    for k in (1, 2):
        tokens.sibling(k)
        normalise(net.slot(k, o))
    arrange(heads_in_over, slice(128, 256), slice(256, 512))

    def project_inner(slot):
        b, half = lax.div(slot, 2), lax.rem(slot, 2)
        at = pl.multiple_of(half * 256, 256)
        inner = dot(r.normed[slot], r.w2[:, 256:512]).astype(BF).astype(F32)
        for n in range(2):
            r.inner[b * 2 + n, pl.ds(at + 8, 256), :] = inner[:, n * 128 : (n + 1) * 128]

    def project_gate(slot):
        b, half = lax.div(slot, 2), lax.rem(slot, 2)
        at = pl.multiple_of(half * 256, 256)
        gate = dot(r.normed[slot], r.w2[:, 0:256])
        for n in range(2):
            r.gp[b * 2 + n, pl.ds(at, 256), :] = gate[:, n * 128 : (n + 1) * 128]

    out_in.relay()
    for k in (0, 1, 2):
        project_inner(net.slot(k, c))
        project_inner(net.slot(k, o))
    tokens.last()
    normalise(net.slot(3, c))
    project_inner(net.slot(3, c))
    tokens.sibling(3)
    normalise(net.slot(3, o))
    project_inner(net.slot(3, o))
    edge = net.reserve(1)

    def edge_copy():
        return net.describe(
            r.inner.at[:, pl.ds(512, 8)], r.inner.at[:, pl.ds(0, 8)], net.line(net.up(1), c), edge, edge
        )

    @pl.when(z < 3)
    def _():
        edge_copy().start()

    @pl.when(z == 0)
    def _():
        r.inner[:, 0:8, :] = jnp.zeros((8, 8, 128), F32)

    gates_over = share(gates_out, r.g3)
    stored = net.local(r.normed, r.normed_far)
    cots = Gather(net, r.g_all.at[mine], r.g_all)
    cots.start()
    tokens.release()
    gates_over.wait_recv()
    for i in range(4):
        at = c * 128 + i * 64
        value = r.g3[lax.div(at, 192), pl.ds(pl.multiple_of(lax.rem(at, 192), 64), 64), :]
        r.wri[i // 2, (i % 2) * 64 : (i % 2 + 1) * 64, :] = value
    heads_gate, heads_gate_over = heads_start(wg_rows)

    @pl.when(z > 0)
    def _():
        edge_copy().wait_recv()


    def conv_tile(i):
        b, tile = lax.div(i, 8), lax.rem(i, 8)
        rows = tile_rows(tile)
        offset = r.off[b, rows, :]
        for n in range(2):
            s = b * 2 + n
            window = r.inner[s, pl.ds(pl.multiple_of(tile * TILE, 8), TILE + 8), :]
            chan = r.chan[n]
            total = chan[4:5, :] + chan[0:1, :] * window[8:, :]
            for k in (1, 2, 3):
                total = total + chan[k : k + 1, :] * jnp.where(offset >= k, window[8 - k : TILE + 8 - k, :], 0.0)
            r.conv[s, rows, :] = total.astype(BF)

    loop(32, conv_tile)
    feed.start(2, (0,))
    out_rows_in = exchange(out_in, r.wq, r.w3)

    def gate_products(i):
        s, half = lax.div(i, 2), lax.rem(i, 2)
        n = lax.rem(s, 2)
        rows = pl.ds(pl.multiple_of(half * 256, 256), 256)
        pre = dot(r.conv[s, rows, :], r.wri[n])
        r.sr[s, rows, :] = pre[:, :128]
        r.si[s, rows, :] = pre[:, 128:]

    loop(16, gate_products)
    heads_gate.relay()

    def terms(b):
        starts_b = r.starts_all[b]

        def tile(i, sums):
            rows = tile_rows(i)
            offset = r.off[b, rows, :]
            at = lax.convert_element_type(z * 512 + i * TILE, F32)
            begun = at + lax.broadcasted_iota(jnp.int32, (TILE, 128), 0).astype(F32) - offset
            restart = offset == 0.0
            added = []
            for n in range(2):
                s = b * 2 + n
                chan = r.chan[n]
                sr = jax.nn.sigmoid(r.sr[s, rows, :] + chan[5:6, :])
                si = jax.nn.sigmoid(r.si[s, rows, :] + chan[6:7, :])
                r.sr[s, rows, :] = sr
                r.si[s, rows, :] = si
                a, m2 = decay_parts(sr, chan[7:8, :])
                r.dec[s, rows, :] = jnp.where(restart, 0.0, a)
                m = jnp.where(restart, 1.0, m2 * lax.rsqrt(m2))
                r.drv[s, rows, :] = m * si * r.conv[s, rows, :].astype(F32)
                for row in range(5):
                    inside = jnp.where(begun == starts_b[row : row + 1, :], a, 0.0)
                    added.append(sums[n * 5 + row] + column_sum(inside))
            return tuple(added)

        sums = lax.fori_loop(0, 512 // TILE, tile, tuple(jnp.zeros((8, 128), F32) for _ in range(10)))
        for n in range(2):
            rows = [jnp.sum(part, axis=0, keepdims=True) for part in sums[n * 5 : n * 5 + 5]]
            r.rs_all[z, b * 2 + n] = jnp.concatenate(rows + [jnp.zeros((3, 128), F32)], axis=0)

    loop(4, terms)
    cots.forward()
    ends = scan_slabs(r.dec, r.drv, False)
    ends = exchange_ends(r, net, ends, 0)
    feed.start(2, (1,))
    feed.start(1, (0, 1))
    feed.start(3, (0, 1))
    r.wgu_all[q] = r.wgu_out[c]
    feed_over = net.copy(r.wgu_out.at[o], r.wgu_all.at[q], sibling)
    hand_over(heads_gate, wg_rows, heads_gate_over)
    arrange(heads_gate_over, slice(0, 128), slice(0, 256))
    for made in handed:
        made.wait_send()
    heads_in.drain()
    heads_gate.drain()
    for k in (2, 1, 3):
        feed_down.start(k, (0,))
    for slot in range(8):
        project_gate(slot)

    def gelu_tile(i):
        s, rows = lax.div(i, 8), tile_rows(lax.rem(i, 8))
        v = r.gp[s, rows, :]
        t = jnp.tanh(GELU_SCALE * v * (1.0 + GELU_CUBE * v * v))
        r.gb[s, rows, :] = 0.5 * v * (1.0 + t)

    loop(64, gelu_tile)
    out_over = share(out_rows_in, r.w3)
    entering_states(r, net, ends, 0, False)
    row_sums = [net.copy(r.rs_all.at[z], r.rs_all.at[z], net.line(net.up(k), c)) for k in (1, 2, 3)]
    out_over.wait_recv()

    def own_rows(i):
        at = c * 128 + i * 64
        value = r.w3[lax.div(at, 192), pl.ds(pl.multiple_of(lax.rem(at, 192), 64), 64), :]
        r.wo[pl.ds(pl.multiple_of(i * 64, 64), 64), :] = value

    loop(4, own_rows)
    for s in range(8):
        r.states[s, 7:8, :] = r.inc[s : s + 1, :]

    def mix_tile(i):
        s, tile = lax.div(i, 8), lax.rem(i, 8)
        b, n = lax.div(s, 2), lax.rem(s, 2)
        rows = tile_rows(tile)
        states = r.drv[s, rows, :] + r.dec[s, rows, :] * r.inc[pl.ds(s, 1), :]
        r.states[s, pl.ds(pl.multiple_of(tile * TILE + 8, 8), TILE), :] = states
        lanes = pl.ds(pl.multiple_of(n * 128, 128), 128)
        r.mixed[b * 2 + lax.div(tile, 4), tile_rows(lax.rem(tile, 4)), lanes] = (states * r.gb[s, rows, :]).astype(BF)

    loop(64, mix_tile)
    stored.wait()
    lane = lax.broadcasted_iota(jnp.int32, (1, 256), 1)
    counted = jnp.where((lane >= 64 * c) & (lane < 192 + 64 * c), 1.0, 0.0)
    counted_two = jnp.concatenate([counted, counted], axis=1)

    def masked(value, mask):
        return (value.astype(F32) * mask).astype(BF)

    total = Reduce(
        net, r, lambda k, core: dot(masked(r.mixed[net.slot(k, core)], counted), r.wo[...])
    )
    for k in (3, 1, 2, 0):
        total.other(k)
    total.far()
    total.near()
    cots.middle()
    total.own()
    cots.last()
    for k in (0, 1, 2, 3):
        cots.sibling(k)
    cots.release()
    total.relay()
    feed_down.relay()
    feed.relay()
    def wmd():
        return r.wmd_all[...].reshape(cols, -1)

    total.finish()
    gain2 = r.gain[1:2, :]
    for h in range(2):

        def residual_rows(i, h=h):
            rows = pl.ds(pl.multiple_of(h * 128 + i * 32, 32), 32)
            v = r.x[rows, :].astype(F32) + total.total(h, i, 32)
            r.residual[rows, :] = v
            s = lax.rsqrt(jnp.mean(v * v, axis=-1, keepdims=True) + NORM_EPS)
            r.normed[mine, rows, :] = (v * s * gain2).astype(BF)

        loop(4, residual_rows)

    n2_all = r.normed
    acts = Gather(net, n2_all.at[mine], n2_all, tokens.at)
    acts.start()

    def gate_up(which):
        return r.wgu_all[:, which * 128 : (which + 1) * 128, :].reshape(-1, cols)

    def d_normed2(k, core):
        slot = net.slot(k, core)
        return dot(r.dgu[slot, :, 0:cols], gate_up(0), NT) + dot(r.dgu[slot, :, cols:], gate_up(1), NT)

    back = Reduce(net, r, d_normed2, total.at)

    def part(k, core):
        slot = net.slot(k, core)
        h = n2_all[slot]
        r.ug[...] = dot(h, gate_up(0))
        r.ul[...] = dot(h, gate_up(1))

        def body(i):
            rows = pl.ds(pl.multiple_of(i * 32, 32), 32)
            gelu, slope = gelu_parts(r.ug[rows, :])
            ul, dh = r.ul[rows, :], r.dgu[slot, rows, 0:cols].astype(F32)
            r.hid[slot, rows, :] = (gelu * ul).astype(BF)
            r.dgu[slot, rows, 0:cols] = (dh * ul * slope).astype(BF)
            r.dgu[slot, rows, cols:] = (dh * gelu).astype(BF)

        loop(8, body)

    feed_down.end()
    for slot in range(8):
        r.dgu[slot, :, 0:cols] = dot(r.g_all[slot], wmd(), NT).astype(BF)
    feed_over.wait_recv()
    feed.end()
    part(0, c)
    acts.sibling(0)
    part(0, o)
    back.other(0)
    acts.forward()
    acts.middle()
    part(1, c)
    part(2, c)
    acts.sibling(1)
    part(1, o)
    back.other(1)
    acts.sibling(2)
    part(2, o)
    back.other(2)
    back.near()
    acts.last()
    acts.sibling(3)
    part(3, o)
    back.other(3)
    part(3, c)
    back.far()
    back.relay()
    back.own()
    acts.release()
    for i in range(4):
        rows = n2_all[:, :, i * 256 : (i + 1) * 256].reshape(-1, 256)
        r.gm[i] = dot(rows, r.dgu[...].reshape(-1, 2 * cols), TN).astype(BF)

    def gm_in(k):
        return r.wgi3.at[k - 1]

    mlp_m = LineSum(net, lambda t: r.gm.at[t], gm_in)
    mlp_m.start()
    hid = r.hid[...].reshape(-1, cols)
    for half in range(2):
        lanes = slice(half * 512, half * 512 + 512)
        value = dot(hid, r.g_all[:, :, lanes].reshape(-1, 512), TN).astype(BF)
        for i in range(4):
            r.gd[i, :, lanes] = value[i * piece : (i + 1) * piece, :]
    mlp_d = LineSum(net, lambda t: r.gd.at[t], lambda k: r.gd_in.at[k - 1])
    back.finish()
    sums = jnp.zeros((8, r.x.shape[1]), F32)
    for h in range(2):

        def residual_back(i, sums, h=h):
            rows = pl.ds(pl.multiple_of(h * 128 + i * 32, 32), 32)
            v = r.residual[rows, :]
            dn = back.total(h, i, 32)
            s = lax.rsqrt(jnp.mean(v * v, axis=-1, keepdims=True) + NORM_EPS)
            u = dn * gain2
            pulled = s * u - v * (s * s * s * jnp.mean(u * v, axis=-1, keepdims=True))
            d_res = r.g_all[mine, rows, :].astype(F32) + pulled
            r.d_res[rows, :] = d_res
            r.do_all[mine, rows, :] = d_res.astype(BF)
            return sums + jnp.sum((dn * v * s).reshape(4, 8, -1), axis=0)

        sums = lax.fori_loop(0, 4, residual_back, sums)
    r.gain2_sum[...] = sums

    owners, returned = [], []

    def to_chips(src, dst):
        for k in (1, 2, 3):
            owners.append(net.copy(src, dst.at[p], net.plane(k, c)))
        returned.append(net.local(src, dst.at[p]))

    fo_at = net.reserve(4)

    def vector_copy(k):
        return net.describe(r.vout.at[p], r.vout.at[p], net.plane(k, c), fo_at + k, fo_at)

    owners_m = Owners(net, r.gm_sum, r.fm, r.fm_x)
    owners_d = Owners(net, r.gd_sum, r.fd)
    owners_a = Owners(net, r.ga_sum, r.fa, r.fa_x)
    owners_b = Owners(net, r.gb2_sum, r.fb)

    def mlp_sums():
        mlp_m.end(r.gm_sum)
        owners_m.start()

    grads = Gather(net, r.do_all.at[mine], r.do_all, cots.at)
    grads.start()

    def back_out(slot):
        b, half = lax.div(slot, 2), lax.rem(slot, 2)
        dm = dot(r.do_all[slot], r.wo[...], NT)
        for n in range(2):
            r.dconv[b * 2 + n, pl.ds(pl.multiple_of(half * 256, 256), 256), :] = dm[:, n * 128 : (n + 1) * 128]

    back_out(mine)
    grads.sibling(0)
    back_out(net.slot(0, o))
    out = Reduce(net, r, lambda k, core: dot(r.hid[net.slot(k, core)], wmd()), total.at)
    for k in (3, 1, 2, 0):
        out.other(k)
    grads.forward()
    out.far()
    out.near()
    out.own()
    grads.middle()
    mlp_m.relay()
    for k in (1, 2):
        back_out(net.slot(k, c))
    for k in (1, 2):
        grads.sibling(k)
        back_out(net.slot(k, o))
    grads.last()
    back_out(net.slot(3, c))
    grads.sibling(3)
    back_out(net.slot(3, o))

    def first_pass(i):
        b, tile = lax.div(i, 8), lax.rem(i, 8)
        rows = tile_rows(tile)
        live = r.off[b, rows, :] != 0.0
        for n in range(2):
            s = b * 2 + n
            gelu, slope = gelu_parts(r.gp[s, rows, :])
            dm = r.dconv[s, rows, :]
            states = r.states[s, pl.ds(pl.multiple_of(tile * TILE + 8, 8), TILE), :]
            lanes = slice(n * 128, (n + 1) * 128)
            r.dgi[b * 2 + lax.div(tile, 4), tile_rows(lax.rem(tile, 4)), lanes] = (dm * states * slope).astype(BF)
            r.drv[s, rows, :] = dm * gelu
            a = jnp.exp(-DECAY_SCALE * r.sr[s, rows, :] * r.chan[n, 7:8, :])
            r.dec[s, rows, :] = jnp.where(live, a, 0.0)

    loop(32, first_pass)
    ends = scan_slabs(r.dec, r.drv, True)
    ends = exchange_ends(r, net, ends, 1)
    out.relay()
    go_in, go_line_in = r.go_q, r.go_l
    mixed = r.mixed[...].reshape(-1, 256)
    for half in range(2):
        lanes = slice(half * 512, half * 512 + 512)
        r.go[:, lanes] = dot(mixed, r.do_all[:, :, lanes].reshape(-1, 512), TN).astype(BF)
    grads.release()
    fetched = net.local(r.normed_far, r.do_all)
    go_rows = [pl.ds(pl.multiple_of(c * 64 + near * 48, 16), 48) for near in net.near]

    def go_start(lanes):
        return [net.copy(r.go.at[go_rows[k], lanes], go_in.at[p, :, lanes], net.plane(k, c)) for k in (1, 2, 3)]

    go_out = go_start(pl.ds(0, 1024))
    mlp_sums()
    entering_states(r, net, ends, 1, True)
    r.vec[...] = jnp.zeros((2, 8, 8, 128), F32)
    dri = r.normed

    def second_pass(s):
        b, n = lax.div(s, 2), lax.rem(s, 2)
        chan = r.chan[n]
        enter = r.inc[pl.ds(s, 1), :]
        lanes_r = pl.ds(pl.multiple_of(n * 256, 128), 128)
        lanes_i = pl.ds(pl.multiple_of(n * 256 + 128, 128), 128)

        def tile(i, sums):
            rows = tile_rows(i)
            live = r.off[b, rows, :] != 0.0
            ds = r.drv[s, rows, :] + r.dec[s, rows, :] * enter
            window = r.states[s, pl.ds(pl.multiple_of(i * TILE, 8), TILE + 8), :]
            before = window[7 : TILE + 7, :]
            sr, si = r.sr[s, rows, :], r.si[s, rows, :]
            cv = r.conv[s, rows, :].astype(F32)
            a, m2 = decay_parts(sr, chan[7:8, :])
            inv = lax.rsqrt(m2)
            m = jnp.where(live, m2 * inv, 1.0)
            dsi = ds * si
            d_log = jnp.where(live, a * (ds * before - dsi * cv * a * inv), 0.0)
            lam_term = d_log * sr
            d_r = (-DECAY_SCALE) * chan[7:8, :] * lam_term * (1.0 - sr)
            dm_i = dsi * m
            d_i = dm_i * cv * (1.0 - si)
            d_r, d_i = d_r.astype(BF), d_i.astype(BF)
            at = tile_rows(lax.rem(i, 4))
            dri[b * 2 + lax.div(i, 4), at, lanes_r] = d_r
            dri[b * 2 + lax.div(i, 4), at, lanes_i] = d_i
            r.dconv[s, rows, :] = dm_i
            return (
                sums[0] + column_sum(d_r.astype(F32)),
                sums[1] + column_sum(d_i.astype(F32)),
                sums[2] + column_sum(lam_term),
            )

        zero = jnp.zeros((8, 128), F32)
        sums = lax.fori_loop(0, 512 // TILE, tile, (zero, zero, zero))
        for j in range(3):
            r.vec[n, 5 + j] = r.vec[n, 5 + j] + sums[j]

    loop(8, second_pass)

    def gate_back(i):
        s, half = lax.div(i, 2), lax.rem(i, 2)
        b, n = lax.div(s, 2), lax.rem(s, 2)
        rows = pl.ds(pl.multiple_of(half * 256, 256), 256)
        lanes = pl.ds(pl.multiple_of(n * 256, 256), 256)
        r.dconv[s, rows, :] = r.dconv[s, rows, :] + dot(dri[b * 2 + half, :, lanes], r.wri[n], NT)

    loop(16, gate_back)
    edge_back = net.reserve(1)

    def edge_back_copy():
        return net.describe(
            r.dconv.at[:, pl.ds(0, 8)], r.dconv.at[:, pl.ds(512, 8)], net.line(net.down(1), c), edge_back, edge_back
        )

    @pl.when(z > 0)
    def _():
        edge_back_copy().start()

    mlp_d.start()

    @pl.when(z == 3)
    def _():
        r.dconv[:, 512:520, :] = jnp.zeros((8, 8, 128), F32)

    for n in range(2):
        total_ri = None
        for b in range(4):
            for half in range(2):
                term = dot(
                    r.conv[b * 2 + n, half * 256 : (half + 1) * 256, :],
                    dri[b * 2 + half, :, n * 256 : (n + 1) * 256],
                    TN,
                )
                total_ri = term if total_ri is None else total_ri + term
        r.go[n * 128 : (n + 1) * 128, 1024:1280] = total_ri.astype(BF)
    go_out += go_start(pl.ds(1024, 256))

    @pl.when(z < 3)
    def _():
        edge_back_copy().wait_recv()


    def conv_back(s):
        b, n = lax.div(s, 2), lax.rem(s, 2)
        chan = r.chan[n]
        lanes = pl.ds(pl.multiple_of(256 + n * 128, 128), 128)

        def tile(i, sums):
            offset = r.off[b, pl.ds(pl.multiple_of(i * TILE, 8), TILE + 8), :]
            window = r.dconv[s, pl.ds(pl.multiple_of(i * TILE, 8), TILE + 8), :]
            inner = r.inner[s, pl.ds(pl.multiple_of(i * TILE, 8), TILE + 8), :]
            value = chan[0:1, :] * window[:TILE, :]
            added = [sums[0] + column_sum(window[:TILE, :] * inner[8:, :])]
            for k in (1, 2, 3):
                held = jnp.where(offset >= k, window, 0.0)
                value = value + chan[k : k + 1, :] * held[k : TILE + k, :]
                added.append(sums[k] + column_sum(held[:TILE, :] * inner[8 - k : TILE + 8 - k, :]))
            added.append(sums[4] + column_sum(window[:TILE, :]))
            r.dgi[b * 2 + lax.div(i, 4), tile_rows(lax.rem(i, 4)), lanes] = value.astype(BF)
            return tuple(added)

        sums = lax.fori_loop(0, 512 // TILE, tile, tuple(jnp.zeros((8, 128), F32) for _ in range(5)))
        for j in range(5):
            r.vec[n, j] = r.vec[n, j] + sums[j]

    loop(8, conv_back)
    out.finish()
    for h in range(2):

        def out_rows(i, h=h):
            rows = pl.ds(pl.multiple_of(h * 128 + i * 32, 32), 32)
            value = (r.residual[rows, :] + out.total(h, i, 32)).astype(BF)
            for j in range(4):
                r.dgu[j, rows, 512:768] = value[:, j * 256 : (j + 1) * 256]

        loop(4, out_rows)
    for j in range(4):
        returned.append(net.local(r.dgu.at[j, :, pl.ds(512, 256)], r.block_out.at[:, pl.ds(j * 256, 256)]))
    for partner in (sibling, net.plane(1, c), net.plane(2, c)):
        pl.semaphore_signal(r.free, inc=1, device_id=partner, device_id_type=pl.DeviceIdType.MESH)
    for n in range(2):
        sums = [jnp.sum(r.vec[n, j], axis=0, keepdims=True) for j in range(8)]
        sums[7] = sums[7] * (DECAY_SCALE * r.chan[n, 8:9, :])
        r.vsum[z, :, n * 128 : (n + 1) * 128] = jnp.concatenate(sums, axis=0)
    vec = [net.copy(r.vsum.at[z], r.vsum.at[z], net.line(net.up(k), c)) for k in (1, 2, 3)]
    fetched.wait()
    flat = r.dgi[:, :, 0:512].reshape(-1, 512)
    for i in range(4):
        value = dot(r.do_all[:, :, i * 256 : (i + 1) * 256].reshape(-1, 256), flat, TN)
        for j in range(2):
            n0, n1 = value[:, j * 256 : j * 256 + 128], value[:, j * 256 + 128 : j * 256 + 256]
            r.ga[i][:, j * 128 : (j + 1) * 128] = lax.select(c == 0, n0, n1).astype(BF)
            shared = lax.select(c == 0, n1, n0)
            r.gb2[i][:, j * 128 : (j + 1) * 128] = lax.select(c == 0, shared[0:128], shared[128:256]).astype(BF)

    def ga_in(k):
        return r.g_all.at[7, :, pl.ds((k - 1) * 256, 256)]

    def gb_in(k):
        return r.g_all.at[3 + k, pl.ds(128, 128), pl.ds(0, 256)]

    sum_a = LineSum(net, lambda t: r.hid.at[t, :, 0:256], ga_in)
    sum_b = LineSum(net, lambda t: r.hid.at[4 + t, 0:128, 0:256], gb_in)
    sum_a.start()
    sum_b.start()
    mlp_d.relay()
    owners_m.forward()
    first_back = Reduce(
        net,
        r,
        lambda k, core: dot(masked(r.dgi[net.slot(k, core), :, 0:512], counted_two), r.w2[...], NT),
        total.at,
    )
    pl.semaphore_wait(r.free, 3)
    for k in (3, 1, 2, 0):
        first_back.other(k)
    first_back.far()
    first_back.near()
    go_in[p] = r.go[go_rows[0], :]
    for made in go_out:
        made.wait_recv()
    go_line = LineSum(net, lambda t: go_in.at[t], lambda k: go_line_in.at[k - 1])
    go_line.start()
    first_back.relay()
    mlp_d.end(r.gd_sum)
    owners_d.start()
    first_back.own()
    owners_m.middle()
    sum_a.relay()
    sum_b.relay()
    go_line.relay()
    first_back.finish()
    sums = jnp.zeros((8, r.x.shape[1]), F32)
    for h in range(2):

        def input_rows(i, sums, h=h):
            rows = pl.ds(pl.multiple_of(h * 128 + i * 32, 32), 32)
            v = r.x[rows, :].astype(F32)
            dn = first_back.total(h, i, 32)
            s = lax.rsqrt(jnp.mean(v * v, axis=-1, keepdims=True) + NORM_EPS)
            u = dn * r.gain[0:1, :]
            r.d_res[rows, :] = r.d_res[rows, :] + (
                s * u - v * (s * s * s * jnp.mean(u * v, axis=-1, keepdims=True))
            )
            return sums + jnp.sum((dn * v * s).reshape(4, 8, -1), axis=0)

        sums = lax.fori_loop(0, 4, input_rows, sums)
    returned.append(net.local(r.d_res, r.d_in))
    gains = jnp.concatenate(
        [
            jnp.sum(sums, axis=0, keepdims=True),
            jnp.sum(r.gain2_sum[...], axis=0, keepdims=True),
            jnp.zeros((6, sums.shape[1]), F32),
        ],
        axis=0,
    )
    for i in range(8):
        r.gsum[i] = gains[:, i * 128 : (i + 1) * 128]
    r.gline[q] = r.gsum[q]
    gain_line = [
        net.copy(r.gsum.at[net.up(k) * 2 + core], r.gline.at[q], net.line(net.up(k), core))
        for k in (1, 2, 3)
        for core in (c, o)
    ]
    gain_line.append(net.copy(r.gsum.at[z * 2 + o], r.gline.at[q], sibling))
    for made in row_sums:
        made.wait_recv()
    r.rows_sum[...] = r.rs_all[0] + r.rs_all[1] + r.rs_all[2] + r.rs_all[3]
    for k in (1, 2, 3):
        for core in (c, o):
            owners.append(net.copy(r.rows_sum.at[pl.ds(net.near[k] * 2, 2)], r.fr.at[mine], net.plane(k, core)))
    owners.append(net.copy(r.rows_sum.at[pl.ds(p * 2, 2)], r.fr.at[mine], sibling))
    returned.append(net.local(r.rows_sum.at[pl.ds(p * 2, 2)], r.fr.at[mine]))
    for made in vec:
        made.wait_recv()
    r.vout[p] = r.vsum[0] + r.vsum[1] + r.vsum[2] + r.vsum[3]

    @pl.when(z == p)
    def _():
        for k in (1, 2, 3):
            vector_copy(k).start()

    sum_a.end(r.ga_sum)
    owners_a.start()
    sum_b.end(r.gb2_sum)
    owners_b.start()
    go_line.end(r.go_sum)
    to_chips(r.go_sum, r.fo)
    owners_d.forward()
    owners_m.last()
    owners_a.forward()
    owners_b.forward()
    for made in gain_line:
        made.wait_recv()
    sums = r.gline[0]
    for i in range(1, 8):
        sums = sums + r.gline[i]
    r.gplane[p] = sums
    gain_plane = [net.copy(r.gplane.at[p], r.gplane.at[p], net.plane(k, c)) for k in (1, 2, 3)]

    @pl.when(z != p)
    def _():
        vector_copy(1).wait_recv()

    @pl.when(z == p)
    def _():
        for k in (1, 2, 3):
            vector_copy(k).wait_send()

    owners_d.middle()
    owners_a.middle()
    owners_b.middle()
    for each in (owners_d, owners_a, owners_b):
        each.last()
    for each in (owners_m, owners_d, owners_a, owners_b):
        each.end()
    for made in owners + gain_plane:
        made.wait_recv()
    r.gain_out[...] = r.gplane[0] + r.gplane[1] + r.gplane[2] + r.gplane[3]
    r.vec_out[...] = r.vout[z]
    for made in returned:
        made.wait()
    @pl.when(z < 3)
    def _():
        edge_copy().wait_send()

    @pl.when(z > 0)
    def _():
        edge_back_copy().wait_send()

    gates_in.drain()
    out_in.drain()
    feed.drain()
    feed_down.drain()
    for made in (mlp_m, mlp_d, go_line, sum_a, sum_b):
        made.drain()
    net.drain()


def assemble(r):
    c = lax.rem(lax.axis_index("seq"), 2)
    count = 0
    stores = []

    def start(src, dst):
        nonlocal count
        made = pltpu.make_async_copy(src, dst, r.local.at[count])
        count += 1
        made.start()
        return made

    mine = pl.ds(pl.multiple_of(c * 128, 128), 128)
    loads = [
        [start(r.fm.at[:, mine], r.vm.at[c]), start(r.fm_x, r.vm.at[1 - c])],
        [start(r.fa.at[:, mine], r.va.at[c]), start(r.fa_x, r.va.at[1 - c]), start(r.fb, r.vb)],
        [start(r.fd, r.vd)],
        [start(r.fo, r.vo)],
    ]

    def loaded(which):
        for made in loads[which]:
            made.wait()

    passed = [start(r.d_in, r.v_din), start(r.block_out, r.v_block)]
    vec = r.vec_in[...]
    vec = lax.select(c == 0, vec[:, 0:192], vec[:, 64:256])
    r.o_cw[...] = vec[0:4]
    for j, out in enumerate((r.o_cb, r.o_rb, r.o_ib, r.o_lam)):
        out[...] = vec[4 + j : 5 + j]
    r.o_ngain[...] = r.gains[0:1, :]
    r.o_mgain[...] = r.gains[1:2, :]
    counts = [jnp.broadcast_to(r.lens[0:1, row : row + 1].astype(F32), (1, 128)) for row in range(5)]
    for chip in range(4):
        for half, (slot, n) in enumerate(((chip * 2, 0), (chip * 2, 1), (chip * 2 + 1, 1))):
            at = chip * 384 + half * 128
            for row in range(5):
                r.o_mean[row, :, at : at + 128] = r.fr[slot, n, row : row + 1, :] / counts[row]
    cols = r.fm.shape[2] // 2
    piece = cols // 4
    loaded(0)
    for j, (stage, out) in enumerate(((r.s_mgate, r.o_mgate), (r.s_mup, r.o_mup))):
        for part in range(4):
            for core in range(2):
                at = (part * 2 + core) * cols
                lanes = slice(j * cols + part * piece, j * cols + (part + 1) * piece)
                stage[:, at : at + cols] = jnp.concatenate(
                    [r.vm[core, chip, :, lanes].astype(F32) for chip in range(4)], axis=1
                )
            here = pl.ds(part * 2 * cols, 2 * cols)
            stores.append(start(stage.at[:, here], out.at[:, here]))
    for made, src, dst in zip(passed, (r.v_din, r.v_block), (r.o_din, r.o_block)):
        made.wait()
        stores.append(start(src, dst))
    loaded(1)
    for j, (stage, out) in enumerate(((r.s_gate, r.o_gate), (r.s_in, r.o_in))):
        lanes = slice(j * 128, (j + 1) * 128)
        for chip in range(4):
            at = chip * 384
            stage[:, at : at + 128] = r.va[0, chip, :, lanes].astype(F32)
            stage[:, at + 128 : at + 256] = r.vb[chip, :, lanes].astype(F32)
            stage[:, at + 256 : at + 384] = r.va[1, chip, :, lanes].astype(F32)
        stores.append(start(stage, out))
    loaded(2)
    for chip in range(4):
        r.s_down[chip * piece : (chip + 1) * piece, :] = r.vd[chip].astype(F32)
    stores.append(start(r.s_down, r.o_mdown))
    loaded(3)
    for chip in range(4):
        rows = slice(chip * 48, (chip + 1) * 48)
        r.s_out[rows, :] = r.vo[chip, :, 0:1024].astype(F32)
        r.o_r[rows, :] = r.vo[chip, :, 1024:1152].astype(F32)
        r.o_i[rows, :] = r.vo[chip, :, 1152:1280].astype(F32)
    stores.append(start(r.s_out, r.o_out))
    for made in stores:
        made.wait()


def shifted(value, axis, by):
    count = lax.axis_size(axis)
    pairs = [(i, i + by) for i in range(count) if 0 <= i + by < count]
    return lax.ppermute(value, axis, pairs)


def entering(value, axis, combine, identity, reverse):
    count, place = (lax.axis_size(axis), lax.axis_index(axis))
    everything = jax.tree.map(lambda part: lax.all_gather(part, axis), value)
    start = jax.tree.map(
        lambda part, zero: jnp.broadcast_to(jnp.asarray(zero, part.dtype), part.shape),
        value,
        identity,
    )

    def step(k, before):
        at = count - 1 - k if reverse else k
        reached = at > place if reverse else at < place
        new = combine(before, jax.tree.map(lambda part: part[at], everything))
        return jax.tree.map(lambda a, b: jnp.where(reached, a, b), new, before)

    return lax.fori_loop(0, count, step, start)


def rms_scale(values):
    return values * lax.rsqrt(jnp.mean(values * values, axis=-1, keepdims=True) + NORM_EPS)


def gelu_tanh(values):
    return jax.nn.gelu(values, approximate=True)


def link(earlier, later):
    return (earlier[0] * later[0], later[0] * earlier[1] + later[1])


def block_product(values, weight):
    count, channels = values.shape
    block_size = weight.shape[1]
    shaped = values.reshape(count, channels // block_size, block_size)
    result = jnp.einsum(
        "lni,nij->lnj",
        shaped,
        weight.reshape(channels // block_size, block_size, block_size),
        preferred_element_type=jnp.float32,
    )
    return result.reshape(count, channels)


def block_back(grads, weight):
    count, channels = grads.shape
    block_size = weight.shape[1]
    shaped = grads.reshape(count, channels // block_size, block_size)
    result = jnp.einsum(
        "lnj,nij->lni",
        shaped,
        weight.reshape(channels // block_size, block_size, block_size),
        preferred_element_type=jnp.float32,
    )
    return result.reshape(count, channels)


def block_weight_grad(values, grads, block_size):
    count, channels = values.shape
    left = values.reshape(count, channels // block_size, block_size)
    right = grads.reshape(count, channels // block_size, block_size)
    return jnp.einsum("lni,lnj->nij", left, right, preferred_element_type=jnp.float32).reshape(
        channels, block_size
    )


def recurrence_terms(conv_in, r_in, i_in, lam_in, restart):
    log_a = -DECAY_SCALE * jax.nn.sigmoid(r_in) * jax.nn.softplus(-lam_in)
    decays = jnp.exp(log_a)
    factor = jnp.where(restart[:, None] > 0, 1.0, jnp.sqrt(-jnp.expm1(2.0 * log_a)))
    return (decays * (1.0 - restart[:, None]), factor * jax.nn.sigmoid(i_in) * conv_in, decays)


def shards(
    inputs,
    out_grad,
    row_lengths,
    norm_gain,
    w_gate,
    w_in,
    conv_w,
    conv_b,
    w_rgate,
    b_rgate,
    w_igate,
    b_igate,
    lam,
    w_out,
    mlp_gain,
    w_mlp_gate,
    w_mlp_up,
    w_mlp_down,
):
    gathered = (
        lax.all_gather(norm_gain, "seq", axis=0, tiled=True),
        lax.all_gather(w_gate, "seq", axis=0, tiled=True),
        lax.all_gather(w_in, "seq", axis=0, tiled=True),
        lax.all_gather(conv_w, "seq", axis=1, tiled=True),
        lax.all_gather(conv_b, "seq", axis=0, tiled=True),
        lax.all_gather(w_rgate, "seq", axis=0, tiled=True),
        lax.all_gather(b_rgate, "seq", axis=0, tiled=True),
        lax.all_gather(w_igate, "seq", axis=0, tiled=True),
        lax.all_gather(b_igate, "seq", axis=0, tiled=True),
        lax.all_gather(lam, "seq", axis=0, tiled=True),
        lax.all_gather(w_out, "seq", axis=0, tiled=True),
        lax.all_gather(mlp_gain, "seq", axis=0, tiled=True),
        lax.all_gather(w_mlp_gate, "seq", axis=0, tiled=True),
        lax.all_gather(w_mlp_up, "seq", axis=0, tiled=True),
        lax.all_gather(w_mlp_down, "seq", axis=0, tiled=True),
    )
    gain_first = gathered[0].astype(jnp.float32)
    conv_taps = gathered[3].astype(jnp.float32)
    conv_bias = gathered[4].astype(jnp.float32)
    lam_value = gathered[9].astype(jnp.float32)
    gain_second = gathered[11].astype(jnp.float32)
    tokens = inputs[0].astype(jnp.float32)
    local_len = tokens.shape[0]
    channels = gathered[2].shape[1]
    block_size = gathered[5].shape[1]
    kernel_taps = conv_taps.shape[0]
    lengths = row_lengths[0]
    row_ends = jnp.cumsum(lengths)
    row_starts = row_ends - lengths
    positions = lax.axis_index("seq") * local_len + jnp.arange(local_len, dtype=jnp.int32)
    started = positions[:, None] >= row_starts[None, :]
    row_index = jnp.sum(started.astype(jnp.int32), axis=1) - 1
    row_first = jnp.max(jnp.where(started, row_starts[None, :], 0), axis=1)
    offset = positions - row_first
    restart = (offset == 0).astype(jnp.float32)
    members = (row_index[:, None] == jnp.arange(lengths.shape[0], dtype=jnp.int32)[None, :]).astype(
        jnp.float32
    )
    tap_masks = [(offset >= tap).astype(jnp.float32)[:, None] for tap in range(kernel_taps)]
    scaled, norm_pull = jax.vjp(rms_scale, tokens)
    normed = (scaled * gain_first).astype(jnp.bfloat16)
    gate_pre = jnp.dot(normed, gathered[1], preferred_element_type=jnp.float32)
    gate_branch, gate_pull = jax.vjp(gelu_tanh, gate_pre)
    inner = jnp.dot(normed, gathered[2], preferred_element_type=jnp.float32).astype(jnp.bfloat16)
    edge_rows = shifted(inner[local_len - kernel_taps + 1 :], "seq", 1)
    extended = jnp.concatenate([edge_rows, inner], axis=0).astype(jnp.float32)
    conv_sum = conv_bias + jnp.zeros((local_len, channels), jnp.float32)
    for tap in range(kernel_taps):
        start_row = kernel_taps - 1 - tap
        conv_sum = (
            conv_sum + conv_taps[tap] * extended[start_row : start_row + local_len] * tap_masks[tap]
        )
    conv_low = conv_sum.astype(jnp.bfloat16)
    conv_value = conv_low.astype(jnp.float32)
    r_pre = block_product(conv_low, gathered[5]) + gathered[6].astype(jnp.float32)
    i_pre = block_product(conv_low, gathered[7]) + gathered[8].astype(jnp.float32)

    def local_terms(conv_in, r_in, i_in, lam_in):
        return recurrence_terms(conv_in, r_in, i_in, lam_in, restart)

    (carried, drive_term, decays), recur_pull = jax.vjp(
        local_terms, conv_value, r_pre, i_pre, lam_value
    )
    prefix_decay, local_state = lax.associative_scan(link, (carried, drive_term), axis=0)
    identity = (jnp.ones((channels,), jnp.float32), jnp.zeros((channels,), jnp.float32))
    incoming = entering((prefix_decay[-1], local_state[-1]), "seq", link, identity, False)[1]
    states = local_state + prefix_decay * incoming
    mixed_low = (states * gate_branch).astype(jnp.bfloat16)
    residual = tokens + jnp.dot(mixed_low, gathered[10], preferred_element_type=jnp.float32)
    scaled_two, norm_pull_two = jax.vjp(rms_scale, residual)
    normed_two = (scaled_two * gain_second).astype(jnp.bfloat16)
    up_gate = jnp.dot(normed_two, gathered[12], preferred_element_type=jnp.float32)
    up_lin = jnp.dot(normed_two, gathered[13], preferred_element_type=jnp.float32)
    gelu_up, up_pull = jax.vjp(gelu_tanh, up_gate)
    hidden = (gelu_up * up_lin).astype(jnp.bfloat16)
    block_out = (
        residual + jnp.dot(hidden, gathered[14], preferred_element_type=jnp.float32)
    ).astype(jnp.bfloat16)
    row_sums = lax.psum(jnp.dot(members.T, decays, precision=lax.Precision.HIGHEST), "seq")
    gate_mean = row_sums / lengths.astype(jnp.float32)[:, None]
    grad_top = out_grad[0]
    grad_mdown = jnp.einsum("tf,td->fd", hidden, grad_top, preferred_element_type=jnp.float32)
    d_hidden = jnp.einsum("td,fd->tf", grad_top, gathered[14], preferred_element_type=jnp.float32)
    d_upgate = up_pull(d_hidden * up_lin)[0].astype(jnp.bfloat16)
    d_uplin = (d_hidden * gelu_up).astype(jnp.bfloat16)
    grad_mgate = jnp.einsum("td,tf->df", normed_two, d_upgate, preferred_element_type=jnp.float32)
    grad_mup = jnp.einsum("td,tf->df", normed_two, d_uplin, preferred_element_type=jnp.float32)
    d_normed_two = jnp.einsum(
        "tf,df->td", d_upgate, gathered[12], preferred_element_type=jnp.float32
    )
    d_normed_two = d_normed_two + jnp.einsum(
        "tf,df->td", d_uplin, gathered[13], preferred_element_type=jnp.float32
    )
    grad_mgain = jnp.sum(d_normed_two * scaled_two, axis=0)
    d_residual = grad_top.astype(jnp.float32) + norm_pull_two(d_normed_two * gain_second)[0]
    d_outlow = d_residual.astype(jnp.bfloat16)
    grad_outw = jnp.einsum("tr,td->rd", mixed_low, d_outlow, preferred_element_type=jnp.float32)
    d_mixed = jnp.einsum("td,rd->tr", d_outlow, gathered[10], preferred_element_type=jnp.float32)
    direct = d_mixed * gate_branch
    d_gatelow = gate_pull(d_mixed * states)[0].astype(jnp.bfloat16)
    grad_gatew = jnp.einsum("td,tr->dr", normed, d_gatelow, preferred_element_type=jnp.float32)
    next_decay = jnp.concatenate([carried[1:], jnp.ones((1, channels), jnp.float32)], axis=0)
    suffix_decay, local_grad = lax.associative_scan(
        link, (next_decay, direct), axis=0, reverse=True
    )
    arriving = entering(
        (carried[0] * suffix_decay[0], carried[0] * local_grad[0]), "seq", link, identity, True
    )[1]
    d_states = local_grad + suffix_decay * arriving
    previous = jnp.concatenate([incoming[None, :], states[:-1]], axis=0)
    grad_convval, d_rpre, d_ipre, grad_lambda = recur_pull(
        (d_states * previous, d_states, jnp.zeros_like(decays))
    )
    d_rlow = d_rpre.astype(jnp.bfloat16)
    d_ilow = d_ipre.astype(jnp.bfloat16)
    grad_rw = block_weight_grad(conv_low, d_rlow, block_size)
    grad_rb = jnp.sum(d_rlow.astype(jnp.float32), axis=0)
    grad_iw = block_weight_grad(conv_low, d_ilow, block_size)
    grad_ib = jnp.sum(d_ilow.astype(jnp.float32), axis=0)
    grad_convsum = grad_convval + block_back(d_rlow, gathered[5]) + block_back(d_ilow, gathered[7])
    grad_cb = jnp.sum(grad_convsum, axis=0)
    conv_again = gathered[3].astype(jnp.float32)
    grad_extended = jnp.zeros((local_len + kernel_taps - 1, channels), jnp.float32)
    tap_grads = []
    for tap in range(kernel_taps):
        start_row = kernel_taps - 1 - tap
        masked = grad_convsum * tap_masks[tap]
        tap_grads.append(jnp.sum(masked * extended[start_row : start_row + local_len], axis=0))
        grad_extended = grad_extended + jnp.pad(
            masked * conv_again[tap], ((start_row, tap), (0, 0))
        )
    grad_cw = jnp.stack(tap_grads)
    edge_grads = shifted(grad_extended[: kernel_taps - 1], "seq", -1)
    d_inner = (
        grad_extended[kernel_taps - 1 :]
        + jnp.pad(edge_grads, ((local_len - kernel_taps + 1, 0), (0, 0)))
    ).astype(jnp.bfloat16)
    grad_inw = jnp.einsum("td,tr->dr", normed, d_inner, preferred_element_type=jnp.float32)
    d_normed = jnp.einsum("tr,dr->td", d_gatelow, gathered[1], preferred_element_type=jnp.float32)
    d_normed = d_normed + jnp.einsum(
        "tr,dr->td", d_inner, gathered[2], preferred_element_type=jnp.float32
    )
    grad_gain = jnp.sum(d_normed * scaled, axis=0)
    d_tokens = d_residual + norm_pull(d_normed * gain_first)[0]
    shares = (
        lax.psum_scatter(grad_gain, "seq", scatter_dimension=0, tiled=True),
        lax.psum_scatter(grad_gatew, "seq", scatter_dimension=0, tiled=True),
        lax.psum_scatter(grad_inw, "seq", scatter_dimension=0, tiled=True),
        lax.psum_scatter(grad_cw, "seq", scatter_dimension=1, tiled=True),
        lax.psum_scatter(grad_cb, "seq", scatter_dimension=0, tiled=True),
        lax.psum_scatter(grad_rw, "seq", scatter_dimension=0, tiled=True),
        lax.psum_scatter(grad_rb, "seq", scatter_dimension=0, tiled=True),
        lax.psum_scatter(grad_iw, "seq", scatter_dimension=0, tiled=True),
        lax.psum_scatter(grad_ib, "seq", scatter_dimension=0, tiled=True),
        lax.psum_scatter(grad_lambda, "seq", scatter_dimension=0, tiled=True),
        lax.psum_scatter(grad_outw, "seq", scatter_dimension=0, tiled=True),
        lax.psum_scatter(grad_mgain, "seq", scatter_dimension=0, tiled=True),
        lax.psum_scatter(grad_mgate, "seq", scatter_dimension=0, tiled=True),
        lax.psum_scatter(grad_mup, "seq", scatter_dimension=0, tiled=True),
        lax.psum_scatter(grad_mdown, "seq", scatter_dimension=0, tiled=True),
    )
    totals = (
        lax.psum(shares[0].astype(jnp.bfloat16), "batch").astype(jnp.float32),
        lax.psum(shares[1].astype(jnp.bfloat16), "batch").astype(jnp.float32),
        lax.psum(shares[2].astype(jnp.bfloat16), "batch").astype(jnp.float32),
        lax.psum(shares[3].astype(jnp.bfloat16), "batch").astype(jnp.float32),
        lax.psum(shares[4].astype(jnp.bfloat16), "batch").astype(jnp.float32),
        lax.psum(shares[5].astype(jnp.bfloat16), "batch").astype(jnp.float32),
        lax.psum(shares[6].astype(jnp.bfloat16), "batch").astype(jnp.float32),
        lax.psum(shares[7].astype(jnp.bfloat16), "batch").astype(jnp.float32),
        lax.psum(shares[8].astype(jnp.bfloat16), "batch").astype(jnp.float32),
        lax.psum(shares[9].astype(jnp.bfloat16), "batch").astype(jnp.float32),
        lax.psum(shares[10].astype(jnp.bfloat16), "batch").astype(jnp.float32),
        lax.psum(shares[11].astype(jnp.bfloat16), "batch").astype(jnp.float32),
        lax.psum(shares[12].astype(jnp.bfloat16), "batch").astype(jnp.float32),
        lax.psum(shares[13].astype(jnp.bfloat16), "batch").astype(jnp.float32),
        lax.psum(shares[14].astype(jnp.bfloat16), "batch").astype(jnp.float32),
    )
    return (
        block_out[None],
        d_tokens[None],
        totals[0],
        totals[1],
        totals[2],
        totals[3],
        totals[4],
        totals[5],
        totals[6],
        totals[7],
        totals[8],
        totals[9],
        totals[10],
        totals[11],
        totals[12],
        totals[13],
        totals[14],
        gate_mean[None],
    )


def planes(
    inputs,
    out_grad,
    row_lengths,
    norm_gain,
    w_gate,
    w_in,
    conv_w,
    conv_b,
    w_rgate,
    b_rgate,
    w_igate,
    b_igate,
    lam,
    w_out,
    mlp_gain,
    w_mlp_gate,
    w_mlp_up,
    w_mlp_down,
):
    vmem = pltpu.VMEM
    done = kernel_call(
        layer,
        dict(
            x=inputs[0], cw=conv_w, cb=conv_b, br=b_rgate, bi=b_igate, lam=lam, ngain=norm_gain, mgain=mlp_gain,
            lens=row_lengths, g=out_grad[0], wg=w_gate, wi=w_in, wr=w_rgate, wv=w_igate, wout=w_out,
            wmg=w_mlp_gate, wmu=w_mlp_up, wmd=w_mlp_down,
        ),
        dict(
            block_out=array(256, 1024, dtype=BF),
            d_in=array(256, 1024),
            fm=array(4, 256, 768, dtype=BF),
            fm_x=array(4, 128, 768, dtype=BF),
            fd=array(4, 96, 1024, dtype=BF),
            fa=array(4, 256, 256, dtype=BF),
            fa_x=array(4, 128, 256, dtype=BF),
            fb=array(4, 128, 256, dtype=BF),
            fo=array(4, 48, 1280, dtype=BF),
            fr=array(8, 2, 8, 128),
            vec_out=array(8, 256),
            gain_out=array(8, 128),
            normed_far=array(8, 256, 1024, dtype=BF),
        ),
        dict(
            x_all=vmem((8, 256, 1024), BF),
            normed=vmem((8, 256, 1024), BF),
            g_all=vmem((8, 256, 1024), BF),
            small_rows=vmem((16, 256), F32),
            small=vmem((16, 256), BF),
            small_all=vmem((8, 16, 256), BF),
            lens_out=vmem((8, 128), F32),
            lens_all=vmem((4, 8, 128), F32),
            off=vmem((4, 520, 128), F32),
            starts_all=vmem((4, 8, 128), F32),
            chan=vmem((2, 16, 128), F32),
            gain=vmem((8, 1024), F32),
            wgi3=vmem((4, 256, 768), BF),
            w2=vmem((1024, 512), BF),
            gq=vmem((4, 48, 256), BF),
            g3=vmem((2, 192, 256), BF),
            wq=vmem((4, 48, 1024), BF),
            wri=vmem((2, 128, 256), BF),
            w3=vmem((2, 192, 1024), BF),
            wo=vmem((256, 1024), BF),
            wgu_out=vmem((2, 256, 384), BF),
            wgu_all=vmem((8, 256, 384), BF),
            wmd_all=vmem((4, 96, 1024), BF),
            gp=vmem((8, 512, 128), F32),
            gb=vmem((8, 520, 128), F32),
            inner=vmem((8, 520, 128), F32),
            conv=vmem((8, 512, 128), BF),
            sr=vmem((8, 512, 128), F32),
            si=vmem((8, 512, 128), F32),
            dec=vmem((8, 512, 128), F32),
            drv=vmem((8, 512, 128), F32),
            states=vmem((8, 520, 128), F32),
            mixed=vmem((8, 256, 256), BF),
            tot=vmem((2, 4, 2, 8, 128), F32),
            inc=vmem((8, 128), F32),
            rs_all=vmem((4, 8, 8, 128), F32),
            rows_sum=vmem((8, 8, 128), F32),
            residual=vmem((256, 1024), F32),
            d_res=vmem((256, 1024), F32),
            hid=vmem((8, 256, 384), BF),
            dgu=vmem((8, 256, 768), BF),
            gm=vmem((4, 256, 768), BF),
            gm_sum=vmem((256, 768), BF),
            gd=vmem((4, 96, 1024), BF),
            gd_in=vmem((3, 96, 1024), BF),
            gd_sum=vmem((96, 1024), BF),
            go=vmem((256, 1280), BF),
            go_q=vmem((4, 48, 1280), BF),
            go_l=vmem((3, 48, 1280), BF),
            go_sum=vmem((48, 1280), BF),
            ga_sum=vmem((256, 256), BF),
            gb2_sum=vmem((128, 256), BF),
            gain2_sum=vmem((8, 1024), F32),
            vec=vmem((2, 8, 8, 128), F32),
            vsum=vmem((4, 8, 256), F32),
            vout=vmem((4, 8, 256), F32),
            gsum=vmem((8, 8, 128), F32),
            gline=vmem((8, 8, 128), F32),
            gplane=vmem((4, 8, 128), F32),
            free=pltpu.SemaphoreType.REGULAR,
            **reduce_scratch(256, 1024),
        ),
        176,
        36,
        (
            "g", "wg", "wi", "wr", "wv", "wout", "wmg", "wmu", "wmd", "d_in", "block_out", "fm", "fm_x", "fd", "fa", "fa_x", "fb", "fo",
            "fr", "normed_far",
        ),
    )
    out = kernel_call(
        assemble,
        dict(
            {name: done[name] for name in ("d_in", "block_out", "fm", "fm_x", "fd", "fa", "fa_x", "fb", "fo", "fr")},
            vec_in=done["vec_out"], gains=done["gain_out"], lens=row_lengths,
        ),
        dict(
            o_din=array(256, 1024),
            o_block=array(256, 1024, dtype=BF),
            o_gate=array(128, 1536),
            o_in=array(128, 1536),
            o_mgate=array(128, 3072),
            o_mup=array(128, 3072),
            o_mdown=array(384, 1024),
            o_out=array(192, 1024),
            o_r=array(192, 128),
            o_i=array(192, 128),
            o_cw=array(4, 192),
            o_cb=array(1, 192),
            o_rb=array(1, 192),
            o_ib=array(1, 192),
            o_lam=array(1, 192),
            o_ngain=array(1, 128),
            o_mgain=array(1, 128),
            o_mean=array(5, 1, 1536),
        ),
        dict(
            v_din=vmem((256, 1024), F32),
            v_block=vmem((256, 1024), BF),
            vm=vmem((2, 4, 128, 768), BF),
            va=vmem((2, 4, 128, 256), BF),
            vb=vmem((4, 128, 256), BF),
            vd=vmem((4, 96, 1024), BF),
            vo=vmem((4, 48, 1280), BF),
            s_mgate=vmem((128, 3072), F32),
            s_mup=vmem((128, 3072), F32),
            s_gate=vmem((128, 1536), F32),
            s_in=vmem((128, 1536), F32),
            s_down=vmem((384, 1024), F32),
            s_out=vmem((192, 1024), F32),
        ),
        0,
        23,
        (
            "d_in", "block_out", "fm", "fm_x", "fd", "fa", "fa_x", "fb", "fo", "o_din", "o_block", "o_gate", "o_in", "o_mgate", "o_mup",
            "o_mdown", "o_out",
        ),
    )
    return (
        out["o_block"][None],
        out["o_din"][None],
        out["o_ngain"][0],
        out["o_gate"],
        out["o_in"],
        out["o_cw"],
        out["o_cb"][0],
        out["o_r"],
        out["o_rb"][0],
        out["o_i"],
        out["o_ib"][0],
        out["o_lam"][0],
        out["o_out"],
        out["o_mgain"][0],
        out["o_mgate"],
        out["o_mup"],
        out["o_mdown"],
        jnp.transpose(out["o_mean"], (1, 0, 2)),
    )


def solution(mesh):
    in_specs = (
        P("batch", "seq", None),
        P("batch", "seq", None),
        P("batch", None),
        P("seq"),
        P("seq", None),
        P("seq", None),
        P(None, "seq"),
        P("seq"),
        P("seq", None),
        P("seq"),
        P("seq", None),
        P("seq"),
        P("seq"),
        P("seq", None),
        P("seq"),
        P("seq", None),
        P("seq", None),
        P("seq", None),
    )
    out_specs = (
        P("batch", "seq", None),
        P("batch", "seq", None),
        P("seq"),
        P("seq", None),
        P("seq", None),
        P(None, "seq"),
        P("seq"),
        P("seq", None),
        P("seq"),
        P("seq", None),
        P("seq"),
        P("seq"),
        P("seq", None),
        P("seq"),
        P("seq", None),
        P("seq", None),
        P("seq", None),
        P("batch", None, None),
    )
    in_planes = mesh.shape["batch"] == 4 and mesh.shape["seq"] == 8
    body = planes if in_planes else shards
    return jax.shard_map(body, mesh=mesh, in_specs=in_specs, out_specs=out_specs, check_vma=False)
```

```python
import functools
import types

import jax
import jax.numpy as jnp
from jax import lax
from jax.experimental import pallas as pl
from jax.experimental.pallas import tpu as pltpu
from jax.sharding import PartitionSpec as P

NORM_EPS = 1e-06
DECAY_SCALE = 8.0
BF = jnp.bfloat16
F32 = jnp.float32
GELU_SCALE = 0.7978845608028654
GELU_CUBE = 0.044715
TILE = 64
NN = (((1,), (0,)), ((), ()))
NT = (((1,), (1,)), ((), ()))
TN = (((0,), (0,)), ((), ()))


def dot(left, right, dims=NN):
    return lax.dot_general(left, right, dims, preferred_element_type=F32)


def loop(count, body):
    def step(i, carry):
        body(i)
        return carry

    lax.fori_loop(0, count, step, 0)


class Net:
    def __init__(self, r):
        self.send, self.recv, self.count = r.send, r.recv, 0
        self.here, self.here_count = r.local, 0
        self.pending = []
        self.p = lax.axis_index("batch")
        self.q = lax.axis_index("seq")
        self.z = lax.div(self.q, 2)
        self.c = lax.rem(self.q, 2)
        self.o = 1 - self.c
        p = self.p
        self.near = (p, p + 1 - 2 * lax.rem(p, 2), lax.rem(p + 2, 4), 3 - p)

    def plane(self, k, core):
        return {"batch": self.near[k], "seq": self.z * 2 + core}

    def line(self, z, core):
        return {"batch": self.p, "seq": z * 2 + core}

    def up(self, k):
        return lax.rem(self.z + k, 4)

    def down(self, k):
        return lax.rem(self.z + 4 - k, 4)

    def slot(self, k, core):
        return self.near[k] * 2 + core

    def greet(self):
        barrier = pltpu.get_barrier_semaphore()
        partners = [self.plane(k, core) for k in (1, 2, 3) for core in (0, 1)]
        partners += [self.line(self.up(k), core) for k in (1, 2, 3) for core in (0, 1)]
        partners += [self.line(self.z, self.o)]
        for partner in partners:
            pl.semaphore_signal(barrier, inc=1, device_id=partner, device_id_type=pl.DeviceIdType.MESH)
        pl.semaphore_wait(barrier, len(partners))

    def reserve(self, count):
        first = self.count
        self.count += count
        return first

    def describe(self, src, dst, device, send_at, recv_at):
        return pltpu.make_async_remote_copy(
            src_ref=src,
            dst_ref=dst,
            send_sem=self.send.at[send_at],
            recv_sem=self.recv.at[recv_at],
            device_id=device,
            device_id_type=pl.DeviceIdType.MESH,
        )

    def copy(self, src, dst, device, sent=None, at=None):
        at = self.reserve(1) if at is None else at
        made = self.describe(src, dst, device, at, at)
        made.start()
        (self.pending if sent is None else sent).append(made)
        return made

    def local(self, src, dst):
        made = pltpu.make_async_copy(src, dst, self.here.at[self.here_count])
        self.here_count += 1
        made.start()
        return made

    def drain(self):
        assert (self.count, self.here_count) == (self.send.shape[0], self.here.shape[0]), (self.count, self.here_count)
        for made in self.pending:
            made.wait_send()
        self.pending = []


class Gather:
    def __init__(self, net, own, everything, at=None):
        self.net, self.own, self.all = net, own, everything
        self.sent = []
        self.at = net.reserve(14) if at is None else at
        self.half = everything.shape[1] // 2
        self.x0, self.y1, self.x1, self.y0 = [], [], [], []

    def half_of(self, slot, h):
        return self.all.at[slot, pl.ds(h * self.half, self.half)]

    def send(self, src, dst, device, at):
        return self.net.copy(src, dst, device, self.sent, self.at + at)

    def start(self, part):
        net = self.net
        mine = net.slot(0, net.c)
        size = self.half // 2
        low, high = pl.ds(part * size, size), pl.ds(self.half + part * size, size)
        for made, rows, k, at in ((self.x0, low, 1, 0), (self.y1, high, 2, 2), (self.x1, high, 1, 4), (self.y0, low, 2, 6)):
            made.append(self.send(self.own.at[rows], self.all.at[mine, rows], net.plane(k, net.c), at + part))
        if part == 1:
            self.s = [self.send(self.own, self.all.at[mine], net.plane(0, net.o), 8)]

    def forward(self):
        net = self.net
        for made in self.x0:
            made.wait_recv()
        block = self.half_of(net.slot(1, net.c), 0)
        self.d0 = self.send(block, block, net.plane(2, net.c), 9)
        for made in self.y1:
            made.wait_recv()
        block = self.half_of(net.slot(2, net.c), 1)
        self.d1 = self.send(block, block, net.plane(1, net.c), 10)

    def across(self, k):
        net = self.net
        block = self.all.at[net.slot(k, net.c)]
        self.s.append(self.send(block, block, net.plane(0, net.o), 10 + k))

    def middle(self):
        for made in self.x1:
            made.wait_recv()
        self.across(1)
        for made in self.y0:
            made.wait_recv()
        self.across(2)

    def last(self):
        self.d0.wait_recv()
        self.d1.wait_recv()
        self.across(3)

    def sibling(self, k):
        self.s[k].wait_recv()

    def release(self):
        for made in self.sent:
            made.wait_send()
        self.sent = []


class Owners:
    def __init__(self, net, own, everything, extra=None, at=None):
        self.net, self.own, self.all, self.extra = net, own, everything, extra
        self.at = net.reserve(6 if extra is None else 10) if at is None else at
        self.half = everything.shape[1] // 2
        self.s = [None] * 4

    def part(self, k, h):
        return self.all.at[self.net.near[k], pl.ds(h * self.half, self.half)]

    def across(self, k, block):
        if self.extra is not None:
            net = self.net
            rows = pl.ds(pl.multiple_of(net.o * self.half, 16), self.half)
            self.s[k] = net.copy(block.at[rows], self.extra.at[net.near[k]], net.plane(0, net.o), None, self.at + 6 + k)

    def start(self):
        net = self.net
        low, high = self.own.at[pl.ds(0, self.half)], self.own.at[pl.ds(self.half, self.half)]
        self.x0 = net.copy(low, self.part(0, 0), net.plane(1, net.c), None, self.at + 0)
        self.y1 = net.copy(high, self.part(0, 1), net.plane(2, net.c), None, self.at + 1)
        self.x1 = net.copy(high, self.part(0, 1), net.plane(1, net.c), None, self.at + 2)
        self.y0 = net.copy(low, self.part(0, 0), net.plane(2, net.c), None, self.at + 3)
        self.across(0, self.own)
        self.kept = net.local(self.own, self.all.at[net.p])

    def forward(self):
        net = self.net
        self.x0.wait_recv()
        self.d0 = net.copy(self.part(1, 0), self.part(1, 0), net.plane(2, net.c), None, self.at + 4)
        self.y1.wait_recv()
        self.d1 = net.copy(self.part(2, 1), self.part(2, 1), net.plane(1, net.c), None, self.at + 5)

    def middle(self):
        self.x1.wait_recv()
        self.across(1, self.all.at[self.net.near[1]])
        self.y0.wait_recv()
        self.across(2, self.all.at[self.net.near[2]])

    def last(self):
        self.d0.wait_recv()
        self.d1.wait_recv()
        self.across(3, self.all.at[self.net.near[3]])

    def end(self):
        if self.extra is not None:
            for made in self.s:
                made.wait_recv()
        self.kept.wait()


class LineGather:
    def __init__(self, net, own, first, place):
        self.net, self.own, self.first, self.place = net, own, first, place
        self.at = net.reserve(4 * len(own))

    def made(self, k, j):
        net = self.net
        src, core = self.own[j]
        at = self.at + 4 * j + k - 1
        return net.describe(src, self.first(j), net.line(net.up(k), core), at, at)

    def handed(self, j):
        net = self.net
        far = 6 - 3 * net.z
        here = self.place(j, far)
        at = self.at + 4 * j
        return net.describe(here, here, net.line(3 - far, net.c), at + 3, at + 2 * net.z - 2)

    def direct(self, k, body):
        z = self.net.z
        if k == 2:
            body()
        else:
            pl.when(z != (0 if k == 3 else 3))(body)

    def start(self, k, items):
        def send():
            for j in items:
                self.made(k, j).start()

        self.direct(k, send)

    def inside(self, body):
        z = self.net.z
        pl.when((z == 1) | (z == 2))(body)

    def relay(self):
        @self.inside
        def _():
            for j in range(len(self.own)):
                self.made(2, j).wait_recv()
                self.handed(j).start()

    def end(self):
        z = self.net.z
        for k in (1, 3):
            for j in range(len(self.own)):
                self.made(k, j).wait_recv()

        @pl.when((z == 0) | (z == 3))
        def _():
            for j in range(len(self.own)):
                self.made(2, j).wait_recv()

    def drain(self):
        for k in (1, 2, 3):

            def wait(k=k):
                for j in range(len(self.own)):
                    self.made(k, j).wait_send()

            self.direct(k, wait)

        @self.inside
        def _():
            for j in range(len(self.own)):
                self.handed(j).wait_send()


class LineSum:
    def __init__(self, net, block, slot):
        self.net, self.block, self.slot = net, block, slot
        self.at = net.reserve(3)

    def made(self, k):
        net = self.net
        at = self.at + k - 1
        to = lax.rem(2 * net.z + 1, 5) if k == 2 else net.up(k)
        return net.describe(self.block(net.up(k)), self.slot(k), net.line(to, net.c), at, at)

    def start(self):
        z = self.net.z
        self.made(2).start()
        pl.when(z != 1)(lambda: self.made(1).start())
        pl.when(z != 2)(lambda: self.made(3).start())

    def relay(self, step=16):
        z = self.net.z

        @pl.when((z == 1) | (z == 2))
        def _():
            self.made(2).wait_recv()
            mine, extra = self.block(3 - z), self.slot(2)

            def body(i):
                rows = pl.ds(pl.multiple_of(i * step, step), step)
                mine[rows, :] = (mine[rows, :].astype(F32) + extra[rows, :].astype(F32)).astype(BF)

            loop(mine.shape[0] // step, body)

        pl.when(z == 1)(lambda: self.made(1).start())
        pl.when(z == 2)(lambda: self.made(3).start())

    def end(self, dst, step=16):
        z = self.net.z
        self.made(1).wait_recv()
        self.made(3).wait_recv()
        edge = (z == 0) | (z == 3)
        pl.when(edge)(lambda: self.made(2).wait_recv())
        share = jnp.where(edge, 1.0, 0.0)
        own = self.block(z)

        def body(i):
            rows = pl.ds(pl.multiple_of(i * step, step), step)
            value = own[rows, :].astype(F32) + share * self.slot(2)[rows, :].astype(F32)
            value = value + self.slot(1)[rows, :].astype(F32) + self.slot(3)[rows, :].astype(F32)
            dst[rows, :] = value.astype(BF)

        loop(dst.shape[0] // step, body)

    def drain(self):
        for k in (1, 2, 3):
            self.made(k).wait_send()


class Reduce:
    def __init__(self, net, r, value, at=None):
        self.net, self.value = net, value
        self.at = net.reserve(12) if at is None else at
        self.keep, self.out, self.into = r.rs_keep, r.rs_out, r.rs_in
        self.xs, self.ys, self.xr, self.yr = r.rs_xs, r.rs_ys, r.rs_xr, r.rs_yr
        self.half = self.keep.shape[1]
        self.cross = [None] * 4
        self.sent = []

    def other(self, k):
        net = self.net
        self.out[k] = self.value(k, net.o).astype(BF)
        self.cross[k] = net.copy(self.out.at[k], self.into.at[k], net.plane(0, net.o), self.sent, self.at + k)

    def mine(self, k):
        self.cross[k].wait_recv()
        value = self.value(k, self.net.c) + self.into[k].astype(F32)
        return value[: self.half], value[self.half :]

    def send(self, src, dst, j, k, part=None):
        net = self.net
        at = self.at + 4 + j + (part or 0) + (0 if src is self.xs else 4)
        src, dst = src.at[j], dst.at[j]
        if part is not None:
            rows = pl.ds(part * self.half // 2, self.half // 2)
            src, dst = src.at[rows], dst.at[rows]
        return net.copy(src, dst, net.plane(k, net.c), self.sent, at)

    def far(self):
        low, high = self.mine(3)
        self.xs[0] = low.astype(BF)
        self.x0 = self.send(self.xs, self.xr, 0, 1)
        self.ys[0] = high.astype(BF)
        self.y0 = self.send(self.ys, self.yr, 0, 2)

    def near(self):
        low, high = self.mine(1)
        self.xs[1] = low.astype(BF)
        self.x1 = self.send(self.xs, self.xr, 1, 1)
        self.keep[2] = high
        low, high = self.mine(2)
        self.ys[1] = high.astype(BF)
        self.y1 = self.send(self.ys, self.yr, 1, 2)
        self.keep[3] = low

    def relay(self):
        size = self.half // 2
        self.x2, self.y2 = [], []
        for part in (0, 1):
            rows = slice(part * size, (part + 1) * size)
            if part == 0:
                self.x0.wait_recv()
            self.ys[2, rows, :] = (self.keep[3, rows, :] + self.xr[0, rows, :].astype(F32)).astype(BF)
            self.y2.append(self.send(self.ys, self.yr, 2, 2, part))
            if part == 0:
                self.y0.wait_recv()
            self.xs[2, rows, :] = (self.keep[2, rows, :] + self.yr[0, rows, :].astype(F32)).astype(BF)
            self.x2.append(self.send(self.xs, self.xr, 2, 1, part))

    def own(self):
        self.keep[0], self.keep[1] = self.mine(0)

    def finish(self, part):
        if part == 0:
            self.x1.wait_recv()
            self.y1.wait_recv()
        self.x2[part].wait_recv()
        self.y2[part].wait_recv()
        if part == 1:
            for made in self.sent:
                made.wait_send()
            self.sent = []

    def total(self, h, i, step):
        rows = pl.ds(pl.multiple_of(i * step, step), step)
        first, second = (self.xr, self.yr) if h == 0 else (self.yr, self.xr)
        return self.keep[h, rows, :] + first[1, rows, :].astype(F32) + second[2, rows, :].astype(F32)


def reduce_scratch(rows, width):
    half = rows // 2
    return dict(
        rs_keep=pltpu.VMEM((4, half, width), F32),
        rs_out=pltpu.VMEM((4, rows, width), BF),
        rs_in=pltpu.VMEM((4, rows, width), BF),
        rs_xs=pltpu.VMEM((3, half, width), BF),
        rs_ys=pltpu.VMEM((3, half, width), BF),
        rs_xr=pltpu.VMEM((3, half, width), BF),
        rs_yr=pltpu.VMEM((3, half, width), BF),
    )


def kernel_call(body, ins, outs, scratch, copies, local, far):
    names = list(ins) + list(outs) + list(scratch)
    near = pl.BlockSpec(memory_space=pltpu.VMEM)
    away = pl.BlockSpec(memory_space=pl.ANY)
    shapes = list(scratch.values())
    if copies:
        names += ["send", "recv"]
        shapes += [pltpu.SemaphoreType.DMA((copies,))] * 2
    if local:
        names.append("local")
        shapes.append(pltpu.SemaphoreType.DMA((local,)))

    def kernel(*refs):
        body(types.SimpleNamespace(**dict(zip(names, refs))))

    params = dict(vmem_limit_bytes=62 * 2**20)
    if copies:
        params.update(collective_id=0, has_side_effects=True)
    results = pl.pallas_call(
        kernel,
        out_shape=list(outs.values()),
        in_specs=[away if name in far else near for name in ins],
        out_specs=[away if name in far else near for name in outs],
        scratch_shapes=shapes,
        compiler_params=pltpu.CompilerParams(**params),
        name=body.__name__,
    )(*ins.values())
    return dict(zip(outs, results))


def array(*shape, dtype=F32):
    return jax.ShapeDtypeStruct(shape, dtype)


def gelu_parts(v):
    square = v * v
    t = jnp.tanh(GELU_SCALE * v * (1.0 + GELU_CUBE * square))
    half = 0.5 + 0.5 * t
    slope = half + 0.5 * v * (1.0 - t * t) * (GELU_SCALE * (1.0 + 3.0 * GELU_CUBE * square))
    return v * half, slope


def decay_parts(sr, rate):
    log_a = -DECAY_SCALE * sr * rate
    a = jnp.exp(log_a)
    y = 2.0 * log_a
    series = 1.0 + y * (1 / 6) * (1.0 + y * (1 / 7))
    for n in (5, 4, 3, 2):
        series = 1.0 + y * (1 / n) * series
    m2 = jnp.where(y > -0.35, -y * series, 1.0 - a * a)
    return a, jnp.maximum(m2, 1e-36)


def column_sum(value):
    return jnp.sum(value.reshape(-1, 8, 128), axis=0)


def scan_slabs(decay, value, reverse):
    count = decay.shape[1] // 8
    row = lax.broadcasted_iota(jnp.int32, (8, 128), 0)

    def step(i, carry):
        t = count - 1 - i if reverse else i
        at = pl.ds(pl.multiple_of(t * 8, 8), 8)
        done = []
        for s in range(8):
            pc, vc = carry[s]
            p, own = decay[s, at, :], value[s, at, :]
            v = p * own if reverse else own
            for d in (1, 2, 4):
                by = 8 - d if reverse else d
                inside = row < 8 - d if reverse else row >= d
                v = v + p * jnp.where(inside, pltpu.roll(v, by, 0), 0.0)
                p = p * jnp.where(inside, pltpu.roll(p, by, 0), 1.0)
            v = v + p * vc
            p = p * pc
            if reverse:
                edge = row == 7
                value[s, at, :] = own + jnp.where(edge, vc, pltpu.roll(v, 7, 0))
                decay[s, at, :] = jnp.where(edge, pc, pltpu.roll(p, 7, 0))
                last = slice(0, 1)
            else:
                value[s, at, :] = v
                decay[s, at, :] = p
                last = slice(7, 8)
            done.append((jnp.broadcast_to(p[last], (8, 128)), jnp.broadcast_to(v[last], (8, 128))))
        return tuple(done)

    start = tuple((jnp.ones((8, 128), F32), jnp.zeros((8, 128), F32)) for _ in range(8))
    return lax.fori_loop(0, count, step, start)


def exchange_ends(r, net, ends, at):
    for s in range(8):
        r.tot[at, net.z, 0, s : s + 1, :] = ends[s][0][0:1, :]
        r.tot[at, net.z, 1, s : s + 1, :] = ends[s][1][0:1, :]
    mine = r.tot.at[at, net.z]
    return [net.copy(mine, mine, net.line(net.up(k), net.c)) for k in (1, 2, 3)]


def entering_states(r, net, copies, at, reverse):
    for made in copies:
        made.wait_recv()
    state = jnp.zeros((8, 128), F32)
    for i in range(4):
        z = 3 - i if reverse else i
        new = r.tot[at, z, 0] * state + r.tot[at, z, 1]
        state = jnp.where((z > net.z) if reverse else (z < net.z), new, state)
    r.inc[...] = state


def tile_rows(i):
    return pl.ds(pl.multiple_of(i * TILE, TILE), TILE)


def layer(r):
    r.do_all = r.x_all
    r.dconv = r.gb
    r.dgi = r.dgu
    r.ug, r.ul = r.d_res.at[:, 0:384], r.d_res.at[:, 384:768]
    r.ga = [r.hid.at[i, :, 0:256] for i in range(4)]
    r.gb2 = [r.hid.at[4 + i, 0:128, 0:256] for i in range(4)]
    net = Net(r)
    p, z, c, o, q = net.p, net.z, net.c, net.o, net.q
    sibling = net.plane(0, o)
    mine = net.slot(0, c)
    cols = r.wgu_out.shape[2]
    piece = cols // 4
    down = pl.ds(pl.multiple_of(p * piece, 16), piece)
    quarter = pl.ds(pl.multiple_of(p * 48, 16), 48)
    staged = []
    for j in range(8):
        lanes = pl.ds(j * cols, cols)
        staged.append(net.local(r.wmg.at[:, lanes], r.hid.at[j, pl.ds(0, 128)]))
        staged.append(net.local(r.wmu.at[:, lanes], r.hid.at[j, pl.ds(128, 128)]))
    width = 3 * 128
    first = pl.multiple_of(p * width, 128)
    chip = pl.ds(first, width)
    own_lanes = pl.ds(pl.multiple_of(c * width, 128), width)
    wi_rows, wg_rows = pl.ds(128, 128), pl.ds(0, 128)
    placed = [
        net.local(r.wg.at[:, chip], r.wgi3.at[z, wg_rows, own_lanes]),
        net.local(r.wi.at[:, chip], r.wgi3.at[z, wi_rows, own_lanes]),
        net.local(r.wmd.at[down], r.wmd_all.at[z]),
        net.local(r.wout.at[quarter], r.wq.at[z]),
        net.local(r.wr.at[quarter], r.gq.at[z, :, pl.ds(0, 128)]),
        net.local(r.wv.at[quarter], r.gq.at[z, :, pl.ds(128, 128)]),
        net.local(r.g, r.g_all.at[mine]),
    ]
    r.lens_out[0:1, 0:5] = r.lens[...].astype(F32)
    r.small_rows[...] = jnp.zeros((16, 256), F32)
    r.small_rows[0:4, 0:192] = r.cw[...].astype(F32)
    for at, ref in ((4, r.cb), (5, r.br), (6, r.bi), (7, r.lam)):
        r.small_rows[at : at + 1, 0:192] = ref[...].astype(F32).reshape(1, 192)
    for at, ref in ((0, r.ngain), (128, r.mgain)):
        r.small_rows[10:11, at : at + 128] = ref[...].astype(F32).reshape(1, 128)
    r.small[...] = r.small_rows[...].astype(BF)
    net.greet()
    r.small_all[q] = r.small[...]
    r.lens_all[p] = r.lens_out[...]
    small = [net.copy(r.small, r.small_all.at[q], net.line(net.up(k), core)) for k in (1, 2, 3) for core in (c, o)]
    small.append(net.copy(r.small, r.small_all.at[q], sibling))
    lens = [net.copy(r.lens_out, r.lens_all.at[p], net.plane(k, c)) for k in (1, 2, 3)]
    tokens = Gather(net, r.x, r.x_all)
    tokens.start(0)
    tokens.start(1)
    theirs = pl.ds(pl.multiple_of(c * width + o * 128, 128), 256)

    def along(place):
        made = LineGather(net, [(place(z), c)], lambda j: place(z), lambda j, at: place(at))
        for k in (2, 1, 3):
            made.start(k, (0,))
        return made

    handed = []

    def heads_start(rows):
        here = r.wgi3.at[z, rows, theirs]
        made = along(lambda at: r.wgi3.at[at, rows, own_lanes])
        return made, [net.copy(here, here, sibling, handed)]

    for made in placed:
        made.wait()
    heads_in, heads_in_over = heads_start(wi_rows)
    gates_in = along(lambda at: r.gq.at[at])

    def hand_over(arrivals, rows, over):
        arrivals.end()
        for k in (1, 2, 3):
            here = r.wgi3.at[net.down(k), rows, theirs]
            over.append(net.copy(here, here, sibling, handed))

    def arrange(over, rows, lanes):
        for made in over:
            made.wait_recv()
        for core in range(2):
            cols_in = pl.ds(pl.multiple_of(core * width + c * 128, 128), 256)
            for at in range(4):
                to = slice((at * 2 + core) * 128, (at * 2 + core + 1) * 128)
                r.w2[to, lanes] = r.wgi3[at, rows, cols_in]

    def exchange(arrivals, src, dst):
        arrivals.end()
        dst[c, quarter, :] = src[p]
        return [net.copy(src.at[net.near[k]], dst.at[c, quarter], net.plane(k, c)) for k in (1, 2, 3)]

    def share(copies, dst):
        for made in copies:
            made.wait_recv()
        return net.copy(dst.at[c], dst.at[c], sibling)

    selects = []
    k_at = lax.broadcasted_iota(jnp.int32, (cols, cols), 0)
    j_at = lax.broadcasted_iota(jnp.int32, (cols, cols), 1)
    for part in range(4):
        inside = (j_at >= part * piece) & (j_at < (part + 1) * piece)
        chosen = inside & (k_at == j_at + (p - part) * piece)
        selects.append(jnp.where(chosen, 1.0, 0.0).astype(BF))
    for made in staged:
        made.wait()
    for which in range(2):
        rows = slice(which * 128, (which + 1) * 128)
        for core in (0, 1):
            picked = None
            for part in range(4):
                term = dot(r.hid[part * 2 + core, rows, :], selects[part])
                picked = term if picked is None else picked + term
            r.wgu_out[core, rows, :] = picked.astype(BF)
    for made in small + lens:
        made.wait_recv()
    low, high = r.small_all[2 * p].astype(F32), r.small_all[2 * p + 1].astype(F32)
    at_first = jnp.concatenate([low[:, :192], high[:, :64]], axis=1)
    at_second = jnp.concatenate([low[:, 128:192], high[:, :192]], axis=1)
    both = lax.select(c == 0, at_first, at_second)
    for n in range(2):
        r.chan[n] = both[:, n * 128 : (n + 1) * 128]
        lam = -r.chan[n, 7:8, :]
        e = jnp.exp(-jnp.abs(lam))
        series = 1.0 - e * (6 / 7)
        for k in (6, 5, 4, 3, 2):
            series = 1.0 - e * ((k - 1) / k) * series
        rate = jnp.maximum(lam, 0.0) + jnp.where(e < 0.05, e * series, jnp.log(1.0 + e))
        r.chan[n, 7:8, :] = rate
        r.chan[n, 8:9, :] = jax.nn.sigmoid(lam)
    for i in range(8):
        gains = r.small_all[i].astype(F32)[10:11, :]
        r.gain[0:1, i * 128 : (i + 1) * 128] = gains[:, 0:128]
        r.gain[1:2, i * 128 : (i + 1) * 128] = gains[:, 128:256]
    gain = r.gain[0:1, :]
    for b in range(4):
        start = jnp.zeros((1, 128), F32)
        for row in range(5):
            r.starts_all[b, row : row + 1, :] = start
            start = start + jnp.broadcast_to(r.lens_all[b, 0:1, row : row + 1], (1, 128))


    def offset_rows(i):
        b, tile = lax.div(i, 13), lax.rem(i, 13)
        starts = r.starts_all[b]
        at = lax.convert_element_type(z * 512 + tile * 40, F32)
        at = at + lax.broadcasted_iota(jnp.int32, (40, 128), 0).astype(F32)
        begun = jnp.zeros((40, 128), F32)
        for row in range(1, 5):
            start = starts[row : row + 1, :]
            begun = jnp.where(at >= start, start, begun)
        r.off[b, pl.ds(pl.multiple_of(tile * 40, 8), 40), :] = at - begun

    loop(52, offset_rows)

    def normalise(slot):
        def body(i):
            rows = pl.ds(pl.multiple_of(i * 32, 32), 32)
            v = r.x_all[slot, rows, :].astype(F32)
            s = lax.rsqrt(jnp.mean(v * v, axis=-1, keepdims=True) + NORM_EPS)
            r.normed[slot, rows, :] = (v * s * gain).astype(BF)

        loop(8, body)

    r.x_all[mine] = r.x[...]
    normalise(mine)
    tokens.sibling(0)
    normalise(net.slot(0, o))
    tokens.forward()
    heads_in.relay()
    gates_in.relay()
    out_in = along(lambda at: r.wq.at[at])
    feed = LineGather(
        net,
        [(r.wgu_out.at[core], core) for core in (c, o)],
        lambda j: r.wgu_all.at[q],
        lambda j, at: r.wgu_all.at[at * 2 + (c, o)[j]],
    )
    feed_down = LineGather(net, [(r.wmd.at[down], c)], lambda j: r.wmd_all.at[z], lambda j, at: r.wmd_all.at[at])
    tokens.middle()
    for k in (1, 2):
        normalise(net.slot(k, c))
    hand_over(heads_in, wi_rows, heads_in_over)
    for k in (1, 2):
        tokens.sibling(k)
        normalise(net.slot(k, o))
    gates_out = exchange(gates_in, r.gq, r.g3)
    arrange(heads_in_over, slice(128, 256), slice(256, 512))

    def project_inner(slot):
        b, half = lax.div(slot, 2), lax.rem(slot, 2)
        at = pl.multiple_of(half * 256, 256)
        inner = dot(r.normed[slot], r.w2[:, 256:512]).astype(BF).astype(F32)
        for n in range(2):
            r.inner[b * 2 + n, pl.ds(at + 8, 256), :] = inner[:, n * 128 : (n + 1) * 128]

    def project_gate(slot):
        b, half = lax.div(slot, 2), lax.rem(slot, 2)
        at = pl.multiple_of(half * 256, 256)
        gate = dot(r.normed[slot], r.w2[:, 0:256])
        for n in range(2):
            r.gp[b * 2 + n, pl.ds(at, 256), :] = gate[:, n * 128 : (n + 1) * 128]

    out_in.relay()
    for k in (0, 1, 2):
        project_inner(net.slot(k, c))
        project_inner(net.slot(k, o))
    tokens.last()
    normalise(net.slot(3, c))
    project_inner(net.slot(3, c))
    tokens.sibling(3)
    normalise(net.slot(3, o))
    project_inner(net.slot(3, o))
    edge = net.reserve(1)

    def edge_copy():
        return net.describe(
            r.inner.at[:, pl.ds(512, 8)], r.inner.at[:, pl.ds(0, 8)], net.line(net.up(1), c), edge, edge
        )

    @pl.when(z < 3)
    def _():
        edge_copy().start()

    @pl.when(z == 0)
    def _():
        r.inner[:, 0:8, :] = jnp.zeros((8, 8, 128), F32)

    gates_over = share(gates_out, r.g3)
    stored = net.local(r.normed, r.normed_far)
    cots = Gather(net, r.g_all.at[mine], r.g_all)
    cots.start(0)
    cots.start(1)
    tokens.release()
    gates_over.wait_recv()
    for i in range(4):
        at = c * 128 + i * 64
        value = r.g3[lax.div(at, 192), pl.ds(pl.multiple_of(lax.rem(at, 192), 64), 64), :]
        r.wri[i // 2, (i % 2) * 64 : (i % 2 + 1) * 64, :] = value
    heads_gate, heads_gate_over = heads_start(wg_rows)

    @pl.when(z > 0)
    def _():
        edge_copy().wait_recv()


    def conv_tile(i):
        b, tile = lax.div(i, 8), lax.rem(i, 8)
        rows = tile_rows(tile)
        offset = r.off[b, rows, :]
        for n in range(2):
            s = b * 2 + n
            window = r.inner[s, pl.ds(pl.multiple_of(tile * TILE, 8), TILE + 8), :]
            chan = r.chan[n]
            total = chan[4:5, :] + chan[0:1, :] * window[8:, :]
            for k in (1, 2, 3):
                total = total + chan[k : k + 1, :] * jnp.where(offset >= k, window[8 - k : TILE + 8 - k, :], 0.0)
            r.conv[s, rows, :] = total.astype(BF)

    loop(32, conv_tile)
    out_rows_in = exchange(out_in, r.wq, r.w3)

    def gate_products(i):
        s, half = lax.div(i, 2), lax.rem(i, 2)
        n = lax.rem(s, 2)
        rows = pl.ds(pl.multiple_of(half * 256, 256), 256)
        pre = dot(r.conv[s, rows, :], r.wri[n])
        r.sr[s, rows, :] = pre[:, :128]
        r.si[s, rows, :] = pre[:, 128:]

    loop(16, gate_products)
    heads_gate.relay()
    feed.start(2, (0,))

    def terms(b):
        starts_b = r.starts_all[b]

        def tile(i, sums):
            rows = tile_rows(i)
            offset = r.off[b, rows, :]
            at = lax.convert_element_type(z * 512 + i * TILE, F32)
            begun = at + lax.broadcasted_iota(jnp.int32, (TILE, 128), 0).astype(F32) - offset
            restart = offset == 0.0
            added = []
            for n in range(2):
                s = b * 2 + n
                chan = r.chan[n]
                sr = jax.nn.sigmoid(r.sr[s, rows, :] + chan[5:6, :])
                si = jax.nn.sigmoid(r.si[s, rows, :] + chan[6:7, :])
                r.sr[s, rows, :] = sr
                r.si[s, rows, :] = si
                a, m2 = decay_parts(sr, chan[7:8, :])
                r.dec[s, rows, :] = jnp.where(restart, 0.0, a)
                m = jnp.where(restart, 1.0, m2 * lax.rsqrt(m2))
                r.drv[s, rows, :] = m * si * r.conv[s, rows, :].astype(F32)
                for row in range(5):
                    inside = jnp.where(begun == starts_b[row : row + 1, :], a, 0.0)
                    added.append(sums[n * 5 + row] + column_sum(inside))
            return tuple(added)

        sums = lax.fori_loop(0, 512 // TILE, tile, tuple(jnp.zeros((8, 128), F32) for _ in range(10)))
        for n in range(2):
            rows = [jnp.sum(part, axis=0, keepdims=True) for part in sums[n * 5 : n * 5 + 5]]
            r.rs_all[z, b * 2 + n] = jnp.concatenate(rows + [jnp.zeros((3, 128), F32)], axis=0)

    loop(4, terms)
    cots.forward()
    ends = scan_slabs(r.dec, r.drv, False)
    ends = exchange_ends(r, net, ends, 0)
    feed.start(2, (1,))
    feed.start(1, (0, 1))
    feed.start(3, (0, 1))
    r.wgu_all[q] = r.wgu_out[c]
    feed_over = net.copy(r.wgu_out.at[o], r.wgu_all.at[q], sibling)
    hand_over(heads_gate, wg_rows, heads_gate_over)
    arrange(heads_gate_over, slice(0, 128), slice(0, 256))
    for made in handed:
        made.wait_send()
    heads_in.drain()
    heads_gate.drain()
    for k in (2, 1, 3):
        feed_down.start(k, (0,))
    for slot in range(8):
        project_gate(slot)

    def gelu_tile(i):
        s, rows = lax.div(i, 8), tile_rows(lax.rem(i, 8))
        v = r.gp[s, rows, :]
        t = jnp.tanh(GELU_SCALE * v * (1.0 + GELU_CUBE * v * v))
        r.gb[s, rows, :] = 0.5 * v * (1.0 + t)

    loop(64, gelu_tile)
    out_over = share(out_rows_in, r.w3)
    entering_states(r, net, ends, 0, False)
    row_sums = [net.copy(r.rs_all.at[z], r.rs_all.at[z], net.line(net.up(k), c)) for k in (1, 2, 3)]
    out_over.wait_recv()

    def own_rows(i):
        at = c * 128 + i * 64
        value = r.w3[lax.div(at, 192), pl.ds(pl.multiple_of(lax.rem(at, 192), 64), 64), :]
        r.wo[pl.ds(pl.multiple_of(i * 64, 64), 64), :] = value

    loop(4, own_rows)
    for s in range(8):
        r.states[s, 7:8, :] = r.inc[s : s + 1, :]

    def mix_tile(i):
        s, tile = lax.div(i, 8), lax.rem(i, 8)
        b, n = lax.div(s, 2), lax.rem(s, 2)
        rows = tile_rows(tile)
        states = r.drv[s, rows, :] + r.dec[s, rows, :] * r.inc[pl.ds(s, 1), :]
        r.states[s, pl.ds(pl.multiple_of(tile * TILE + 8, 8), TILE), :] = states
        lanes = pl.ds(pl.multiple_of(n * 128, 128), 128)
        r.mixed[b * 2 + lax.div(tile, 4), tile_rows(lax.rem(tile, 4)), lanes] = (states * r.gb[s, rows, :]).astype(BF)

    loop(64, mix_tile)
    stored.wait()
    lane = lax.broadcasted_iota(jnp.int32, (1, 256), 1)
    counted = jnp.where((lane >= 64 * c) & (lane < 192 + 64 * c), 1.0, 0.0)
    counted_two = jnp.concatenate([counted, counted], axis=1)

    def masked(value, mask):
        return (value.astype(F32) * mask).astype(BF)

    total = Reduce(
        net, r, lambda k, core: dot(masked(r.mixed[net.slot(k, core)], counted), r.wo[...])
    )
    for k in (3, 1, 2, 0):
        total.other(k)
    total.far()
    total.near()
    cots.middle()
    total.own()
    cots.last()
    for k in (0, 1, 2, 3):
        cots.sibling(k)
    cots.release()
    total.relay()
    feed_down.relay()
    feed.relay()
    def wmd():
        return r.wmd_all[...].reshape(cols, -1)

    gain2 = r.gain[1:2, :]
    n2_all = r.normed
    acts = Gather(net, n2_all.at[mine], n2_all, tokens.at)
    for part in range(2):
        total.finish(part)
        for h in range(2):

            def residual_rows(i, h=h, part=part):
                i = part * 2 + i
                rows = pl.ds(pl.multiple_of(h * 128 + i * 32, 32), 32)
                v = r.x[rows, :].astype(F32) + total.total(h, i, 32)
                r.residual[rows, :] = v
                s = lax.rsqrt(jnp.mean(v * v, axis=-1, keepdims=True) + NORM_EPS)
                r.normed[mine, rows, :] = (v * s * gain2).astype(BF)

            loop(2, residual_rows)
        acts.start(part)

    def gate_up(which):
        return r.wgu_all[:, which * 128 : (which + 1) * 128, :].reshape(-1, cols)

    def d_normed2(k, core):
        slot = net.slot(k, core)
        return dot(r.dgu[slot, :, 0:cols], gate_up(0), NT) + dot(r.dgu[slot, :, cols:], gate_up(1), NT)

    back = Reduce(net, r, d_normed2, total.at)

    def part(k, core):
        slot = net.slot(k, core)
        h = n2_all[slot]
        r.ug[...] = dot(h, gate_up(0))
        r.ul[...] = dot(h, gate_up(1))

        def body(i):
            rows = pl.ds(pl.multiple_of(i * 32, 32), 32)
            gelu, slope = gelu_parts(r.ug[rows, :])
            ul, dh = r.ul[rows, :], r.dgu[slot, rows, 0:cols].astype(F32)
            r.hid[slot, rows, :] = (gelu * ul).astype(BF)
            r.dgu[slot, rows, 0:cols] = (dh * ul * slope).astype(BF)
            r.dgu[slot, rows, cols:] = (dh * gelu).astype(BF)

        loop(8, body)

    feed_down.end()
    for slot in range(8):
        r.dgu[slot, :, 0:cols] = dot(r.g_all[slot], wmd(), NT).astype(BF)
    feed_over.wait_recv()
    feed.end()
    part(0, c)
    acts.sibling(0)
    part(0, o)
    back.other(0)
    acts.forward()
    acts.middle()
    part(1, c)
    part(2, c)
    acts.sibling(1)
    part(1, o)
    back.other(1)
    acts.sibling(2)
    part(2, o)
    back.other(2)
    back.near()
    acts.last()
    acts.sibling(3)
    part(3, o)
    back.other(3)
    part(3, c)
    back.far()
    back.relay()
    back.own()
    acts.release()
    for i in range(4):
        rows = n2_all[:, :, i * 256 : (i + 1) * 256].reshape(-1, 256)
        r.gm[i] = dot(rows, r.dgu[...].reshape(-1, 2 * cols), TN).astype(BF)

    def gm_in(k):
        return r.wgi3.at[k - 1]

    mlp_m = LineSum(net, lambda t: r.gm.at[t], gm_in)
    mlp_m.start()
    hid = r.hid[...].reshape(-1, cols)
    for half in range(2):
        lanes = slice(half * 512, half * 512 + 512)
        value = dot(hid, r.g_all[:, :, lanes].reshape(-1, 512), TN).astype(BF)
        for i in range(4):
            r.gd[i, :, lanes] = value[i * piece : (i + 1) * piece, :]
    mlp_d = LineSum(net, lambda t: r.gd.at[t], lambda k: r.gd_in.at[k - 1])
    sums = jnp.zeros((8, r.x.shape[1]), F32)
    grads = Gather(net, r.do_all.at[mine], r.do_all, cots.at)
    for part in range(2):
        back.finish(part)
        for h in range(2):

            def residual_back(i, sums, h=h, part=part):
                i = part * 2 + i
                rows = pl.ds(pl.multiple_of(h * 128 + i * 32, 32), 32)
                v = r.residual[rows, :]
                dn = back.total(h, i, 32)
                s = lax.rsqrt(jnp.mean(v * v, axis=-1, keepdims=True) + NORM_EPS)
                u = dn * gain2
                pulled = s * u - v * (s * s * s * jnp.mean(u * v, axis=-1, keepdims=True))
                d_res = r.g_all[mine, rows, :].astype(F32) + pulled
                r.d_res[rows, :] = d_res
                r.do_all[mine, rows, :] = d_res.astype(BF)
                return sums + jnp.sum((dn * v * s).reshape(4, 8, -1), axis=0)

            sums = lax.fori_loop(0, 2, residual_back, sums)
        grads.start(part)
    r.gain2_sum[...] = sums

    owners, returned = [], []

    def to_chips(src, dst):
        for k in (1, 2, 3):
            owners.append(net.copy(src, dst.at[p], net.plane(k, c)))
        returned.append(net.local(src, dst.at[p]))

    fo_at = net.reserve(4)

    def vector_copy(k):
        return net.describe(r.vout.at[p], r.vout.at[p], net.plane(k, c), fo_at + k, fo_at)

    owners_m = Owners(net, r.gm_sum, r.fm, r.fm_x, tokens.at)
    owners_d = Owners(net, r.gd_sum, r.fd)
    owners_a = Owners(net, r.ga_sum, r.fa, r.fa_x, cots.at)
    owners_b = Owners(net, r.gb2_sum, r.fb)

    def mlp_sums():
        mlp_m.end(r.gm_sum)
        owners_m.start()

    def back_out(slot):
        b, half = lax.div(slot, 2), lax.rem(slot, 2)
        dm = dot(r.do_all[slot], r.wo[...], NT)
        for n in range(2):
            r.dconv[b * 2 + n, pl.ds(pl.multiple_of(half * 256, 256), 256), :] = dm[:, n * 128 : (n + 1) * 128]

    back_out(mine)
    grads.sibling(0)
    back_out(net.slot(0, o))
    out = Reduce(net, r, lambda k, core: dot(r.hid[net.slot(k, core)], wmd()), total.at)
    for k in (3, 1, 2, 0):
        out.other(k)
    grads.forward()
    out.far()
    out.near()
    out.own()
    grads.middle()
    mlp_m.relay()
    for k in (1, 2):
        back_out(net.slot(k, c))
    for k in (1, 2):
        grads.sibling(k)
        back_out(net.slot(k, o))
    grads.last()
    back_out(net.slot(3, c))
    grads.sibling(3)
    back_out(net.slot(3, o))

    def first_pass(i):
        b, tile = lax.div(i, 8), lax.rem(i, 8)
        rows = tile_rows(tile)
        live = r.off[b, rows, :] != 0.0
        for n in range(2):
            s = b * 2 + n
            gelu, slope = gelu_parts(r.gp[s, rows, :])
            dm = r.dconv[s, rows, :]
            states = r.states[s, pl.ds(pl.multiple_of(tile * TILE + 8, 8), TILE), :]
            lanes = slice(n * 128, (n + 1) * 128)
            r.dgi[b * 2 + lax.div(tile, 4), tile_rows(lax.rem(tile, 4)), lanes] = (dm * states * slope).astype(BF)
            r.drv[s, rows, :] = dm * gelu
            a = jnp.exp(-DECAY_SCALE * r.sr[s, rows, :] * r.chan[n, 7:8, :])
            r.dec[s, rows, :] = jnp.where(live, a, 0.0)

    loop(32, first_pass)
    ends = scan_slabs(r.dec, r.drv, True)
    ends = exchange_ends(r, net, ends, 1)
    out.relay()
    go_in, go_line_in = r.go_q, r.go_l
    mixed = r.mixed[...].reshape(-1, 256)
    for half in range(2):
        lanes = slice(half * 512, half * 512 + 512)
        r.go[:, lanes] = dot(mixed, r.do_all[:, :, lanes].reshape(-1, 512), TN).astype(BF)
    grads.release()
    fetched = net.local(r.normed_far, r.do_all)
    go_rows = [pl.ds(pl.multiple_of(c * 64 + near * 48, 16), 48) for near in net.near]

    def go_start(lanes):
        return [net.copy(r.go.at[go_rows[k], lanes], go_in.at[p, :, lanes], net.plane(k, c)) for k in (1, 2, 3)]

    go_out = go_start(pl.ds(0, 1024))
    mlp_sums()
    entering_states(r, net, ends, 1, True)
    r.vec[...] = jnp.zeros((2, 8, 8, 128), F32)
    dri = r.normed

    def second_pass(s):
        b, n = lax.div(s, 2), lax.rem(s, 2)
        chan = r.chan[n]
        enter = r.inc[pl.ds(s, 1), :]
        lanes_r = pl.ds(pl.multiple_of(n * 256, 128), 128)
        lanes_i = pl.ds(pl.multiple_of(n * 256 + 128, 128), 128)

        def tile(i, sums):
            rows = tile_rows(i)
            live = r.off[b, rows, :] != 0.0
            ds = r.drv[s, rows, :] + r.dec[s, rows, :] * enter
            window = r.states[s, pl.ds(pl.multiple_of(i * TILE, 8), TILE + 8), :]
            before = window[7 : TILE + 7, :]
            sr, si = r.sr[s, rows, :], r.si[s, rows, :]
            cv = r.conv[s, rows, :].astype(F32)
            a, m2 = decay_parts(sr, chan[7:8, :])
            inv = lax.rsqrt(m2)
            m = jnp.where(live, m2 * inv, 1.0)
            dsi = ds * si
            d_log = jnp.where(live, a * (ds * before - dsi * cv * a * inv), 0.0)
            lam_term = d_log * sr
            d_r = (-DECAY_SCALE) * chan[7:8, :] * lam_term * (1.0 - sr)
            dm_i = dsi * m
            d_i = dm_i * cv * (1.0 - si)
            d_r, d_i = d_r.astype(BF), d_i.astype(BF)
            at = tile_rows(lax.rem(i, 4))
            dri[b * 2 + lax.div(i, 4), at, lanes_r] = d_r
            dri[b * 2 + lax.div(i, 4), at, lanes_i] = d_i
            r.dconv[s, rows, :] = dm_i
            return (
                sums[0] + column_sum(d_r.astype(F32)),
                sums[1] + column_sum(d_i.astype(F32)),
                sums[2] + column_sum(lam_term),
            )

        zero = jnp.zeros((8, 128), F32)
        sums = lax.fori_loop(0, 512 // TILE, tile, (zero, zero, zero))
        for j in range(3):
            r.vec[n, 5 + j] = r.vec[n, 5 + j] + sums[j]

    loop(8, second_pass)

    def gate_back(i):
        s, half = lax.div(i, 2), lax.rem(i, 2)
        b, n = lax.div(s, 2), lax.rem(s, 2)
        rows = pl.ds(pl.multiple_of(half * 256, 256), 256)
        lanes = pl.ds(pl.multiple_of(n * 256, 256), 256)
        r.dconv[s, rows, :] = r.dconv[s, rows, :] + dot(dri[b * 2 + half, :, lanes], r.wri[n], NT)

    loop(16, gate_back)
    edge_back = net.reserve(1)

    def edge_back_copy():
        return net.describe(
            r.dconv.at[:, pl.ds(0, 8)], r.dconv.at[:, pl.ds(512, 8)], net.line(net.down(1), c), edge_back, edge_back
        )

    @pl.when(z > 0)
    def _():
        edge_back_copy().start()

    mlp_d.start()

    @pl.when(z == 3)
    def _():
        r.dconv[:, 512:520, :] = jnp.zeros((8, 8, 128), F32)

    for n in range(2):
        total_ri = None
        for b in range(4):
            for half in range(2):
                term = dot(
                    r.conv[b * 2 + n, half * 256 : (half + 1) * 256, :],
                    dri[b * 2 + half, :, n * 256 : (n + 1) * 256],
                    TN,
                )
                total_ri = term if total_ri is None else total_ri + term
        r.go[n * 128 : (n + 1) * 128, 1024:1280] = total_ri.astype(BF)
    go_out += go_start(pl.ds(1024, 256))

    @pl.when(z < 3)
    def _():
        edge_back_copy().wait_recv()


    def conv_back(s):
        b, n = lax.div(s, 2), lax.rem(s, 2)
        chan = r.chan[n]
        lanes = pl.ds(pl.multiple_of(256 + n * 128, 128), 128)

        def tile(i, sums):
            offset = r.off[b, pl.ds(pl.multiple_of(i * TILE, 8), TILE + 8), :]
            window = r.dconv[s, pl.ds(pl.multiple_of(i * TILE, 8), TILE + 8), :]
            inner = r.inner[s, pl.ds(pl.multiple_of(i * TILE, 8), TILE + 8), :]
            value = chan[0:1, :] * window[:TILE, :]
            added = [sums[0] + column_sum(window[:TILE, :] * inner[8:, :])]
            for k in (1, 2, 3):
                held = jnp.where(offset >= k, window, 0.0)
                value = value + chan[k : k + 1, :] * held[k : TILE + k, :]
                added.append(sums[k] + column_sum(held[:TILE, :] * inner[8 - k : TILE + 8 - k, :]))
            added.append(sums[4] + column_sum(window[:TILE, :]))
            r.dgi[b * 2 + lax.div(i, 4), tile_rows(lax.rem(i, 4)), lanes] = value.astype(BF)
            return tuple(added)

        sums = lax.fori_loop(0, 512 // TILE, tile, tuple(jnp.zeros((8, 128), F32) for _ in range(5)))
        for j in range(5):
            r.vec[n, j] = r.vec[n, j] + sums[j]

    loop(8, conv_back)
    out.finish(0)
    out.finish(1)
    for h in range(2):

        def out_rows(i, h=h):
            rows = pl.ds(pl.multiple_of(h * 128 + i * 32, 32), 32)
            value = (r.residual[rows, :] + out.total(h, i, 32)).astype(BF)
            for j in range(4):
                r.dgu[j, rows, 512:768] = value[:, j * 256 : (j + 1) * 256]

        loop(4, out_rows)
    for j in range(4):
        returned.append(net.local(r.dgu.at[j, :, pl.ds(512, 256)], r.block_out.at[:, pl.ds(j * 256, 256)]))
    for partner in (sibling, net.plane(1, c), net.plane(2, c)):
        pl.semaphore_signal(r.free, inc=1, device_id=partner, device_id_type=pl.DeviceIdType.MESH)
    for n in range(2):
        sums = [jnp.sum(r.vec[n, j], axis=0, keepdims=True) for j in range(8)]
        sums[7] = sums[7] * (DECAY_SCALE * r.chan[n, 8:9, :])
        r.vsum[z, :, n * 128 : (n + 1) * 128] = jnp.concatenate(sums, axis=0)
    vec = [net.copy(r.vsum.at[z], r.vsum.at[z], net.line(net.up(k), c)) for k in (1, 2, 3)]
    fetched.wait()
    flat = r.dgi[:, :, 0:512].reshape(-1, 512)
    for i in range(4):
        value = dot(r.do_all[:, :, i * 256 : (i + 1) * 256].reshape(-1, 256), flat, TN)
        for j in range(2):
            n0, n1 = value[:, j * 256 : j * 256 + 128], value[:, j * 256 + 128 : j * 256 + 256]
            r.ga[i][:, j * 128 : (j + 1) * 128] = lax.select(c == 0, n0, n1).astype(BF)
            shared = lax.select(c == 0, n1, n0)
            r.gb2[i][:, j * 128 : (j + 1) * 128] = lax.select(c == 0, shared[0:128], shared[128:256]).astype(BF)

    def ga_in(k):
        return r.g_all.at[7, :, pl.ds((k - 1) * 256, 256)]

    def gb_in(k):
        return r.g_all.at[3 + k, pl.ds(128, 128), pl.ds(0, 256)]

    sum_a = LineSum(net, lambda t: r.hid.at[t, :, 0:256], ga_in)
    sum_b = LineSum(net, lambda t: r.hid.at[4 + t, 0:128, 0:256], gb_in)
    sum_a.start()
    sum_b.start()
    mlp_d.relay()
    owners_m.forward()
    first_back = Reduce(
        net,
        r,
        lambda k, core: dot(masked(r.dgi[net.slot(k, core), :, 0:512], counted_two), r.w2[...], NT),
        total.at,
    )
    pl.semaphore_wait(r.free, 3)
    for k in (3, 1, 2, 0):
        first_back.other(k)
    first_back.far()
    first_back.near()
    go_in[p] = r.go[go_rows[0], :]
    for made in go_out:
        made.wait_recv()
    go_line = LineSum(net, lambda t: go_in.at[t], lambda k: go_line_in.at[k - 1])
    go_line.start()
    first_back.relay()
    mlp_d.end(r.gd_sum)
    owners_d.start()
    first_back.own()
    owners_m.middle()
    sum_a.relay()
    sum_b.relay()
    go_line.relay()
    first_back.finish(0)
    first_back.finish(1)
    sums = jnp.zeros((8, r.x.shape[1]), F32)
    for h in range(2):

        def input_rows(i, sums, h=h):
            rows = pl.ds(pl.multiple_of(h * 128 + i * 32, 32), 32)
            v = r.x[rows, :].astype(F32)
            dn = first_back.total(h, i, 32)
            s = lax.rsqrt(jnp.mean(v * v, axis=-1, keepdims=True) + NORM_EPS)
            u = dn * r.gain[0:1, :]
            r.d_res[rows, :] = r.d_res[rows, :] + (
                s * u - v * (s * s * s * jnp.mean(u * v, axis=-1, keepdims=True))
            )
            return sums + jnp.sum((dn * v * s).reshape(4, 8, -1), axis=0)

        sums = lax.fori_loop(0, 4, input_rows, sums)
    returned.append(net.local(r.d_res, r.d_in))
    gains = jnp.concatenate(
        [
            jnp.sum(sums, axis=0, keepdims=True),
            jnp.sum(r.gain2_sum[...], axis=0, keepdims=True),
            jnp.zeros((6, sums.shape[1]), F32),
        ],
        axis=0,
    )
    for i in range(8):
        r.gsum[i] = gains[:, i * 128 : (i + 1) * 128]
    r.gline[q] = r.gsum[q]
    gain_line = [
        net.copy(r.gsum.at[net.up(k) * 2 + core], r.gline.at[q], net.line(net.up(k), core))
        for k in (1, 2, 3)
        for core in (c, o)
    ]
    gain_line.append(net.copy(r.gsum.at[z * 2 + o], r.gline.at[q], sibling))
    for made in row_sums:
        made.wait_recv()
    r.rows_sum[...] = r.rs_all[0] + r.rs_all[1] + r.rs_all[2] + r.rs_all[3]
    for k in (1, 2, 3):
        for core in (c, o):
            owners.append(net.copy(r.rows_sum.at[pl.ds(net.near[k] * 2, 2)], r.fr.at[mine], net.plane(k, core)))
    owners.append(net.copy(r.rows_sum.at[pl.ds(p * 2, 2)], r.fr.at[mine], sibling))
    returned.append(net.local(r.rows_sum.at[pl.ds(p * 2, 2)], r.fr.at[mine]))
    for made in vec:
        made.wait_recv()
    r.vout[p] = r.vsum[0] + r.vsum[1] + r.vsum[2] + r.vsum[3]

    @pl.when(z == p)
    def _():
        for k in (1, 2, 3):
            vector_copy(k).start()

    sum_a.end(r.ga_sum)
    owners_a.start()
    sum_b.end(r.gb2_sum)
    owners_b.start()
    go_line.end(r.go_sum)
    to_chips(r.go_sum, r.fo)
    owners_d.forward()
    owners_m.last()
    owners_a.forward()
    owners_b.forward()
    for made in gain_line:
        made.wait_recv()
    sums = r.gline[0]
    for i in range(1, 8):
        sums = sums + r.gline[i]
    r.gplane[p] = sums
    gain_plane = [net.copy(r.gplane.at[p], r.gplane.at[p], net.plane(k, c)) for k in (1, 2, 3)]

    @pl.when(z != p)
    def _():
        vector_copy(1).wait_recv()

    @pl.when(z == p)
    def _():
        for k in (1, 2, 3):
            vector_copy(k).wait_send()

    owners_d.middle()
    owners_a.middle()
    owners_b.middle()
    for each in (owners_d, owners_a, owners_b):
        each.last()
    for each in (owners_m, owners_d, owners_a, owners_b):
        each.end()
    for made in owners + gain_plane:
        made.wait_recv()
    r.gain_out[...] = r.gplane[0] + r.gplane[1] + r.gplane[2] + r.gplane[3]
    r.vec_out[...] = r.vout[z]
    for made in returned:
        made.wait()
    @pl.when(z < 3)
    def _():
        edge_copy().wait_send()

    @pl.when(z > 0)
    def _():
        edge_back_copy().wait_send()

    gates_in.drain()
    out_in.drain()
    feed.drain()
    feed_down.drain()
    for made in (mlp_m, mlp_d, go_line, sum_a, sum_b):
        made.drain()
    net.drain()


def assemble(r):
    c = lax.rem(lax.axis_index("seq"), 2)
    count = 0
    stores = []

    def start(src, dst):
        nonlocal count
        made = pltpu.make_async_copy(src, dst, r.local.at[count])
        count += 1
        made.start()
        return made

    mine = pl.ds(pl.multiple_of(c * 128, 128), 128)
    loads = [
        [start(r.fm.at[:, mine], r.vm.at[c]), start(r.fm_x, r.vm.at[1 - c])],
        [start(r.fa.at[:, mine], r.va.at[c]), start(r.fa_x, r.va.at[1 - c]), start(r.fb, r.vb)],
        [start(r.fd, r.vd)],
        [start(r.fo, r.vo)],
    ]

    def loaded(which):
        for made in loads[which]:
            made.wait()

    passed = [start(r.d_in, r.v_din), start(r.block_out, r.v_block)]
    vec = r.vec_in[...]
    vec = lax.select(c == 0, vec[:, 0:192], vec[:, 64:256])
    r.o_cw[...] = vec[0:4]
    for j, out in enumerate((r.o_cb, r.o_rb, r.o_ib, r.o_lam)):
        out[...] = vec[4 + j : 5 + j]
    r.o_ngain[...] = r.gains[0:1, :]
    r.o_mgain[...] = r.gains[1:2, :]
    counts = [jnp.broadcast_to(r.lens[0:1, row : row + 1].astype(F32), (1, 128)) for row in range(5)]
    for chip in range(4):
        for half, (slot, n) in enumerate(((chip * 2, 0), (chip * 2, 1), (chip * 2 + 1, 1))):
            at = chip * 384 + half * 128
            for row in range(5):
                r.o_mean[row, :, at : at + 128] = r.fr[slot, n, row : row + 1, :] / counts[row]
    cols = r.fm.shape[2] // 2
    piece = cols // 4
    loaded(0)
    for j, (stage, out) in enumerate(((r.s_mgate, r.o_mgate), (r.s_mup, r.o_mup))):
        for part in range(4):
            for core in range(2):
                at = (part * 2 + core) * cols
                lanes = slice(j * cols + part * piece, j * cols + (part + 1) * piece)
                stage[:, at : at + cols] = jnp.concatenate(
                    [r.vm[core, chip, :, lanes].astype(F32) for chip in range(4)], axis=1
                )
            here = pl.ds(part * 2 * cols, 2 * cols)
            stores.append(start(stage.at[:, here], out.at[:, here]))
    for made, src, dst in zip(passed, (r.v_din, r.v_block), (r.o_din, r.o_block)):
        made.wait()
        stores.append(start(src, dst))
    loaded(1)
    for j, (stage, out) in enumerate(((r.s_gate, r.o_gate), (r.s_in, r.o_in))):
        lanes = slice(j * 128, (j + 1) * 128)
        for chip in range(4):
            at = chip * 384
            stage[:, at : at + 128] = r.va[0, chip, :, lanes].astype(F32)
            stage[:, at + 128 : at + 256] = r.vb[chip, :, lanes].astype(F32)
            stage[:, at + 256 : at + 384] = r.va[1, chip, :, lanes].astype(F32)
        stores.append(start(stage, out))
    loaded(2)
    for chip in range(4):
        r.s_down[chip * piece : (chip + 1) * piece, :] = r.vd[chip].astype(F32)
    stores.append(start(r.s_down, r.o_mdown))
    loaded(3)
    for chip in range(4):
        rows = slice(chip * 48, (chip + 1) * 48)
        r.s_out[rows, :] = r.vo[chip, :, 0:1024].astype(F32)
        r.o_r[rows, :] = r.vo[chip, :, 1024:1152].astype(F32)
        r.o_i[rows, :] = r.vo[chip, :, 1152:1280].astype(F32)
    stores.append(start(r.s_out, r.o_out))
    for made in stores:
        made.wait()


def shifted(value, axis, by):
    count = lax.axis_size(axis)
    pairs = [(i, i + by) for i in range(count) if 0 <= i + by < count]
    return lax.ppermute(value, axis, pairs)


def entering(value, axis, combine, identity, reverse):
    count, place = (lax.axis_size(axis), lax.axis_index(axis))
    everything = jax.tree.map(lambda part: lax.all_gather(part, axis), value)
    start = jax.tree.map(
        lambda part, zero: jnp.broadcast_to(jnp.asarray(zero, part.dtype), part.shape),
        value,
        identity,
    )

    def step(k, before):
        at = count - 1 - k if reverse else k
        reached = at > place if reverse else at < place
        new = combine(before, jax.tree.map(lambda part: part[at], everything))
        return jax.tree.map(lambda a, b: jnp.where(reached, a, b), new, before)

    return lax.fori_loop(0, count, step, start)


def rms_scale(values):
    return values * lax.rsqrt(jnp.mean(values * values, axis=-1, keepdims=True) + NORM_EPS)


def gelu_tanh(values):
    return jax.nn.gelu(values, approximate=True)


def link(earlier, later):
    return (earlier[0] * later[0], later[0] * earlier[1] + later[1])


def block_product(values, weight):
    count, channels = values.shape
    block_size = weight.shape[1]
    shaped = values.reshape(count, channels // block_size, block_size)
    result = jnp.einsum(
        "lni,nij->lnj",
        shaped,
        weight.reshape(channels // block_size, block_size, block_size),
        preferred_element_type=jnp.float32,
    )
    return result.reshape(count, channels)


def block_back(grads, weight):
    count, channels = grads.shape
    block_size = weight.shape[1]
    shaped = grads.reshape(count, channels // block_size, block_size)
    result = jnp.einsum(
        "lnj,nij->lni",
        shaped,
        weight.reshape(channels // block_size, block_size, block_size),
        preferred_element_type=jnp.float32,
    )
    return result.reshape(count, channels)


def block_weight_grad(values, grads, block_size):
    count, channels = values.shape
    left = values.reshape(count, channels // block_size, block_size)
    right = grads.reshape(count, channels // block_size, block_size)
    return jnp.einsum("lni,lnj->nij", left, right, preferred_element_type=jnp.float32).reshape(
        channels, block_size
    )


def recurrence_terms(conv_in, r_in, i_in, lam_in, restart):
    log_a = -DECAY_SCALE * jax.nn.sigmoid(r_in) * jax.nn.softplus(-lam_in)
    decays = jnp.exp(log_a)
    factor = jnp.where(restart[:, None] > 0, 1.0, jnp.sqrt(-jnp.expm1(2.0 * log_a)))
    return (decays * (1.0 - restart[:, None]), factor * jax.nn.sigmoid(i_in) * conv_in, decays)


def shards(
    inputs,
    out_grad,
    row_lengths,
    norm_gain,
    w_gate,
    w_in,
    conv_w,
    conv_b,
    w_rgate,
    b_rgate,
    w_igate,
    b_igate,
    lam,
    w_out,
    mlp_gain,
    w_mlp_gate,
    w_mlp_up,
    w_mlp_down,
):
    gathered = (
        lax.all_gather(norm_gain, "seq", axis=0, tiled=True),
        lax.all_gather(w_gate, "seq", axis=0, tiled=True),
        lax.all_gather(w_in, "seq", axis=0, tiled=True),
        lax.all_gather(conv_w, "seq", axis=1, tiled=True),
        lax.all_gather(conv_b, "seq", axis=0, tiled=True),
        lax.all_gather(w_rgate, "seq", axis=0, tiled=True),
        lax.all_gather(b_rgate, "seq", axis=0, tiled=True),
        lax.all_gather(w_igate, "seq", axis=0, tiled=True),
        lax.all_gather(b_igate, "seq", axis=0, tiled=True),
        lax.all_gather(lam, "seq", axis=0, tiled=True),
        lax.all_gather(w_out, "seq", axis=0, tiled=True),
        lax.all_gather(mlp_gain, "seq", axis=0, tiled=True),
        lax.all_gather(w_mlp_gate, "seq", axis=0, tiled=True),
        lax.all_gather(w_mlp_up, "seq", axis=0, tiled=True),
        lax.all_gather(w_mlp_down, "seq", axis=0, tiled=True),
    )
    gain_first = gathered[0].astype(jnp.float32)
    conv_taps = gathered[3].astype(jnp.float32)
    conv_bias = gathered[4].astype(jnp.float32)
    lam_value = gathered[9].astype(jnp.float32)
    gain_second = gathered[11].astype(jnp.float32)
    tokens = inputs[0].astype(jnp.float32)
    local_len = tokens.shape[0]
    channels = gathered[2].shape[1]
    block_size = gathered[5].shape[1]
    kernel_taps = conv_taps.shape[0]
    lengths = row_lengths[0]
    row_ends = jnp.cumsum(lengths)
    row_starts = row_ends - lengths
    positions = lax.axis_index("seq") * local_len + jnp.arange(local_len, dtype=jnp.int32)
    started = positions[:, None] >= row_starts[None, :]
    row_index = jnp.sum(started.astype(jnp.int32), axis=1) - 1
    row_first = jnp.max(jnp.where(started, row_starts[None, :], 0), axis=1)
    offset = positions - row_first
    restart = (offset == 0).astype(jnp.float32)
    members = (row_index[:, None] == jnp.arange(lengths.shape[0], dtype=jnp.int32)[None, :]).astype(
        jnp.float32
    )
    tap_masks = [(offset >= tap).astype(jnp.float32)[:, None] for tap in range(kernel_taps)]
    scaled, norm_pull = jax.vjp(rms_scale, tokens)
    normed = (scaled * gain_first).astype(jnp.bfloat16)
    gate_pre = jnp.dot(normed, gathered[1], preferred_element_type=jnp.float32)
    gate_branch, gate_pull = jax.vjp(gelu_tanh, gate_pre)
    inner = jnp.dot(normed, gathered[2], preferred_element_type=jnp.float32).astype(jnp.bfloat16)
    edge_rows = shifted(inner[local_len - kernel_taps + 1 :], "seq", 1)
    extended = jnp.concatenate([edge_rows, inner], axis=0).astype(jnp.float32)
    conv_sum = conv_bias + jnp.zeros((local_len, channels), jnp.float32)
    for tap in range(kernel_taps):
        start_row = kernel_taps - 1 - tap
        conv_sum = (
            conv_sum + conv_taps[tap] * extended[start_row : start_row + local_len] * tap_masks[tap]
        )
    conv_low = conv_sum.astype(jnp.bfloat16)
    conv_value = conv_low.astype(jnp.float32)
    r_pre = block_product(conv_low, gathered[5]) + gathered[6].astype(jnp.float32)
    i_pre = block_product(conv_low, gathered[7]) + gathered[8].astype(jnp.float32)

    def local_terms(conv_in, r_in, i_in, lam_in):
        return recurrence_terms(conv_in, r_in, i_in, lam_in, restart)

    (carried, drive_term, decays), recur_pull = jax.vjp(
        local_terms, conv_value, r_pre, i_pre, lam_value
    )
    prefix_decay, local_state = lax.associative_scan(link, (carried, drive_term), axis=0)
    identity = (jnp.ones((channels,), jnp.float32), jnp.zeros((channels,), jnp.float32))
    incoming = entering((prefix_decay[-1], local_state[-1]), "seq", link, identity, False)[1]
    states = local_state + prefix_decay * incoming
    mixed_low = (states * gate_branch).astype(jnp.bfloat16)
    residual = tokens + jnp.dot(mixed_low, gathered[10], preferred_element_type=jnp.float32)
    scaled_two, norm_pull_two = jax.vjp(rms_scale, residual)
    normed_two = (scaled_two * gain_second).astype(jnp.bfloat16)
    up_gate = jnp.dot(normed_two, gathered[12], preferred_element_type=jnp.float32)
    up_lin = jnp.dot(normed_two, gathered[13], preferred_element_type=jnp.float32)
    gelu_up, up_pull = jax.vjp(gelu_tanh, up_gate)
    hidden = (gelu_up * up_lin).astype(jnp.bfloat16)
    block_out = (
        residual + jnp.dot(hidden, gathered[14], preferred_element_type=jnp.float32)
    ).astype(jnp.bfloat16)
    row_sums = lax.psum(jnp.dot(members.T, decays, precision=lax.Precision.HIGHEST), "seq")
    gate_mean = row_sums / lengths.astype(jnp.float32)[:, None]
    grad_top = out_grad[0]
    grad_mdown = jnp.einsum("tf,td->fd", hidden, grad_top, preferred_element_type=jnp.float32)
    d_hidden = jnp.einsum("td,fd->tf", grad_top, gathered[14], preferred_element_type=jnp.float32)
    d_upgate = up_pull(d_hidden * up_lin)[0].astype(jnp.bfloat16)
    d_uplin = (d_hidden * gelu_up).astype(jnp.bfloat16)
    grad_mgate = jnp.einsum("td,tf->df", normed_two, d_upgate, preferred_element_type=jnp.float32)
    grad_mup = jnp.einsum("td,tf->df", normed_two, d_uplin, preferred_element_type=jnp.float32)
    d_normed_two = jnp.einsum(
        "tf,df->td", d_upgate, gathered[12], preferred_element_type=jnp.float32
    )
    d_normed_two = d_normed_two + jnp.einsum(
        "tf,df->td", d_uplin, gathered[13], preferred_element_type=jnp.float32
    )
    grad_mgain = jnp.sum(d_normed_two * scaled_two, axis=0)
    d_residual = grad_top.astype(jnp.float32) + norm_pull_two(d_normed_two * gain_second)[0]
    d_outlow = d_residual.astype(jnp.bfloat16)
    grad_outw = jnp.einsum("tr,td->rd", mixed_low, d_outlow, preferred_element_type=jnp.float32)
    d_mixed = jnp.einsum("td,rd->tr", d_outlow, gathered[10], preferred_element_type=jnp.float32)
    direct = d_mixed * gate_branch
    d_gatelow = gate_pull(d_mixed * states)[0].astype(jnp.bfloat16)
    grad_gatew = jnp.einsum("td,tr->dr", normed, d_gatelow, preferred_element_type=jnp.float32)
    next_decay = jnp.concatenate([carried[1:], jnp.ones((1, channels), jnp.float32)], axis=0)
    suffix_decay, local_grad = lax.associative_scan(
        link, (next_decay, direct), axis=0, reverse=True
    )
    arriving = entering(
        (carried[0] * suffix_decay[0], carried[0] * local_grad[0]), "seq", link, identity, True
    )[1]
    d_states = local_grad + suffix_decay * arriving
    previous = jnp.concatenate([incoming[None, :], states[:-1]], axis=0)
    grad_convval, d_rpre, d_ipre, grad_lambda = recur_pull(
        (d_states * previous, d_states, jnp.zeros_like(decays))
    )
    d_rlow = d_rpre.astype(jnp.bfloat16)
    d_ilow = d_ipre.astype(jnp.bfloat16)
    grad_rw = block_weight_grad(conv_low, d_rlow, block_size)
    grad_rb = jnp.sum(d_rlow.astype(jnp.float32), axis=0)
    grad_iw = block_weight_grad(conv_low, d_ilow, block_size)
    grad_ib = jnp.sum(d_ilow.astype(jnp.float32), axis=0)
    grad_convsum = grad_convval + block_back(d_rlow, gathered[5]) + block_back(d_ilow, gathered[7])
    grad_cb = jnp.sum(grad_convsum, axis=0)
    conv_again = gathered[3].astype(jnp.float32)
    grad_extended = jnp.zeros((local_len + kernel_taps - 1, channels), jnp.float32)
    tap_grads = []
    for tap in range(kernel_taps):
        start_row = kernel_taps - 1 - tap
        masked = grad_convsum * tap_masks[tap]
        tap_grads.append(jnp.sum(masked * extended[start_row : start_row + local_len], axis=0))
        grad_extended = grad_extended + jnp.pad(
            masked * conv_again[tap], ((start_row, tap), (0, 0))
        )
    grad_cw = jnp.stack(tap_grads)
    edge_grads = shifted(grad_extended[: kernel_taps - 1], "seq", -1)
    d_inner = (
        grad_extended[kernel_taps - 1 :]
        + jnp.pad(edge_grads, ((local_len - kernel_taps + 1, 0), (0, 0)))
    ).astype(jnp.bfloat16)
    grad_inw = jnp.einsum("td,tr->dr", normed, d_inner, preferred_element_type=jnp.float32)
    d_normed = jnp.einsum("tr,dr->td", d_gatelow, gathered[1], preferred_element_type=jnp.float32)
    d_normed = d_normed + jnp.einsum(
        "tr,dr->td", d_inner, gathered[2], preferred_element_type=jnp.float32
    )
    grad_gain = jnp.sum(d_normed * scaled, axis=0)
    d_tokens = d_residual + norm_pull(d_normed * gain_first)[0]
    shares = (
        lax.psum_scatter(grad_gain, "seq", scatter_dimension=0, tiled=True),
        lax.psum_scatter(grad_gatew, "seq", scatter_dimension=0, tiled=True),
        lax.psum_scatter(grad_inw, "seq", scatter_dimension=0, tiled=True),
        lax.psum_scatter(grad_cw, "seq", scatter_dimension=1, tiled=True),
        lax.psum_scatter(grad_cb, "seq", scatter_dimension=0, tiled=True),
        lax.psum_scatter(grad_rw, "seq", scatter_dimension=0, tiled=True),
        lax.psum_scatter(grad_rb, "seq", scatter_dimension=0, tiled=True),
        lax.psum_scatter(grad_iw, "seq", scatter_dimension=0, tiled=True),
        lax.psum_scatter(grad_ib, "seq", scatter_dimension=0, tiled=True),
        lax.psum_scatter(grad_lambda, "seq", scatter_dimension=0, tiled=True),
        lax.psum_scatter(grad_outw, "seq", scatter_dimension=0, tiled=True),
        lax.psum_scatter(grad_mgain, "seq", scatter_dimension=0, tiled=True),
        lax.psum_scatter(grad_mgate, "seq", scatter_dimension=0, tiled=True),
        lax.psum_scatter(grad_mup, "seq", scatter_dimension=0, tiled=True),
        lax.psum_scatter(grad_mdown, "seq", scatter_dimension=0, tiled=True),
    )
    totals = (
        lax.psum(shares[0].astype(jnp.bfloat16), "batch").astype(jnp.float32),
        lax.psum(shares[1].astype(jnp.bfloat16), "batch").astype(jnp.float32),
        lax.psum(shares[2].astype(jnp.bfloat16), "batch").astype(jnp.float32),
        lax.psum(shares[3].astype(jnp.bfloat16), "batch").astype(jnp.float32),
        lax.psum(shares[4].astype(jnp.bfloat16), "batch").astype(jnp.float32),
        lax.psum(shares[5].astype(jnp.bfloat16), "batch").astype(jnp.float32),
        lax.psum(shares[6].astype(jnp.bfloat16), "batch").astype(jnp.float32),
        lax.psum(shares[7].astype(jnp.bfloat16), "batch").astype(jnp.float32),
        lax.psum(shares[8].astype(jnp.bfloat16), "batch").astype(jnp.float32),
        lax.psum(shares[9].astype(jnp.bfloat16), "batch").astype(jnp.float32),
        lax.psum(shares[10].astype(jnp.bfloat16), "batch").astype(jnp.float32),
        lax.psum(shares[11].astype(jnp.bfloat16), "batch").astype(jnp.float32),
        lax.psum(shares[12].astype(jnp.bfloat16), "batch").astype(jnp.float32),
        lax.psum(shares[13].astype(jnp.bfloat16), "batch").astype(jnp.float32),
        lax.psum(shares[14].astype(jnp.bfloat16), "batch").astype(jnp.float32),
    )
    return (
        block_out[None],
        d_tokens[None],
        totals[0],
        totals[1],
        totals[2],
        totals[3],
        totals[4],
        totals[5],
        totals[6],
        totals[7],
        totals[8],
        totals[9],
        totals[10],
        totals[11],
        totals[12],
        totals[13],
        totals[14],
        gate_mean[None],
    )


def planes(
    inputs,
    out_grad,
    row_lengths,
    norm_gain,
    w_gate,
    w_in,
    conv_w,
    conv_b,
    w_rgate,
    b_rgate,
    w_igate,
    b_igate,
    lam,
    w_out,
    mlp_gain,
    w_mlp_gate,
    w_mlp_up,
    w_mlp_down,
):
    vmem = pltpu.VMEM
    done = kernel_call(
        layer,
        dict(
            x=inputs[0], cw=conv_w, cb=conv_b, br=b_rgate, bi=b_igate, lam=lam, ngain=norm_gain, mgain=mlp_gain,
            lens=row_lengths, g=out_grad[0], wg=w_gate, wi=w_in, wr=w_rgate, wv=w_igate, wout=w_out,
            wmg=w_mlp_gate, wmu=w_mlp_up, wmd=w_mlp_down,
        ),
        dict(
            block_out=array(256, 1024, dtype=BF),
            d_in=array(256, 1024),
            fm=array(4, 256, 768, dtype=BF),
            fm_x=array(4, 128, 768, dtype=BF),
            fd=array(4, 96, 1024, dtype=BF),
            fa=array(4, 256, 256, dtype=BF),
            fa_x=array(4, 128, 256, dtype=BF),
            fb=array(4, 128, 256, dtype=BF),
            fo=array(4, 48, 1280, dtype=BF),
            fr=array(8, 2, 8, 128),
            vec_out=array(8, 256),
            gain_out=array(8, 128),
            normed_far=array(8, 256, 1024, dtype=BF),
        ),
        dict(
            x_all=vmem((8, 256, 1024), BF),
            normed=vmem((8, 256, 1024), BF),
            g_all=vmem((8, 256, 1024), BF),
            small_rows=vmem((16, 256), F32),
            small=vmem((16, 256), BF),
            small_all=vmem((8, 16, 256), BF),
            lens_out=vmem((8, 128), F32),
            lens_all=vmem((4, 8, 128), F32),
            off=vmem((4, 520, 128), F32),
            starts_all=vmem((4, 8, 128), F32),
            chan=vmem((2, 16, 128), F32),
            gain=vmem((8, 1024), F32),
            wgi3=vmem((4, 256, 768), BF),
            w2=vmem((1024, 512), BF),
            gq=vmem((4, 48, 256), BF),
            g3=vmem((2, 192, 256), BF),
            wq=vmem((4, 48, 1024), BF),
            wri=vmem((2, 128, 256), BF),
            w3=vmem((2, 192, 1024), BF),
            wo=vmem((256, 1024), BF),
            wgu_out=vmem((2, 256, 384), BF),
            wgu_all=vmem((8, 256, 384), BF),
            wmd_all=vmem((4, 96, 1024), BF),
            gp=vmem((8, 512, 128), F32),
            gb=vmem((8, 520, 128), F32),
            inner=vmem((8, 520, 128), F32),
            conv=vmem((8, 512, 128), BF),
            sr=vmem((8, 512, 128), F32),
            si=vmem((8, 512, 128), F32),
            dec=vmem((8, 512, 128), F32),
            drv=vmem((8, 512, 128), F32),
            states=vmem((8, 520, 128), F32),
            mixed=vmem((8, 256, 256), BF),
            tot=vmem((2, 4, 2, 8, 128), F32),
            inc=vmem((8, 128), F32),
            rs_all=vmem((4, 8, 8, 128), F32),
            rows_sum=vmem((8, 8, 128), F32),
            residual=vmem((256, 1024), F32),
            d_res=vmem((256, 1024), F32),
            hid=vmem((8, 256, 384), BF),
            dgu=vmem((8, 256, 768), BF),
            gm=vmem((4, 256, 768), BF),
            gm_sum=vmem((256, 768), BF),
            gd=vmem((4, 96, 1024), BF),
            gd_in=vmem((3, 96, 1024), BF),
            gd_sum=vmem((96, 1024), BF),
            go=vmem((256, 1280), BF),
            go_q=vmem((4, 48, 1280), BF),
            go_l=vmem((3, 48, 1280), BF),
            go_sum=vmem((48, 1280), BF),
            ga_sum=vmem((256, 256), BF),
            gb2_sum=vmem((128, 256), BF),
            gain2_sum=vmem((8, 1024), F32),
            vec=vmem((2, 8, 8, 128), F32),
            vsum=vmem((4, 8, 256), F32),
            vout=vmem((4, 8, 256), F32),
            gsum=vmem((8, 8, 128), F32),
            gline=vmem((8, 8, 128), F32),
            gplane=vmem((4, 8, 128), F32),
            free=pltpu.SemaphoreType.REGULAR,
            **reduce_scratch(256, 1024),
        ),
        166,
        36,
        (
            "g", "wg", "wi", "wr", "wv", "wout", "wmg", "wmu", "wmd", "d_in", "block_out", "fm", "fm_x", "fd", "fa", "fa_x", "fb", "fo",
            "fr", "normed_far",
        ),
    )
    out = kernel_call(
        assemble,
        dict(
            {name: done[name] for name in ("d_in", "block_out", "fm", "fm_x", "fd", "fa", "fa_x", "fb", "fo", "fr")},
            vec_in=done["vec_out"], gains=done["gain_out"], lens=row_lengths,
        ),
        dict(
            o_din=array(256, 1024),
            o_block=array(256, 1024, dtype=BF),
            o_gate=array(128, 1536),
            o_in=array(128, 1536),
            o_mgate=array(128, 3072),
            o_mup=array(128, 3072),
            o_mdown=array(384, 1024),
            o_out=array(192, 1024),
            o_r=array(192, 128),
            o_i=array(192, 128),
            o_cw=array(4, 192),
            o_cb=array(1, 192),
            o_rb=array(1, 192),
            o_ib=array(1, 192),
            o_lam=array(1, 192),
            o_ngain=array(1, 128),
            o_mgain=array(1, 128),
            o_mean=array(5, 1, 1536),
        ),
        dict(
            v_din=vmem((256, 1024), F32),
            v_block=vmem((256, 1024), BF),
            vm=vmem((2, 4, 128, 768), BF),
            va=vmem((2, 4, 128, 256), BF),
            vb=vmem((4, 128, 256), BF),
            vd=vmem((4, 96, 1024), BF),
            vo=vmem((4, 48, 1280), BF),
            s_mgate=vmem((128, 3072), F32),
            s_mup=vmem((128, 3072), F32),
            s_gate=vmem((128, 1536), F32),
            s_in=vmem((128, 1536), F32),
            s_down=vmem((384, 1024), F32),
            s_out=vmem((192, 1024), F32),
        ),
        0,
        23,
        (
            "d_in", "block_out", "fm", "fm_x", "fd", "fa", "fa_x", "fb", "fo", "o_din", "o_block", "o_gate", "o_in", "o_mgate", "o_mup",
            "o_mdown", "o_out",
        ),
    )
    return (
        out["o_block"][None],
        out["o_din"][None],
        out["o_ngain"][0],
        out["o_gate"],
        out["o_in"],
        out["o_cw"],
        out["o_cb"][0],
        out["o_r"],
        out["o_rb"][0],
        out["o_i"],
        out["o_ib"][0],
        out["o_lam"][0],
        out["o_out"],
        out["o_mgain"][0],
        out["o_mgate"],
        out["o_mup"],
        out["o_mdown"],
        jnp.transpose(out["o_mean"], (1, 0, 2)),
    )


def solution(mesh):
    in_specs = (
        P("batch", "seq", None),
        P("batch", "seq", None),
        P("batch", None),
        P("seq"),
        P("seq", None),
        P("seq", None),
        P(None, "seq"),
        P("seq"),
        P("seq", None),
        P("seq"),
        P("seq", None),
        P("seq"),
        P("seq"),
        P("seq", None),
        P("seq"),
        P("seq", None),
        P("seq", None),
        P("seq", None),
    )
    out_specs = (
        P("batch", "seq", None),
        P("batch", "seq", None),
        P("seq"),
        P("seq", None),
        P("seq", None),
        P(None, "seq"),
        P("seq"),
        P("seq", None),
        P("seq"),
        P("seq", None),
        P("seq"),
        P("seq"),
        P("seq", None),
        P("seq"),
        P("seq", None),
        P("seq", None),
        P("seq", None),
        P("batch", None, None),
    )
    in_planes = mesh.shape["batch"] == 4 and mesh.shape["seq"] == 8
    body = planes if in_planes else shards
    return jax.shard_map(body, mesh=mesh, in_specs=in_specs, out_specs=out_specs, check_vma=False)
```

```python
import functools
import types

import jax
import jax.numpy as jnp
from jax import lax
from jax.experimental import pallas as pl
from jax.experimental.pallas import tpu as pltpu
from jax.sharding import PartitionSpec as P

NORM_EPS = 1e-06
DECAY_SCALE = 8.0
BF = jnp.bfloat16
F32 = jnp.float32
GELU_SCALE = 0.7978845608028654
GELU_CUBE = 0.044715
TILE = 64
NN = (((1,), (0,)), ((), ()))
NT = (((1,), (1,)), ((), ()))
TN = (((0,), (0,)), ((), ()))


def dot(left, right, dims=NN):
    return lax.dot_general(left, right, dims, preferred_element_type=F32)


def loop(count, body):
    def step(i, carry):
        body(i)
        return carry

    lax.fori_loop(0, count, step, 0)


class Net:
    def __init__(self, r):
        self.send, self.recv, self.count = r.send, r.recv, 0
        self.here, self.here_count = r.local, 0
        self.pending = []
        self.p = lax.axis_index("batch")
        self.q = lax.axis_index("seq")
        self.z = lax.div(self.q, 2)
        self.c = lax.rem(self.q, 2)
        self.o = 1 - self.c
        p = self.p
        self.near = (p, p + 1 - 2 * lax.rem(p, 2), lax.rem(p + 2, 4), 3 - p)

    def plane(self, k, core):
        return {"batch": self.near[k], "seq": self.z * 2 + core}

    def line(self, z, core):
        return {"batch": self.p, "seq": z * 2 + core}

    def up(self, k):
        return lax.rem(self.z + k, 4)

    def down(self, k):
        return lax.rem(self.z + 4 - k, 4)

    def slot(self, k, core):
        return self.near[k] * 2 + core

    def greet(self):
        barrier = pltpu.get_barrier_semaphore()
        partners = [self.plane(k, core) for k in (1, 2, 3) for core in (0, 1)]
        partners += [self.line(self.up(k), core) for k in (1, 2, 3) for core in (0, 1)]
        partners += [self.line(self.z, self.o)]
        for partner in partners:
            pl.semaphore_signal(barrier, inc=1, device_id=partner, device_id_type=pl.DeviceIdType.MESH)
        pl.semaphore_wait(barrier, len(partners))

    def reserve(self, count):
        first = self.count
        self.count += count
        return first

    def describe(self, src, dst, device, send_at, recv_at):
        return pltpu.make_async_remote_copy(
            src_ref=src,
            dst_ref=dst,
            send_sem=self.send.at[send_at],
            recv_sem=self.recv.at[recv_at],
            device_id=device,
            device_id_type=pl.DeviceIdType.MESH,
        )

    def copy(self, src, dst, device, sent=None, at=None):
        at = self.reserve(1) if at is None else at
        made = self.describe(src, dst, device, at, at)
        made.start()
        (self.pending if sent is None else sent).append(made)
        return made

    def local(self, src, dst):
        made = pltpu.make_async_copy(src, dst, self.here.at[self.here_count])
        self.here_count += 1
        made.start()
        return made

    def drain(self):
        assert (self.count, self.here_count) == (self.send.shape[0], self.here.shape[0]), (self.count, self.here_count)
        for made in self.pending:
            made.wait_send()
        self.pending = []


class Gather:
    def __init__(self, net, own, everything, at=None):
        self.net, self.own, self.all = net, own, everything
        self.sent = []
        self.at = net.reserve(14) if at is None else at
        self.half = everything.shape[1] // 2
        self.x0, self.y1, self.x1, self.y0 = [], [], [], []

    def half_of(self, slot, h):
        return self.all.at[slot, pl.ds(h * self.half, self.half)]

    def send(self, src, dst, device, at):
        return self.net.copy(src, dst, device, self.sent, self.at + at)

    def start(self, part):
        net = self.net
        mine = net.slot(0, net.c)
        size = self.half // 2
        low, high = pl.ds(part * size, size), pl.ds(self.half + part * size, size)
        for made, rows, k, at in ((self.x0, low, 1, 0), (self.y1, high, 2, 2), (self.x1, high, 1, 4), (self.y0, low, 2, 6)):
            made.append(self.send(self.own.at[rows], self.all.at[mine, rows], net.plane(k, net.c), at + part))
        if part == 1:
            self.s = [self.send(self.own, self.all.at[mine], net.plane(0, net.o), 8)]

    def forward(self):
        net = self.net
        for made in self.x0:
            made.wait_recv()
        block = self.half_of(net.slot(1, net.c), 0)
        self.d0 = self.send(block, block, net.plane(2, net.c), 9)
        for made in self.y1:
            made.wait_recv()
        block = self.half_of(net.slot(2, net.c), 1)
        self.d1 = self.send(block, block, net.plane(1, net.c), 10)

    def across(self, k):
        net = self.net
        block = self.all.at[net.slot(k, net.c)]
        self.s.append(self.send(block, block, net.plane(0, net.o), 10 + k))

    def middle(self):
        for made in self.x1:
            made.wait_recv()
        self.across(1)
        for made in self.y0:
            made.wait_recv()
        self.across(2)

    def last(self):
        self.d0.wait_recv()
        self.d1.wait_recv()
        self.across(3)

    def sibling(self, k):
        self.s[k].wait_recv()

    def release(self):
        for made in self.sent:
            made.wait_send()
        self.sent = []


class Owners:
    def __init__(self, net, own, everything, extra=None, at=None):
        self.net, self.own, self.all, self.extra = net, own, everything, extra
        self.at = net.reserve(6 if extra is None else 10) if at is None else at
        self.half = everything.shape[1] // 2
        self.s = [None] * 4

    def part(self, k, h):
        return self.all.at[self.net.near[k], pl.ds(h * self.half, self.half)]

    def across(self, k, block):
        if self.extra is not None:
            net = self.net
            rows = pl.ds(pl.multiple_of(net.o * self.half, 16), self.half)
            self.s[k] = net.copy(block.at[rows], self.extra.at[net.near[k]], net.plane(0, net.o), None, self.at + 6 + k)

    def start(self):
        net = self.net
        low, high = self.own.at[pl.ds(0, self.half)], self.own.at[pl.ds(self.half, self.half)]
        self.x0 = net.copy(low, self.part(0, 0), net.plane(1, net.c), None, self.at + 0)
        self.y1 = net.copy(high, self.part(0, 1), net.plane(2, net.c), None, self.at + 1)
        self.x1 = net.copy(high, self.part(0, 1), net.plane(1, net.c), None, self.at + 2)
        self.y0 = net.copy(low, self.part(0, 0), net.plane(2, net.c), None, self.at + 3)
        self.across(0, self.own)
        self.kept = net.local(self.own, self.all.at[net.p])

    def forward(self):
        net = self.net
        self.x0.wait_recv()
        self.d0 = net.copy(self.part(1, 0), self.part(1, 0), net.plane(2, net.c), None, self.at + 4)
        self.y1.wait_recv()
        self.d1 = net.copy(self.part(2, 1), self.part(2, 1), net.plane(1, net.c), None, self.at + 5)

    def middle(self):
        self.x1.wait_recv()
        self.across(1, self.all.at[self.net.near[1]])
        self.y0.wait_recv()
        self.across(2, self.all.at[self.net.near[2]])

    def last(self):
        self.d0.wait_recv()
        self.d1.wait_recv()
        self.across(3, self.all.at[self.net.near[3]])

    def end(self):
        if self.extra is not None:
            for made in self.s:
                made.wait_recv()
        self.kept.wait()


class LineGather:
    def __init__(self, net, own, first, place):
        self.net, self.own, self.first, self.place = net, own, first, place
        self.at = net.reserve(4 * len(own))

    def made(self, k, j):
        net = self.net
        src, core = self.own[j]
        at = self.at + 4 * j + k - 1
        return net.describe(src, self.first(j), net.line(net.up(k), core), at, at)

    def handed(self, j):
        net = self.net
        far = 6 - 3 * net.z
        here = self.place(j, far)
        at = self.at + 4 * j
        return net.describe(here, here, net.line(3 - far, net.c), at + 3, at + 2 * net.z - 2)

    def direct(self, k, body):
        z = self.net.z
        if k == 2:
            body()
        else:
            pl.when(z != (0 if k == 3 else 3))(body)

    def start(self, k, items):
        def send():
            for j in items:
                self.made(k, j).start()

        self.direct(k, send)

    def inside(self, body):
        z = self.net.z
        pl.when((z == 1) | (z == 2))(body)

    def relay(self):
        @self.inside
        def _():
            for j in range(len(self.own)):
                self.made(2, j).wait_recv()
                self.handed(j).start()

    def end(self):
        z = self.net.z
        for k in (1, 3):
            for j in range(len(self.own)):
                self.made(k, j).wait_recv()

        @pl.when((z == 0) | (z == 3))
        def _():
            for j in range(len(self.own)):
                self.made(2, j).wait_recv()

    def drain(self):
        for k in (1, 2, 3):

            def wait(k=k):
                for j in range(len(self.own)):
                    self.made(k, j).wait_send()

            self.direct(k, wait)

        @self.inside
        def _():
            for j in range(len(self.own)):
                self.handed(j).wait_send()


class LineSum:
    def __init__(self, net, block, slot, at=None):
        self.net, self.block, self.slot = net, block, slot
        self.at = net.reserve(3) if at is None else at

    def made(self, k):
        net = self.net
        at = self.at + k - 1
        to = lax.rem(2 * net.z + 1, 5) if k == 2 else net.up(k)
        return net.describe(self.block(net.up(k)), self.slot(k), net.line(to, net.c), at, at)

    def start(self):
        z = self.net.z
        self.made(2).start()
        pl.when(z != 1)(lambda: self.made(1).start())
        pl.when(z != 2)(lambda: self.made(3).start())

    def relay(self, step=16):
        z = self.net.z

        @pl.when((z == 1) | (z == 2))
        def _():
            self.made(2).wait_recv()
            mine, extra = self.block(3 - z), self.slot(2)

            def body(i):
                rows = pl.ds(pl.multiple_of(i * step, step), step)
                mine[rows, :] = (mine[rows, :].astype(F32) + extra[rows, :].astype(F32)).astype(BF)

            loop(mine.shape[0] // step, body)

        pl.when(z == 1)(lambda: self.made(1).start())
        pl.when(z == 2)(lambda: self.made(3).start())

    def end(self, dst, step=16):
        z = self.net.z
        self.made(1).wait_recv()
        self.made(3).wait_recv()
        edge = (z == 0) | (z == 3)
        pl.when(edge)(lambda: self.made(2).wait_recv())
        share = jnp.where(edge, 1.0, 0.0)
        own = self.block(z)

        def body(i):
            rows = pl.ds(pl.multiple_of(i * step, step), step)
            value = own[rows, :].astype(F32) + share * self.slot(2)[rows, :].astype(F32)
            value = value + self.slot(1)[rows, :].astype(F32) + self.slot(3)[rows, :].astype(F32)
            dst[rows, :] = value.astype(BF)

        loop(dst.shape[0] // step, body)

    def drain(self):
        for k in (1, 2, 3):
            self.made(k).wait_send()


class Reduce:
    def __init__(self, net, r, value, at=None):
        self.net, self.value = net, value
        self.at = net.reserve(12) if at is None else at
        self.keep, self.out, self.into = r.rs_keep, r.rs_out, r.rs_in
        self.xs, self.ys, self.xr, self.yr = r.rs_xs, r.rs_ys, r.rs_xr, r.rs_yr
        self.half = self.keep.shape[1]
        self.cross = [None] * 4
        self.sent = []

    def other(self, k):
        net = self.net
        self.out[k] = self.value(k, net.o).astype(BF)
        self.cross[k] = net.copy(self.out.at[k], self.into.at[k], net.plane(0, net.o), self.sent, self.at + k)

    def mine(self, k):
        self.cross[k].wait_recv()
        value = self.value(k, self.net.c) + self.into[k].astype(F32)
        return value[: self.half], value[self.half :]

    def send(self, src, dst, j, k, part=None):
        net = self.net
        at = self.at + 4 + j + (part or 0) + (0 if src is self.xs else 4)
        src, dst = src.at[j], dst.at[j]
        if part is not None:
            rows = pl.ds(part * self.half // 2, self.half // 2)
            src, dst = src.at[rows], dst.at[rows]
        return net.copy(src, dst, net.plane(k, net.c), self.sent, at)

    def far(self):
        low, high = self.mine(3)
        self.xs[0] = low.astype(BF)
        self.x0 = self.send(self.xs, self.xr, 0, 1)
        self.ys[0] = high.astype(BF)
        self.y0 = self.send(self.ys, self.yr, 0, 2)

    def near(self):
        low, high = self.mine(1)
        self.xs[1] = low.astype(BF)
        self.x1 = self.send(self.xs, self.xr, 1, 1)
        self.keep[2] = high
        low, high = self.mine(2)
        self.ys[1] = high.astype(BF)
        self.y1 = self.send(self.ys, self.yr, 1, 2)
        self.keep[3] = low

    def relay(self):
        size = self.half // 2
        self.x2, self.y2 = [], []
        for part in (0, 1):
            rows = slice(part * size, (part + 1) * size)
            if part == 0:
                self.x0.wait_recv()
            self.ys[2, rows, :] = (self.keep[3, rows, :] + self.xr[0, rows, :].astype(F32)).astype(BF)
            self.y2.append(self.send(self.ys, self.yr, 2, 2, part))
            if part == 0:
                self.y0.wait_recv()
            self.xs[2, rows, :] = (self.keep[2, rows, :] + self.yr[0, rows, :].astype(F32)).astype(BF)
            self.x2.append(self.send(self.xs, self.xr, 2, 1, part))

    def own(self):
        self.keep[0], self.keep[1] = self.mine(0)

    def finish(self, part):
        if part == 0:
            self.x1.wait_recv()
            self.y1.wait_recv()
        self.x2[part].wait_recv()
        self.y2[part].wait_recv()
        if part == 1:
            for made in self.sent:
                made.wait_send()
            self.sent = []

    def total(self, h, i, step):
        rows = pl.ds(pl.multiple_of(i * step, step), step)
        first, second = (self.xr, self.yr) if h == 0 else (self.yr, self.xr)
        return self.keep[h, rows, :] + first[1, rows, :].astype(F32) + second[2, rows, :].astype(F32)


def reduce_scratch(rows, width):
    half = rows // 2
    return dict(
        rs_keep=pltpu.VMEM((4, half, width), F32),
        rs_out=pltpu.VMEM((4, rows, width), BF),
        rs_in=pltpu.VMEM((4, rows, width), BF),
        rs_xs=pltpu.VMEM((3, half, width), BF),
        rs_ys=pltpu.VMEM((3, half, width), BF),
        rs_xr=pltpu.VMEM((3, half, width), BF),
        rs_yr=pltpu.VMEM((3, half, width), BF),
    )


def kernel_call(body, ins, outs, scratch, copies, local, far):
    names = list(ins) + list(outs) + list(scratch)
    near = pl.BlockSpec(memory_space=pltpu.VMEM)
    away = pl.BlockSpec(memory_space=pl.ANY)
    shapes = list(scratch.values())
    if copies:
        names += ["send", "recv"]
        shapes += [pltpu.SemaphoreType.DMA((copies,))] * 2
    if local:
        names.append("local")
        shapes.append(pltpu.SemaphoreType.DMA((local,)))

    def kernel(*refs):
        body(types.SimpleNamespace(**dict(zip(names, refs))))

    params = dict(vmem_limit_bytes=62 * 2**20)
    if copies:
        params.update(collective_id=0, has_side_effects=True)
    results = pl.pallas_call(
        kernel,
        out_shape=list(outs.values()),
        in_specs=[away if far is None or name in far else near for name in ins],
        out_specs=[away if far is None or name in far else near for name in outs],
        scratch_shapes=shapes,
        compiler_params=pltpu.CompilerParams(**params),
        name=body.__name__,
    )(*ins.values())
    return dict(zip(outs, results))


def array(*shape, dtype=F32):
    return jax.ShapeDtypeStruct(shape, dtype)


def gelu_parts(v):
    square = v * v
    t = jnp.tanh(GELU_SCALE * v * (1.0 + GELU_CUBE * square))
    half = 0.5 + 0.5 * t
    slope = half + 0.5 * v * (1.0 - t * t) * (GELU_SCALE * (1.0 + 3.0 * GELU_CUBE * square))
    return v * half, slope


def decay_parts(sr, rate):
    log_a = -DECAY_SCALE * sr * rate
    a = jnp.exp(log_a)
    y = 2.0 * log_a
    series = 1.0 + y * (1 / 6) * (1.0 + y * (1 / 7))
    for n in (5, 4, 3, 2):
        series = 1.0 + y * (1 / n) * series
    m2 = jnp.where(y > -0.35, -y * series, 1.0 - a * a)
    return a, jnp.maximum(m2, 1e-36)


def column_sum(value):
    return jnp.sum(value.reshape(-1, 8, 128), axis=0)


def scan_slabs(decay, value, reverse):
    count = decay.shape[1] // 8
    row = lax.broadcasted_iota(jnp.int32, (8, 128), 0)

    def step(i, carry):
        t = count - 1 - i if reverse else i
        at = pl.ds(pl.multiple_of(t * 8, 8), 8)
        done = []
        for s in range(8):
            pc, vc = carry[s]
            p, own = decay[s, at, :], value[s, at, :]
            v = p * own if reverse else own
            for d in (1, 2, 4):
                by = 8 - d if reverse else d
                inside = row < 8 - d if reverse else row >= d
                v = v + p * jnp.where(inside, pltpu.roll(v, by, 0), 0.0)
                p = p * jnp.where(inside, pltpu.roll(p, by, 0), 1.0)
            v = v + p * vc
            p = p * pc
            if reverse:
                edge = row == 7
                value[s, at, :] = own + jnp.where(edge, vc, pltpu.roll(v, 7, 0))
                decay[s, at, :] = jnp.where(edge, pc, pltpu.roll(p, 7, 0))
                last = slice(0, 1)
            else:
                value[s, at, :] = v
                decay[s, at, :] = p
                last = slice(7, 8)
            done.append((jnp.broadcast_to(p[last], (8, 128)), jnp.broadcast_to(v[last], (8, 128))))
        return tuple(done)

    start = tuple((jnp.ones((8, 128), F32), jnp.zeros((8, 128), F32)) for _ in range(8))
    return lax.fori_loop(0, count, step, start)


def exchange_ends(r, net, ends, at):
    for s in range(8):
        r.tot[at, net.z, 0, s : s + 1, :] = ends[s][0][0:1, :]
        r.tot[at, net.z, 1, s : s + 1, :] = ends[s][1][0:1, :]
    mine = r.tot.at[at, net.z]
    return [net.copy(mine, mine, net.line(net.up(k), net.c)) for k in (1, 2, 3)]


def entering_states(r, net, copies, at, reverse):
    for made in copies:
        made.wait_recv()
    state = jnp.zeros((8, 128), F32)
    for i in range(4):
        z = 3 - i if reverse else i
        new = r.tot[at, z, 0] * state + r.tot[at, z, 1]
        state = jnp.where((z > net.z) if reverse else (z < net.z), new, state)
    r.inc[...] = state


def tile_rows(i):
    return pl.ds(pl.multiple_of(i * TILE, TILE), TILE)


def layer(r):
    r.do_all = r.x_all
    r.dconv = r.gb
    r.dgi = r.dgu
    r.up = r.d_res.at[:, 0:768]
    r.ga = [r.hid.at[i, :, 0:256] for i in range(4)]
    r.gb2 = [r.hid.at[4 + i, 0:128, 0:256] for i in range(4)]
    net = Net(r)
    p, z, c, o, q = net.p, net.z, net.c, net.o, net.q
    sibling = net.plane(0, o)
    mine = net.slot(0, c)
    cols = r.wgu_out.shape[2] // 2
    piece = cols // 4
    down = pl.ds(pl.multiple_of(p * piece, 16), piece)
    quarter = pl.ds(pl.multiple_of(p * 48, 16), 48)
    x_here = net.local(r.x_in, r.x)
    staged = []
    for j in range(8):
        lanes = pl.ds(j * cols, cols)
        staged.append(net.local(r.wmg.at[:, lanes], r.hid.at[j, pl.ds(0, 128)]))
        staged.append(net.local(r.wmu.at[:, lanes], r.hid.at[j, pl.ds(128, 128)]))
    width = 3 * 128
    first = pl.multiple_of(p * width, 128)
    chip = pl.ds(first, width)
    own_lanes = pl.ds(pl.multiple_of(c * width, 128), width)
    wi_rows, wg_rows = pl.ds(128, 128), pl.ds(0, 128)
    placed = [
        net.local(r.wg.at[:, chip], r.wgi3.at[z, wg_rows, own_lanes]),
        net.local(r.wi.at[:, chip], r.wgi3.at[z, wi_rows, own_lanes]),
        net.local(r.wmd.at[down], r.wmd_all.at[z]),
        net.local(r.wout.at[quarter], r.wq.at[z]),
        net.local(r.wr.at[quarter], r.gq.at[z, :, pl.ds(0, 128)]),
        net.local(r.wv.at[quarter], r.gq.at[z, :, pl.ds(128, 128)]),
        net.local(r.g, r.g_all.at[mine]),
    ]
    r.lens_out[0:1, 0:5] = r.lens[...].astype(F32)
    r.small_rows[...] = jnp.zeros((16, 256), F32)
    r.small_rows[0:4, 0:192] = r.cw[...].astype(F32)
    for at, ref in ((4, r.cb), (5, r.br), (6, r.bi), (7, r.lam)):
        r.small_rows[at : at + 1, 0:192] = ref[...].astype(F32).reshape(1, 192)
    for at, ref in ((0, r.ngain), (128, r.mgain)):
        r.small_rows[10:11, at : at + 128] = ref[...].astype(F32).reshape(1, 128)
    r.small[...] = r.small_rows[...].astype(BF)
    net.greet()
    r.small_all[q] = r.small[...]
    r.lens_all[p] = r.lens_out[...]
    small = [net.copy(r.small, r.small_all.at[q], net.line(net.up(k), core)) for k in (1, 2, 3) for core in (c, o)]
    small.append(net.copy(r.small, r.small_all.at[q], sibling))
    lens = [net.copy(r.lens_out, r.lens_all.at[p], net.plane(k, c)) for k in (1, 2, 3)]
    x_here.wait()
    tokens = Gather(net, r.x, r.x_all)
    tokens.start(0)
    tokens.start(1)
    theirs = pl.ds(pl.multiple_of(c * width + o * 128, 128), 256)

    def along(place):
        made = LineGather(net, [(place(z), c)], lambda j: place(z), lambda j, at: place(at))
        for k in (2, 1, 3):
            made.start(k, (0,))
        return made

    handed = []

    def heads_start(rows):
        here = r.wgi3.at[z, rows, theirs]
        made = along(lambda at: r.wgi3.at[at, rows, own_lanes])
        return made, [net.copy(here, here, sibling, handed)]

    for made in placed:
        made.wait()
    heads_in, heads_in_over = heads_start(wi_rows)
    gates_in = along(lambda at: r.gq.at[at])

    def hand_over(arrivals, rows, over):
        arrivals.end()
        for k in (1, 2, 3):
            here = r.wgi3.at[net.down(k), rows, theirs]
            over.append(net.copy(here, here, sibling, handed))

    def arrange(over, rows, lanes):
        for made in over:
            made.wait_recv()
        for core in range(2):
            cols_in = pl.ds(pl.multiple_of(core * width + c * 128, 128), 256)
            for at in range(4):
                to = slice((at * 2 + core) * 128, (at * 2 + core + 1) * 128)
                r.w2[to, lanes] = r.wgi3[at, rows, cols_in]

    def exchange(arrivals, src, dst):
        arrivals.end()
        dst[c, quarter, :] = src[p]
        return [net.copy(src.at[net.near[k]], dst.at[c, quarter], net.plane(k, c)) for k in (1, 2, 3)]

    def share(copies, dst):
        for made in copies:
            made.wait_recv()
        return net.copy(dst.at[c], dst.at[c], sibling)

    selects = []
    k_at = lax.broadcasted_iota(jnp.int32, (cols, cols), 0)
    j_at = lax.broadcasted_iota(jnp.int32, (cols, cols), 1)
    for part in range(4):
        inside = (j_at >= part * piece) & (j_at < (part + 1) * piece)
        chosen = inside & (k_at == j_at + (p - part) * piece)
        selects.append(jnp.where(chosen, 1.0, 0.0).astype(BF))
    for made in staged:
        made.wait()
    for which in range(2):
        rows = slice(which * 128, (which + 1) * 128)
        for core in (0, 1):
            picked = None
            for part in range(4):
                term = dot(r.hid[part * 2 + core, rows, :], selects[part])
                picked = term if picked is None else picked + term
            r.wgu_out[core, :, which * cols : (which + 1) * cols] = picked.astype(BF)
    for made in small + lens:
        made.wait_recv()
    low, high = r.small_all[2 * p].astype(F32), r.small_all[2 * p + 1].astype(F32)
    at_first = jnp.concatenate([low[:, :192], high[:, :64]], axis=1)
    at_second = jnp.concatenate([low[:, 128:192], high[:, :192]], axis=1)
    both = lax.select(c == 0, at_first, at_second)
    for n in range(2):
        r.chan[n] = both[:, n * 128 : (n + 1) * 128]
        lam = -r.chan[n, 7:8, :]
        e = jnp.exp(-jnp.abs(lam))
        series = 1.0 - e * (6 / 7)
        for k in (6, 5, 4, 3, 2):
            series = 1.0 - e * ((k - 1) / k) * series
        rate = jnp.maximum(lam, 0.0) + jnp.where(e < 0.05, e * series, jnp.log(1.0 + e))
        r.chan[n, 7:8, :] = rate
        r.chan[n, 8:9, :] = jax.nn.sigmoid(lam)
    for i in range(8):
        gains = r.small_all[i].astype(F32)[10:11, :]
        r.gain[0:1, i * 128 : (i + 1) * 128] = gains[:, 0:128]
        r.gain[1:2, i * 128 : (i + 1) * 128] = gains[:, 128:256]
    gain = r.gain[0:1, :]
    for b in range(4):
        start = jnp.zeros((1, 128), F32)
        for row in range(5):
            r.starts_all[b, row : row + 1, :] = start
            start = start + jnp.broadcast_to(r.lens_all[b, 0:1, row : row + 1], (1, 128))


    def offset_rows(i):
        b, tile = lax.div(i, 13), lax.rem(i, 13)
        starts = r.starts_all[b]
        at = lax.convert_element_type(z * 512 + tile * 40, F32)
        at = at + lax.broadcasted_iota(jnp.int32, (40, 128), 0).astype(F32)
        begun = jnp.zeros((40, 128), F32)
        for row in range(1, 5):
            start = starts[row : row + 1, :]
            begun = jnp.where(at >= start, start, begun)
        r.off[b, pl.ds(pl.multiple_of(tile * 40, 8), 40), :] = at - begun

    loop(52, offset_rows)

    def normalise(slot):
        def body(i):
            rows = pl.ds(pl.multiple_of(i * 32, 32), 32)
            v = r.x_all[slot, rows, :].astype(F32)
            s = lax.rsqrt(jnp.mean(v * v, axis=-1, keepdims=True) + NORM_EPS)
            r.normed[slot, rows, :] = (v * s * gain).astype(BF)

        loop(8, body)

    r.x_all[mine] = r.x[...]
    normalise(mine)
    tokens.sibling(0)
    normalise(net.slot(0, o))
    tokens.forward()
    heads_in.relay()
    gates_in.relay()
    out_in = along(lambda at: r.wq.at[at])
    feed = LineGather(
        net,
        [(r.wgu_out.at[core], core) for core in (c, o)],
        lambda j: r.wgu_all.at[q],
        lambda j, at: r.wgu_all.at[at * 2 + (c, o)[j]],
    )
    feed_down = LineGather(net, [(r.wmd.at[down], c)], lambda j: r.wmd_all.at[z], lambda j, at: r.wmd_all.at[at])
    tokens.middle()
    for k in (1, 2):
        normalise(net.slot(k, c))
    hand_over(heads_in, wi_rows, heads_in_over)
    for k in (1, 2):
        tokens.sibling(k)
        normalise(net.slot(k, o))
    gates_out = exchange(gates_in, r.gq, r.g3)
    arrange(heads_in_over, slice(128, 256), slice(256, 512))

    def project_inner(slot):
        b, half = lax.div(slot, 2), lax.rem(slot, 2)
        at = pl.multiple_of(half * 256, 256)
        inner = dot(r.normed[slot], r.w2[:, 256:512]).astype(BF).astype(F32)
        for n in range(2):
            r.inner[b * 2 + n, pl.ds(at + 8, 256), :] = inner[:, n * 128 : (n + 1) * 128]

    def project_gate(slot):
        b, half = lax.div(slot, 2), lax.rem(slot, 2)
        at = pl.multiple_of(half * 256, 256)
        gate = dot(r.normed[slot], r.w2[:, 0:256])
        for n in range(2):
            r.gp[b * 2 + n, pl.ds(at, 256), :] = gate[:, n * 128 : (n + 1) * 128]

    out_in.relay()
    for k in (0, 1, 2):
        project_inner(net.slot(k, c))
        project_inner(net.slot(k, o))
    tokens.last()
    normalise(net.slot(3, c))
    project_inner(net.slot(3, c))
    tokens.sibling(3)
    normalise(net.slot(3, o))
    project_inner(net.slot(3, o))
    edge = net.reserve(1)

    def edge_copy():
        return net.describe(
            r.inner.at[:, pl.ds(512, 8)], r.inner.at[:, pl.ds(0, 8)], net.line(net.up(1), c), edge, edge
        )

    @pl.when(z < 3)
    def _():
        edge_copy().start()

    @pl.when(z == 0)
    def _():
        r.inner[:, 0:8, :] = jnp.zeros((8, 8, 128), F32)

    gates_over = share(gates_out, r.g3)
    stored = net.local(r.normed, r.normed_far)
    cots = Gather(net, r.g_all.at[mine], r.g_all)
    cots.start(0)
    cots.start(1)
    tokens.release()
    gates_over.wait_recv()
    for i in range(4):
        at = c * 128 + i * 64
        value = r.g3[lax.div(at, 192), pl.ds(pl.multiple_of(lax.rem(at, 192), 64), 64), :]
        r.wri[i // 2, (i % 2) * 64 : (i % 2 + 1) * 64, :] = value
    heads_gate, heads_gate_over = heads_start(wg_rows)

    @pl.when(z > 0)
    def _():
        edge_copy().wait_recv()


    def conv_tile(i):
        b, tile = lax.div(i, 8), lax.rem(i, 8)
        rows = tile_rows(tile)
        offset = r.off[b, rows, :]
        for n in range(2):
            s = b * 2 + n
            window = r.inner[s, pl.ds(pl.multiple_of(tile * TILE, 8), TILE + 8), :]
            chan = r.chan[n]
            total = chan[4:5, :] + chan[0:1, :] * window[8:, :]
            for k in (1, 2, 3):
                total = total + chan[k : k + 1, :] * jnp.where(offset >= k, window[8 - k : TILE + 8 - k, :], 0.0)
            r.conv[s, rows, :] = total.astype(BF)

    loop(32, conv_tile)
    out_rows_in = exchange(out_in, r.wq, r.w3)

    def gate_products(i):
        s, half = lax.div(i, 2), lax.rem(i, 2)
        n = lax.rem(s, 2)
        rows = pl.ds(pl.multiple_of(half * 256, 256), 256)
        pre = dot(r.conv[s, rows, :], r.wri[n])
        r.sr[s, rows, :] = pre[:, :128]
        r.si[s, rows, :] = pre[:, 128:]

    loop(16, gate_products)
    heads_gate.relay()
    feed.start(2, (0,))

    def terms(b):
        starts_b = r.starts_all[b]

        def tile(i, sums):
            rows = tile_rows(i)
            offset = r.off[b, rows, :]
            at = lax.convert_element_type(z * 512 + i * TILE, F32)
            begun = at + lax.broadcasted_iota(jnp.int32, (TILE, 128), 0).astype(F32) - offset
            restart = offset == 0.0
            added = []
            for n in range(2):
                s = b * 2 + n
                chan = r.chan[n]
                sr = jax.nn.sigmoid(r.sr[s, rows, :] + chan[5:6, :])
                si = jax.nn.sigmoid(r.si[s, rows, :] + chan[6:7, :])
                r.sr[s, rows, :] = sr
                r.si[s, rows, :] = si
                a, m2 = decay_parts(sr, chan[7:8, :])
                r.dec[s, rows, :] = jnp.where(restart, 0.0, a)
                m = jnp.where(restart, 1.0, m2 * lax.rsqrt(m2))
                r.drv[s, rows, :] = m * si * r.conv[s, rows, :].astype(F32)
                for row in range(5):
                    inside = jnp.where(begun == starts_b[row : row + 1, :], a, 0.0)
                    added.append(sums[n * 5 + row] + column_sum(inside))
            return tuple(added)

        sums = lax.fori_loop(0, 512 // TILE, tile, tuple(jnp.zeros((8, 128), F32) for _ in range(10)))
        for n in range(2):
            rows = [jnp.sum(part, axis=0, keepdims=True) for part in sums[n * 5 : n * 5 + 5]]
            r.rs_all[z, b * 2 + n] = jnp.concatenate(rows + [jnp.zeros((3, 128), F32)], axis=0)

    loop(4, terms)
    cots.forward()
    ends = scan_slabs(r.dec, r.drv, False)
    ends = exchange_ends(r, net, ends, 0)
    feed.start(2, (1,))
    feed.start(1, (0, 1))
    feed.start(3, (0, 1))
    r.wgu_all[q] = r.wgu_out[c]
    feed_over = net.copy(r.wgu_out.at[o], r.wgu_all.at[q], sibling)
    hand_over(heads_gate, wg_rows, heads_gate_over)
    arrange(heads_gate_over, slice(0, 128), slice(0, 256))
    for made in handed:
        made.wait_send()
    heads_in.drain()
    heads_gate.drain()
    gates_in.drain()
    out_in.drain()
    for k in (2, 1, 3):
        feed_down.start(k, (0,))
    for slot in range(8):
        project_gate(slot)

    def gelu_tile(i):
        s, rows = lax.div(i, 8), tile_rows(lax.rem(i, 8))
        v = r.gp[s, rows, :]
        t = jnp.tanh(GELU_SCALE * v * (1.0 + GELU_CUBE * v * v))
        r.gb[s, rows, :] = 0.5 * v * (1.0 + t)

    loop(64, gelu_tile)
    out_over = share(out_rows_in, r.w3)
    entering_states(r, net, ends, 0, False)
    row_sums = [net.copy(r.rs_all.at[z], r.rs_all.at[z], net.line(net.up(k), c)) for k in (1, 2, 3)]
    out_over.wait_recv()

    def own_rows(i):
        at = c * 128 + i * 64
        value = r.w3[lax.div(at, 192), pl.ds(pl.multiple_of(lax.rem(at, 192), 64), 64), :]
        r.wo[pl.ds(pl.multiple_of(i * 64, 64), 64), :] = value

    loop(4, own_rows)
    for s in range(8):
        r.states[s, 7:8, :] = r.inc[s : s + 1, :]

    def mix_tile(i):
        s, tile = lax.div(i, 8), lax.rem(i, 8)
        b, n = lax.div(s, 2), lax.rem(s, 2)
        rows = tile_rows(tile)
        states = r.drv[s, rows, :] + r.dec[s, rows, :] * r.inc[pl.ds(s, 1), :]
        r.states[s, pl.ds(pl.multiple_of(tile * TILE + 8, 8), TILE), :] = states
        lanes = pl.ds(pl.multiple_of(n * 128, 128), 128)
        r.mixed[b * 2 + lax.div(tile, 4), tile_rows(lax.rem(tile, 4)), lanes] = (states * r.gb[s, rows, :]).astype(BF)

    loop(64, mix_tile)
    stored.wait()
    lane = lax.broadcasted_iota(jnp.int32, (1, 256), 1)
    counted = jnp.where((lane >= 64 * c) & (lane < 192 + 64 * c), 1.0, 0.0)
    counted_two = jnp.concatenate([counted, counted], axis=1)

    def masked(value, mask):
        return (value.astype(F32) * mask).astype(BF)

    total = Reduce(
        net, r, lambda k, core: dot(masked(r.mixed[net.slot(k, core)], counted), r.wo[...])
    )
    for k in (3, 1, 2, 0):
        total.other(k)
    total.far()
    total.near()
    cots.middle()
    total.own()
    cots.last()
    for k in (0, 1, 2, 3):
        cots.sibling(k)
    cots.release()
    total.relay()
    feed_down.relay()
    feed.relay()
    def wmd():
        return r.wmd_all[...].reshape(cols, -1)

    gain2 = r.gain[1:2, :]
    n2_all = r.normed
    acts = Gather(net, n2_all.at[mine], n2_all, tokens.at)
    for part in range(2):
        total.finish(part)
        for h in range(2):

            def residual_rows(i, h=h, part=part):
                i = part * 2 + i
                rows = pl.ds(pl.multiple_of(h * 128 + i * 32, 32), 32)
                v = r.x[rows, :].astype(F32) + total.total(h, i, 32)
                r.residual[rows, :] = v
                s = lax.rsqrt(jnp.mean(v * v, axis=-1, keepdims=True) + NORM_EPS)
                r.normed[mine, rows, :] = (v * s * gain2).astype(BF)

            loop(2, residual_rows)
        acts.start(part)

    def gate_up():
        return r.wgu_all[...].reshape(-1, 2 * cols)

    def d_normed2(k, core):
        return dot(r.dgu[net.slot(k, core)], gate_up(), NT)

    back = Reduce(net, r, d_normed2, total.at)

    def part(k, core):
        slot = net.slot(k, core)
        h = n2_all[slot]
        r.up[...] = dot(h, gate_up())

        def body(i):
            rows = pl.ds(pl.multiple_of(i * 32, 32), 32)
            gelu, slope = gelu_parts(r.up[rows, 0:cols])
            ul, dh = r.up[rows, cols:], r.dgu[slot, rows, 0:cols].astype(F32)
            r.hid[slot, rows, :] = (gelu * ul).astype(BF)
            r.dgu[slot, rows, 0:cols] = (dh * ul * slope).astype(BF)
            r.dgu[slot, rows, cols:] = (dh * gelu).astype(BF)

        loop(8, body)

    feed_down.end()
    for slot in range(8):
        r.dgu[slot, :, 0:cols] = dot(r.g_all[slot], wmd(), NT).astype(BF)
    feed_over.wait_recv()
    feed.end()
    part(0, c)
    acts.sibling(0)
    part(0, o)
    back.other(0)
    acts.forward()
    acts.middle()
    part(1, c)
    part(2, c)
    acts.sibling(1)
    part(1, o)
    back.other(1)
    acts.sibling(2)
    part(2, o)
    back.other(2)
    back.near()
    acts.last()
    acts.sibling(3)
    part(3, o)
    back.other(3)
    part(3, c)
    back.far()
    back.relay()
    back.own()
    acts.release()
    for i in range(4):
        rows = n2_all[:, :, i * 256 : (i + 1) * 256].reshape(-1, 256)
        r.gm[i] = dot(rows, r.dgu[...].reshape(-1, 2 * cols), TN).astype(BF)

    def gm_in(k):
        return r.wgi3.at[k - 1]

    mlp_m = LineSum(net, lambda t: r.gm.at[t], gm_in)
    mlp_m.start()
    hid = r.hid[...].reshape(-1, cols)
    for half in range(2):
        lanes = slice(half * 512, half * 512 + 512)
        value = dot(hid, r.g_all[:, :, lanes].reshape(-1, 512), TN).astype(BF)
        for i in range(4):
            r.gd[i, :, lanes] = value[i * piece : (i + 1) * piece, :]
    mlp_d = LineSum(net, lambda t: r.gd.at[t], lambda k: r.gd_in.at[k - 1], out_in.at)
    sums = jnp.zeros((8, r.x.shape[1]), F32)
    grads = Gather(net, r.do_all.at[mine], r.do_all, cots.at)
    for part in range(2):
        back.finish(part)
        for h in range(2):

            def residual_back(i, sums, h=h, part=part):
                i = part * 2 + i
                rows = pl.ds(pl.multiple_of(h * 128 + i * 32, 32), 32)
                v = r.residual[rows, :]
                dn = back.total(h, i, 32)
                s = lax.rsqrt(jnp.mean(v * v, axis=-1, keepdims=True) + NORM_EPS)
                u = dn * gain2
                pulled = s * u - v * (s * s * s * jnp.mean(u * v, axis=-1, keepdims=True))
                d_res = r.g_all[mine, rows, :].astype(F32) + pulled
                r.d_res[rows, :] = d_res
                r.do_all[mine, rows, :] = d_res.astype(BF)
                return sums + jnp.sum((dn * v * s).reshape(4, 8, -1), axis=0)

            sums = lax.fori_loop(0, 2, residual_back, sums)
        grads.start(part)
    r.gain2_sum[...] = sums

    owners, returned = [], []

    def to_chips(src, dst):
        for k in (1, 2, 3):
            owners.append(net.copy(src, dst.at[p], net.plane(k, c)))
        returned.append(net.local(src, dst.at[p]))

    fo_at = net.reserve(4)

    def vector_copy(k):
        return net.describe(r.vout.at[p], r.vout.at[p], net.plane(k, c), fo_at + k, fo_at)

    owners_m = Owners(net, r.gm_sum, r.fm, r.fm_x, tokens.at)
    owners_d = Owners(net, r.gd_sum, r.fd)
    owners_a = Owners(net, r.ga_sum, r.fa, r.fa_x, cots.at)
    owners_b = Owners(net, r.gb2_sum, r.fb)

    def mlp_sums():
        mlp_m.end(r.gm_sum)
        owners_m.start()

    def back_out(slot):
        b, half = lax.div(slot, 2), lax.rem(slot, 2)
        dm = dot(r.do_all[slot], r.wo[...], NT)
        for n in range(2):
            r.dconv[b * 2 + n, pl.ds(pl.multiple_of(half * 256, 256), 256), :] = dm[:, n * 128 : (n + 1) * 128]

    back_out(mine)
    grads.sibling(0)
    back_out(net.slot(0, o))
    out = Reduce(net, r, lambda k, core: dot(r.hid[net.slot(k, core)], wmd()), total.at)
    for k in (3, 1, 2, 0):
        out.other(k)
    grads.forward()
    out.far()
    out.near()
    out.own()
    grads.middle()
    mlp_m.relay()
    for k in (1, 2):
        back_out(net.slot(k, c))
    for k in (1, 2):
        grads.sibling(k)
        back_out(net.slot(k, o))
    grads.last()
    back_out(net.slot(3, c))
    grads.sibling(3)
    back_out(net.slot(3, o))

    def first_pass(i):
        b, tile = lax.div(i, 8), lax.rem(i, 8)
        rows = tile_rows(tile)
        live = r.off[b, rows, :] != 0.0
        for n in range(2):
            s = b * 2 + n
            gelu, slope = gelu_parts(r.gp[s, rows, :])
            dm = r.dconv[s, rows, :]
            states = r.states[s, pl.ds(pl.multiple_of(tile * TILE + 8, 8), TILE), :]
            lanes = slice(n * 128, (n + 1) * 128)
            r.dgi[b * 2 + lax.div(tile, 4), tile_rows(lax.rem(tile, 4)), lanes] = (dm * states * slope).astype(BF)
            r.drv[s, rows, :] = dm * gelu
            a = jnp.exp(-DECAY_SCALE * r.sr[s, rows, :] * r.chan[n, 7:8, :])
            r.dec[s, rows, :] = jnp.where(live, a, 0.0)

    loop(32, first_pass)
    ends = scan_slabs(r.dec, r.drv, True)
    ends = exchange_ends(r, net, ends, 1)
    out.relay()
    go_in, go_line_in = r.go_q, r.go_l
    mixed = r.mixed[...].reshape(-1, 256)
    for half in range(2):
        lanes = slice(half * 512, half * 512 + 512)
        r.go[:, lanes] = dot(mixed, r.do_all[:, :, lanes].reshape(-1, 512), TN).astype(BF)
    grads.release()
    fetched = net.local(r.normed_far, r.do_all)
    go_rows = [pl.ds(pl.multiple_of(c * 64 + near * 48, 16), 48) for near in net.near]

    def go_start(lanes):
        return [net.copy(r.go.at[go_rows[k], lanes], go_in.at[p, :, lanes], net.plane(k, c)) for k in (1, 2, 3)]

    go_out = go_start(pl.ds(0, 1024))
    entering_states(r, net, ends, 1, True)
    r.vec[...] = jnp.zeros((2, 8, 8, 128), F32)
    dri = r.normed

    def second_pass(s):
        b, n = lax.div(s, 2), lax.rem(s, 2)
        chan = r.chan[n]
        enter = r.inc[pl.ds(s, 1), :]
        lanes_r = pl.ds(pl.multiple_of(n * 256, 128), 128)
        lanes_i = pl.ds(pl.multiple_of(n * 256 + 128, 128), 128)

        def tile(i, sums):
            rows = tile_rows(i)
            live = r.off[b, rows, :] != 0.0
            ds = r.drv[s, rows, :] + r.dec[s, rows, :] * enter
            window = r.states[s, pl.ds(pl.multiple_of(i * TILE, 8), TILE + 8), :]
            before = window[7 : TILE + 7, :]
            sr, si = r.sr[s, rows, :], r.si[s, rows, :]
            cv = r.conv[s, rows, :].astype(F32)
            a, m2 = decay_parts(sr, chan[7:8, :])
            inv = lax.rsqrt(m2)
            m = jnp.where(live, m2 * inv, 1.0)
            dsi = ds * si
            d_log = jnp.where(live, a * (ds * before - dsi * cv * a * inv), 0.0)
            lam_term = d_log * sr
            d_r = (-DECAY_SCALE) * chan[7:8, :] * lam_term * (1.0 - sr)
            dm_i = dsi * m
            d_i = dm_i * cv * (1.0 - si)
            d_r, d_i = d_r.astype(BF), d_i.astype(BF)
            at = tile_rows(lax.rem(i, 4))
            dri[b * 2 + lax.div(i, 4), at, lanes_r] = d_r
            dri[b * 2 + lax.div(i, 4), at, lanes_i] = d_i
            r.dconv[s, rows, :] = dm_i
            return (
                sums[0] + column_sum(d_r.astype(F32)),
                sums[1] + column_sum(d_i.astype(F32)),
                sums[2] + column_sum(lam_term),
            )

        zero = jnp.zeros((8, 128), F32)
        sums = lax.fori_loop(0, 512 // TILE, tile, (zero, zero, zero))
        for j in range(3):
            r.vec[n, 5 + j] = r.vec[n, 5 + j] + sums[j]

    loop(8, second_pass)
    mlp_sums()

    def gate_back(i):
        s, half = lax.div(i, 2), lax.rem(i, 2)
        b, n = lax.div(s, 2), lax.rem(s, 2)
        rows = pl.ds(pl.multiple_of(half * 256, 256), 256)
        lanes = pl.ds(pl.multiple_of(n * 256, 256), 256)
        r.dconv[s, rows, :] = r.dconv[s, rows, :] + dot(dri[b * 2 + half, :, lanes], r.wri[n], NT)

    loop(16, gate_back)
    edge_back = net.reserve(1)

    def edge_back_copy():
        return net.describe(
            r.dconv.at[:, pl.ds(0, 8)], r.dconv.at[:, pl.ds(512, 8)], net.line(net.down(1), c), edge_back, edge_back
        )

    @pl.when(z > 0)
    def _():
        edge_back_copy().start()

    mlp_d.start()

    @pl.when(z == 3)
    def _():
        r.dconv[:, 512:520, :] = jnp.zeros((8, 8, 128), F32)

    for n in range(2):
        total_ri = None
        for b in range(4):
            for half in range(2):
                term = dot(
                    r.conv[b * 2 + n, half * 256 : (half + 1) * 256, :],
                    dri[b * 2 + half, :, n * 256 : (n + 1) * 256],
                    TN,
                )
                total_ri = term if total_ri is None else total_ri + term
        r.go[n * 128 : (n + 1) * 128, 1024:1280] = total_ri.astype(BF)
    go_out += go_start(pl.ds(1024, 256))

    @pl.when(z < 3)
    def _():
        edge_back_copy().wait_recv()


    def conv_back(s):
        b, n = lax.div(s, 2), lax.rem(s, 2)
        chan = r.chan[n]
        lanes = pl.ds(pl.multiple_of(256 + n * 128, 128), 128)

        def tile(i, sums):
            offset = r.off[b, pl.ds(pl.multiple_of(i * TILE, 8), TILE + 8), :]
            window = r.dconv[s, pl.ds(pl.multiple_of(i * TILE, 8), TILE + 8), :]
            inner = r.inner[s, pl.ds(pl.multiple_of(i * TILE, 8), TILE + 8), :]
            value = chan[0:1, :] * window[:TILE, :]
            added = [sums[0] + column_sum(window[:TILE, :] * inner[8:, :])]
            for k in (1, 2, 3):
                held = jnp.where(offset >= k, window, 0.0)
                value = value + chan[k : k + 1, :] * held[k : TILE + k, :]
                added.append(sums[k] + column_sum(held[:TILE, :] * inner[8 - k : TILE + 8 - k, :]))
            added.append(sums[4] + column_sum(window[:TILE, :]))
            r.dgi[b * 2 + lax.div(i, 4), tile_rows(lax.rem(i, 4)), lanes] = value.astype(BF)
            return tuple(added)

        sums = lax.fori_loop(0, 512 // TILE, tile, tuple(jnp.zeros((8, 128), F32) for _ in range(5)))
        for j in range(5):
            r.vec[n, j] = r.vec[n, j] + sums[j]

    loop(8, conv_back)
    out.finish(0)
    out.finish(1)
    for h in range(2):

        def out_rows(i, h=h):
            rows = pl.ds(pl.multiple_of(h * 128 + i * 32, 32), 32)
            value = (r.residual[rows, :] + out.total(h, i, 32)).astype(BF)
            for j in range(4):
                r.dgu[j, rows, 512:768] = value[:, j * 256 : (j + 1) * 256]

        loop(4, out_rows)
    for j in range(4):
        returned.append(net.local(r.dgu.at[j, :, pl.ds(512, 256)], r.block_out.at[:, pl.ds(j * 256, 256)]))
    for partner in (sibling, net.plane(1, c), net.plane(2, c)):
        pl.semaphore_signal(r.free, inc=1, device_id=partner, device_id_type=pl.DeviceIdType.MESH)
    for n in range(2):
        sums = [jnp.sum(r.vec[n, j], axis=0, keepdims=True) for j in range(8)]
        sums[7] = sums[7] * (DECAY_SCALE * r.chan[n, 8:9, :])
        r.vsum[z, :, n * 128 : (n + 1) * 128] = jnp.concatenate(sums, axis=0)
    vec = [net.copy(r.vsum.at[z], r.vsum.at[z], net.line(net.up(k), c)) for k in (1, 2, 3)]
    fetched.wait()
    flat = r.dgi[:, :, 0:512].reshape(-1, 512)
    for i in range(4):
        value = dot(r.do_all[:, :, i * 256 : (i + 1) * 256].reshape(-1, 256), flat, TN)
        for j in range(2):
            n0, n1 = value[:, j * 256 : j * 256 + 128], value[:, j * 256 + 128 : j * 256 + 256]
            r.ga[i][:, j * 128 : (j + 1) * 128] = lax.select(c == 0, n0, n1).astype(BF)
            shared = lax.select(c == 0, n1, n0)
            r.gb2[i][:, j * 128 : (j + 1) * 128] = lax.select(c == 0, shared[0:128], shared[128:256]).astype(BF)

    def ga_in(k):
        return r.g_all.at[7, :, pl.ds((k - 1) * 256, 256)]

    def gb_in(k):
        return r.g_all.at[3 + k, pl.ds(128, 128), pl.ds(0, 256)]

    sum_a = LineSum(net, lambda t: r.hid.at[t, :, 0:256], ga_in, heads_in.at)
    sum_b = LineSum(net, lambda t: r.hid.at[4 + t, 0:128, 0:256], gb_in, heads_gate.at)
    sum_a.start()
    sum_b.start()
    mlp_d.relay()
    owners_m.forward()
    first_back = Reduce(
        net,
        r,
        lambda k, core: dot(masked(r.dgi[net.slot(k, core), :, 0:512], counted_two), r.w2[...], NT),
        total.at,
    )
    pl.semaphore_wait(r.free, 3)
    for k in (3, 1, 2, 0):
        first_back.other(k)
    first_back.far()
    first_back.near()
    go_in[p] = r.go[go_rows[0], :]
    for made in go_out:
        made.wait_recv()
    go_line = LineSum(net, lambda t: go_in.at[t], lambda k: go_line_in.at[k - 1], gates_in.at)
    go_line.start()
    first_back.relay()
    mlp_d.end(r.gd_sum)
    owners_d.start()
    first_back.own()
    owners_m.middle()
    sum_a.relay()
    sum_b.relay()
    go_line.relay()
    first_back.finish(0)
    first_back.finish(1)
    sums = jnp.zeros((8, r.x.shape[1]), F32)
    for h in range(2):

        def input_rows(i, sums, h=h):
            rows = pl.ds(pl.multiple_of(h * 128 + i * 32, 32), 32)
            v = r.x[rows, :].astype(F32)
            dn = first_back.total(h, i, 32)
            s = lax.rsqrt(jnp.mean(v * v, axis=-1, keepdims=True) + NORM_EPS)
            u = dn * r.gain[0:1, :]
            r.d_res[rows, :] = r.d_res[rows, :] + (
                s * u - v * (s * s * s * jnp.mean(u * v, axis=-1, keepdims=True))
            )
            return sums + jnp.sum((dn * v * s).reshape(4, 8, -1), axis=0)

        sums = lax.fori_loop(0, 4, input_rows, sums)
    returned.append(net.local(r.d_res, r.d_in))
    gains = jnp.concatenate(
        [
            jnp.sum(sums, axis=0, keepdims=True),
            jnp.sum(r.gain2_sum[...], axis=0, keepdims=True),
            jnp.zeros((6, sums.shape[1]), F32),
        ],
        axis=0,
    )
    for i in range(8):
        r.gsum[i] = gains[:, i * 128 : (i + 1) * 128]
    r.gline[q] = r.gsum[q]
    gain_line = [
        net.copy(r.gsum.at[net.up(k) * 2 + core], r.gline.at[q], net.line(net.up(k), core))
        for k in (1, 2, 3)
        for core in (c, o)
    ]
    gain_line.append(net.copy(r.gsum.at[z * 2 + o], r.gline.at[q], sibling))
    for made in row_sums:
        made.wait_recv()
    r.rows_sum[...] = r.rs_all[0] + r.rs_all[1] + r.rs_all[2] + r.rs_all[3]
    for k in (1, 2, 3):
        for core in (c, o):
            owners.append(net.copy(r.rows_sum.at[pl.ds(net.near[k] * 2, 2)], r.fr.at[mine], net.plane(k, core)))
    owners.append(net.copy(r.rows_sum.at[pl.ds(p * 2, 2)], r.fr.at[mine], sibling))
    returned.append(net.local(r.rows_sum.at[pl.ds(p * 2, 2)], r.fr.at[mine]))
    for made in vec:
        made.wait_recv()
    r.vout[p] = r.vsum[0] + r.vsum[1] + r.vsum[2] + r.vsum[3]

    @pl.when(z == p)
    def _():
        for k in (1, 2, 3):
            vector_copy(k).start()

    sum_a.end(r.ga_sum)
    owners_a.start()
    sum_b.end(r.gb2_sum)
    owners_b.start()
    go_line.end(r.go_sum)
    to_chips(r.go_sum, r.fo)
    owners_d.forward()
    owners_m.last()
    owners_a.forward()
    owners_b.forward()
    for made in gain_line:
        made.wait_recv()
    sums = r.gline[0]
    for i in range(1, 8):
        sums = sums + r.gline[i]
    r.gplane[p] = sums
    gain_plane = [net.copy(r.gplane.at[p], r.gplane.at[p], net.plane(k, c)) for k in (1, 2, 3)]

    @pl.when(z != p)
    def _():
        vector_copy(1).wait_recv()

    @pl.when(z == p)
    def _():
        for k in (1, 2, 3):
            vector_copy(k).wait_send()

    owners_d.middle()
    owners_a.middle()
    owners_b.middle()
    for each in (owners_d, owners_a, owners_b):
        each.last()
    for each in (owners_m, owners_d, owners_a, owners_b):
        each.end()
    for made in owners + gain_plane:
        made.wait_recv()
    r.gain_out[...] = r.gplane[0] + r.gplane[1] + r.gplane[2] + r.gplane[3]
    r.vec_out[...] = r.vout[z]
    for made in returned:
        made.wait()
    @pl.when(z < 3)
    def _():
        edge_copy().wait_send()

    @pl.when(z > 0)
    def _():
        edge_back_copy().wait_send()

    feed.drain()
    feed_down.drain()
    for made in (mlp_m, mlp_d, go_line, sum_a, sum_b):
        made.drain()
    net.drain()


def assemble(r):
    c = lax.rem(lax.axis_index("seq"), 2)
    count = 0
    stores = []

    def start(src, dst):
        nonlocal count
        made = pltpu.make_async_copy(src, dst, r.local.at[count])
        count += 1
        made.start()
        return made

    mine = pl.ds(pl.multiple_of(c * 128, 128), 128)
    loads = [
        [start(r.fm.at[:, mine], r.vm.at[c]), start(r.fm_x, r.vm.at[1 - c])],
        [start(r.fa.at[:, mine], r.va.at[c]), start(r.fa_x, r.va.at[1 - c]), start(r.fb, r.vb)],
        [start(r.fd, r.vd)],
        [start(r.fo, r.vo)],
    ]

    def loaded(which):
        for made in loads[which]:
            made.wait()

    little = [start(r.vec_in, r.v_vec), start(r.gains, r.v_gains), start(r.fr, r.v_fr), start(r.lens, r.v_lens)]
    passed = [start(r.d_in, r.v_din), start(r.block_out, r.v_block)]
    cols = r.fm.shape[2] // 2
    piece = cols // 4
    loaded(0)
    for j, (stage, out) in enumerate(((r.s_mgate, r.o_mgate), (r.s_mup, r.o_mup))):
        for part in range(4):
            for core in range(2):
                at = (part * 2 + core) * cols
                lanes = slice(j * cols + part * piece, j * cols + (part + 1) * piece)
                stage[:, at : at + cols] = jnp.concatenate(
                    [r.vm[core, chip, :, lanes].astype(F32) for chip in range(4)], axis=1
                )
            here = pl.ds(part * 2 * cols, 2 * cols)
            stores.append(start(stage.at[:, here], out.at[:, here]))
    for made, src, dst in zip(passed, (r.v_din, r.v_block), (r.o_din, r.o_block)):
        made.wait()
        stores.append(start(src, dst))
    loaded(1)
    for j, (stage, out) in enumerate(((r.s_gate, r.o_gate), (r.s_in, r.o_in))):
        lanes = slice(j * 128, (j + 1) * 128)
        for chip in range(4):
            at = chip * 384
            stage[:, at : at + 128] = r.va[0, chip, :, lanes].astype(F32)
            stage[:, at + 128 : at + 256] = r.vb[chip, :, lanes].astype(F32)
            stage[:, at + 256 : at + 384] = r.va[1, chip, :, lanes].astype(F32)
        stores.append(start(stage, out))
    loaded(2)
    for chip in range(4):
        r.s_down[chip * piece : (chip + 1) * piece, :] = r.vd[chip].astype(F32)
    stores.append(start(r.s_down, r.o_mdown))
    for made in little:
        made.wait()
    vec = r.v_vec[...]
    vec = lax.select(c == 0, vec[:, 0:192], vec[:, 64:256])
    r.s_cw[...] = vec[0:4]
    stores.append(start(r.s_cw, r.o_cw))
    for j, (stage, out) in enumerate(((r.s_cb, r.o_cb), (r.s_rb, r.o_rb), (r.s_ib, r.o_ib), (r.s_lam, r.o_lam))):
        stage[...] = vec[4 + j : 5 + j]
        stores.append(start(stage, out))
    for j, (stage, out) in enumerate(((r.s_ngain, r.o_ngain), (r.s_mgain, r.o_mgain))):
        stage[...] = r.v_gains[j : j + 1, :]
        stores.append(start(stage, out))
    counts = [jnp.broadcast_to(r.v_lens[0:1, row : row + 1].astype(F32), (1, 128)) for row in range(5)]
    for chip in range(4):
        for half, (slot, n) in enumerate(((chip * 2, 0), (chip * 2, 1), (chip * 2 + 1, 1))):
            at = chip * 384 + half * 128
            for row in range(5):
                r.s_mean[row, :, at : at + 128] = r.v_fr[slot, n, row : row + 1, :] / counts[row]
    stores.append(start(r.s_mean, r.o_mean))
    loaded(3)
    for chip in range(4):
        rows = slice(chip * 48, (chip + 1) * 48)
        r.s_out[rows, :] = r.vo[chip, :, 0:1024].astype(F32)
        r.s_r[rows, :] = r.vo[chip, :, 1024:1152].astype(F32)
        r.s_i[rows, :] = r.vo[chip, :, 1152:1280].astype(F32)
    for stage, out in ((r.s_out, r.o_out), (r.s_r, r.o_r), (r.s_i, r.o_i)):
        stores.append(start(stage, out))
    for made in stores:
        made.wait()


def shifted(value, axis, by):
    count = lax.axis_size(axis)
    pairs = [(i, i + by) for i in range(count) if 0 <= i + by < count]
    return lax.ppermute(value, axis, pairs)


def entering(value, axis, combine, identity, reverse):
    count, place = (lax.axis_size(axis), lax.axis_index(axis))
    everything = jax.tree.map(lambda part: lax.all_gather(part, axis), value)
    start = jax.tree.map(
        lambda part, zero: jnp.broadcast_to(jnp.asarray(zero, part.dtype), part.shape),
        value,
        identity,
    )

    def step(k, before):
        at = count - 1 - k if reverse else k
        reached = at > place if reverse else at < place
        new = combine(before, jax.tree.map(lambda part: part[at], everything))
        return jax.tree.map(lambda a, b: jnp.where(reached, a, b), new, before)

    return lax.fori_loop(0, count, step, start)


def rms_scale(values):
    return values * lax.rsqrt(jnp.mean(values * values, axis=-1, keepdims=True) + NORM_EPS)


def gelu_tanh(values):
    return jax.nn.gelu(values, approximate=True)


def link(earlier, later):
    return (earlier[0] * later[0], later[0] * earlier[1] + later[1])


def block_product(values, weight):
    count, channels = values.shape
    block_size = weight.shape[1]
    shaped = values.reshape(count, channels // block_size, block_size)
    result = jnp.einsum(
        "lni,nij->lnj",
        shaped,
        weight.reshape(channels // block_size, block_size, block_size),
        preferred_element_type=jnp.float32,
    )
    return result.reshape(count, channels)


def block_back(grads, weight):
    count, channels = grads.shape
    block_size = weight.shape[1]
    shaped = grads.reshape(count, channels // block_size, block_size)
    result = jnp.einsum(
        "lnj,nij->lni",
        shaped,
        weight.reshape(channels // block_size, block_size, block_size),
        preferred_element_type=jnp.float32,
    )
    return result.reshape(count, channels)


def block_weight_grad(values, grads, block_size):
    count, channels = values.shape
    left = values.reshape(count, channels // block_size, block_size)
    right = grads.reshape(count, channels // block_size, block_size)
    return jnp.einsum("lni,lnj->nij", left, right, preferred_element_type=jnp.float32).reshape(
        channels, block_size
    )


def recurrence_terms(conv_in, r_in, i_in, lam_in, restart):
    log_a = -DECAY_SCALE * jax.nn.sigmoid(r_in) * jax.nn.softplus(-lam_in)
    decays = jnp.exp(log_a)
    factor = jnp.where(restart[:, None] > 0, 1.0, jnp.sqrt(-jnp.expm1(2.0 * log_a)))
    return (decays * (1.0 - restart[:, None]), factor * jax.nn.sigmoid(i_in) * conv_in, decays)


def shards(
    inputs,
    out_grad,
    row_lengths,
    norm_gain,
    w_gate,
    w_in,
    conv_w,
    conv_b,
    w_rgate,
    b_rgate,
    w_igate,
    b_igate,
    lam,
    w_out,
    mlp_gain,
    w_mlp_gate,
    w_mlp_up,
    w_mlp_down,
):
    gathered = (
        lax.all_gather(norm_gain, "seq", axis=0, tiled=True),
        lax.all_gather(w_gate, "seq", axis=0, tiled=True),
        lax.all_gather(w_in, "seq", axis=0, tiled=True),
        lax.all_gather(conv_w, "seq", axis=1, tiled=True),
        lax.all_gather(conv_b, "seq", axis=0, tiled=True),
        lax.all_gather(w_rgate, "seq", axis=0, tiled=True),
        lax.all_gather(b_rgate, "seq", axis=0, tiled=True),
        lax.all_gather(w_igate, "seq", axis=0, tiled=True),
        lax.all_gather(b_igate, "seq", axis=0, tiled=True),
        lax.all_gather(lam, "seq", axis=0, tiled=True),
        lax.all_gather(w_out, "seq", axis=0, tiled=True),
        lax.all_gather(mlp_gain, "seq", axis=0, tiled=True),
        lax.all_gather(w_mlp_gate, "seq", axis=0, tiled=True),
        lax.all_gather(w_mlp_up, "seq", axis=0, tiled=True),
        lax.all_gather(w_mlp_down, "seq", axis=0, tiled=True),
    )
    gain_first = gathered[0].astype(jnp.float32)
    conv_taps = gathered[3].astype(jnp.float32)
    conv_bias = gathered[4].astype(jnp.float32)
    lam_value = gathered[9].astype(jnp.float32)
    gain_second = gathered[11].astype(jnp.float32)
    tokens = inputs[0].astype(jnp.float32)
    local_len = tokens.shape[0]
    channels = gathered[2].shape[1]
    block_size = gathered[5].shape[1]
    kernel_taps = conv_taps.shape[0]
    lengths = row_lengths[0]
    row_ends = jnp.cumsum(lengths)
    row_starts = row_ends - lengths
    positions = lax.axis_index("seq") * local_len + jnp.arange(local_len, dtype=jnp.int32)
    started = positions[:, None] >= row_starts[None, :]
    row_index = jnp.sum(started.astype(jnp.int32), axis=1) - 1
    row_first = jnp.max(jnp.where(started, row_starts[None, :], 0), axis=1)
    offset = positions - row_first
    restart = (offset == 0).astype(jnp.float32)
    members = (row_index[:, None] == jnp.arange(lengths.shape[0], dtype=jnp.int32)[None, :]).astype(
        jnp.float32
    )
    tap_masks = [(offset >= tap).astype(jnp.float32)[:, None] for tap in range(kernel_taps)]
    scaled, norm_pull = jax.vjp(rms_scale, tokens)
    normed = (scaled * gain_first).astype(jnp.bfloat16)
    gate_pre = jnp.dot(normed, gathered[1], preferred_element_type=jnp.float32)
    gate_branch, gate_pull = jax.vjp(gelu_tanh, gate_pre)
    inner = jnp.dot(normed, gathered[2], preferred_element_type=jnp.float32).astype(jnp.bfloat16)
    edge_rows = shifted(inner[local_len - kernel_taps + 1 :], "seq", 1)
    extended = jnp.concatenate([edge_rows, inner], axis=0).astype(jnp.float32)
    conv_sum = conv_bias + jnp.zeros((local_len, channels), jnp.float32)
    for tap in range(kernel_taps):
        start_row = kernel_taps - 1 - tap
        conv_sum = (
            conv_sum + conv_taps[tap] * extended[start_row : start_row + local_len] * tap_masks[tap]
        )
    conv_low = conv_sum.astype(jnp.bfloat16)
    conv_value = conv_low.astype(jnp.float32)
    r_pre = block_product(conv_low, gathered[5]) + gathered[6].astype(jnp.float32)
    i_pre = block_product(conv_low, gathered[7]) + gathered[8].astype(jnp.float32)

    def local_terms(conv_in, r_in, i_in, lam_in):
        return recurrence_terms(conv_in, r_in, i_in, lam_in, restart)

    (carried, drive_term, decays), recur_pull = jax.vjp(
        local_terms, conv_value, r_pre, i_pre, lam_value
    )
    prefix_decay, local_state = lax.associative_scan(link, (carried, drive_term), axis=0)
    identity = (jnp.ones((channels,), jnp.float32), jnp.zeros((channels,), jnp.float32))
    incoming = entering((prefix_decay[-1], local_state[-1]), "seq", link, identity, False)[1]
    states = local_state + prefix_decay * incoming
    mixed_low = (states * gate_branch).astype(jnp.bfloat16)
    residual = tokens + jnp.dot(mixed_low, gathered[10], preferred_element_type=jnp.float32)
    scaled_two, norm_pull_two = jax.vjp(rms_scale, residual)
    normed_two = (scaled_two * gain_second).astype(jnp.bfloat16)
    up_gate = jnp.dot(normed_two, gathered[12], preferred_element_type=jnp.float32)
    up_lin = jnp.dot(normed_two, gathered[13], preferred_element_type=jnp.float32)
    gelu_up, up_pull = jax.vjp(gelu_tanh, up_gate)
    hidden = (gelu_up * up_lin).astype(jnp.bfloat16)
    block_out = (
        residual + jnp.dot(hidden, gathered[14], preferred_element_type=jnp.float32)
    ).astype(jnp.bfloat16)
    row_sums = lax.psum(jnp.dot(members.T, decays, precision=lax.Precision.HIGHEST), "seq")
    gate_mean = row_sums / lengths.astype(jnp.float32)[:, None]
    grad_top = out_grad[0]
    grad_mdown = jnp.einsum("tf,td->fd", hidden, grad_top, preferred_element_type=jnp.float32)
    d_hidden = jnp.einsum("td,fd->tf", grad_top, gathered[14], preferred_element_type=jnp.float32)
    d_upgate = up_pull(d_hidden * up_lin)[0].astype(jnp.bfloat16)
    d_uplin = (d_hidden * gelu_up).astype(jnp.bfloat16)
    grad_mgate = jnp.einsum("td,tf->df", normed_two, d_upgate, preferred_element_type=jnp.float32)
    grad_mup = jnp.einsum("td,tf->df", normed_two, d_uplin, preferred_element_type=jnp.float32)
    d_normed_two = jnp.einsum(
        "tf,df->td", d_upgate, gathered[12], preferred_element_type=jnp.float32
    )
    d_normed_two = d_normed_two + jnp.einsum(
        "tf,df->td", d_uplin, gathered[13], preferred_element_type=jnp.float32
    )
    grad_mgain = jnp.sum(d_normed_two * scaled_two, axis=0)
    d_residual = grad_top.astype(jnp.float32) + norm_pull_two(d_normed_two * gain_second)[0]
    d_outlow = d_residual.astype(jnp.bfloat16)
    grad_outw = jnp.einsum("tr,td->rd", mixed_low, d_outlow, preferred_element_type=jnp.float32)
    d_mixed = jnp.einsum("td,rd->tr", d_outlow, gathered[10], preferred_element_type=jnp.float32)
    direct = d_mixed * gate_branch
    d_gatelow = gate_pull(d_mixed * states)[0].astype(jnp.bfloat16)
    grad_gatew = jnp.einsum("td,tr->dr", normed, d_gatelow, preferred_element_type=jnp.float32)
    next_decay = jnp.concatenate([carried[1:], jnp.ones((1, channels), jnp.float32)], axis=0)
    suffix_decay, local_grad = lax.associative_scan(
        link, (next_decay, direct), axis=0, reverse=True
    )
    arriving = entering(
        (carried[0] * suffix_decay[0], carried[0] * local_grad[0]), "seq", link, identity, True
    )[1]
    d_states = local_grad + suffix_decay * arriving
    previous = jnp.concatenate([incoming[None, :], states[:-1]], axis=0)
    grad_convval, d_rpre, d_ipre, grad_lambda = recur_pull(
        (d_states * previous, d_states, jnp.zeros_like(decays))
    )
    d_rlow = d_rpre.astype(jnp.bfloat16)
    d_ilow = d_ipre.astype(jnp.bfloat16)
    grad_rw = block_weight_grad(conv_low, d_rlow, block_size)
    grad_rb = jnp.sum(d_rlow.astype(jnp.float32), axis=0)
    grad_iw = block_weight_grad(conv_low, d_ilow, block_size)
    grad_ib = jnp.sum(d_ilow.astype(jnp.float32), axis=0)
    grad_convsum = grad_convval + block_back(d_rlow, gathered[5]) + block_back(d_ilow, gathered[7])
    grad_cb = jnp.sum(grad_convsum, axis=0)
    conv_again = gathered[3].astype(jnp.float32)
    grad_extended = jnp.zeros((local_len + kernel_taps - 1, channels), jnp.float32)
    tap_grads = []
    for tap in range(kernel_taps):
        start_row = kernel_taps - 1 - tap
        masked = grad_convsum * tap_masks[tap]
        tap_grads.append(jnp.sum(masked * extended[start_row : start_row + local_len], axis=0))
        grad_extended = grad_extended + jnp.pad(
            masked * conv_again[tap], ((start_row, tap), (0, 0))
        )
    grad_cw = jnp.stack(tap_grads)
    edge_grads = shifted(grad_extended[: kernel_taps - 1], "seq", -1)
    d_inner = (
        grad_extended[kernel_taps - 1 :]
        + jnp.pad(edge_grads, ((local_len - kernel_taps + 1, 0), (0, 0)))
    ).astype(jnp.bfloat16)
    grad_inw = jnp.einsum("td,tr->dr", normed, d_inner, preferred_element_type=jnp.float32)
    d_normed = jnp.einsum("tr,dr->td", d_gatelow, gathered[1], preferred_element_type=jnp.float32)
    d_normed = d_normed + jnp.einsum(
        "tr,dr->td", d_inner, gathered[2], preferred_element_type=jnp.float32
    )
    grad_gain = jnp.sum(d_normed * scaled, axis=0)
    d_tokens = d_residual + norm_pull(d_normed * gain_first)[0]
    shares = (
        lax.psum_scatter(grad_gain, "seq", scatter_dimension=0, tiled=True),
        lax.psum_scatter(grad_gatew, "seq", scatter_dimension=0, tiled=True),
        lax.psum_scatter(grad_inw, "seq", scatter_dimension=0, tiled=True),
        lax.psum_scatter(grad_cw, "seq", scatter_dimension=1, tiled=True),
        lax.psum_scatter(grad_cb, "seq", scatter_dimension=0, tiled=True),
        lax.psum_scatter(grad_rw, "seq", scatter_dimension=0, tiled=True),
        lax.psum_scatter(grad_rb, "seq", scatter_dimension=0, tiled=True),
        lax.psum_scatter(grad_iw, "seq", scatter_dimension=0, tiled=True),
        lax.psum_scatter(grad_ib, "seq", scatter_dimension=0, tiled=True),
        lax.psum_scatter(grad_lambda, "seq", scatter_dimension=0, tiled=True),
        lax.psum_scatter(grad_outw, "seq", scatter_dimension=0, tiled=True),
        lax.psum_scatter(grad_mgain, "seq", scatter_dimension=0, tiled=True),
        lax.psum_scatter(grad_mgate, "seq", scatter_dimension=0, tiled=True),
        lax.psum_scatter(grad_mup, "seq", scatter_dimension=0, tiled=True),
        lax.psum_scatter(grad_mdown, "seq", scatter_dimension=0, tiled=True),
    )
    totals = (
        lax.psum(shares[0].astype(jnp.bfloat16), "batch").astype(jnp.float32),
        lax.psum(shares[1].astype(jnp.bfloat16), "batch").astype(jnp.float32),
        lax.psum(shares[2].astype(jnp.bfloat16), "batch").astype(jnp.float32),
        lax.psum(shares[3].astype(jnp.bfloat16), "batch").astype(jnp.float32),
        lax.psum(shares[4].astype(jnp.bfloat16), "batch").astype(jnp.float32),
        lax.psum(shares[5].astype(jnp.bfloat16), "batch").astype(jnp.float32),
        lax.psum(shares[6].astype(jnp.bfloat16), "batch").astype(jnp.float32),
        lax.psum(shares[7].astype(jnp.bfloat16), "batch").astype(jnp.float32),
        lax.psum(shares[8].astype(jnp.bfloat16), "batch").astype(jnp.float32),
        lax.psum(shares[9].astype(jnp.bfloat16), "batch").astype(jnp.float32),
        lax.psum(shares[10].astype(jnp.bfloat16), "batch").astype(jnp.float32),
        lax.psum(shares[11].astype(jnp.bfloat16), "batch").astype(jnp.float32),
        lax.psum(shares[12].astype(jnp.bfloat16), "batch").astype(jnp.float32),
        lax.psum(shares[13].astype(jnp.bfloat16), "batch").astype(jnp.float32),
        lax.psum(shares[14].astype(jnp.bfloat16), "batch").astype(jnp.float32),
    )
    return (
        block_out[None],
        d_tokens[None],
        totals[0],
        totals[1],
        totals[2],
        totals[3],
        totals[4],
        totals[5],
        totals[6],
        totals[7],
        totals[8],
        totals[9],
        totals[10],
        totals[11],
        totals[12],
        totals[13],
        totals[14],
        gate_mean[None],
    )


def planes(
    inputs,
    out_grad,
    row_lengths,
    norm_gain,
    w_gate,
    w_in,
    conv_w,
    conv_b,
    w_rgate,
    b_rgate,
    w_igate,
    b_igate,
    lam,
    w_out,
    mlp_gain,
    w_mlp_gate,
    w_mlp_up,
    w_mlp_down,
):
    vmem = pltpu.VMEM
    done = kernel_call(
        layer,
        dict(
            x_in=inputs[0], cw=conv_w, cb=conv_b, br=b_rgate, bi=b_igate, lam=lam, ngain=norm_gain, mgain=mlp_gain,
            lens=row_lengths, g=out_grad[0], wg=w_gate, wi=w_in, wr=w_rgate, wv=w_igate, wout=w_out,
            wmg=w_mlp_gate, wmu=w_mlp_up, wmd=w_mlp_down,
        ),
        dict(
            block_out=array(256, 1024, dtype=BF),
            d_in=array(256, 1024),
            fm=array(4, 256, 768, dtype=BF),
            fm_x=array(4, 128, 768, dtype=BF),
            fd=array(4, 96, 1024, dtype=BF),
            fa=array(4, 256, 256, dtype=BF),
            fa_x=array(4, 128, 256, dtype=BF),
            fb=array(4, 128, 256, dtype=BF),
            fo=array(4, 48, 1280, dtype=BF),
            fr=array(8, 2, 8, 128),
            vec_out=array(8, 256),
            gain_out=array(8, 128),
            normed_far=array(8, 256, 1024, dtype=BF),
        ),
        dict(
            x=vmem((256, 1024), BF),
            x_all=vmem((8, 256, 1024), BF),
            normed=vmem((8, 256, 1024), BF),
            g_all=vmem((8, 256, 1024), BF),
            small_rows=vmem((16, 256), F32),
            small=vmem((16, 256), BF),
            small_all=vmem((8, 16, 256), BF),
            lens_out=vmem((8, 128), F32),
            lens_all=vmem((4, 8, 128), F32),
            off=vmem((4, 520, 128), F32),
            starts_all=vmem((4, 8, 128), F32),
            chan=vmem((2, 16, 128), F32),
            gain=vmem((8, 1024), F32),
            wgi3=vmem((4, 256, 768), BF),
            w2=vmem((1024, 512), BF),
            gq=vmem((4, 48, 256), BF),
            g3=vmem((2, 192, 256), BF),
            wq=vmem((4, 48, 1024), BF),
            wri=vmem((2, 128, 256), BF),
            w3=vmem((2, 192, 1024), BF),
            wo=vmem((256, 1024), BF),
            wgu_out=vmem((2, 128, 768), BF),
            wgu_all=vmem((8, 128, 768), BF),
            wmd_all=vmem((4, 96, 1024), BF),
            gp=vmem((8, 512, 128), F32),
            gb=vmem((8, 520, 128), F32),
            inner=vmem((8, 520, 128), F32),
            conv=vmem((8, 512, 128), BF),
            sr=vmem((8, 512, 128), F32),
            si=vmem((8, 512, 128), F32),
            dec=vmem((8, 512, 128), F32),
            drv=vmem((8, 512, 128), F32),
            states=vmem((8, 520, 128), F32),
            mixed=vmem((8, 256, 256), BF),
            tot=vmem((2, 4, 2, 8, 128), F32),
            inc=vmem((8, 128), F32),
            rs_all=vmem((4, 8, 8, 128), F32),
            rows_sum=vmem((8, 8, 128), F32),
            residual=vmem((256, 1024), F32),
            d_res=vmem((256, 1024), F32),
            hid=vmem((8, 256, 384), BF),
            dgu=vmem((8, 256, 768), BF),
            gm=vmem((4, 256, 768), BF),
            gm_sum=vmem((256, 768), BF),
            gd=vmem((4, 96, 1024), BF),
            gd_in=vmem((3, 96, 1024), BF),
            gd_sum=vmem((96, 1024), BF),
            go=vmem((256, 1280), BF),
            go_q=vmem((4, 48, 1280), BF),
            go_l=vmem((3, 48, 1280), BF),
            go_sum=vmem((48, 1280), BF),
            ga_sum=vmem((256, 256), BF),
            gb2_sum=vmem((128, 256), BF),
            gain2_sum=vmem((8, 1024), F32),
            vec=vmem((2, 8, 8, 128), F32),
            vsum=vmem((4, 8, 256), F32),
            vout=vmem((4, 8, 256), F32),
            gsum=vmem((8, 8, 128), F32),
            gline=vmem((8, 8, 128), F32),
            gplane=vmem((4, 8, 128), F32),
            free=pltpu.SemaphoreType.REGULAR,
            **reduce_scratch(256, 1024),
        ),
        154,
        37,
        (
            "x_in", "g", "wg", "wi", "wr", "wv", "wout", "wmg", "wmu", "wmd", "d_in", "block_out", "fm", "fm_x", "fd", "fa", "fa_x", "fb", "fo",
            "fr", "normed_far",
        ),
    )
    out = kernel_call(
        assemble,
        dict(
            {name: done[name] for name in ("d_in", "block_out", "fm", "fm_x", "fd", "fa", "fa_x", "fb", "fo", "fr")},
            vec_in=done["vec_out"], gains=done["gain_out"], lens=row_lengths,
        ),
        dict(
            o_din=array(256, 1024),
            o_block=array(256, 1024, dtype=BF),
            o_gate=array(128, 1536),
            o_in=array(128, 1536),
            o_mgate=array(128, 3072),
            o_mup=array(128, 3072),
            o_mdown=array(384, 1024),
            o_out=array(192, 1024),
            o_r=array(192, 128),
            o_i=array(192, 128),
            o_cw=array(4, 192),
            o_cb=array(1, 192),
            o_rb=array(1, 192),
            o_ib=array(1, 192),
            o_lam=array(1, 192),
            o_ngain=array(1, 128),
            o_mgain=array(1, 128),
            o_mean=array(5, 1, 1536),
        ),
        dict(
            v_din=vmem((256, 1024), F32),
            v_block=vmem((256, 1024), BF),
            vm=vmem((2, 4, 128, 768), BF),
            va=vmem((2, 4, 128, 256), BF),
            vb=vmem((4, 128, 256), BF),
            vd=vmem((4, 96, 1024), BF),
            vo=vmem((4, 48, 1280), BF),
            s_mgate=vmem((128, 3072), F32),
            s_mup=vmem((128, 3072), F32),
            s_gate=vmem((128, 1536), F32),
            s_in=vmem((128, 1536), F32),
            s_down=vmem((384, 1024), F32),
            s_out=vmem((192, 1024), F32),
            s_r=vmem((192, 128), F32),
            s_i=vmem((192, 128), F32),
            s_cw=vmem((4, 192), F32),
            s_cb=vmem((1, 192), F32),
            s_rb=vmem((1, 192), F32),
            s_ib=vmem((1, 192), F32),
            s_lam=vmem((1, 192), F32),
            s_ngain=vmem((1, 128), F32),
            s_mgain=vmem((1, 128), F32),
            s_mean=vmem((5, 1, 1536), F32),
            v_vec=vmem((8, 256), F32),
            v_gains=vmem((8, 128), F32),
            v_fr=vmem((8, 2, 8, 128), F32),
            v_lens=vmem((1, 5), jnp.int32),
        ),
        0,
        37,
        None,
    )
    return (
        out["o_block"][None],
        out["o_din"][None],
        out["o_ngain"][0],
        out["o_gate"],
        out["o_in"],
        out["o_cw"],
        out["o_cb"][0],
        out["o_r"],
        out["o_rb"][0],
        out["o_i"],
        out["o_ib"][0],
        out["o_lam"][0],
        out["o_out"],
        out["o_mgain"][0],
        out["o_mgate"],
        out["o_mup"],
        out["o_mdown"],
        jnp.transpose(out["o_mean"], (1, 0, 2)),
    )


def solution(mesh):
    in_specs = (
        P("batch", "seq", None),
        P("batch", "seq", None),
        P("batch", None),
        P("seq"),
        P("seq", None),
        P("seq", None),
        P(None, "seq"),
        P("seq"),
        P("seq", None),
        P("seq"),
        P("seq", None),
        P("seq"),
        P("seq"),
        P("seq", None),
        P("seq"),
        P("seq", None),
        P("seq", None),
        P("seq", None),
    )
    out_specs = (
        P("batch", "seq", None),
        P("batch", "seq", None),
        P("seq"),
        P("seq", None),
        P("seq", None),
        P(None, "seq"),
        P("seq"),
        P("seq", None),
        P("seq"),
        P("seq", None),
        P("seq"),
        P("seq"),
        P("seq", None),
        P("seq"),
        P("seq", None),
        P("seq", None),
        P("seq", None),
        P("batch", None, None),
    )
    in_planes = mesh.shape["batch"] == 4 and mesh.shape["seq"] == 8
    body = planes if in_planes else shards
    return jax.shard_map(body, mesh=mesh, in_specs=in_specs, out_specs=out_specs, check_vma=False)
```

```python
import functools
import types

import jax
import jax.numpy as jnp
from jax import lax
from jax.experimental import pallas as pl
from jax.experimental.pallas import tpu as pltpu
from jax.sharding import PartitionSpec as P

NORM_EPS = 1e-06
DECAY_SCALE = 8.0
BF = jnp.bfloat16
F32 = jnp.float32
GELU_SCALE = 0.7978845608028654
GELU_CUBE = 0.044715
TILE = 64
NN = (((1,), (0,)), ((), ()))
NT = (((1,), (1,)), ((), ()))
TN = (((0,), (0,)), ((), ()))


def dot(left, right, dims=NN):
    return lax.dot_general(left, right, dims, preferred_element_type=F32)


def loop(count, body):
    def step(i, carry):
        body(i)
        return carry

    lax.fori_loop(0, count, step, 0)


class Net:
    def __init__(self, r):
        self.send, self.recv, self.count = r.send, r.recv, 0
        self.here, self.here_count = r.local, 0
        self.pending = []
        self.p = lax.axis_index("batch")
        self.q = lax.axis_index("seq")
        self.z = lax.div(self.q, 2)
        self.c = lax.rem(self.q, 2)
        self.o = 1 - self.c
        p = self.p
        self.near = (p, p + 1 - 2 * lax.rem(p, 2), lax.rem(p + 2, 4), 3 - p)

    def plane(self, k, core):
        return {"batch": self.near[k], "seq": self.z * 2 + core}

    def line(self, z, core):
        return {"batch": self.p, "seq": z * 2 + core}

    def up(self, k):
        return lax.rem(self.z + k, 4)

    def down(self, k):
        return lax.rem(self.z + 4 - k, 4)

    def slot(self, k, core):
        return self.near[k] * 2 + core

    def greet(self):
        barrier = pltpu.get_barrier_semaphore()
        partners = [self.plane(k, core) for k in (1, 2, 3) for core in (0, 1)]
        partners += [self.line(self.up(k), core) for k in (1, 2, 3) for core in (0, 1)]
        partners += [self.line(self.z, self.o)]
        for partner in partners:
            pl.semaphore_signal(barrier, inc=1, device_id=partner, device_id_type=pl.DeviceIdType.MESH)
        pl.semaphore_wait(barrier, len(partners))

    def reserve(self, count):
        first = self.count
        self.count += count
        return first

    def describe(self, src, dst, device, send_at, recv_at):
        return pltpu.make_async_remote_copy(
            src_ref=src,
            dst_ref=dst,
            send_sem=self.send.at[send_at],
            recv_sem=self.recv.at[recv_at],
            device_id=device,
            device_id_type=pl.DeviceIdType.MESH,
        )

    def copy(self, src, dst, device, sent=None, at=None):
        at = self.reserve(1) if at is None else at
        made = self.describe(src, dst, device, at, at)
        made.start()
        (self.pending if sent is None else sent).append(made)
        return made

    def local(self, src, dst):
        made = pltpu.make_async_copy(src, dst, self.here.at[self.here_count])
        self.here_count += 1
        made.start()
        return made

    def drain(self):
        assert (self.count, self.here_count) == (self.send.shape[0], self.here.shape[0]), (self.count, self.here_count)
        for made in self.pending:
            made.wait_send()
        self.pending = []


class Gather:
    def __init__(self, net, own, everything, at=None):
        self.net, self.own, self.all = net, own, everything
        self.sent = []
        self.at = net.reserve(14) if at is None else at
        self.half = everything.shape[1] // 2
        self.x0, self.y1, self.x1, self.y0 = [], [], [], []

    def half_of(self, slot, h):
        return self.all.at[slot, pl.ds(h * self.half, self.half)]

    def send(self, src, dst, device, at):
        return self.net.copy(src, dst, device, self.sent, self.at + at)

    def start(self, part):
        net = self.net
        mine = net.slot(0, net.c)
        size = self.half // 2
        low, high = pl.ds(part * size, size), pl.ds(self.half + part * size, size)
        for made, rows, k, at in ((self.x0, low, 1, 0), (self.y1, high, 2, 2), (self.x1, high, 1, 4), (self.y0, low, 2, 6)):
            made.append(self.send(self.own.at[rows], self.all.at[mine, rows], net.plane(k, net.c), at + part))
        if part == 1:
            self.s = [self.send(self.own, self.all.at[mine], net.plane(0, net.o), 8)]

    def forward(self):
        net = self.net
        for made in self.x0:
            made.wait_recv()
        block = self.half_of(net.slot(1, net.c), 0)
        self.d0 = self.send(block, block, net.plane(2, net.c), 9)
        for made in self.y1:
            made.wait_recv()
        block = self.half_of(net.slot(2, net.c), 1)
        self.d1 = self.send(block, block, net.plane(1, net.c), 10)

    def across(self, k):
        net = self.net
        block = self.all.at[net.slot(k, net.c)]
        self.s.append(self.send(block, block, net.plane(0, net.o), 10 + k))

    def middle(self):
        for made in self.x1:
            made.wait_recv()
        self.across(1)
        for made in self.y0:
            made.wait_recv()
        self.across(2)

    def last(self):
        self.d0.wait_recv()
        self.d1.wait_recv()
        self.across(3)

    def sibling(self, k):
        self.s[k].wait_recv()

    def release(self):
        for made in self.sent:
            made.wait_send()
        self.sent = []


class Owners:
    def __init__(self, net, own, everything, extra=None, at=None, cut=None):
        self.net, self.own, self.all, self.extra = net, own, everything, extra
        self.at = net.reserve(6 if extra is None else 10) if at is None else at
        self.half = everything.shape[1] // 2 if cut is None else cut
        self.rows = (pl.ds(0, self.half), pl.ds(self.half, everything.shape[1] - self.half))
        self.s = [None] * 4

    def part(self, k, h):
        return self.all.at[self.net.near[k], self.rows[h]]

    def across(self, k, block):
        if self.extra is not None:
            net = self.net
            rows = pl.ds(pl.multiple_of(net.o * self.half, 16), self.half)
            self.s[k] = net.copy(block.at[rows], self.extra.at[net.near[k]], net.plane(0, net.o), None, self.at + 6 + k)

    def start(self):
        net = self.net
        low, high = self.own.at[self.rows[0]], self.own.at[self.rows[1]]
        self.x0 = net.copy(low, self.part(0, 0), net.plane(1, net.c), None, self.at + 0)
        self.y1 = net.copy(high, self.part(0, 1), net.plane(2, net.c), None, self.at + 1)
        self.x1 = net.copy(high, self.part(0, 1), net.plane(1, net.c), None, self.at + 2)
        self.y0 = net.copy(low, self.part(0, 0), net.plane(2, net.c), None, self.at + 3)
        self.across(0, self.own)
        self.kept = net.local(self.own, self.all.at[net.p])

    def forward(self):
        net = self.net
        self.x0.wait_recv()
        self.d0 = net.copy(self.part(1, 0), self.part(1, 0), net.plane(2, net.c), None, self.at + 4)
        self.y1.wait_recv()
        self.d1 = net.copy(self.part(2, 1), self.part(2, 1), net.plane(1, net.c), None, self.at + 5)

    def middle(self):
        self.x1.wait_recv()
        self.across(1, self.all.at[self.net.near[1]])
        self.y0.wait_recv()
        self.across(2, self.all.at[self.net.near[2]])

    def last(self):
        self.d0.wait_recv()
        self.d1.wait_recv()
        self.across(3, self.all.at[self.net.near[3]])

    def end(self):
        if self.extra is not None:
            for made in self.s:
                made.wait_recv()
        self.kept.wait()


class LineGather:
    def __init__(self, net, own, first, place):
        self.net, self.own, self.first, self.place = net, own, first, place
        self.at = net.reserve(4 * len(own))

    def made(self, k, j):
        net = self.net
        src, core = self.own[j]
        at = self.at + 4 * j + k - 1
        return net.describe(src, self.first(j), net.line(net.up(k), core), at, at)

    def handed(self, j):
        net = self.net
        far = 6 - 3 * net.z
        here = self.place(j, far)
        at = self.at + 4 * j
        return net.describe(here, here, net.line(3 - far, net.c), at + 3, at + 2 * net.z - 2)

    def direct(self, k, body):
        z = self.net.z
        if k == 2:
            body()
        else:
            pl.when(z != (0 if k == 3 else 3))(body)

    def start(self, k, items):
        def send():
            for j in items:
                self.made(k, j).start()

        self.direct(k, send)

    def inside(self, body):
        z = self.net.z
        pl.when((z == 1) | (z == 2))(body)

    def relay(self):
        @self.inside
        def _():
            for j in range(len(self.own)):
                self.made(2, j).wait_recv()
                self.handed(j).start()

    def end(self):
        z = self.net.z
        for k in (1, 3):
            for j in range(len(self.own)):
                self.made(k, j).wait_recv()

        @pl.when((z == 0) | (z == 3))
        def _():
            for j in range(len(self.own)):
                self.made(2, j).wait_recv()

    def drain(self):
        for k in (1, 2, 3):

            def wait(k=k):
                for j in range(len(self.own)):
                    self.made(k, j).wait_send()

            self.direct(k, wait)

        @self.inside
        def _():
            for j in range(len(self.own)):
                self.handed(j).wait_send()


class LineSum:
    def __init__(self, net, block, slot, at=None):
        self.net, self.block, self.slot = net, block, slot
        self.at = net.reserve(3) if at is None else at

    def made(self, k):
        net = self.net
        at = self.at + k - 1
        to = lax.rem(2 * net.z + 1, 5) if k == 2 else net.up(k)
        return net.describe(self.block(net.up(k)), self.slot(k), net.line(to, net.c), at, at)

    def start(self):
        z = self.net.z
        self.made(2).start()
        pl.when(z != 1)(lambda: self.made(1).start())
        pl.when(z != 2)(lambda: self.made(3).start())

    def relay(self, step=16):
        z = self.net.z

        @pl.when((z == 1) | (z == 2))
        def _():
            self.made(2).wait_recv()
            mine, extra = self.block(3 - z), self.slot(2)

            def body(i):
                rows = pl.ds(pl.multiple_of(i * step, step), step)
                mine[rows, :] = (mine[rows, :].astype(F32) + extra[rows, :].astype(F32)).astype(BF)

            loop(mine.shape[0] // step, body)

        pl.when(z == 1)(lambda: self.made(1).start())
        pl.when(z == 2)(lambda: self.made(3).start())

    def end(self, dst, step=16):
        z = self.net.z
        self.made(1).wait_recv()
        self.made(3).wait_recv()
        edge = (z == 0) | (z == 3)
        pl.when(edge)(lambda: self.made(2).wait_recv())
        share = jnp.where(edge, 1.0, 0.0)
        own = self.block(z)

        def body(i):
            rows = pl.ds(pl.multiple_of(i * step, step), step)
            value = own[rows, :].astype(F32) + share * self.slot(2)[rows, :].astype(F32)
            value = value + self.slot(1)[rows, :].astype(F32) + self.slot(3)[rows, :].astype(F32)
            dst[rows, :] = value.astype(BF)

        loop(dst.shape[0] // step, body)

    def drain(self):
        for k in (1, 2, 3):
            self.made(k).wait_send()


class Reduce:
    def __init__(self, net, r, value, at=None):
        self.net, self.value = net, value
        self.at = net.reserve(12) if at is None else at
        self.keep, self.out, self.into = r.rs_keep, r.rs_out, r.rs_in
        self.xs, self.ys, self.xr, self.yr = r.rs_xs, r.rs_ys, r.rs_xr, r.rs_yr
        self.half = self.keep.shape[1]
        self.cross = [None] * 4
        self.sent = []

    def other(self, k):
        net = self.net
        self.out[k] = self.value(k, net.o).astype(BF)
        self.cross[k] = net.copy(self.out.at[k], self.into.at[k], net.plane(0, net.o), self.sent, self.at + k)

    def mine(self, k):
        self.cross[k].wait_recv()
        value = self.value(k, self.net.c) + self.into[k].astype(F32)
        return value[: self.half], value[self.half :]

    def send(self, src, dst, j, k, part=None):
        net = self.net
        at = self.at + 4 + j + (part or 0) + (0 if src is self.xs else 4)
        src, dst = src.at[j], dst.at[j]
        if part is not None:
            rows = pl.ds(part * self.half // 2, self.half // 2)
            src, dst = src.at[rows], dst.at[rows]
        return net.copy(src, dst, net.plane(k, net.c), self.sent, at)

    def far(self):
        low, high = self.mine(3)
        self.xs[0] = low.astype(BF)
        self.x0 = self.send(self.xs, self.xr, 0, 1)
        self.ys[0] = high.astype(BF)
        self.y0 = self.send(self.ys, self.yr, 0, 2)

    def near(self):
        low, high = self.mine(1)
        self.xs[1] = low.astype(BF)
        self.x1 = self.send(self.xs, self.xr, 1, 1)
        self.keep[2] = high
        low, high = self.mine(2)
        self.ys[1] = high.astype(BF)
        self.y1 = self.send(self.ys, self.yr, 1, 2)
        self.keep[3] = low

    def relay(self):
        size = self.half // 2
        self.x2, self.y2 = [], []
        for part in (0, 1):
            rows = slice(part * size, (part + 1) * size)
            if part == 0:
                self.x0.wait_recv()
            self.ys[2, rows, :] = (self.keep[3, rows, :] + self.xr[0, rows, :].astype(F32)).astype(BF)
            self.y2.append(self.send(self.ys, self.yr, 2, 2, part))
            if part == 0:
                self.y0.wait_recv()
            self.xs[2, rows, :] = (self.keep[2, rows, :] + self.yr[0, rows, :].astype(F32)).astype(BF)
            self.x2.append(self.send(self.xs, self.xr, 2, 1, part))

    def own(self):
        self.keep[0], self.keep[1] = self.mine(0)

    def finish(self, part):
        if part == 0:
            self.x1.wait_recv()
            self.y1.wait_recv()
        self.x2[part].wait_recv()
        self.y2[part].wait_recv()
        if part == 1:
            for made in self.sent:
                made.wait_send()
            self.sent = []

    def total(self, h, i, step):
        rows = pl.ds(pl.multiple_of(i * step, step), step)
        first, second = (self.xr, self.yr) if h == 0 else (self.yr, self.xr)
        return self.keep[h, rows, :] + first[1, rows, :].astype(F32) + second[2, rows, :].astype(F32)


def reduce_scratch(rows, width):
    half = rows // 2
    return dict(
        rs_keep=pltpu.VMEM((4, half, width), F32),
        rs_out=pltpu.VMEM((4, rows, width), BF),
        rs_in=pltpu.VMEM((4, rows, width), BF),
        rs_xs=pltpu.VMEM((3, half, width), BF),
        rs_ys=pltpu.VMEM((3, half, width), BF),
        rs_xr=pltpu.VMEM((3, half, width), BF),
        rs_yr=pltpu.VMEM((3, half, width), BF),
    )


def kernel_call(body, ins, outs, scratch, copies, local, far):
    names = list(ins) + list(outs) + list(scratch)
    near = pl.BlockSpec(memory_space=pltpu.VMEM)
    away = pl.BlockSpec(memory_space=pl.ANY)
    shapes = list(scratch.values())
    if copies:
        names += ["send", "recv"]
        shapes += [pltpu.SemaphoreType.DMA((copies,))] * 2
    if local:
        names.append("local")
        shapes.append(pltpu.SemaphoreType.DMA((local,)))

    def kernel(*refs):
        body(types.SimpleNamespace(**dict(zip(names, refs))))

    params = dict(vmem_limit_bytes=62 * 2**20)
    if copies:
        params.update(collective_id=0, has_side_effects=True)
    results = pl.pallas_call(
        kernel,
        out_shape=list(outs.values()),
        in_specs=[away if far is None or name in far else near for name in ins],
        out_specs=[away if far is None or name in far else near for name in outs],
        scratch_shapes=shapes,
        compiler_params=pltpu.CompilerParams(**params),
        name=body.__name__,
    )(*ins.values())
    return dict(zip(outs, results))


def array(*shape, dtype=F32):
    return jax.ShapeDtypeStruct(shape, dtype)


def gelu_parts(v):
    square = v * v
    t = jnp.tanh(GELU_SCALE * v * (1.0 + GELU_CUBE * square))
    half = 0.5 + 0.5 * t
    slope = half + 0.5 * v * (1.0 - t * t) * (GELU_SCALE * (1.0 + 3.0 * GELU_CUBE * square))
    return v * half, slope


def decay_parts(sr, rate):
    log_a = -DECAY_SCALE * sr * rate
    a = jnp.exp(log_a)
    y = 2.0 * log_a
    series = 1.0 + y * (1 / 6) * (1.0 + y * (1 / 7))
    for n in (5, 4, 3, 2):
        series = 1.0 + y * (1 / n) * series
    m2 = jnp.where(y > -0.35, -y * series, 1.0 - a * a)
    return a, jnp.maximum(m2, 1e-36)


def column_sum(value):
    return jnp.sum(value.reshape(-1, 8, 128), axis=0)


def scan_slabs(decay, value, reverse):
    count = decay.shape[1] // 8
    row = lax.broadcasted_iota(jnp.int32, (8, 128), 0)

    def step(i, carry):
        t = count - 1 - i if reverse else i
        at = pl.ds(pl.multiple_of(t * 8, 8), 8)
        done = []
        for s in range(8):
            pc, vc = carry[s]
            p, own = decay[s, at, :], value[s, at, :]
            v = p * own if reverse else own
            for d in (1, 2, 4):
                by = 8 - d if reverse else d
                inside = row < 8 - d if reverse else row >= d
                v = v + p * jnp.where(inside, pltpu.roll(v, by, 0), 0.0)
                p = p * jnp.where(inside, pltpu.roll(p, by, 0), 1.0)
            v = v + p * vc
            p = p * pc
            if reverse:
                edge = row == 7
                value[s, at, :] = own + jnp.where(edge, vc, pltpu.roll(v, 7, 0))
                decay[s, at, :] = jnp.where(edge, pc, pltpu.roll(p, 7, 0))
                last = slice(0, 1)
            else:
                value[s, at, :] = v
                decay[s, at, :] = p
                last = slice(7, 8)
            done.append((jnp.broadcast_to(p[last], (8, 128)), jnp.broadcast_to(v[last], (8, 128))))
        return tuple(done)

    start = tuple((jnp.ones((8, 128), F32), jnp.zeros((8, 128), F32)) for _ in range(8))
    return lax.fori_loop(0, count, step, start)


def exchange_ends(r, net, ends, at):
    for s in range(8):
        r.tot[at, net.z, 0, s : s + 1, :] = ends[s][0][0:1, :]
        r.tot[at, net.z, 1, s : s + 1, :] = ends[s][1][0:1, :]
    mine = r.tot.at[at, net.z]
    return [net.copy(mine, mine, net.line(net.up(k), net.c)) for k in (1, 2, 3)]


def entering_states(r, net, copies, at, reverse):
    for made in copies:
        made.wait_recv()
    state = jnp.zeros((8, 128), F32)
    for i in range(4):
        z = 3 - i if reverse else i
        new = r.tot[at, z, 0] * state + r.tot[at, z, 1]
        state = jnp.where((z > net.z) if reverse else (z < net.z), new, state)
    r.inc[...] = state


def tile_rows(i):
    return pl.ds(pl.multiple_of(i * TILE, TILE), TILE)


def layer(r):
    r.do_all = r.x_all
    r.dconv = r.gb
    r.dgi = r.dgu
    r.up = r.d_res.at[:, 0:768]
    r.ga = [r.hid.at[i, :, 0:256] for i in range(4)]
    r.gb2 = [r.hid.at[4 + i, 0:128, 0:256] for i in range(4)]
    net = Net(r)
    p, z, c, o, q = net.p, net.z, net.c, net.o, net.q
    sibling = net.plane(0, o)
    mine = net.slot(0, c)
    cols = r.wgu_out.shape[2] // 2
    piece = cols // 4
    down = pl.ds(pl.multiple_of(p * piece, 16), piece)
    quarter = pl.ds(pl.multiple_of(p * 48, 16), 48)
    x_here = net.local(r.x_in, r.x)
    staged = []
    for j in range(8):
        lanes = pl.ds(j * cols, cols)
        staged.append(net.local(r.wmg.at[:, lanes], r.hid.at[j, pl.ds(0, 128)]))
        staged.append(net.local(r.wmu.at[:, lanes], r.hid.at[j, pl.ds(128, 128)]))
    width = 3 * 128
    first = pl.multiple_of(p * width, 128)
    chip = pl.ds(first, width)
    own_lanes = pl.ds(pl.multiple_of(c * width, 128), width)
    wi_rows, wg_rows = pl.ds(128, 128), pl.ds(0, 128)
    placed = [
        net.local(r.wg.at[:, chip], r.wgi3.at[z, wg_rows, own_lanes]),
        net.local(r.wi.at[:, chip], r.wgi3.at[z, wi_rows, own_lanes]),
        net.local(r.wmd.at[down], r.wmd_all.at[z]),
        net.local(r.wout.at[quarter], r.wq.at[z]),
        net.local(r.wr.at[quarter], r.gq.at[z, :, pl.ds(0, 128)]),
        net.local(r.wv.at[quarter], r.gq.at[z, :, pl.ds(128, 128)]),
        net.local(r.g, r.g_all.at[mine]),
    ]
    r.lens_out[0:1, 0:5] = r.lens[...].astype(F32)
    r.small_rows[...] = jnp.zeros((16, 256), F32)
    r.small_rows[0:4, 0:192] = r.cw[...].astype(F32)
    for at, ref in ((4, r.cb), (5, r.br), (6, r.bi), (7, r.lam)):
        r.small_rows[at : at + 1, 0:192] = ref[...].astype(F32).reshape(1, 192)
    for at, ref in ((0, r.ngain), (128, r.mgain)):
        r.small_rows[10:11, at : at + 128] = ref[...].astype(F32).reshape(1, 128)
    r.small[...] = r.small_rows[...].astype(BF)
    net.greet()
    r.small_all[c, z] = r.small[...]
    r.lens_all[p] = r.lens_out[...]
    small = [net.copy(r.small, r.small_all.at[c, z], net.line(net.up(k), c)) for k in (1, 2, 3)]
    lens = [net.copy(r.lens_out, r.lens_all.at[p], net.plane(k, c)) for k in (1, 2, 3)]
    x_here.wait()
    tokens = Gather(net, r.x, r.x_all)
    tokens.start(0)
    tokens.start(1)
    theirs = pl.ds(pl.multiple_of(c * width + o * 128, 128), 256)

    def along(place):
        made = LineGather(net, [(place(z), c)], lambda j: place(z), lambda j, at: place(at))
        for k in (2, 1, 3):
            made.start(k, (0,))
        return made

    handed = []

    def heads_start(rows):
        here = r.wgi3.at[z, rows, theirs]
        made = along(lambda at: r.wgi3.at[at, rows, own_lanes])
        return made, [net.copy(here, here, sibling, handed)]

    for made in placed:
        made.wait()
    heads_in, heads_in_over = heads_start(wi_rows)
    gates_in = along(lambda at: r.gq.at[at])

    def hand_over(arrivals, rows, over):
        arrivals.end()
        for k in (1, 2, 3):
            here = r.wgi3.at[net.down(k), rows, theirs]
            over.append(net.copy(here, here, sibling, handed))

    def arrange(over, rows, lanes):
        for made in over:
            made.wait_recv()
        for core in range(2):
            cols_in = pl.ds(pl.multiple_of(core * width + c * 128, 128), 256)
            for at in range(4):
                to = slice((at * 2 + core) * 128, (at * 2 + core + 1) * 128)
                r.w2[to, lanes] = r.wgi3[at, rows, cols_in]

    def exchange(arrivals, src, dst):
        arrivals.end()
        dst[c, quarter, :] = src[p]
        return [net.copy(src.at[net.near[k]], dst.at[c, quarter], net.plane(k, c)) for k in (1, 2, 3)]

    def share(copies, dst):
        for made in copies:
            made.wait_recv()
        return net.copy(dst.at[c], dst.at[c], sibling)

    for made in small:
        made.wait_recv()
    small_over = net.copy(r.small_all.at[c], r.small_all.at[c], sibling)
    selects = []
    k_at = lax.broadcasted_iota(jnp.int32, (cols, cols), 0)
    j_at = lax.broadcasted_iota(jnp.int32, (cols, cols), 1)
    for part in range(4):
        inside = (j_at >= part * piece) & (j_at < (part + 1) * piece)
        chosen = inside & (k_at == j_at + (p - part) * piece)
        selects.append(jnp.where(chosen, 1.0, 0.0).astype(BF))
    for made in staged:
        made.wait()
    for which in range(2):
        rows = slice(which * 128, (which + 1) * 128)
        for core in (0, 1):
            picked = None
            for part in range(4):
                term = dot(r.hid[part * 2 + core, rows, :], selects[part])
                picked = term if picked is None else picked + term
            r.wgu_out[core, :, which * cols : (which + 1) * cols] = picked.astype(BF)
    for made in lens:
        made.wait_recv()
    small_over.wait_recv()
    low, high = r.small_all[0, p].astype(F32), r.small_all[1, p].astype(F32)
    at_first = jnp.concatenate([low[:, :192], high[:, :64]], axis=1)
    at_second = jnp.concatenate([low[:, 128:192], high[:, :192]], axis=1)
    both = lax.select(c == 0, at_first, at_second)
    for n in range(2):
        r.chan[n] = both[:, n * 128 : (n + 1) * 128]
        lam = -r.chan[n, 7:8, :]
        e = jnp.exp(-jnp.abs(lam))
        series = 1.0 - e * (6 / 7)
        for k in (6, 5, 4, 3, 2):
            series = 1.0 - e * ((k - 1) / k) * series
        rate = jnp.maximum(lam, 0.0) + jnp.where(e < 0.05, e * series, jnp.log(1.0 + e))
        r.chan[n, 7:8, :] = rate
        r.chan[n, 8:9, :] = jax.nn.sigmoid(lam)
    for i in range(8):
        gains = r.small_all[i % 2, i // 2].astype(F32)[10:11, :]
        r.gain[0:1, i * 128 : (i + 1) * 128] = gains[:, 0:128]
        r.gain[1:2, i * 128 : (i + 1) * 128] = gains[:, 128:256]
    gain = r.gain[0:1, :]
    for b in range(4):
        start = jnp.zeros((1, 128), F32)
        for row in range(5):
            r.starts_all[b, row : row + 1, :] = start
            start = start + jnp.broadcast_to(r.lens_all[b, 0:1, row : row + 1], (1, 128))


    def offset_rows(i):
        b, tile = lax.div(i, 13), lax.rem(i, 13)
        starts = r.starts_all[b]
        at = lax.convert_element_type(z * 512 + tile * 40, F32)
        at = at + lax.broadcasted_iota(jnp.int32, (40, 128), 0).astype(F32)
        begun = jnp.zeros((40, 128), F32)
        for row in range(1, 5):
            start = starts[row : row + 1, :]
            begun = jnp.where(at >= start, start, begun)
        r.off[b, pl.ds(pl.multiple_of(tile * 40, 8), 40), :] = at - begun

    loop(52, offset_rows)

    def normalise(slot):
        def body(i):
            rows = pl.ds(pl.multiple_of(i * 32, 32), 32)
            v = r.x_all[slot, rows, :].astype(F32)
            s = lax.rsqrt(jnp.mean(v * v, axis=-1, keepdims=True) + NORM_EPS)
            r.normed[slot, rows, :] = (v * s * gain).astype(BF)

        loop(8, body)

    r.x_all[mine] = r.x[...]
    normalise(mine)
    tokens.sibling(0)
    normalise(net.slot(0, o))
    tokens.forward()
    heads_in.relay()
    gates_in.relay()
    out_in = along(lambda at: r.wq.at[at])
    feed = LineGather(
        net,
        [(r.wgu_out.at[core], core) for core in (c, o)],
        lambda j: r.wgu_all.at[q],
        lambda j, at: r.wgu_all.at[at * 2 + (c, o)[j]],
    )
    feed_down = LineGather(net, [(r.wmd.at[down], c)], lambda j: r.wmd_all.at[z], lambda j, at: r.wmd_all.at[at])
    tokens.middle()
    for k in (1, 2):
        normalise(net.slot(k, c))
    hand_over(heads_in, wi_rows, heads_in_over)
    for k in (1, 2):
        tokens.sibling(k)
        normalise(net.slot(k, o))
    gates_out = exchange(gates_in, r.gq, r.g3)
    arrange(heads_in_over, slice(128, 256), slice(256, 512))

    def project_inner(slot):
        b, half = lax.div(slot, 2), lax.rem(slot, 2)
        at = pl.multiple_of(half * 256, 256)
        inner = dot(r.normed[slot], r.w2[:, 256:512]).astype(BF).astype(F32)
        for n in range(2):
            r.inner[b * 2 + n, pl.ds(at + 8, 256), :] = inner[:, n * 128 : (n + 1) * 128]

    def project_gate(slot):
        b, half = lax.div(slot, 2), lax.rem(slot, 2)
        at = pl.multiple_of(half * 256, 256)
        gate = dot(r.normed[slot], r.w2[:, 0:256])
        for n in range(2):
            r.gp[b * 2 + n, pl.ds(at, 256), :] = gate[:, n * 128 : (n + 1) * 128]

    out_in.relay()
    for k in (0, 1, 2):
        project_inner(net.slot(k, c))
        project_inner(net.slot(k, o))
    tokens.last()
    normalise(net.slot(3, c))
    project_inner(net.slot(3, c))
    tokens.sibling(3)
    normalise(net.slot(3, o))
    project_inner(net.slot(3, o))
    edge = net.reserve(1)

    def edge_copy():
        return net.describe(
            r.inner.at[:, pl.ds(512, 8)], r.inner.at[:, pl.ds(0, 8)], net.line(net.up(1), c), edge, edge
        )

    @pl.when(z < 3)
    def _():
        edge_copy().start()

    @pl.when(z == 0)
    def _():
        r.inner[:, 0:8, :] = jnp.zeros((8, 8, 128), F32)

    gates_over = share(gates_out, r.g3)
    stored = net.local(r.normed, r.normed_far)
    cots = Gather(net, r.g_all.at[mine], r.g_all)
    cots.start(0)
    cots.start(1)
    tokens.release()
    gates_over.wait_recv()
    for i in range(4):
        at = c * 128 + i * 64
        value = r.g3[lax.div(at, 192), pl.ds(pl.multiple_of(lax.rem(at, 192), 64), 64), :]
        r.wri[i // 2, (i % 2) * 64 : (i % 2 + 1) * 64, :] = value
    heads_gate, heads_gate_over = heads_start(wg_rows)

    @pl.when(z > 0)
    def _():
        edge_copy().wait_recv()


    def conv_tile(i):
        b, tile = lax.div(i, 8), lax.rem(i, 8)
        rows = tile_rows(tile)
        offset = r.off[b, rows, :]
        for n in range(2):
            s = b * 2 + n
            window = r.inner[s, pl.ds(pl.multiple_of(tile * TILE, 8), TILE + 8), :]
            chan = r.chan[n]
            total = chan[4:5, :] + chan[0:1, :] * window[8:, :]
            for k in (1, 2, 3):
                total = total + chan[k : k + 1, :] * jnp.where(offset >= k, window[8 - k : TILE + 8 - k, :], 0.0)
            r.conv[s, rows, :] = total.astype(BF)

    loop(32, conv_tile)
    out_rows_in = exchange(out_in, r.wq, r.w3)

    def gate_products(i):
        s, half = lax.div(i, 2), lax.rem(i, 2)
        n = lax.rem(s, 2)
        rows = pl.ds(pl.multiple_of(half * 256, 256), 256)
        pre = dot(r.conv[s, rows, :], r.wri[n])
        r.sr[s, rows, :] = pre[:, :128]
        r.si[s, rows, :] = pre[:, 128:]

    loop(16, gate_products)
    heads_gate.relay()
    feed.start(2, (0,))

    def terms(b):
        starts_b = r.starts_all[b]

        def tile(i, sums):
            rows = tile_rows(i)
            offset = r.off[b, rows, :]
            at = lax.convert_element_type(z * 512 + i * TILE, F32)
            begun = at + lax.broadcasted_iota(jnp.int32, (TILE, 128), 0).astype(F32) - offset
            restart = offset == 0.0
            added = []
            for n in range(2):
                s = b * 2 + n
                chan = r.chan[n]
                sr = jax.nn.sigmoid(r.sr[s, rows, :] + chan[5:6, :])
                si = jax.nn.sigmoid(r.si[s, rows, :] + chan[6:7, :])
                r.sr[s, rows, :] = sr
                r.si[s, rows, :] = si
                a, m2 = decay_parts(sr, chan[7:8, :])
                r.dec[s, rows, :] = jnp.where(restart, 0.0, a)
                m = jnp.where(restart, 1.0, m2 * lax.rsqrt(m2))
                r.drv[s, rows, :] = m * si * r.conv[s, rows, :].astype(F32)
                for row in range(5):
                    inside = jnp.where(begun == starts_b[row : row + 1, :], a, 0.0)
                    added.append(sums[n * 5 + row] + column_sum(inside))
            return tuple(added)

        sums = lax.fori_loop(0, 512 // TILE, tile, tuple(jnp.zeros((8, 128), F32) for _ in range(10)))
        for n in range(2):
            rows = [jnp.sum(part, axis=0, keepdims=True) for part in sums[n * 5 : n * 5 + 5]]
            r.rs_all[z, b * 2 + n] = jnp.concatenate(rows + [jnp.zeros((3, 128), F32)], axis=0)

    loop(4, terms)
    cots.forward()
    ends = scan_slabs(r.dec, r.drv, False)
    ends = exchange_ends(r, net, ends, 0)
    for k in (2, 1, 3):
        feed_down.start(k, (0,))
    r.wgu_all[q] = r.wgu_out[c]
    feed_over = net.copy(r.wgu_out.at[o], r.wgu_all.at[q], sibling)
    hand_over(heads_gate, wg_rows, heads_gate_over)
    arrange(heads_gate_over, slice(0, 128), slice(0, 256))
    for made in handed:
        made.wait_send()
    heads_in.drain()
    heads_gate.drain()
    gates_in.drain()
    out_in.drain()
    feed.start(2, (1,))
    feed.start(1, (0, 1))
    feed.start(3, (0, 1))
    for slot in range(8):
        project_gate(slot)

    def gelu_tile(i):
        s, rows = lax.div(i, 8), tile_rows(lax.rem(i, 8))
        v = r.gp[s, rows, :]
        t = jnp.tanh(GELU_SCALE * v * (1.0 + GELU_CUBE * v * v))
        r.gb[s, rows, :] = 0.5 * v * (1.0 + t)

    loop(64, gelu_tile)
    out_over = share(out_rows_in, r.w3)
    entering_states(r, net, ends, 0, False)
    row_sums = [net.copy(r.rs_all.at[z], r.rs_all.at[z], net.line(net.up(k), c)) for k in (1, 2, 3)]
    out_over.wait_recv()

    def own_rows(i):
        at = c * 128 + i * 64
        value = r.w3[lax.div(at, 192), pl.ds(pl.multiple_of(lax.rem(at, 192), 64), 64), :]
        r.wo[pl.ds(pl.multiple_of(i * 64, 64), 64), :] = value

    loop(4, own_rows)
    for s in range(8):
        r.states[s, 7:8, :] = r.inc[s : s + 1, :]

    def mix_tile(i):
        s, tile = lax.div(i, 8), lax.rem(i, 8)
        b, n = lax.div(s, 2), lax.rem(s, 2)
        rows = tile_rows(tile)
        states = r.drv[s, rows, :] + r.dec[s, rows, :] * r.inc[pl.ds(s, 1), :]
        r.states[s, pl.ds(pl.multiple_of(tile * TILE + 8, 8), TILE), :] = states
        lanes = pl.ds(pl.multiple_of(n * 128, 128), 128)
        r.mixed[b * 2 + lax.div(tile, 4), tile_rows(lax.rem(tile, 4)), lanes] = (states * r.gb[s, rows, :]).astype(BF)

    loop(64, mix_tile)
    stored.wait()
    lane = lax.broadcasted_iota(jnp.int32, (1, 256), 1)
    counted = jnp.where((lane >= 64 * c) & (lane < 192 + 64 * c), 1.0, 0.0)
    counted_two = jnp.concatenate([counted, counted], axis=1)

    def masked(value, mask):
        return (value.astype(F32) * mask).astype(BF)

    total = Reduce(
        net, r, lambda k, core: dot(masked(r.mixed[net.slot(k, core)], counted), r.wo[...])
    )
    for k in (3, 1, 2, 0):
        total.other(k)
    total.far()
    total.near()
    cots.middle()
    total.own()
    cots.last()
    for k in (0, 1, 2, 3):
        cots.sibling(k)
    cots.release()
    total.relay()
    feed_down.relay()
    feed.relay()
    def wmd():
        return r.wmd_all[...].reshape(cols, -1)

    gain2 = r.gain[1:2, :]
    n2_all = r.normed
    acts = Gather(net, n2_all.at[mine], n2_all, tokens.at)
    for part in range(2):
        total.finish(part)
        for h in range(2):

            def residual_rows(i, h=h, part=part):
                i = part * 2 + i
                rows = pl.ds(pl.multiple_of(h * 128 + i * 32, 32), 32)
                v = r.x[rows, :].astype(F32) + total.total(h, i, 32)
                r.residual[rows, :] = v
                s = lax.rsqrt(jnp.mean(v * v, axis=-1, keepdims=True) + NORM_EPS)
                r.normed[mine, rows, :] = (v * s * gain2).astype(BF)

            loop(2, residual_rows)
        acts.start(part)

    owners, returned = [], []
    def gate_up():
        return r.wgu_all[...].reshape(-1, 2 * cols)

    def d_normed2(k, core):
        return dot(r.dgu[net.slot(k, core)], gate_up(), NT)

    back = Reduce(net, r, d_normed2, total.at)

    def part(k, core):
        slot = net.slot(k, core)
        h = n2_all[slot]
        r.up[...] = dot(h, gate_up())

        def body(i):
            rows = pl.ds(pl.multiple_of(i * 32, 32), 32)
            gelu, slope = gelu_parts(r.up[rows, 0:cols])
            ul, dh = r.up[rows, cols:], r.dgu[slot, rows, 0:cols].astype(F32)
            r.hid[slot, rows, :] = (gelu * ul).astype(BF)
            r.dgu[slot, rows, 0:cols] = (dh * ul * slope).astype(BF)
            r.dgu[slot, rows, cols:] = (dh * gelu).astype(BF)

        loop(8, body)

    feed_down.end()
    for slot in range(8):
        r.dgu[slot, :, 0:cols] = dot(r.g_all[slot], wmd(), NT).astype(BF)
    feed_over.wait_recv()
    feed.end()
    part(0, c)
    acts.sibling(0)
    part(0, o)
    back.other(0)
    acts.forward()
    acts.middle()
    part(1, c)
    part(2, c)
    acts.sibling(1)
    part(1, o)
    back.other(1)
    acts.sibling(2)
    part(2, o)
    back.other(2)
    for made in row_sums:
        made.wait_recv()
    r.rows_sum[...] = r.rs_all[0] + r.rs_all[1] + r.rs_all[2] + r.rs_all[3]
    for k in (1, 2, 3):
        for core in (c, o):
            owners.append(net.copy(r.rows_sum.at[pl.ds(net.near[k] * 2, 2)], r.fr.at[mine], net.plane(k, core)))
    owners.append(net.copy(r.rows_sum.at[pl.ds(p * 2, 2)], r.fr.at[mine], sibling))
    returned.append(net.local(r.rows_sum.at[pl.ds(p * 2, 2)], r.fr.at[mine]))
    back.near()
    acts.last()
    acts.sibling(3)
    part(3, o)
    back.other(3)
    part(3, c)
    back.far()
    back.relay()
    back.own()
    acts.release()
    for i in range(4):
        rows = n2_all[:, :, i * 256 : (i + 1) * 256].reshape(-1, 256)
        r.gm[i] = dot(rows, r.dgu[...].reshape(-1, 2 * cols), TN).astype(BF)

    def gm_in(k):
        return r.wgi3.at[k - 1]

    mlp_m = LineSum(net, lambda t: r.gm.at[t], gm_in)
    mlp_m.start()
    hid = r.hid[...].reshape(-1, cols)
    for half in range(2):
        lanes = slice(half * 512, half * 512 + 512)
        value = dot(hid, r.g_all[:, :, lanes].reshape(-1, 512), TN).astype(BF)
        for i in range(4):
            r.gd[i, :, lanes] = value[i * piece : (i + 1) * piece, :]
    mlp_d = LineSum(net, lambda t: r.gd.at[t], lambda k: r.gd_in.at[k - 1], out_in.at)
    sums = jnp.zeros((8, r.x.shape[1]), F32)
    grads = Gather(net, r.do_all.at[mine], r.do_all, cots.at)
    for part in range(2):
        back.finish(part)
        for h in range(2):

            def residual_back(i, sums, h=h, part=part):
                i = part * 2 + i
                rows = pl.ds(pl.multiple_of(h * 128 + i * 32, 32), 32)
                v = r.residual[rows, :]
                dn = back.total(h, i, 32)
                s = lax.rsqrt(jnp.mean(v * v, axis=-1, keepdims=True) + NORM_EPS)
                u = dn * gain2
                pulled = s * u - v * (s * s * s * jnp.mean(u * v, axis=-1, keepdims=True))
                d_res = r.g_all[mine, rows, :].astype(F32) + pulled
                r.d_res[rows, :] = d_res
                r.do_all[mine, rows, :] = d_res.astype(BF)
                return sums + jnp.sum((dn * v * s).reshape(4, 8, -1), axis=0)

            sums = lax.fori_loop(0, 2, residual_back, sums)
        grads.start(part)
    r.gain2_sum[...] = sums


    fo_at = net.reserve(4)

    def vector_copy(k):
        return net.describe(r.vout.at[p], r.vout.at[p], net.plane(k, c), fo_at + k, fo_at)

    owners_m = Owners(net, r.gm_sum, r.fm, r.fm_x, tokens.at)
    owners_d = Owners(net, r.gd_sum, r.fd)
    owners_a = Owners(net, r.ga_sum, r.fa, r.fa_x, cots.at)
    owners_b = Owners(net, r.gb2_sum, r.fb)
    owners_o = Owners(net, r.go_sum, r.fo, cut=32)

    def mlp_sums():
        mlp_m.end(r.gm_sum)
        owners_m.start()

    def back_out(slot):
        b, half = lax.div(slot, 2), lax.rem(slot, 2)
        dm = dot(r.do_all[slot], r.wo[...], NT)
        for n in range(2):
            r.dconv[b * 2 + n, pl.ds(pl.multiple_of(half * 256, 256), 256), :] = dm[:, n * 128 : (n + 1) * 128]

    back_out(mine)
    grads.sibling(0)
    back_out(net.slot(0, o))
    out = Reduce(net, r, lambda k, core: dot(r.hid[net.slot(k, core)], wmd()), total.at)
    for k in (3, 1, 2, 0):
        out.other(k)
    grads.forward()
    out.far()
    out.near()
    out.own()
    grads.middle()
    mlp_m.relay()
    for k in (1, 2):
        back_out(net.slot(k, c))
    for k in (1, 2):
        grads.sibling(k)
        back_out(net.slot(k, o))
    grads.last()
    back_out(net.slot(3, c))
    grads.sibling(3)
    back_out(net.slot(3, o))

    def first_pass(i):
        b, tile = lax.div(i, 8), lax.rem(i, 8)
        rows = tile_rows(tile)
        live = r.off[b, rows, :] != 0.0
        for n in range(2):
            s = b * 2 + n
            gelu, slope = gelu_parts(r.gp[s, rows, :])
            dm = r.dconv[s, rows, :]
            states = r.states[s, pl.ds(pl.multiple_of(tile * TILE + 8, 8), TILE), :]
            lanes = slice(n * 128, (n + 1) * 128)
            r.dgi[b * 2 + lax.div(tile, 4), tile_rows(lax.rem(tile, 4)), lanes] = (dm * states * slope).astype(BF)
            r.drv[s, rows, :] = dm * gelu
            a = jnp.exp(-DECAY_SCALE * r.sr[s, rows, :] * r.chan[n, 7:8, :])
            r.dec[s, rows, :] = jnp.where(live, a, 0.0)

    loop(32, first_pass)
    ends = scan_slabs(r.dec, r.drv, True)
    ends = exchange_ends(r, net, ends, 1)
    out.relay()
    go_in, go_line_in = r.go_q, r.go_l
    mixed = r.mixed[...].reshape(-1, 256)
    for half in range(2):
        lanes = slice(half * 512, half * 512 + 512)
        r.go[:, lanes] = dot(mixed, r.do_all[:, :, lanes].reshape(-1, 512), TN).astype(BF)
    grads.release()
    fetched = net.local(r.normed_far, r.do_all)
    go_rows = [pl.ds(pl.multiple_of(c * 64 + near * 48, 16), 48) for near in net.near]

    def go_start(lanes):
        return [net.copy(r.go.at[go_rows[k], lanes], go_in.at[p, :, lanes], net.plane(k, c)) for k in (1, 2, 3)]

    go_out = go_start(pl.ds(0, 1024))
    entering_states(r, net, ends, 1, True)
    r.vec[...] = jnp.zeros((2, 8, 8, 128), F32)
    dri = r.normed

    def second_pass(s):
        b, n = lax.div(s, 2), lax.rem(s, 2)
        chan = r.chan[n]
        enter = r.inc[pl.ds(s, 1), :]
        lanes_r = pl.ds(pl.multiple_of(n * 256, 128), 128)
        lanes_i = pl.ds(pl.multiple_of(n * 256 + 128, 128), 128)

        def tile(i, sums):
            rows = tile_rows(i)
            live = r.off[b, rows, :] != 0.0
            ds = r.drv[s, rows, :] + r.dec[s, rows, :] * enter
            window = r.states[s, pl.ds(pl.multiple_of(i * TILE, 8), TILE + 8), :]
            before = window[7 : TILE + 7, :]
            sr, si = r.sr[s, rows, :], r.si[s, rows, :]
            cv = r.conv[s, rows, :].astype(F32)
            a, m2 = decay_parts(sr, chan[7:8, :])
            inv = lax.rsqrt(m2)
            m = jnp.where(live, m2 * inv, 1.0)
            dsi = ds * si
            d_log = jnp.where(live, a * (ds * before - dsi * cv * a * inv), 0.0)
            lam_term = d_log * sr
            d_r = (-DECAY_SCALE) * chan[7:8, :] * lam_term * (1.0 - sr)
            dm_i = dsi * m
            d_i = dm_i * cv * (1.0 - si)
            d_r, d_i = d_r.astype(BF), d_i.astype(BF)
            at = tile_rows(lax.rem(i, 4))
            dri[b * 2 + lax.div(i, 4), at, lanes_r] = d_r
            dri[b * 2 + lax.div(i, 4), at, lanes_i] = d_i
            r.dconv[s, rows, :] = dm_i
            return (
                sums[0] + column_sum(d_r.astype(F32)),
                sums[1] + column_sum(d_i.astype(F32)),
                sums[2] + column_sum(lam_term),
            )

        zero = jnp.zeros((8, 128), F32)
        sums = lax.fori_loop(0, 512 // TILE, tile, (zero, zero, zero))
        for j in range(3):
            r.vec[n, 5 + j] = r.vec[n, 5 + j] + sums[j]

    loop(8, second_pass)
    mlp_sums()

    def gate_back(i):
        s, half = lax.div(i, 2), lax.rem(i, 2)
        b, n = lax.div(s, 2), lax.rem(s, 2)
        rows = pl.ds(pl.multiple_of(half * 256, 256), 256)
        lanes = pl.ds(pl.multiple_of(n * 256, 256), 256)
        r.dconv[s, rows, :] = r.dconv[s, rows, :] + dot(dri[b * 2 + half, :, lanes], r.wri[n], NT)

    loop(16, gate_back)
    edge_back = net.reserve(1)

    def edge_back_copy():
        return net.describe(
            r.dconv.at[:, pl.ds(0, 8)], r.dconv.at[:, pl.ds(512, 8)], net.line(net.down(1), c), edge_back, edge_back
        )

    @pl.when(z > 0)
    def _():
        edge_back_copy().start()

    mlp_d.start()

    @pl.when(z == 3)
    def _():
        r.dconv[:, 512:520, :] = jnp.zeros((8, 8, 128), F32)

    for n in range(2):
        total_ri = None
        for b in range(4):
            for half in range(2):
                term = dot(
                    r.conv[b * 2 + n, half * 256 : (half + 1) * 256, :],
                    dri[b * 2 + half, :, n * 256 : (n + 1) * 256],
                    TN,
                )
                total_ri = term if total_ri is None else total_ri + term
        r.go[n * 128 : (n + 1) * 128, 1024:1280] = total_ri.astype(BF)
    go_out += go_start(pl.ds(1024, 256))

    @pl.when(z < 3)
    def _():
        edge_back_copy().wait_recv()


    def conv_back(s):
        b, n = lax.div(s, 2), lax.rem(s, 2)
        chan = r.chan[n]
        lanes = pl.ds(pl.multiple_of(256 + n * 128, 128), 128)

        def tile(i, sums):
            offset = r.off[b, pl.ds(pl.multiple_of(i * TILE, 8), TILE + 8), :]
            window = r.dconv[s, pl.ds(pl.multiple_of(i * TILE, 8), TILE + 8), :]
            inner = r.inner[s, pl.ds(pl.multiple_of(i * TILE, 8), TILE + 8), :]
            value = chan[0:1, :] * window[:TILE, :]
            added = [sums[0] + column_sum(window[:TILE, :] * inner[8:, :])]
            for k in (1, 2, 3):
                held = jnp.where(offset >= k, window, 0.0)
                value = value + chan[k : k + 1, :] * held[k : TILE + k, :]
                added.append(sums[k] + column_sum(held[:TILE, :] * inner[8 - k : TILE + 8 - k, :]))
            added.append(sums[4] + column_sum(window[:TILE, :]))
            r.dgi[b * 2 + lax.div(i, 4), tile_rows(lax.rem(i, 4)), lanes] = value.astype(BF)
            return tuple(added)

        sums = lax.fori_loop(0, 512 // TILE, tile, tuple(jnp.zeros((8, 128), F32) for _ in range(5)))
        for j in range(5):
            r.vec[n, j] = r.vec[n, j] + sums[j]

    loop(8, conv_back)
    out.finish(0)
    out.finish(1)
    for h in range(2):

        def out_rows(i, h=h):
            rows = pl.ds(pl.multiple_of(h * 128 + i * 32, 32), 32)
            value = (r.residual[rows, :] + out.total(h, i, 32)).astype(BF)
            for j in range(4):
                r.dgu[j, rows, 512:768] = value[:, j * 256 : (j + 1) * 256]

        loop(4, out_rows)
    for j in range(4):
        returned.append(net.local(r.dgu.at[j, :, pl.ds(512, 256)], r.block_out.at[:, pl.ds(j * 256, 256)]))
    for partner in (sibling, net.plane(1, c), net.plane(2, c)):
        pl.semaphore_signal(r.free, inc=1, device_id=partner, device_id_type=pl.DeviceIdType.MESH)
    for n in range(2):
        sums = [jnp.sum(r.vec[n, j], axis=0, keepdims=True) for j in range(8)]
        sums[7] = sums[7] * (DECAY_SCALE * r.chan[n, 8:9, :])
        r.vsum[z, :, n * 128 : (n + 1) * 128] = jnp.concatenate(sums, axis=0)
    vec = [net.copy(r.vsum.at[z], r.vsum.at[z], net.line(net.up(k), c)) for k in (1, 2, 3)]
    fetched.wait()
    flat = r.dgi[:, :, 0:512].reshape(-1, 512)
    for i in range(4):
        value = dot(r.do_all[:, :, i * 256 : (i + 1) * 256].reshape(-1, 256), flat, TN)
        for j in range(2):
            n0, n1 = value[:, j * 256 : j * 256 + 128], value[:, j * 256 + 128 : j * 256 + 256]
            r.ga[i][:, j * 128 : (j + 1) * 128] = lax.select(c == 0, n0, n1).astype(BF)
            shared = lax.select(c == 0, n1, n0)
            r.gb2[i][:, j * 128 : (j + 1) * 128] = lax.select(c == 0, shared[0:128], shared[128:256]).astype(BF)

    def ga_in(k):
        return r.g_all.at[7, :, pl.ds((k - 1) * 256, 256)]

    def gb_in(k):
        return r.g_all.at[3 + k, pl.ds(128, 128), pl.ds(0, 256)]

    sum_a = LineSum(net, lambda t: r.hid.at[t, :, 0:256], ga_in, heads_in.at)
    sum_b = LineSum(net, lambda t: r.hid.at[4 + t, 0:128, 0:256], gb_in, heads_gate.at)
    sum_a.start()
    sum_b.start()
    mlp_d.relay()
    owners_m.forward()
    first_back = Reduce(
        net,
        r,
        lambda k, core: dot(masked(r.dgi[net.slot(k, core), :, 0:512], counted_two), r.w2[...], NT),
        total.at,
    )
    pl.semaphore_wait(r.free, 3)
    for k in (3, 1, 2, 0):
        first_back.other(k)
    first_back.far()
    first_back.near()
    go_in[p] = r.go[go_rows[0], :]
    for made in go_out:
        made.wait_recv()
    go_line = LineSum(net, lambda t: go_in.at[t], lambda k: go_line_in.at[k - 1], gates_in.at)
    go_line.start()
    first_back.relay()
    mlp_d.end(r.gd_sum)
    owners_d.start()
    first_back.own()
    owners_m.middle()
    sum_a.relay()
    sum_b.relay()
    go_line.relay()
    first_back.finish(0)
    first_back.finish(1)
    sums = jnp.zeros((8, r.x.shape[1]), F32)
    for h in range(2):

        def input_rows(i, sums, h=h):
            rows = pl.ds(pl.multiple_of(h * 128 + i * 32, 32), 32)
            v = r.x[rows, :].astype(F32)
            dn = first_back.total(h, i, 32)
            s = lax.rsqrt(jnp.mean(v * v, axis=-1, keepdims=True) + NORM_EPS)
            u = dn * r.gain[0:1, :]
            r.d_res[rows, :] = r.d_res[rows, :] + (
                s * u - v * (s * s * s * jnp.mean(u * v, axis=-1, keepdims=True))
            )
            return sums + jnp.sum((dn * v * s).reshape(4, 8, -1), axis=0)

        sums = lax.fori_loop(0, 4, input_rows, sums)
    returned.append(net.local(r.d_res, r.d_in))
    gains = jnp.concatenate(
        [
            jnp.sum(sums, axis=0, keepdims=True),
            jnp.sum(r.gain2_sum[...], axis=0, keepdims=True),
            jnp.zeros((6, sums.shape[1]), F32),
        ],
        axis=0,
    )
    for i in range(8):
        r.gsum[i] = gains[:, i * 128 : (i + 1) * 128]
    r.gline[q] = r.gsum[q]
    gain_line = [
        net.copy(r.gsum.at[net.up(k) * 2 + core], r.gline.at[q], net.line(net.up(k), core))
        for k in (1, 2, 3)
        for core in (c, o)
    ]
    gain_line.append(net.copy(r.gsum.at[z * 2 + o], r.gline.at[q], sibling))
    for made in vec:
        made.wait_recv()
    r.vout[p] = r.vsum[0] + r.vsum[1] + r.vsum[2] + r.vsum[3]

    @pl.when(z == p)
    def _():
        for k in (1, 2, 3):
            vector_copy(k).start()

    sum_a.end(r.ga_sum)
    owners_a.start()
    sum_b.end(r.gb2_sum)
    owners_b.start()
    go_line.end(r.go_sum)
    owners_o.start()
    owners_d.forward()
    owners_m.last()
    owners_a.forward()
    owners_b.forward()
    owners_o.forward()
    for made in gain_line:
        made.wait_recv()
    sums = r.gline[0]
    for i in range(1, 8):
        sums = sums + r.gline[i]
    r.gplane[p] = sums
    gain_plane = [net.copy(r.gplane.at[p], r.gplane.at[p], net.plane(k, c)) for k in (1, 2, 3)]

    @pl.when(z != p)
    def _():
        vector_copy(1).wait_recv()

    @pl.when(z == p)
    def _():
        for k in (1, 2, 3):
            vector_copy(k).wait_send()

    owners_d.middle()
    owners_a.middle()
    owners_b.middle()
    owners_o.middle()
    for each in (owners_d, owners_a, owners_b, owners_o):
        each.last()
    for each in (owners_m, owners_d, owners_a, owners_b, owners_o):
        each.end()
    for made in owners + gain_plane:
        made.wait_recv()
    r.gain_out[...] = r.gplane[0] + r.gplane[1] + r.gplane[2] + r.gplane[3]
    r.vec_out[...] = r.vout[z]
    for made in returned:
        made.wait()
    @pl.when(z < 3)
    def _():
        edge_copy().wait_send()

    @pl.when(z > 0)
    def _():
        edge_back_copy().wait_send()

    feed.drain()
    feed_down.drain()
    for made in (mlp_m, mlp_d, go_line, sum_a, sum_b):
        made.drain()
    net.drain()


def assemble(r):
    c = lax.rem(lax.axis_index("seq"), 2)
    count = 0
    stores = []

    def start(src, dst):
        nonlocal count
        made = pltpu.make_async_copy(src, dst, r.local.at[count])
        count += 1
        made.start()
        return made

    mine = pl.ds(pl.multiple_of(c * 128, 128), 128)
    loads = [
        [start(r.fm.at[:, mine], r.vm.at[c]), start(r.fm_x, r.vm.at[1 - c])],
        [start(r.fa.at[:, mine], r.va.at[c]), start(r.fa_x, r.va.at[1 - c]), start(r.fb, r.vb)],
        [start(r.fd, r.vd)],
        [start(r.fo, r.vo)],
    ]

    def loaded(which):
        for made in loads[which]:
            made.wait()

    little = [start(r.vec_in, r.v_vec), start(r.gains, r.v_gains), start(r.fr, r.v_fr), start(r.lens, r.v_lens)]
    passed = [start(r.d_in, r.v_din), start(r.block_out, r.v_block)]
    cols = r.fm.shape[2] // 2
    piece = cols // 4
    loaded(0)
    for j, (stage, out) in enumerate(((r.s_mgate, r.o_mgate), (r.s_mup, r.o_mup))):
        for part in range(4):
            for core in range(2):
                at = (part * 2 + core) * cols
                lanes = slice(j * cols + part * piece, j * cols + (part + 1) * piece)
                stage[:, at : at + cols] = jnp.concatenate(
                    [r.vm[core, chip, :, lanes].astype(F32) for chip in range(4)], axis=1
                )
            here = pl.ds(part * 2 * cols, 2 * cols)
            stores.append(start(stage.at[:, here], out.at[:, here]))
    for made, src, dst in zip(passed, (r.v_din, r.v_block), (r.o_din, r.o_block)):
        made.wait()
        stores.append(start(src, dst))
    loaded(1)
    for j, (stage, out) in enumerate(((r.s_gate, r.o_gate), (r.s_in, r.o_in))):
        lanes = slice(j * 128, (j + 1) * 128)
        for chip in range(4):
            at = chip * 384
            stage[:, at : at + 128] = r.va[0, chip, :, lanes].astype(F32)
            stage[:, at + 128 : at + 256] = r.vb[chip, :, lanes].astype(F32)
            stage[:, at + 256 : at + 384] = r.va[1, chip, :, lanes].astype(F32)
        stores.append(start(stage, out))
    loaded(2)
    for chip in range(4):
        r.s_down[chip * piece : (chip + 1) * piece, :] = r.vd[chip].astype(F32)
    stores.append(start(r.s_down, r.o_mdown))
    for made in little:
        made.wait()
    vec = r.v_vec[...]
    vec = lax.select(c == 0, vec[:, 0:192], vec[:, 64:256])
    r.s_cw[...] = vec[0:4]
    stores.append(start(r.s_cw, r.o_cw))
    for j, (stage, out) in enumerate(((r.s_cb, r.o_cb), (r.s_rb, r.o_rb), (r.s_ib, r.o_ib), (r.s_lam, r.o_lam))):
        stage[...] = vec[4 + j : 5 + j]
        stores.append(start(stage, out))
    for j, (stage, out) in enumerate(((r.s_ngain, r.o_ngain), (r.s_mgain, r.o_mgain))):
        stage[...] = r.v_gains[j : j + 1, :]
        stores.append(start(stage, out))
    counts = [jnp.broadcast_to(r.v_lens[0:1, row : row + 1].astype(F32), (1, 128)) for row in range(5)]
    for chip in range(4):
        for half, (slot, n) in enumerate(((chip * 2, 0), (chip * 2, 1), (chip * 2 + 1, 1))):
            at = chip * 384 + half * 128
            for row in range(5):
                r.s_mean[row, :, at : at + 128] = r.v_fr[slot, n, row : row + 1, :] / counts[row]
    stores.append(start(r.s_mean, r.o_mean))
    loaded(3)
    for chip in range(4):
        rows = slice(chip * 48, (chip + 1) * 48)
        r.s_out[rows, :] = r.vo[chip, :, 0:1024].astype(F32)
        r.s_r[rows, :] = r.vo[chip, :, 1024:1152].astype(F32)
        r.s_i[rows, :] = r.vo[chip, :, 1152:1280].astype(F32)
    for stage, out in ((r.s_out, r.o_out), (r.s_r, r.o_r), (r.s_i, r.o_i)):
        stores.append(start(stage, out))
    for made in stores:
        made.wait()


def shifted(value, axis, by):
    count = lax.axis_size(axis)
    pairs = [(i, i + by) for i in range(count) if 0 <= i + by < count]
    return lax.ppermute(value, axis, pairs)


def entering(value, axis, combine, identity, reverse):
    count, place = (lax.axis_size(axis), lax.axis_index(axis))
    everything = jax.tree.map(lambda part: lax.all_gather(part, axis), value)
    start = jax.tree.map(
        lambda part, zero: jnp.broadcast_to(jnp.asarray(zero, part.dtype), part.shape),
        value,
        identity,
    )

    def step(k, before):
        at = count - 1 - k if reverse else k
        reached = at > place if reverse else at < place
        new = combine(before, jax.tree.map(lambda part: part[at], everything))
        return jax.tree.map(lambda a, b: jnp.where(reached, a, b), new, before)

    return lax.fori_loop(0, count, step, start)


def rms_scale(values):
    return values * lax.rsqrt(jnp.mean(values * values, axis=-1, keepdims=True) + NORM_EPS)


def gelu_tanh(values):
    return jax.nn.gelu(values, approximate=True)


def link(earlier, later):
    return (earlier[0] * later[0], later[0] * earlier[1] + later[1])


def block_product(values, weight):
    count, channels = values.shape
    block_size = weight.shape[1]
    shaped = values.reshape(count, channels // block_size, block_size)
    result = jnp.einsum(
        "lni,nij->lnj",
        shaped,
        weight.reshape(channels // block_size, block_size, block_size),
        preferred_element_type=jnp.float32,
    )
    return result.reshape(count, channels)


def block_back(grads, weight):
    count, channels = grads.shape
    block_size = weight.shape[1]
    shaped = grads.reshape(count, channels // block_size, block_size)
    result = jnp.einsum(
        "lnj,nij->lni",
        shaped,
        weight.reshape(channels // block_size, block_size, block_size),
        preferred_element_type=jnp.float32,
    )
    return result.reshape(count, channels)


def block_weight_grad(values, grads, block_size):
    count, channels = values.shape
    left = values.reshape(count, channels // block_size, block_size)
    right = grads.reshape(count, channels // block_size, block_size)
    return jnp.einsum("lni,lnj->nij", left, right, preferred_element_type=jnp.float32).reshape(
        channels, block_size
    )


def recurrence_terms(conv_in, r_in, i_in, lam_in, restart):
    log_a = -DECAY_SCALE * jax.nn.sigmoid(r_in) * jax.nn.softplus(-lam_in)
    decays = jnp.exp(log_a)
    factor = jnp.where(restart[:, None] > 0, 1.0, jnp.sqrt(-jnp.expm1(2.0 * log_a)))
    return (decays * (1.0 - restart[:, None]), factor * jax.nn.sigmoid(i_in) * conv_in, decays)


def shards(
    inputs,
    out_grad,
    row_lengths,
    norm_gain,
    w_gate,
    w_in,
    conv_w,
    conv_b,
    w_rgate,
    b_rgate,
    w_igate,
    b_igate,
    lam,
    w_out,
    mlp_gain,
    w_mlp_gate,
    w_mlp_up,
    w_mlp_down,
):
    gathered = (
        lax.all_gather(norm_gain, "seq", axis=0, tiled=True),
        lax.all_gather(w_gate, "seq", axis=0, tiled=True),
        lax.all_gather(w_in, "seq", axis=0, tiled=True),
        lax.all_gather(conv_w, "seq", axis=1, tiled=True),
        lax.all_gather(conv_b, "seq", axis=0, tiled=True),
        lax.all_gather(w_rgate, "seq", axis=0, tiled=True),
        lax.all_gather(b_rgate, "seq", axis=0, tiled=True),
        lax.all_gather(w_igate, "seq", axis=0, tiled=True),
        lax.all_gather(b_igate, "seq", axis=0, tiled=True),
        lax.all_gather(lam, "seq", axis=0, tiled=True),
        lax.all_gather(w_out, "seq", axis=0, tiled=True),
        lax.all_gather(mlp_gain, "seq", axis=0, tiled=True),
        lax.all_gather(w_mlp_gate, "seq", axis=0, tiled=True),
        lax.all_gather(w_mlp_up, "seq", axis=0, tiled=True),
        lax.all_gather(w_mlp_down, "seq", axis=0, tiled=True),
    )
    gain_first = gathered[0].astype(jnp.float32)
    conv_taps = gathered[3].astype(jnp.float32)
    conv_bias = gathered[4].astype(jnp.float32)
    lam_value = gathered[9].astype(jnp.float32)
    gain_second = gathered[11].astype(jnp.float32)
    tokens = inputs[0].astype(jnp.float32)
    local_len = tokens.shape[0]
    channels = gathered[2].shape[1]
    block_size = gathered[5].shape[1]
    kernel_taps = conv_taps.shape[0]
    lengths = row_lengths[0]
    row_ends = jnp.cumsum(lengths)
    row_starts = row_ends - lengths
    positions = lax.axis_index("seq") * local_len + jnp.arange(local_len, dtype=jnp.int32)
    started = positions[:, None] >= row_starts[None, :]
    row_index = jnp.sum(started.astype(jnp.int32), axis=1) - 1
    row_first = jnp.max(jnp.where(started, row_starts[None, :], 0), axis=1)
    offset = positions - row_first
    restart = (offset == 0).astype(jnp.float32)
    members = (row_index[:, None] == jnp.arange(lengths.shape[0], dtype=jnp.int32)[None, :]).astype(
        jnp.float32
    )
    tap_masks = [(offset >= tap).astype(jnp.float32)[:, None] for tap in range(kernel_taps)]
    scaled, norm_pull = jax.vjp(rms_scale, tokens)
    normed = (scaled * gain_first).astype(jnp.bfloat16)
    gate_pre = jnp.dot(normed, gathered[1], preferred_element_type=jnp.float32)
    gate_branch, gate_pull = jax.vjp(gelu_tanh, gate_pre)
    inner = jnp.dot(normed, gathered[2], preferred_element_type=jnp.float32).astype(jnp.bfloat16)
    edge_rows = shifted(inner[local_len - kernel_taps + 1 :], "seq", 1)
    extended = jnp.concatenate([edge_rows, inner], axis=0).astype(jnp.float32)
    conv_sum = conv_bias + jnp.zeros((local_len, channels), jnp.float32)
    for tap in range(kernel_taps):
        start_row = kernel_taps - 1 - tap
        conv_sum = (
            conv_sum + conv_taps[tap] * extended[start_row : start_row + local_len] * tap_masks[tap]
        )
    conv_low = conv_sum.astype(jnp.bfloat16)
    conv_value = conv_low.astype(jnp.float32)
    r_pre = block_product(conv_low, gathered[5]) + gathered[6].astype(jnp.float32)
    i_pre = block_product(conv_low, gathered[7]) + gathered[8].astype(jnp.float32)

    def local_terms(conv_in, r_in, i_in, lam_in):
        return recurrence_terms(conv_in, r_in, i_in, lam_in, restart)

    (carried, drive_term, decays), recur_pull = jax.vjp(
        local_terms, conv_value, r_pre, i_pre, lam_value
    )
    prefix_decay, local_state = lax.associative_scan(link, (carried, drive_term), axis=0)
    identity = (jnp.ones((channels,), jnp.float32), jnp.zeros((channels,), jnp.float32))
    incoming = entering((prefix_decay[-1], local_state[-1]), "seq", link, identity, False)[1]
    states = local_state + prefix_decay * incoming
    mixed_low = (states * gate_branch).astype(jnp.bfloat16)
    residual = tokens + jnp.dot(mixed_low, gathered[10], preferred_element_type=jnp.float32)
    scaled_two, norm_pull_two = jax.vjp(rms_scale, residual)
    normed_two = (scaled_two * gain_second).astype(jnp.bfloat16)
    up_gate = jnp.dot(normed_two, gathered[12], preferred_element_type=jnp.float32)
    up_lin = jnp.dot(normed_two, gathered[13], preferred_element_type=jnp.float32)
    gelu_up, up_pull = jax.vjp(gelu_tanh, up_gate)
    hidden = (gelu_up * up_lin).astype(jnp.bfloat16)
    block_out = (
        residual + jnp.dot(hidden, gathered[14], preferred_element_type=jnp.float32)
    ).astype(jnp.bfloat16)
    row_sums = lax.psum(jnp.dot(members.T, decays, precision=lax.Precision.HIGHEST), "seq")
    gate_mean = row_sums / lengths.astype(jnp.float32)[:, None]
    grad_top = out_grad[0]
    grad_mdown = jnp.einsum("tf,td->fd", hidden, grad_top, preferred_element_type=jnp.float32)
    d_hidden = jnp.einsum("td,fd->tf", grad_top, gathered[14], preferred_element_type=jnp.float32)
    d_upgate = up_pull(d_hidden * up_lin)[0].astype(jnp.bfloat16)
    d_uplin = (d_hidden * gelu_up).astype(jnp.bfloat16)
    grad_mgate = jnp.einsum("td,tf->df", normed_two, d_upgate, preferred_element_type=jnp.float32)
    grad_mup = jnp.einsum("td,tf->df", normed_two, d_uplin, preferred_element_type=jnp.float32)
    d_normed_two = jnp.einsum(
        "tf,df->td", d_upgate, gathered[12], preferred_element_type=jnp.float32
    )
    d_normed_two = d_normed_two + jnp.einsum(
        "tf,df->td", d_uplin, gathered[13], preferred_element_type=jnp.float32
    )
    grad_mgain = jnp.sum(d_normed_two * scaled_two, axis=0)
    d_residual = grad_top.astype(jnp.float32) + norm_pull_two(d_normed_two * gain_second)[0]
    d_outlow = d_residual.astype(jnp.bfloat16)
    grad_outw = jnp.einsum("tr,td->rd", mixed_low, d_outlow, preferred_element_type=jnp.float32)
    d_mixed = jnp.einsum("td,rd->tr", d_outlow, gathered[10], preferred_element_type=jnp.float32)
    direct = d_mixed * gate_branch
    d_gatelow = gate_pull(d_mixed * states)[0].astype(jnp.bfloat16)
    grad_gatew = jnp.einsum("td,tr->dr", normed, d_gatelow, preferred_element_type=jnp.float32)
    next_decay = jnp.concatenate([carried[1:], jnp.ones((1, channels), jnp.float32)], axis=0)
    suffix_decay, local_grad = lax.associative_scan(
        link, (next_decay, direct), axis=0, reverse=True
    )
    arriving = entering(
        (carried[0] * suffix_decay[0], carried[0] * local_grad[0]), "seq", link, identity, True
    )[1]
    d_states = local_grad + suffix_decay * arriving
    previous = jnp.concatenate([incoming[None, :], states[:-1]], axis=0)
    grad_convval, d_rpre, d_ipre, grad_lambda = recur_pull(
        (d_states * previous, d_states, jnp.zeros_like(decays))
    )
    d_rlow = d_rpre.astype(jnp.bfloat16)
    d_ilow = d_ipre.astype(jnp.bfloat16)
    grad_rw = block_weight_grad(conv_low, d_rlow, block_size)
    grad_rb = jnp.sum(d_rlow.astype(jnp.float32), axis=0)
    grad_iw = block_weight_grad(conv_low, d_ilow, block_size)
    grad_ib = jnp.sum(d_ilow.astype(jnp.float32), axis=0)
    grad_convsum = grad_convval + block_back(d_rlow, gathered[5]) + block_back(d_ilow, gathered[7])
    grad_cb = jnp.sum(grad_convsum, axis=0)
    conv_again = gathered[3].astype(jnp.float32)
    grad_extended = jnp.zeros((local_len + kernel_taps - 1, channels), jnp.float32)
    tap_grads = []
    for tap in range(kernel_taps):
        start_row = kernel_taps - 1 - tap
        masked = grad_convsum * tap_masks[tap]
        tap_grads.append(jnp.sum(masked * extended[start_row : start_row + local_len], axis=0))
        grad_extended = grad_extended + jnp.pad(
            masked * conv_again[tap], ((start_row, tap), (0, 0))
        )
    grad_cw = jnp.stack(tap_grads)
    edge_grads = shifted(grad_extended[: kernel_taps - 1], "seq", -1)
    d_inner = (
        grad_extended[kernel_taps - 1 :]
        + jnp.pad(edge_grads, ((local_len - kernel_taps + 1, 0), (0, 0)))
    ).astype(jnp.bfloat16)
    grad_inw = jnp.einsum("td,tr->dr", normed, d_inner, preferred_element_type=jnp.float32)
    d_normed = jnp.einsum("tr,dr->td", d_gatelow, gathered[1], preferred_element_type=jnp.float32)
    d_normed = d_normed + jnp.einsum(
        "tr,dr->td", d_inner, gathered[2], preferred_element_type=jnp.float32
    )
    grad_gain = jnp.sum(d_normed * scaled, axis=0)
    d_tokens = d_residual + norm_pull(d_normed * gain_first)[0]
    shares = (
        lax.psum_scatter(grad_gain, "seq", scatter_dimension=0, tiled=True),
        lax.psum_scatter(grad_gatew, "seq", scatter_dimension=0, tiled=True),
        lax.psum_scatter(grad_inw, "seq", scatter_dimension=0, tiled=True),
        lax.psum_scatter(grad_cw, "seq", scatter_dimension=1, tiled=True),
        lax.psum_scatter(grad_cb, "seq", scatter_dimension=0, tiled=True),
        lax.psum_scatter(grad_rw, "seq", scatter_dimension=0, tiled=True),
        lax.psum_scatter(grad_rb, "seq", scatter_dimension=0, tiled=True),
        lax.psum_scatter(grad_iw, "seq", scatter_dimension=0, tiled=True),
        lax.psum_scatter(grad_ib, "seq", scatter_dimension=0, tiled=True),
        lax.psum_scatter(grad_lambda, "seq", scatter_dimension=0, tiled=True),
        lax.psum_scatter(grad_outw, "seq", scatter_dimension=0, tiled=True),
        lax.psum_scatter(grad_mgain, "seq", scatter_dimension=0, tiled=True),
        lax.psum_scatter(grad_mgate, "seq", scatter_dimension=0, tiled=True),
        lax.psum_scatter(grad_mup, "seq", scatter_dimension=0, tiled=True),
        lax.psum_scatter(grad_mdown, "seq", scatter_dimension=0, tiled=True),
    )
    totals = (
        lax.psum(shares[0].astype(jnp.bfloat16), "batch").astype(jnp.float32),
        lax.psum(shares[1].astype(jnp.bfloat16), "batch").astype(jnp.float32),
        lax.psum(shares[2].astype(jnp.bfloat16), "batch").astype(jnp.float32),
        lax.psum(shares[3].astype(jnp.bfloat16), "batch").astype(jnp.float32),
        lax.psum(shares[4].astype(jnp.bfloat16), "batch").astype(jnp.float32),
        lax.psum(shares[5].astype(jnp.bfloat16), "batch").astype(jnp.float32),
        lax.psum(shares[6].astype(jnp.bfloat16), "batch").astype(jnp.float32),
        lax.psum(shares[7].astype(jnp.bfloat16), "batch").astype(jnp.float32),
        lax.psum(shares[8].astype(jnp.bfloat16), "batch").astype(jnp.float32),
        lax.psum(shares[9].astype(jnp.bfloat16), "batch").astype(jnp.float32),
        lax.psum(shares[10].astype(jnp.bfloat16), "batch").astype(jnp.float32),
        lax.psum(shares[11].astype(jnp.bfloat16), "batch").astype(jnp.float32),
        lax.psum(shares[12].astype(jnp.bfloat16), "batch").astype(jnp.float32),
        lax.psum(shares[13].astype(jnp.bfloat16), "batch").astype(jnp.float32),
        lax.psum(shares[14].astype(jnp.bfloat16), "batch").astype(jnp.float32),
    )
    return (
        block_out[None],
        d_tokens[None],
        totals[0],
        totals[1],
        totals[2],
        totals[3],
        totals[4],
        totals[5],
        totals[6],
        totals[7],
        totals[8],
        totals[9],
        totals[10],
        totals[11],
        totals[12],
        totals[13],
        totals[14],
        gate_mean[None],
    )


def planes(
    inputs,
    out_grad,
    row_lengths,
    norm_gain,
    w_gate,
    w_in,
    conv_w,
    conv_b,
    w_rgate,
    b_rgate,
    w_igate,
    b_igate,
    lam,
    w_out,
    mlp_gain,
    w_mlp_gate,
    w_mlp_up,
    w_mlp_down,
):
    vmem = pltpu.VMEM
    done = kernel_call(
        layer,
        dict(
            x_in=inputs[0], cw=conv_w, cb=conv_b, br=b_rgate, bi=b_igate, lam=lam, ngain=norm_gain, mgain=mlp_gain,
            lens=row_lengths, g=out_grad[0], wg=w_gate, wi=w_in, wr=w_rgate, wv=w_igate, wout=w_out,
            wmg=w_mlp_gate, wmu=w_mlp_up, wmd=w_mlp_down,
        ),
        dict(
            block_out=array(256, 1024, dtype=BF),
            d_in=array(256, 1024),
            fm=array(4, 256, 768, dtype=BF),
            fm_x=array(4, 128, 768, dtype=BF),
            fd=array(4, 96, 1024, dtype=BF),
            fa=array(4, 256, 256, dtype=BF),
            fa_x=array(4, 128, 256, dtype=BF),
            fb=array(4, 128, 256, dtype=BF),
            fo=array(4, 48, 1280, dtype=BF),
            fr=array(8, 2, 8, 128),
            vec_out=array(8, 256),
            gain_out=array(8, 128),
            normed_far=array(8, 256, 1024, dtype=BF),
        ),
        dict(
            x=vmem((256, 1024), BF),
            x_all=vmem((8, 256, 1024), BF),
            normed=vmem((8, 256, 1024), BF),
            g_all=vmem((8, 256, 1024), BF),
            small_rows=vmem((16, 256), F32),
            small=vmem((16, 256), BF),
            small_all=vmem((2, 4, 16, 256), BF),
            lens_out=vmem((8, 128), F32),
            lens_all=vmem((4, 8, 128), F32),
            off=vmem((4, 520, 128), F32),
            starts_all=vmem((4, 8, 128), F32),
            chan=vmem((2, 16, 128), F32),
            gain=vmem((8, 1024), F32),
            wgi3=vmem((4, 256, 768), BF),
            w2=vmem((1024, 512), BF),
            gq=vmem((4, 48, 256), BF),
            g3=vmem((2, 192, 256), BF),
            wq=vmem((4, 48, 1024), BF),
            wri=vmem((2, 128, 256), BF),
            w3=vmem((2, 192, 1024), BF),
            wo=vmem((256, 1024), BF),
            wgu_out=vmem((2, 128, 768), BF),
            wgu_all=vmem((8, 128, 768), BF),
            wmd_all=vmem((4, 96, 1024), BF),
            gp=vmem((8, 512, 128), F32),
            gb=vmem((8, 520, 128), F32),
            inner=vmem((8, 520, 128), F32),
            conv=vmem((8, 512, 128), BF),
            sr=vmem((8, 512, 128), F32),
            si=vmem((8, 512, 128), F32),
            dec=vmem((8, 512, 128), F32),
            drv=vmem((8, 512, 128), F32),
            states=vmem((8, 520, 128), F32),
            mixed=vmem((8, 256, 256), BF),
            tot=vmem((2, 4, 2, 8, 128), F32),
            inc=vmem((8, 128), F32),
            rs_all=vmem((4, 8, 8, 128), F32),
            rows_sum=vmem((8, 8, 128), F32),
            residual=vmem((256, 1024), F32),
            d_res=vmem((256, 1024), F32),
            hid=vmem((8, 256, 384), BF),
            dgu=vmem((8, 256, 768), BF),
            gm=vmem((4, 256, 768), BF),
            gm_sum=vmem((256, 768), BF),
            gd=vmem((4, 96, 1024), BF),
            gd_in=vmem((3, 96, 1024), BF),
            gd_sum=vmem((96, 1024), BF),
            go=vmem((256, 1280), BF),
            go_q=vmem((4, 48, 1280), BF),
            go_l=vmem((3, 48, 1280), BF),
            go_sum=vmem((48, 1280), BF),
            ga_sum=vmem((256, 256), BF),
            gb2_sum=vmem((128, 256), BF),
            gain2_sum=vmem((8, 1024), F32),
            vec=vmem((2, 8, 8, 128), F32),
            vsum=vmem((4, 8, 256), F32),
            vout=vmem((4, 8, 256), F32),
            gsum=vmem((8, 8, 128), F32),
            gline=vmem((8, 8, 128), F32),
            gplane=vmem((4, 8, 128), F32),
            free=pltpu.SemaphoreType.REGULAR,
            **reduce_scratch(256, 1024),
        ),
        154,
        37,
        (
            "x_in", "g", "wg", "wi", "wr", "wv", "wout", "wmg", "wmu", "wmd", "d_in", "block_out", "fm", "fm_x", "fd", "fa", "fa_x", "fb", "fo",
            "fr", "normed_far",
        ),
    )
    out = kernel_call(
        assemble,
        dict(
            {name: done[name] for name in ("d_in", "block_out", "fm", "fm_x", "fd", "fa", "fa_x", "fb", "fo", "fr")},
            vec_in=done["vec_out"], gains=done["gain_out"], lens=row_lengths,
        ),
        dict(
            o_din=array(256, 1024),
            o_block=array(256, 1024, dtype=BF),
            o_gate=array(128, 1536),
            o_in=array(128, 1536),
            o_mgate=array(128, 3072),
            o_mup=array(128, 3072),
            o_mdown=array(384, 1024),
            o_out=array(192, 1024),
            o_r=array(192, 128),
            o_i=array(192, 128),
            o_cw=array(4, 192),
            o_cb=array(1, 192),
            o_rb=array(1, 192),
            o_ib=array(1, 192),
            o_lam=array(1, 192),
            o_ngain=array(1, 128),
            o_mgain=array(1, 128),
            o_mean=array(5, 1, 1536),
        ),
        dict(
            v_din=vmem((256, 1024), F32),
            v_block=vmem((256, 1024), BF),
            vm=vmem((2, 4, 128, 768), BF),
            va=vmem((2, 4, 128, 256), BF),
            vb=vmem((4, 128, 256), BF),
            vd=vmem((4, 96, 1024), BF),
            vo=vmem((4, 48, 1280), BF),
            s_mgate=vmem((128, 3072), F32),
            s_mup=vmem((128, 3072), F32),
            s_gate=vmem((128, 1536), F32),
            s_in=vmem((128, 1536), F32),
            s_down=vmem((384, 1024), F32),
            s_out=vmem((192, 1024), F32),
            s_r=vmem((192, 128), F32),
            s_i=vmem((192, 128), F32),
            s_cw=vmem((4, 192), F32),
            s_cb=vmem((1, 192), F32),
            s_rb=vmem((1, 192), F32),
            s_ib=vmem((1, 192), F32),
            s_lam=vmem((1, 192), F32),
            s_ngain=vmem((1, 128), F32),
            s_mgain=vmem((1, 128), F32),
            s_mean=vmem((5, 1, 1536), F32),
            v_vec=vmem((8, 256), F32),
            v_gains=vmem((8, 128), F32),
            v_fr=vmem((8, 2, 8, 128), F32),
            v_lens=vmem((1, 5), jnp.int32),
        ),
        0,
        37,
        None,
    )
    return (
        out["o_block"][None],
        out["o_din"][None],
        out["o_ngain"][0],
        out["o_gate"],
        out["o_in"],
        out["o_cw"],
        out["o_cb"][0],
        out["o_r"],
        out["o_rb"][0],
        out["o_i"],
        out["o_ib"][0],
        out["o_lam"][0],
        out["o_out"],
        out["o_mgain"][0],
        out["o_mgate"],
        out["o_mup"],
        out["o_mdown"],
        jnp.transpose(out["o_mean"], (1, 0, 2)),
    )


def solution(mesh):
    in_specs = (
        P("batch", "seq", None),
        P("batch", "seq", None),
        P("batch", None),
        P("seq"),
        P("seq", None),
        P("seq", None),
        P(None, "seq"),
        P("seq"),
        P("seq", None),
        P("seq"),
        P("seq", None),
        P("seq"),
        P("seq"),
        P("seq", None),
        P("seq"),
        P("seq", None),
        P("seq", None),
        P("seq", None),
    )
    out_specs = (
        P("batch", "seq", None),
        P("batch", "seq", None),
        P("seq"),
        P("seq", None),
        P("seq", None),
        P(None, "seq"),
        P("seq"),
        P("seq", None),
        P("seq"),
        P("seq", None),
        P("seq"),
        P("seq"),
        P("seq", None),
        P("seq"),
        P("seq", None),
        P("seq", None),
        P("seq", None),
        P("batch", None, None),
    )
    in_planes = mesh.shape["batch"] == 4 and mesh.shape["seq"] == 8
    body = planes if in_planes else shards
    return jax.shard_map(body, mesh=mesh, in_specs=in_specs, out_specs=out_specs, check_vma=False)
```

```python
import functools
import types

import jax
import jax.numpy as jnp
from jax import lax
from jax.experimental import pallas as pl
from jax.experimental.pallas import tpu as pltpu
from jax.sharding import PartitionSpec as P

NORM_EPS = 1e-06
DECAY_SCALE = 8.0
BF = jnp.bfloat16
F32 = jnp.float32
GELU_SCALE = 0.7978845608028654
GELU_CUBE = 0.044715
TILE = 64
NN = (((1,), (0,)), ((), ()))
NT = (((1,), (1,)), ((), ()))
TN = (((0,), (0,)), ((), ()))


def dot(left, right, dims=NN):
    return lax.dot_general(left, right, dims, preferred_element_type=F32)


def loop(count, body):
    def step(i, carry):
        body(i)
        return carry

    lax.fori_loop(0, count, step, 0)


class Net:
    def __init__(self, r):
        self.send, self.recv, self.count = r.send, r.recv, 0
        self.here, self.here_count = r.local, 0
        self.pending = []
        self.p = lax.axis_index("batch")
        self.q = lax.axis_index("seq")
        self.z = lax.div(self.q, 2)
        self.c = lax.rem(self.q, 2)
        self.o = 1 - self.c
        p = self.p
        self.near = (p, p + 1 - 2 * lax.rem(p, 2), lax.rem(p + 2, 4), 3 - p)

    def plane(self, k, core):
        return {"batch": self.near[k], "seq": self.z * 2 + core}

    def line(self, z, core):
        return {"batch": self.p, "seq": z * 2 + core}

    def up(self, k):
        return lax.rem(self.z + k, 4)

    def down(self, k):
        return lax.rem(self.z + 4 - k, 4)

    def slot(self, k, core):
        return self.near[k] * 2 + core

    def greet(self):
        barrier = pltpu.get_barrier_semaphore()
        partners = [self.plane(k, core) for k in (1, 2, 3) for core in (0, 1)]
        partners += [self.line(self.up(k), core) for k in (1, 2, 3) for core in (0, 1)]
        partners += [self.line(self.z, self.o)]
        for partner in partners:
            pl.semaphore_signal(barrier, inc=1, device_id=partner, device_id_type=pl.DeviceIdType.MESH)
        pl.semaphore_wait(barrier, len(partners))

    def reserve(self, count):
        first = self.count
        self.count += count
        return first

    def describe(self, src, dst, device, send_at, recv_at):
        return pltpu.make_async_remote_copy(
            src_ref=src,
            dst_ref=dst,
            send_sem=self.send.at[send_at],
            recv_sem=self.recv.at[recv_at],
            device_id=device,
            device_id_type=pl.DeviceIdType.MESH,
        )

    def copy(self, src, dst, device, sent=None, at=None):
        at = self.reserve(1) if at is None else at
        made = self.describe(src, dst, device, at, at)
        made.start()
        (self.pending if sent is None else sent).append(made)
        return made

    def local(self, src, dst):
        made = pltpu.make_async_copy(src, dst, self.here.at[self.here_count])
        self.here_count += 1
        made.start()
        return made

    def drain(self):
        assert (self.count, self.here_count) == (self.send.shape[0], self.here.shape[0]), (self.count, self.here_count)
        for made in self.pending:
            made.wait_send()
        self.pending = []


class Gather:
    def __init__(self, net, own, everything, at=None):
        self.net, self.own, self.all = net, own, everything
        self.sent = []
        self.at = net.reserve(14) if at is None else at
        self.half = everything.shape[1] // 2
        self.x0, self.y1, self.x1, self.y0 = [], [], [], []

    def half_of(self, slot, h):
        return self.all.at[slot, pl.ds(h * self.half, self.half)]

    def send(self, src, dst, device, at):
        return self.net.copy(src, dst, device, self.sent, self.at + at)

    def start(self, part):
        net = self.net
        mine = net.slot(0, net.c)
        size = self.half // 2
        low, high = pl.ds(part * size, size), pl.ds(self.half + part * size, size)
        for made, rows, k, at in ((self.x0, low, 1, 0), (self.y1, high, 2, 2), (self.x1, high, 1, 4), (self.y0, low, 2, 6)):
            made.append(self.send(self.own.at[rows], self.all.at[mine, rows], net.plane(k, net.c), at + part))
        if part == 1:
            self.s = [self.send(self.own, self.all.at[mine], net.plane(0, net.o), 8)]

    def forward(self):
        net = self.net
        for made in self.x0:
            made.wait_recv()
        block = self.half_of(net.slot(1, net.c), 0)
        self.d0 = self.send(block, block, net.plane(2, net.c), 9)
        for made in self.y1:
            made.wait_recv()
        block = self.half_of(net.slot(2, net.c), 1)
        self.d1 = self.send(block, block, net.plane(1, net.c), 10)

    def across(self, k):
        net = self.net
        block = self.all.at[net.slot(k, net.c)]
        self.s.append(self.send(block, block, net.plane(0, net.o), 10 + k))

    def middle(self):
        for made in self.x1:
            made.wait_recv()
        self.across(1)
        for made in self.y0:
            made.wait_recv()
        self.across(2)

    def last(self):
        self.d0.wait_recv()
        self.d1.wait_recv()
        self.across(3)

    def sibling(self, k):
        self.s[k].wait_recv()

    def release(self):
        for made in self.sent:
            made.wait_send()
        self.sent = []


class Owners:
    def __init__(self, net, own, everything, extra=None, at=None, cut=None):
        self.net, self.own, self.all, self.extra = net, own, everything, extra
        self.at = net.reserve(6 if extra is None else 10) if at is None else at
        self.half = everything.shape[1] // 2 if cut is None else cut
        self.rows = (pl.ds(0, self.half), pl.ds(self.half, everything.shape[1] - self.half))
        self.s = [None] * 4

    def part(self, k, h):
        return self.all.at[self.net.near[k], self.rows[h]]

    def across(self, k, block):
        if self.extra is not None:
            net = self.net
            rows = pl.ds(pl.multiple_of(net.o * self.half, 16), self.half)
            self.s[k] = net.copy(block.at[rows], self.extra.at[net.near[k]], net.plane(0, net.o), None, self.at + 6 + k)

    def start(self):
        net = self.net
        low, high = self.own.at[self.rows[0]], self.own.at[self.rows[1]]
        self.x0 = net.copy(low, self.part(0, 0), net.plane(1, net.c), None, self.at + 0)
        self.y1 = net.copy(high, self.part(0, 1), net.plane(2, net.c), None, self.at + 1)
        self.x1 = net.copy(high, self.part(0, 1), net.plane(1, net.c), None, self.at + 2)
        self.y0 = net.copy(low, self.part(0, 0), net.plane(2, net.c), None, self.at + 3)
        self.across(0, self.own)
        self.kept = net.local(self.own, self.all.at[net.p])

    def forward(self):
        net = self.net
        self.x0.wait_recv()
        self.d0 = net.copy(self.part(1, 0), self.part(1, 0), net.plane(2, net.c), None, self.at + 4)
        self.y1.wait_recv()
        self.d1 = net.copy(self.part(2, 1), self.part(2, 1), net.plane(1, net.c), None, self.at + 5)

    def middle(self):
        self.x1.wait_recv()
        self.across(1, self.all.at[self.net.near[1]])
        self.y0.wait_recv()
        self.across(2, self.all.at[self.net.near[2]])

    def last(self):
        self.d0.wait_recv()
        self.d1.wait_recv()
        self.across(3, self.all.at[self.net.near[3]])

    def end(self):
        if self.extra is not None:
            for made in self.s:
                made.wait_recv()
        self.kept.wait()


class LineGather:
    def __init__(self, net, own, first, place):
        self.net, self.own, self.first, self.place = net, own, first, place
        self.at = net.reserve(4 * len(own))

    def made(self, k, j):
        net = self.net
        src, core = self.own[j]
        at = self.at + 4 * j + k - 1
        return net.describe(src, self.first(j), net.line(net.up(k), core), at, at)

    def handed(self, j):
        net = self.net
        far = 6 - 3 * net.z
        here = self.place(j, far)
        at = self.at + 4 * j
        return net.describe(here, here, net.line(3 - far, net.c), at + 3, at + 2 * net.z - 2)

    def direct(self, k, body):
        z = self.net.z
        if k == 2:
            body()
        else:
            pl.when(z != (0 if k == 3 else 3))(body)

    def start(self, k, items):
        def send():
            for j in items:
                self.made(k, j).start()

        self.direct(k, send)

    def inside(self, body):
        z = self.net.z
        pl.when((z == 1) | (z == 2))(body)

    def relay(self):
        @self.inside
        def _():
            for j in range(len(self.own)):
                self.made(2, j).wait_recv()
                self.handed(j).start()

    def end(self):
        z = self.net.z
        for k in (1, 3):
            for j in range(len(self.own)):
                self.made(k, j).wait_recv()

        @pl.when((z == 0) | (z == 3))
        def _():
            for j in range(len(self.own)):
                self.made(2, j).wait_recv()

    def drain(self):
        for k in (1, 2, 3):

            def wait(k=k):
                for j in range(len(self.own)):
                    self.made(k, j).wait_send()

            self.direct(k, wait)

        @self.inside
        def _():
            for j in range(len(self.own)):
                self.handed(j).wait_send()


class LineSum:
    def __init__(self, net, block, slot, at=None):
        self.net, self.block, self.slot = net, block, slot
        self.at = net.reserve(3) if at is None else at

    def made(self, k):
        net = self.net
        at = self.at + k - 1
        to = lax.rem(2 * net.z + 1, 5) if k == 2 else net.up(k)
        return net.describe(self.block(net.up(k)), self.slot(k), net.line(to, net.c), at, at)

    def start(self):
        z = self.net.z
        self.made(2).start()
        pl.when(z != 1)(lambda: self.made(1).start())
        pl.when(z != 2)(lambda: self.made(3).start())

    def relay(self, step=16):
        z = self.net.z

        @pl.when((z == 1) | (z == 2))
        def _():
            self.made(2).wait_recv()
            mine, extra = self.block(3 - z), self.slot(2)

            def body(i):
                rows = pl.ds(pl.multiple_of(i * step, step), step)
                mine[rows, :] = (mine[rows, :].astype(F32) + extra[rows, :].astype(F32)).astype(BF)

            loop(mine.shape[0] // step, body)

        pl.when(z == 1)(lambda: self.made(1).start())
        pl.when(z == 2)(lambda: self.made(3).start())

    def end(self, dst, step=16):
        z = self.net.z
        self.made(1).wait_recv()
        self.made(3).wait_recv()
        edge = (z == 0) | (z == 3)
        pl.when(edge)(lambda: self.made(2).wait_recv())
        share = jnp.where(edge, 1.0, 0.0)
        own = self.block(z)

        def body(i):
            rows = pl.ds(pl.multiple_of(i * step, step), step)
            value = own[rows, :].astype(F32) + share * self.slot(2)[rows, :].astype(F32)
            value = value + self.slot(1)[rows, :].astype(F32) + self.slot(3)[rows, :].astype(F32)
            dst[rows, :] = value.astype(BF)

        loop(dst.shape[0] // step, body)

    def drain(self):
        for k in (1, 2, 3):
            self.made(k).wait_send()


class Reduce:
    def __init__(self, net, r, value, at=None):
        self.net, self.value = net, value
        self.at = net.reserve(12) if at is None else at
        self.keep, self.out, self.into = r.rs_keep, r.rs_out, r.rs_in
        self.xs, self.ys, self.xr, self.yr = r.rs_xs, r.rs_ys, r.rs_xr, r.rs_yr
        self.half = self.keep.shape[1]
        self.cross = [None] * 4
        self.sent = []

    def other(self, k):
        net = self.net
        self.out[k] = self.value(k, net.o).astype(BF)
        self.cross[k] = net.copy(self.out.at[k], self.into.at[k], net.plane(0, net.o), self.sent, self.at + k)

    def mine(self, k):
        self.cross[k].wait_recv()
        value = self.value(k, self.net.c) + self.into[k].astype(F32)
        return value[: self.half], value[self.half :]

    def send(self, src, dst, j, k, part=None):
        net = self.net
        at = self.at + 4 + j + (part or 0) + (0 if src is self.xs else 4)
        src, dst = src.at[j], dst.at[j]
        if part is not None:
            rows = pl.ds(part * self.half // 2, self.half // 2)
            src, dst = src.at[rows], dst.at[rows]
        return net.copy(src, dst, net.plane(k, net.c), self.sent, at)

    def far(self):
        low, high = self.mine(3)
        self.xs[0] = low.astype(BF)
        self.x0 = self.send(self.xs, self.xr, 0, 1)
        self.ys[0] = high.astype(BF)
        self.y0 = self.send(self.ys, self.yr, 0, 2)

    def near(self):
        low, high = self.mine(1)
        self.xs[1] = low.astype(BF)
        self.x1 = self.send(self.xs, self.xr, 1, 1)
        self.keep[2] = high
        low, high = self.mine(2)
        self.ys[1] = high.astype(BF)
        self.y1 = self.send(self.ys, self.yr, 1, 2)
        self.keep[3] = low

    def relay(self):
        size = self.half // 2
        self.x2, self.y2 = [], []
        for part in (0, 1):
            rows = slice(part * size, (part + 1) * size)
            if part == 0:
                self.x0.wait_recv()
            self.ys[2, rows, :] = (self.keep[3, rows, :] + self.xr[0, rows, :].astype(F32)).astype(BF)
            self.y2.append(self.send(self.ys, self.yr, 2, 2, part))
            if part == 0:
                self.y0.wait_recv()
            self.xs[2, rows, :] = (self.keep[2, rows, :] + self.yr[0, rows, :].astype(F32)).astype(BF)
            self.x2.append(self.send(self.xs, self.xr, 2, 1, part))

    def own(self):
        self.keep[0], self.keep[1] = self.mine(0)

    def finish(self, part):
        if part == 0:
            self.x1.wait_recv()
            self.y1.wait_recv()
        self.x2[part].wait_recv()
        self.y2[part].wait_recv()
        if part == 1:
            for made in self.sent:
                made.wait_send()
            self.sent = []

    def total(self, h, i, step):
        rows = pl.ds(pl.multiple_of(i * step, step), step)
        first, second = (self.xr, self.yr) if h == 0 else (self.yr, self.xr)
        return self.keep[h, rows, :] + first[1, rows, :].astype(F32) + second[2, rows, :].astype(F32)


def reduce_scratch(rows, width):
    half = rows // 2
    return dict(
        rs_keep=pltpu.VMEM((4, half, width), F32),
        rs_out=pltpu.VMEM((4, rows, width), BF),
        rs_in=pltpu.VMEM((4, rows, width), BF),
        rs_xs=pltpu.VMEM((3, half, width), BF),
        rs_ys=pltpu.VMEM((3, half, width), BF),
        rs_xr=pltpu.VMEM((3, half, width), BF),
        rs_yr=pltpu.VMEM((3, half, width), BF),
    )


def kernel_call(body, ins, outs, scratch, copies, local, far):
    names = list(ins) + list(outs) + list(scratch)
    near = pl.BlockSpec(memory_space=pltpu.VMEM)
    away = pl.BlockSpec(memory_space=pl.ANY)
    shapes = list(scratch.values())
    if copies:
        names += ["send", "recv"]
        shapes += [pltpu.SemaphoreType.DMA((copies,))] * 2
    if local:
        names.append("local")
        shapes.append(pltpu.SemaphoreType.DMA((local,)))

    def kernel(*refs):
        body(types.SimpleNamespace(**dict(zip(names, refs))))

    params = dict(vmem_limit_bytes=62 * 2**20)
    if copies:
        params.update(collective_id=0, has_side_effects=True)
    results = pl.pallas_call(
        kernel,
        out_shape=list(outs.values()),
        in_specs=[away if far is None or name in far else near for name in ins],
        out_specs=[away if far is None or name in far else near for name in outs],
        scratch_shapes=shapes,
        compiler_params=pltpu.CompilerParams(**params),
        name=body.__name__,
    )(*ins.values())
    return dict(zip(outs, results))


def array(*shape, dtype=F32):
    return jax.ShapeDtypeStruct(shape, dtype)


def gelu_parts(v):
    square = v * v
    t = jnp.tanh(GELU_SCALE * v * (1.0 + GELU_CUBE * square))
    half = 0.5 + 0.5 * t
    slope = half + 0.5 * v * (1.0 - t * t) * (GELU_SCALE * (1.0 + 3.0 * GELU_CUBE * square))
    return v * half, slope


def decay_parts(sr, rate):
    log_a = -DECAY_SCALE * sr * rate
    a = jnp.exp(log_a)
    y = 2.0 * log_a
    series = 1.0 + y * (1 / 6) * (1.0 + y * (1 / 7))
    for n in (5, 4, 3, 2):
        series = 1.0 + y * (1 / n) * series
    m2 = jnp.where(y > -0.35, -y * series, 1.0 - a * a)
    return a, jnp.maximum(m2, 1e-36)


def column_sum(value):
    return jnp.sum(value.reshape(-1, 8, 128), axis=0)


def scan_slabs(decay, value, reverse):
    count = decay.shape[1] // 8
    row = lax.broadcasted_iota(jnp.int32, (8, 128), 0)

    def step(i, carry):
        t = count - 1 - i if reverse else i
        at = pl.ds(pl.multiple_of(t * 8, 8), 8)
        done = []
        for s in range(8):
            pc, vc = carry[s]
            p, own = decay[s, at, :], value[s, at, :]
            v = p * own if reverse else own
            for d in (1, 2, 4):
                by = 8 - d if reverse else d
                inside = row < 8 - d if reverse else row >= d
                v = v + p * jnp.where(inside, pltpu.roll(v, by, 0), 0.0)
                p = p * jnp.where(inside, pltpu.roll(p, by, 0), 1.0)
            v = v + p * vc
            p = p * pc
            if reverse:
                edge = row == 7
                value[s, at, :] = own + jnp.where(edge, vc, pltpu.roll(v, 7, 0))
                decay[s, at, :] = jnp.where(edge, pc, pltpu.roll(p, 7, 0))
                last = slice(0, 1)
            else:
                value[s, at, :] = v
                decay[s, at, :] = p
                last = slice(7, 8)
            done.append((jnp.broadcast_to(p[last], (8, 128)), jnp.broadcast_to(v[last], (8, 128))))
        return tuple(done)

    start = tuple((jnp.ones((8, 128), F32), jnp.zeros((8, 128), F32)) for _ in range(8))
    return lax.fori_loop(0, count, step, start)


def exchange_ends(r, net, ends, at):
    for s in range(8):
        r.tot[at, net.z, 0, s : s + 1, :] = ends[s][0][0:1, :]
        r.tot[at, net.z, 1, s : s + 1, :] = ends[s][1][0:1, :]
    mine = r.tot.at[at, net.z]
    return [net.copy(mine, mine, net.line(net.up(k), net.c)) for k in (1, 2, 3)]


class Onward:
    def __init__(self, r, net, ends):
        self.r, self.net = r, net
        self.at = net.reserve(3)
        for s in range(8):
            r.tot[0, net.z, 0, s : s + 1, :] = ends[s][0][0:1, :]
            r.tot[0, net.z, 1, s : s + 1, :] = ends[s][1][0:1, :]
        for k in (1, 2, 3):
            pl.when(net.z + k <= 3)(lambda k=k: self.made(k).start())

    def made(self, k):
        net = self.net
        mine = self.r.tot.at[0, net.z]
        return net.describe(mine, mine, net.line(net.up(k), net.c), self.at + k - 1, self.at + k - 1)

    def wait_recv(self):
        for k in (1, 2, 3):
            pl.when(self.net.z >= k)(lambda k=k: self.made(k).wait_recv())

    def drain(self):
        for k in (1, 2, 3):
            pl.when(self.net.z + k <= 3)(lambda k=k: self.made(k).wait_send())


def entering_states(r, net, copies, at, reverse):
    for made in copies:
        made.wait_recv()
    state = jnp.zeros((8, 128), F32)
    for i in range(4):
        z = 3 - i if reverse else i
        new = r.tot[at, z, 0] * state + r.tot[at, z, 1]
        state = jnp.where((z > net.z) if reverse else (z < net.z), new, state)
    r.inc[...] = state


def tile_rows(i):
    return pl.ds(pl.multiple_of(i * TILE, TILE), TILE)


def layer(r):
    r.do_all = r.x_all
    r.dconv = r.gb
    r.dgi = r.dgu
    r.up = r.d_res.at[:, 0:768]
    r.ga = [r.hid.at[i, :, 0:256] for i in range(4)]
    r.gb2 = [r.hid.at[4 + i, 0:128, 0:256] for i in range(4)]
    net = Net(r)
    p, z, c, o, q = net.p, net.z, net.c, net.o, net.q
    sibling = net.plane(0, o)
    mine = net.slot(0, c)
    cols = r.wgu_out.shape[2] // 2
    piece = cols // 4
    down = pl.ds(pl.multiple_of(p * piece, 16), piece)
    quarter = pl.ds(pl.multiple_of(p * 48, 16), 48)
    x_here = net.local(r.x_in, r.x)
    staged = []
    for j in range(8):
        lanes = pl.ds(j * cols, cols)
        staged.append(net.local(r.wmg.at[:, lanes], r.hid.at[j, pl.ds(0, 128)]))
        staged.append(net.local(r.wmu.at[:, lanes], r.hid.at[j, pl.ds(128, 128)]))
    width = 3 * 128
    first = pl.multiple_of(p * width, 128)
    chip = pl.ds(first, width)
    own_lanes = pl.ds(pl.multiple_of(c * width, 128), width)
    wi_rows, wg_rows = pl.ds(128, 128), pl.ds(0, 128)
    placed = [
        net.local(r.wg.at[:, chip], r.wgi3.at[z, wg_rows, own_lanes]),
        net.local(r.wi.at[:, chip], r.wgi3.at[z, wi_rows, own_lanes]),
        net.local(r.wmd.at[down], r.wmd_all.at[z]),
        net.local(r.wout.at[quarter], r.wq.at[z]),
        net.local(r.wr.at[quarter], r.gq.at[z, :, pl.ds(0, 128)]),
        net.local(r.wv.at[quarter], r.gq.at[z, :, pl.ds(128, 128)]),
        net.local(r.g, r.g_all.at[mine]),
    ]
    r.lens_out[0:1, 0:5] = r.lens[...].astype(F32)
    r.small_rows[...] = jnp.zeros((16, 256), F32)
    r.small_rows[0:4, 0:192] = r.cw[...].astype(F32)
    for at, ref in ((4, r.cb), (5, r.br), (6, r.bi), (7, r.lam)):
        r.small_rows[at : at + 1, 0:192] = ref[...].astype(F32).reshape(1, 192)
    for at, ref in ((0, r.ngain), (128, r.mgain)):
        r.small_rows[10:11, at : at + 128] = ref[...].astype(F32).reshape(1, 128)
    r.small[...] = r.small_rows[...].astype(BF)
    r.tot[0] = jnp.zeros(r.tot.shape[1:], F32)
    net.greet()
    r.small_all[c, z] = r.small[...]
    r.lens_all[p] = r.lens_out[...]
    small = [net.copy(r.small, r.small_all.at[c, z], net.line(net.up(k), c)) for k in (1, 2, 3)]
    lens = [net.copy(r.lens_out, r.lens_all.at[p], net.plane(k, c)) for k in (1, 2, 3)]
    x_here.wait()
    tokens = Gather(net, r.x, r.x_all)
    tokens.start(0)
    tokens.start(1)
    theirs = pl.ds(pl.multiple_of(c * width + o * 128, 128), 256)

    def along(place):
        made = LineGather(net, [(place(z), c)], lambda j: place(z), lambda j, at: place(at))
        for k in (2, 1, 3):
            made.start(k, (0,))
        return made

    handed = []

    def heads_start(rows):
        here = r.wgi3.at[z, rows, theirs]
        made = along(lambda at: r.wgi3.at[at, rows, own_lanes])
        return made, [net.copy(here, here, sibling, handed)]

    for made in placed:
        made.wait()
    heads_in, heads_in_over = heads_start(wi_rows)
    gates_in = along(lambda at: r.gq.at[at])

    def hand_over(arrivals, rows, over):
        arrivals.end()
        for k in (1, 2, 3):
            here = r.wgi3.at[net.down(k), rows, theirs]
            over.append(net.copy(here, here, sibling, handed))

    def arrange(over, rows, lanes):
        for made in over:
            made.wait_recv()
        for core in range(2):
            cols_in = pl.ds(pl.multiple_of(core * width + c * 128, 128), 256)
            for at in range(4):
                to = slice((at * 2 + core) * 128, (at * 2 + core + 1) * 128)
                r.w2[to, lanes] = r.wgi3[at, rows, cols_in]

    def exchange(arrivals, src, dst):
        arrivals.end()
        dst[c, quarter, :] = src[p]
        return [net.copy(src.at[net.near[k]], dst.at[c, quarter], net.plane(k, c)) for k in (1, 2, 3)]

    def share(copies, dst):
        for made in copies:
            made.wait_recv()
        return net.copy(dst.at[c], dst.at[c], sibling)

    for made in small:
        made.wait_recv()
    small_over = net.copy(r.small_all.at[c], r.small_all.at[c], sibling)
    selects = []
    k_at = lax.broadcasted_iota(jnp.int32, (cols, cols), 0)
    j_at = lax.broadcasted_iota(jnp.int32, (cols, cols), 1)
    for part in range(4):
        inside = (j_at >= part * piece) & (j_at < (part + 1) * piece)
        chosen = inside & (k_at == j_at + (p - part) * piece)
        selects.append(jnp.where(chosen, 1.0, 0.0).astype(BF))
    for made in staged:
        made.wait()
    for which in range(2):
        rows = slice(which * 128, (which + 1) * 128)
        for core in (0, 1):
            picked = None
            for part in range(4):
                term = dot(r.hid[part * 2 + core, rows, :], selects[part])
                picked = term if picked is None else picked + term
            r.wgu_out[core, :, which * cols : (which + 1) * cols] = picked.astype(BF)
    for made in lens:
        made.wait_recv()
    small_over.wait_recv()
    low, high = r.small_all[0, p].astype(F32), r.small_all[1, p].astype(F32)
    at_first = jnp.concatenate([low[:, :192], high[:, :64]], axis=1)
    at_second = jnp.concatenate([low[:, 128:192], high[:, :192]], axis=1)
    both = lax.select(c == 0, at_first, at_second)
    for n in range(2):
        r.chan[n] = both[:, n * 128 : (n + 1) * 128]
        lam = -r.chan[n, 7:8, :]
        e = jnp.exp(-jnp.abs(lam))
        series = 1.0 - e * (6 / 7)
        for k in (6, 5, 4, 3, 2):
            series = 1.0 - e * ((k - 1) / k) * series
        rate = jnp.maximum(lam, 0.0) + jnp.where(e < 0.05, e * series, jnp.log(1.0 + e))
        r.chan[n, 7:8, :] = rate
        r.chan[n, 8:9, :] = jax.nn.sigmoid(lam)
    for i in range(8):
        gains = r.small_all[i % 2, i // 2].astype(F32)[10:11, :]
        r.gain[0:1, i * 128 : (i + 1) * 128] = gains[:, 0:128]
        r.gain[1:2, i * 128 : (i + 1) * 128] = gains[:, 128:256]
    gain = r.gain[0:1, :]
    for b in range(4):
        start = jnp.zeros((1, 128), F32)
        for row in range(5):
            r.starts_all[b, row : row + 1, :] = start
            start = start + jnp.broadcast_to(r.lens_all[b, 0:1, row : row + 1], (1, 128))


    def offset_rows(i):
        b, tile = lax.div(i, 13), lax.rem(i, 13)
        starts = r.starts_all[b]
        at = lax.convert_element_type(z * 512 + tile * 40, F32)
        at = at + lax.broadcasted_iota(jnp.int32, (40, 128), 0).astype(F32)
        begun = jnp.zeros((40, 128), F32)
        for row in range(1, 5):
            start = starts[row : row + 1, :]
            begun = jnp.where(at >= start, start, begun)
        r.off[b, pl.ds(pl.multiple_of(tile * 40, 8), 40), :] = at - begun

    loop(52, offset_rows)

    def normalise(slot):
        def body(i):
            rows = pl.ds(pl.multiple_of(i * 32, 32), 32)
            v = r.x_all[slot, rows, :].astype(F32)
            s = lax.rsqrt(jnp.mean(v * v, axis=-1, keepdims=True) + NORM_EPS)
            r.normed[slot, rows, :] = (v * s * gain).astype(BF)

        loop(8, body)

    r.x_all[mine] = r.x[...]
    normalise(mine)
    tokens.sibling(0)
    normalise(net.slot(0, o))
    tokens.forward()
    heads_in.relay()
    gates_in.relay()
    out_in = along(lambda at: r.wq.at[at])
    feed = LineGather(
        net,
        [(r.wgu_out.at[core], core) for core in (c, o)],
        lambda j: r.wgu_all.at[q],
        lambda j, at: r.wgu_all.at[at * 2 + (c, o)[j]],
    )
    feed_down = LineGather(net, [(r.wmd.at[down], c)], lambda j: r.wmd_all.at[z], lambda j, at: r.wmd_all.at[at])
    tokens.middle()
    for k in (1, 2):
        normalise(net.slot(k, c))
    hand_over(heads_in, wi_rows, heads_in_over)
    for k in (1, 2):
        tokens.sibling(k)
        normalise(net.slot(k, o))
    gates_out = exchange(gates_in, r.gq, r.g3)
    arrange(heads_in_over, slice(128, 256), slice(256, 512))

    def project_inner(slot):
        b, half = lax.div(slot, 2), lax.rem(slot, 2)
        at = pl.multiple_of(half * 256, 256)
        inner = dot(r.normed[slot], r.w2[:, 256:512]).astype(BF).astype(F32)
        for n in range(2):
            r.inner[b * 2 + n, pl.ds(at + 8, 256), :] = inner[:, n * 128 : (n + 1) * 128]

    def project_gate(slot):
        b, half = lax.div(slot, 2), lax.rem(slot, 2)
        at = pl.multiple_of(half * 256, 256)
        gate = dot(r.normed[slot], r.w2[:, 0:256])
        for n in range(2):
            r.gp[b * 2 + n, pl.ds(at, 256), :] = gate[:, n * 128 : (n + 1) * 128]

    out_in.relay()
    for k in (0, 1, 2):
        project_inner(net.slot(k, c))
        project_inner(net.slot(k, o))
    tokens.last()
    normalise(net.slot(3, c))
    project_inner(net.slot(3, c))
    tokens.sibling(3)
    normalise(net.slot(3, o))
    project_inner(net.slot(3, o))
    edge = net.reserve(1)

    def edge_copy():
        return net.describe(
            r.inner.at[:, pl.ds(512, 8)], r.inner.at[:, pl.ds(0, 8)], net.line(net.up(1), c), edge, edge
        )

    @pl.when(z < 3)
    def _():
        edge_copy().start()

    @pl.when(z == 0)
    def _():
        r.inner[:, 0:8, :] = jnp.zeros((8, 8, 128), F32)

    gates_over = share(gates_out, r.g3)
    stored = net.local(r.normed, r.normed_far)
    cots = Gather(net, r.g_all.at[mine], r.g_all)
    cots.start(0)
    cots.start(1)
    tokens.release()
    gates_over.wait_recv()
    for i in range(4):
        at = c * 128 + i * 64
        value = r.g3[lax.div(at, 192), pl.ds(pl.multiple_of(lax.rem(at, 192), 64), 64), :]
        r.wri[i // 2, (i % 2) * 64 : (i % 2 + 1) * 64, :] = value
    heads_gate, heads_gate_over = heads_start(wg_rows)

    @pl.when(z > 0)
    def _():
        edge_copy().wait_recv()


    def conv_tile(i):
        b, tile = lax.div(i, 8), lax.rem(i, 8)
        rows = tile_rows(tile)
        offset = r.off[b, rows, :]
        for n in range(2):
            s = b * 2 + n
            window = r.inner[s, pl.ds(pl.multiple_of(tile * TILE, 8), TILE + 8), :]
            chan = r.chan[n]
            total = chan[4:5, :] + chan[0:1, :] * window[8:, :]
            for k in (1, 2, 3):
                total = total + chan[k : k + 1, :] * jnp.where(offset >= k, window[8 - k : TILE + 8 - k, :], 0.0)
            r.conv[s, rows, :] = total.astype(BF)

    loop(32, conv_tile)
    out_rows_in = exchange(out_in, r.wq, r.w3)

    def gate_products(i):
        s, half = lax.div(i, 2), lax.rem(i, 2)
        n = lax.rem(s, 2)
        rows = pl.ds(pl.multiple_of(half * 256, 256), 256)
        pre = dot(r.conv[s, rows, :], r.wri[n])
        r.sr[s, rows, :] = pre[:, :128]
        r.si[s, rows, :] = pre[:, 128:]

    loop(16, gate_products)
    heads_gate.relay()
    feed.start(2, (0,))

    def terms(b):
        starts_b = r.starts_all[b]

        def tile(i, sums):
            rows = tile_rows(i)
            offset = r.off[b, rows, :]
            at = lax.convert_element_type(z * 512 + i * TILE, F32)
            begun = at + lax.broadcasted_iota(jnp.int32, (TILE, 128), 0).astype(F32) - offset
            restart = offset == 0.0
            added = []
            for n in range(2):
                s = b * 2 + n
                chan = r.chan[n]
                sr = jax.nn.sigmoid(r.sr[s, rows, :] + chan[5:6, :])
                si = jax.nn.sigmoid(r.si[s, rows, :] + chan[6:7, :])
                r.sr[s, rows, :] = sr
                r.si[s, rows, :] = si
                a, m2 = decay_parts(sr, chan[7:8, :])
                r.dec[s, rows, :] = jnp.where(restart, 0.0, a)
                m = jnp.where(restart, 1.0, m2 * lax.rsqrt(m2))
                r.drv[s, rows, :] = m * si * r.conv[s, rows, :].astype(F32)
                for row in range(5):
                    inside = jnp.where(begun == starts_b[row : row + 1, :], a, 0.0)
                    added.append(sums[n * 5 + row] + column_sum(inside))
            return tuple(added)

        sums = lax.fori_loop(0, 512 // TILE, tile, tuple(jnp.zeros((8, 128), F32) for _ in range(10)))
        for n in range(2):
            rows = [jnp.sum(part, axis=0, keepdims=True) for part in sums[n * 5 : n * 5 + 5]]
            r.rs_all[z, b * 2 + n] = jnp.concatenate(rows + [jnp.zeros((3, 128), F32)], axis=0)

    loop(4, terms)
    cots.forward()
    ends = scan_slabs(r.dec, r.drv, False)
    onward = Onward(r, net, ends)
    for k in (2, 1, 3):
        feed_down.start(k, (0,))
    r.wgu_all[q] = r.wgu_out[c]
    feed_over = net.copy(r.wgu_out.at[o], r.wgu_all.at[q], sibling)
    hand_over(heads_gate, wg_rows, heads_gate_over)
    arrange(heads_gate_over, slice(0, 128), slice(0, 256))
    for made in handed:
        made.wait_send()
    heads_in.drain()
    heads_gate.drain()
    gates_in.drain()
    out_in.drain()
    feed.start(2, (1,))
    feed.start(1, (0, 1))
    feed.start(3, (0, 1))
    for slot in range(8):
        project_gate(slot)

    def gelu_tile(i):
        s, rows = lax.div(i, 8), tile_rows(lax.rem(i, 8))
        v = r.gp[s, rows, :]
        t = jnp.tanh(GELU_SCALE * v * (1.0 + GELU_CUBE * v * v))
        r.gb[s, rows, :] = 0.5 * v * (1.0 + t)

    loop(64, gelu_tile)
    out_over = share(out_rows_in, r.w3)
    entering_states(r, net, [onward], 0, False)
    row_sums = [net.copy(r.rs_all.at[z], r.rs_all.at[z], net.line(net.up(k), c)) for k in (1, 2, 3)]
    out_over.wait_recv()

    def own_rows(i):
        at = c * 128 + i * 64
        value = r.w3[lax.div(at, 192), pl.ds(pl.multiple_of(lax.rem(at, 192), 64), 64), :]
        r.wo[pl.ds(pl.multiple_of(i * 64, 64), 64), :] = value

    loop(4, own_rows)
    for s in range(8):
        r.states[s, 7:8, :] = r.inc[s : s + 1, :]

    def mix_tile(i):
        s, tile = lax.div(i, 8), lax.rem(i, 8)
        b, n = lax.div(s, 2), lax.rem(s, 2)
        rows = tile_rows(tile)
        states = r.drv[s, rows, :] + r.dec[s, rows, :] * r.inc[pl.ds(s, 1), :]
        r.states[s, pl.ds(pl.multiple_of(tile * TILE + 8, 8), TILE), :] = states
        lanes = pl.ds(pl.multiple_of(n * 128, 128), 128)
        r.mixed[b * 2 + lax.div(tile, 4), tile_rows(lax.rem(tile, 4)), lanes] = (states * r.gb[s, rows, :]).astype(BF)

    loop(64, mix_tile)
    stored.wait()
    lane = lax.broadcasted_iota(jnp.int32, (1, 256), 1)
    counted = jnp.where((lane >= 64 * c) & (lane < 192 + 64 * c), 1.0, 0.0)
    counted_two = jnp.concatenate([counted, counted], axis=1)

    def masked(value, mask):
        return (value.astype(F32) * mask).astype(BF)

    total = Reduce(
        net, r, lambda k, core: dot(masked(r.mixed[net.slot(k, core)], counted), r.wo[...])
    )
    for k in (3, 1, 2, 0):
        total.other(k)
    total.far()
    total.near()
    cots.middle()
    total.own()
    cots.last()
    for k in (0, 1, 2, 3):
        cots.sibling(k)
    cots.release()
    total.relay()
    feed_down.relay()
    feed.relay()
    def wmd():
        return r.wmd_all[...].reshape(cols, -1)

    gain2 = r.gain[1:2, :]
    n2_all = r.normed
    acts = Gather(net, n2_all.at[mine], n2_all, tokens.at)
    for part in range(2):
        total.finish(part)
        for h in range(2):

            def residual_rows(i, h=h, part=part):
                i = part * 2 + i
                rows = pl.ds(pl.multiple_of(h * 128 + i * 32, 32), 32)
                v = r.x[rows, :].astype(F32) + total.total(h, i, 32)
                r.residual[rows, :] = v
                s = lax.rsqrt(jnp.mean(v * v, axis=-1, keepdims=True) + NORM_EPS)
                r.normed[mine, rows, :] = (v * s * gain2).astype(BF)

            loop(2, residual_rows)
        acts.start(part)

    owners, returned = [], []
    def gate_up():
        return r.wgu_all[...].reshape(-1, 2 * cols)

    def d_normed2(k, core):
        return dot(r.dgu[net.slot(k, core)], gate_up(), NT)

    back = Reduce(net, r, d_normed2, total.at)

    def part(k, core):
        slot = net.slot(k, core)
        h = n2_all[slot]
        r.up[...] = dot(h, gate_up())

        def body(i):
            rows = pl.ds(pl.multiple_of(i * 32, 32), 32)
            gelu, slope = gelu_parts(r.up[rows, 0:cols])
            ul, dh = r.up[rows, cols:], r.dgu[slot, rows, 0:cols].astype(F32)
            r.hid[slot, rows, :] = (gelu * ul).astype(BF)
            r.dgu[slot, rows, 0:cols] = (dh * ul * slope).astype(BF)
            r.dgu[slot, rows, cols:] = (dh * gelu).astype(BF)

        loop(8, body)

    feed_down.end()
    for slot in range(8):
        r.dgu[slot, :, 0:cols] = dot(r.g_all[slot], wmd(), NT).astype(BF)
    feed_over.wait_recv()
    feed.end()
    part(0, c)
    acts.sibling(0)
    part(0, o)
    back.other(0)
    acts.forward()
    acts.middle()
    part(1, c)
    part(2, c)
    acts.sibling(1)
    part(1, o)
    back.other(1)
    acts.sibling(2)
    part(2, o)
    back.other(2)
    for made in row_sums:
        made.wait_recv()
    r.rows_sum[...] = r.rs_all[0] + r.rs_all[1] + r.rs_all[2] + r.rs_all[3]
    for k in (1, 2, 3):
        for core in (c, o):
            owners.append(net.copy(r.rows_sum.at[pl.ds(net.near[k] * 2, 2)], r.fr.at[mine], net.plane(k, core)))
    owners.append(net.copy(r.rows_sum.at[pl.ds(p * 2, 2)], r.fr.at[mine], sibling))
    returned.append(net.local(r.rows_sum.at[pl.ds(p * 2, 2)], r.fr.at[mine]))
    back.near()
    acts.last()
    acts.sibling(3)
    part(3, o)
    back.other(3)
    part(3, c)
    back.far()
    back.relay()
    back.own()
    acts.release()
    for i in range(4):
        rows = n2_all[:, :, i * 256 : (i + 1) * 256].reshape(-1, 256)
        r.gm[i] = dot(rows, r.dgu[...].reshape(-1, 2 * cols), TN).astype(BF)

    def gm_in(k):
        return r.wgi3.at[k - 1]

    mlp_m = LineSum(net, lambda t: r.gm.at[t], gm_in)
    mlp_m.start()
    hid = r.hid[...].reshape(-1, cols)
    for half in range(2):
        lanes = slice(half * 512, half * 512 + 512)
        value = dot(hid, r.g_all[:, :, lanes].reshape(-1, 512), TN).astype(BF)
        for i in range(4):
            r.gd[i, :, lanes] = value[i * piece : (i + 1) * piece, :]
    mlp_d = LineSum(net, lambda t: r.gd.at[t], lambda k: r.gd_in.at[k - 1], out_in.at)
    sums = jnp.zeros((8, r.x.shape[1]), F32)
    grads = Gather(net, r.do_all.at[mine], r.do_all, cots.at)
    for part in range(2):
        back.finish(part)
        for h in range(2):

            def residual_back(i, sums, h=h, part=part):
                i = part * 2 + i
                rows = pl.ds(pl.multiple_of(h * 128 + i * 32, 32), 32)
                v = r.residual[rows, :]
                dn = back.total(h, i, 32)
                s = lax.rsqrt(jnp.mean(v * v, axis=-1, keepdims=True) + NORM_EPS)
                u = dn * gain2
                pulled = s * u - v * (s * s * s * jnp.mean(u * v, axis=-1, keepdims=True))
                d_res = r.g_all[mine, rows, :].astype(F32) + pulled
                r.d_res[rows, :] = d_res
                r.do_all[mine, rows, :] = d_res.astype(BF)
                return sums + jnp.sum((dn * v * s).reshape(4, 8, -1), axis=0)

            sums = lax.fori_loop(0, 2, residual_back, sums)
        grads.start(part)
    r.gain2_sum[...] = sums


    fo_at = net.reserve(4)

    def vector_copy(k):
        return net.describe(r.vout.at[p], r.vout.at[p], net.plane(k, c), fo_at + k, fo_at)

    owners_m = Owners(net, r.gm_sum, r.fm, r.fm_x, tokens.at)
    owners_d = Owners(net, r.gd_sum, r.fd)
    owners_a = Owners(net, r.ga_sum, r.fa, r.fa_x, cots.at)
    owners_b = Owners(net, r.gb2_sum, r.fb)
    owners_o = Owners(net, r.go_sum, r.fo, cut=32)

    def mlp_sums():
        mlp_m.end(r.gm_sum)
        owners_m.start()

    def back_out(slot):
        b, half = lax.div(slot, 2), lax.rem(slot, 2)
        dm = dot(r.do_all[slot], r.wo[...], NT)
        for n in range(2):
            r.dconv[b * 2 + n, pl.ds(pl.multiple_of(half * 256, 256), 256), :] = dm[:, n * 128 : (n + 1) * 128]

    back_out(mine)
    grads.sibling(0)
    back_out(net.slot(0, o))
    out = Reduce(net, r, lambda k, core: dot(r.hid[net.slot(k, core)], wmd()), total.at)
    for k in (3, 1, 2, 0):
        out.other(k)
    grads.forward()
    out.far()
    out.near()
    out.own()
    grads.middle()
    mlp_m.relay()
    for k in (1, 2):
        back_out(net.slot(k, c))
    for k in (1, 2):
        grads.sibling(k)
        back_out(net.slot(k, o))
    grads.last()
    back_out(net.slot(3, c))
    grads.sibling(3)
    back_out(net.slot(3, o))

    def first_pass(i):
        b, tile = lax.div(i, 8), lax.rem(i, 8)
        rows = tile_rows(tile)
        live = r.off[b, rows, :] != 0.0
        for n in range(2):
            s = b * 2 + n
            gelu, slope = gelu_parts(r.gp[s, rows, :])
            dm = r.dconv[s, rows, :]
            states = r.states[s, pl.ds(pl.multiple_of(tile * TILE + 8, 8), TILE), :]
            lanes = slice(n * 128, (n + 1) * 128)
            r.dgi[b * 2 + lax.div(tile, 4), tile_rows(lax.rem(tile, 4)), lanes] = (dm * states * slope).astype(BF)
            r.drv[s, rows, :] = dm * gelu
            a = jnp.exp(-DECAY_SCALE * r.sr[s, rows, :] * r.chan[n, 7:8, :])
            r.dec[s, rows, :] = jnp.where(live, a, 0.0)

    loop(32, first_pass)
    ends = scan_slabs(r.dec, r.drv, True)
    ends = exchange_ends(r, net, ends, 1)
    out.relay()
    go_in, go_line_in = r.go_q, r.go_l
    mixed = r.mixed[...].reshape(-1, 256)
    for half in range(2):
        lanes = slice(half * 512, half * 512 + 512)
        r.go[:, lanes] = dot(mixed, r.do_all[:, :, lanes].reshape(-1, 512), TN).astype(BF)
    grads.release()
    fetched = net.local(r.normed_far, r.do_all)
    go_rows = [pl.ds(pl.multiple_of(c * 64 + near * 48, 16), 48) for near in net.near]

    def go_start(lanes):
        return [net.copy(r.go.at[go_rows[k], lanes], go_in.at[p, :, lanes], net.plane(k, c)) for k in (1, 2, 3)]

    go_out = go_start(pl.ds(0, 1024))
    entering_states(r, net, ends, 1, True)
    r.vec[...] = jnp.zeros((2, 8, 8, 128), F32)
    dri = r.normed

    def second_pass(s):
        b, n = lax.div(s, 2), lax.rem(s, 2)
        chan = r.chan[n]
        enter = r.inc[pl.ds(s, 1), :]
        lanes_r = pl.ds(pl.multiple_of(n * 256, 128), 128)
        lanes_i = pl.ds(pl.multiple_of(n * 256 + 128, 128), 128)

        def tile(i, sums):
            rows = tile_rows(i)
            live = r.off[b, rows, :] != 0.0
            ds = r.drv[s, rows, :] + r.dec[s, rows, :] * enter
            window = r.states[s, pl.ds(pl.multiple_of(i * TILE, 8), TILE + 8), :]
            before = window[7 : TILE + 7, :]
            sr, si = r.sr[s, rows, :], r.si[s, rows, :]
            cv = r.conv[s, rows, :].astype(F32)
            a, m2 = decay_parts(sr, chan[7:8, :])
            inv = lax.rsqrt(m2)
            m = jnp.where(live, m2 * inv, 1.0)
            dsi = ds * si
            d_log = jnp.where(live, a * (ds * before - dsi * cv * a * inv), 0.0)
            lam_term = d_log * sr
            d_r = (-DECAY_SCALE) * chan[7:8, :] * lam_term * (1.0 - sr)
            dm_i = dsi * m
            d_i = dm_i * cv * (1.0 - si)
            d_r, d_i = d_r.astype(BF), d_i.astype(BF)
            at = tile_rows(lax.rem(i, 4))
            dri[b * 2 + lax.div(i, 4), at, lanes_r] = d_r
            dri[b * 2 + lax.div(i, 4), at, lanes_i] = d_i
            r.dconv[s, rows, :] = dm_i
            return (
                sums[0] + column_sum(d_r.astype(F32)),
                sums[1] + column_sum(d_i.astype(F32)),
                sums[2] + column_sum(lam_term),
            )

        zero = jnp.zeros((8, 128), F32)
        sums = lax.fori_loop(0, 512 // TILE, tile, (zero, zero, zero))
        for j in range(3):
            r.vec[n, 5 + j] = r.vec[n, 5 + j] + sums[j]

    loop(8, second_pass)
    mlp_sums()

    def gate_back(i):
        s, half = lax.div(i, 2), lax.rem(i, 2)
        b, n = lax.div(s, 2), lax.rem(s, 2)
        rows = pl.ds(pl.multiple_of(half * 256, 256), 256)
        lanes = pl.ds(pl.multiple_of(n * 256, 256), 256)
        r.dconv[s, rows, :] = r.dconv[s, rows, :] + dot(dri[b * 2 + half, :, lanes], r.wri[n], NT)

    loop(16, gate_back)
    edge_back = net.reserve(1)

    def edge_back_copy():
        return net.describe(
            r.dconv.at[:, pl.ds(0, 8)], r.dconv.at[:, pl.ds(512, 8)], net.line(net.down(1), c), edge_back, edge_back
        )

    @pl.when(z > 0)
    def _():
        edge_back_copy().start()

    mlp_d.start()

    @pl.when(z == 3)
    def _():
        r.dconv[:, 512:520, :] = jnp.zeros((8, 8, 128), F32)

    for n in range(2):
        total_ri = None
        for b in range(4):
            for half in range(2):
                term = dot(
                    r.conv[b * 2 + n, half * 256 : (half + 1) * 256, :],
                    dri[b * 2 + half, :, n * 256 : (n + 1) * 256],
                    TN,
                )
                total_ri = term if total_ri is None else total_ri + term
        r.go[n * 128 : (n + 1) * 128, 1024:1280] = total_ri.astype(BF)
    go_out += go_start(pl.ds(1024, 256))

    @pl.when(z < 3)
    def _():
        edge_back_copy().wait_recv()


    def conv_back(s):
        b, n = lax.div(s, 2), lax.rem(s, 2)
        chan = r.chan[n]
        lanes = pl.ds(pl.multiple_of(256 + n * 128, 128), 128)

        def tile(i, sums):
            offset = r.off[b, pl.ds(pl.multiple_of(i * TILE, 8), TILE + 8), :]
            window = r.dconv[s, pl.ds(pl.multiple_of(i * TILE, 8), TILE + 8), :]
            inner = r.inner[s, pl.ds(pl.multiple_of(i * TILE, 8), TILE + 8), :]
            value = chan[0:1, :] * window[:TILE, :]
            added = [sums[0] + column_sum(window[:TILE, :] * inner[8:, :])]
            for k in (1, 2, 3):
                held = jnp.where(offset >= k, window, 0.0)
                value = value + chan[k : k + 1, :] * held[k : TILE + k, :]
                added.append(sums[k] + column_sum(held[:TILE, :] * inner[8 - k : TILE + 8 - k, :]))
            added.append(sums[4] + column_sum(window[:TILE, :]))
            r.dgi[b * 2 + lax.div(i, 4), tile_rows(lax.rem(i, 4)), lanes] = value.astype(BF)
            return tuple(added)

        sums = lax.fori_loop(0, 512 // TILE, tile, tuple(jnp.zeros((8, 128), F32) for _ in range(5)))
        for j in range(5):
            r.vec[n, j] = r.vec[n, j] + sums[j]

    loop(8, conv_back)
    out.finish(0)
    out.finish(1)
    for h in range(2):

        def out_rows(i, h=h):
            rows = pl.ds(pl.multiple_of(h * 128 + i * 32, 32), 32)
            value = (r.residual[rows, :] + out.total(h, i, 32)).astype(BF)
            for j in range(4):
                r.dgu[j, rows, 512:768] = value[:, j * 256 : (j + 1) * 256]

        loop(4, out_rows)
    for j in range(4):
        returned.append(net.local(r.dgu.at[j, :, pl.ds(512, 256)], r.block_out.at[:, pl.ds(j * 256, 256)]))
    for partner in (sibling, net.plane(1, c), net.plane(2, c)):
        pl.semaphore_signal(r.free, inc=1, device_id=partner, device_id_type=pl.DeviceIdType.MESH)
    for n in range(2):
        sums = [jnp.sum(r.vec[n, j], axis=0, keepdims=True) for j in range(8)]
        sums[7] = sums[7] * (DECAY_SCALE * r.chan[n, 8:9, :])
        r.vsum[z, :, n * 128 : (n + 1) * 128] = jnp.concatenate(sums, axis=0)
    vec = [net.copy(r.vsum.at[z], r.vsum.at[z], net.line(net.up(k), c)) for k in (1, 2, 3)]
    fetched.wait()
    flat = r.dgi[:, :, 0:512].reshape(-1, 512)
    for i in range(4):
        value = dot(r.do_all[:, :, i * 256 : (i + 1) * 256].reshape(-1, 256), flat, TN)
        for j in range(2):
            n0, n1 = value[:, j * 256 : j * 256 + 128], value[:, j * 256 + 128 : j * 256 + 256]
            r.ga[i][:, j * 128 : (j + 1) * 128] = lax.select(c == 0, n0, n1).astype(BF)
            shared = lax.select(c == 0, n1, n0)
            r.gb2[i][:, j * 128 : (j + 1) * 128] = lax.select(c == 0, shared[0:128], shared[128:256]).astype(BF)

    def ga_in(k):
        return r.g_all.at[7, :, pl.ds((k - 1) * 256, 256)]

    def gb_in(k):
        return r.g_all.at[3 + k, pl.ds(128, 128), pl.ds(0, 256)]

    sum_a = LineSum(net, lambda t: r.hid.at[t, :, 0:256], ga_in, heads_in.at)
    sum_b = LineSum(net, lambda t: r.hid.at[4 + t, 0:128, 0:256], gb_in, heads_gate.at)
    sum_a.start()
    sum_b.start()
    mlp_d.relay()
    owners_m.forward()
    first_back = Reduce(
        net,
        r,
        lambda k, core: dot(masked(r.dgi[net.slot(k, core), :, 0:512], counted_two), r.w2[...], NT),
        total.at,
    )
    pl.semaphore_wait(r.free, 3)
    for k in (3, 1, 2, 0):
        first_back.other(k)
    first_back.far()
    first_back.near()
    go_in[p] = r.go[go_rows[0], :]
    for made in go_out:
        made.wait_recv()
    go_line = LineSum(net, lambda t: go_in.at[t], lambda k: go_line_in.at[k - 1], gates_in.at)
    go_line.start()
    first_back.relay()
    mlp_d.end(r.gd_sum)
    owners_d.start()
    first_back.own()
    owners_m.middle()
    sum_a.relay()
    sum_b.relay()
    go_line.relay()
    first_back.finish(0)
    first_back.finish(1)
    sums = jnp.zeros((8, r.x.shape[1]), F32)
    for h in range(2):

        def input_rows(i, sums, h=h):
            rows = pl.ds(pl.multiple_of(h * 128 + i * 32, 32), 32)
            v = r.x[rows, :].astype(F32)
            dn = first_back.total(h, i, 32)
            s = lax.rsqrt(jnp.mean(v * v, axis=-1, keepdims=True) + NORM_EPS)
            u = dn * r.gain[0:1, :]
            r.d_res[rows, :] = r.d_res[rows, :] + (
                s * u - v * (s * s * s * jnp.mean(u * v, axis=-1, keepdims=True))
            )
            return sums + jnp.sum((dn * v * s).reshape(4, 8, -1), axis=0)

        sums = lax.fori_loop(0, 4, input_rows, sums)
    returned.append(net.local(r.d_res, r.d_in))
    gains = jnp.concatenate(
        [
            jnp.sum(sums, axis=0, keepdims=True),
            jnp.sum(r.gain2_sum[...], axis=0, keepdims=True),
            jnp.zeros((6, sums.shape[1]), F32),
        ],
        axis=0,
    )
    for i in range(8):
        r.gsum[i] = gains[:, i * 128 : (i + 1) * 128]
    r.gline[q] = r.gsum[q]
    gain_line = [
        net.copy(r.gsum.at[net.up(k) * 2 + core], r.gline.at[q], net.line(net.up(k), core))
        for k in (1, 2, 3)
        for core in (c, o)
    ]
    gain_line.append(net.copy(r.gsum.at[z * 2 + o], r.gline.at[q], sibling))
    for made in vec:
        made.wait_recv()
    r.vout[p] = r.vsum[0] + r.vsum[1] + r.vsum[2] + r.vsum[3]

    @pl.when(z == p)
    def _():
        for k in (1, 2, 3):
            vector_copy(k).start()

    sum_a.end(r.ga_sum)
    owners_a.start()
    sum_b.end(r.gb2_sum)
    owners_b.start()
    go_line.end(r.go_sum)
    owners_o.start()
    owners_d.forward()
    owners_m.last()
    owners_a.forward()
    owners_b.forward()
    owners_o.forward()
    for made in gain_line:
        made.wait_recv()
    sums = r.gline[0]
    for i in range(1, 8):
        sums = sums + r.gline[i]
    r.gplane[p] = sums
    gain_plane = [net.copy(r.gplane.at[p], r.gplane.at[p], net.plane(k, c)) for k in (1, 2, 3)]

    @pl.when(z != p)
    def _():
        vector_copy(1).wait_recv()

    @pl.when(z == p)
    def _():
        for k in (1, 2, 3):
            vector_copy(k).wait_send()

    owners_d.middle()
    owners_a.middle()
    owners_b.middle()
    owners_o.middle()
    for each in (owners_d, owners_a, owners_b, owners_o):
        each.last()
    for each in (owners_m, owners_d, owners_a, owners_b, owners_o):
        each.end()
    for made in owners + gain_plane:
        made.wait_recv()
    r.gain_out[...] = r.gplane[0] + r.gplane[1] + r.gplane[2] + r.gplane[3]
    r.vec_out[...] = r.vout[z]
    for made in returned:
        made.wait()
    @pl.when(z < 3)
    def _():
        edge_copy().wait_send()

    @pl.when(z > 0)
    def _():
        edge_back_copy().wait_send()

    onward.drain()
    feed.drain()
    feed_down.drain()
    for made in (mlp_m, mlp_d, go_line, sum_a, sum_b):
        made.drain()
    net.drain()


def assemble(r):
    c = lax.rem(lax.axis_index("seq"), 2)
    count = 0
    stores = []

    def start(src, dst):
        nonlocal count
        made = pltpu.make_async_copy(src, dst, r.local.at[count])
        count += 1
        made.start()
        return made

    mine = pl.ds(pl.multiple_of(c * 128, 128), 128)
    loads = [
        [start(r.fm.at[:, mine], r.vm.at[c]), start(r.fm_x, r.vm.at[1 - c])],
        [start(r.fa.at[:, mine], r.va.at[c]), start(r.fa_x, r.va.at[1 - c]), start(r.fb, r.vb)],
        [start(r.fd, r.vd)],
        [start(r.fo, r.vo)],
    ]

    def loaded(which):
        for made in loads[which]:
            made.wait()

    little = [start(r.vec_in, r.v_vec), start(r.gains, r.v_gains), start(r.fr, r.v_fr), start(r.lens, r.v_lens)]
    passed = [start(r.d_in, r.v_din), start(r.block_out, r.v_block)]
    cols = r.fm.shape[2] // 2
    piece = cols // 4
    loaded(0)
    for j, (stage, out) in enumerate(((r.s_mgate, r.o_mgate), (r.s_mup, r.o_mup))):
        for part in range(4):
            for core in range(2):
                at = (part * 2 + core) * cols
                lanes = slice(j * cols + part * piece, j * cols + (part + 1) * piece)
                stage[:, at : at + cols] = jnp.concatenate(
                    [r.vm[core, chip, :, lanes].astype(F32) for chip in range(4)], axis=1
                )
            here = pl.ds(part * 2 * cols, 2 * cols)
            stores.append(start(stage.at[:, here], out.at[:, here]))
    for made, src, dst in zip(passed, (r.v_din, r.v_block), (r.o_din, r.o_block)):
        made.wait()
        stores.append(start(src, dst))
    loaded(1)
    for j, (stage, out) in enumerate(((r.s_gate, r.o_gate), (r.s_in, r.o_in))):
        lanes = slice(j * 128, (j + 1) * 128)
        for chip in range(4):
            at = chip * 384
            stage[:, at : at + 128] = r.va[0, chip, :, lanes].astype(F32)
            stage[:, at + 128 : at + 256] = r.vb[chip, :, lanes].astype(F32)
            stage[:, at + 256 : at + 384] = r.va[1, chip, :, lanes].astype(F32)
        stores.append(start(stage, out))
    loaded(2)
    for chip in range(4):
        r.s_down[chip * piece : (chip + 1) * piece, :] = r.vd[chip].astype(F32)
    stores.append(start(r.s_down, r.o_mdown))
    for made in little:
        made.wait()
    vec = r.v_vec[...]
    vec = lax.select(c == 0, vec[:, 0:192], vec[:, 64:256])
    r.s_cw[...] = vec[0:4]
    stores.append(start(r.s_cw, r.o_cw))
    for j, (stage, out) in enumerate(((r.s_cb, r.o_cb), (r.s_rb, r.o_rb), (r.s_ib, r.o_ib), (r.s_lam, r.o_lam))):
        stage[...] = vec[4 + j : 5 + j]
        stores.append(start(stage, out))
    for j, (stage, out) in enumerate(((r.s_ngain, r.o_ngain), (r.s_mgain, r.o_mgain))):
        stage[...] = r.v_gains[j : j + 1, :]
        stores.append(start(stage, out))
    counts = [jnp.broadcast_to(r.v_lens[0:1, row : row + 1].astype(F32), (1, 128)) for row in range(5)]
    for chip in range(4):
        for half, (slot, n) in enumerate(((chip * 2, 0), (chip * 2, 1), (chip * 2 + 1, 1))):
            at = chip * 384 + half * 128
            for row in range(5):
                r.s_mean[row, :, at : at + 128] = r.v_fr[slot, n, row : row + 1, :] / counts[row]
    stores.append(start(r.s_mean, r.o_mean))
    loaded(3)
    for chip in range(4):
        rows = slice(chip * 48, (chip + 1) * 48)
        r.s_out[rows, :] = r.vo[chip, :, 0:1024].astype(F32)
        r.s_r[rows, :] = r.vo[chip, :, 1024:1152].astype(F32)
        r.s_i[rows, :] = r.vo[chip, :, 1152:1280].astype(F32)
    for stage, out in ((r.s_out, r.o_out), (r.s_r, r.o_r), (r.s_i, r.o_i)):
        stores.append(start(stage, out))
    for made in stores:
        made.wait()


def shifted(value, axis, by):
    count = lax.axis_size(axis)
    pairs = [(i, i + by) for i in range(count) if 0 <= i + by < count]
    return lax.ppermute(value, axis, pairs)


def entering(value, axis, combine, identity, reverse):
    count, place = (lax.axis_size(axis), lax.axis_index(axis))
    everything = jax.tree.map(lambda part: lax.all_gather(part, axis), value)
    start = jax.tree.map(
        lambda part, zero: jnp.broadcast_to(jnp.asarray(zero, part.dtype), part.shape),
        value,
        identity,
    )

    def step(k, before):
        at = count - 1 - k if reverse else k
        reached = at > place if reverse else at < place
        new = combine(before, jax.tree.map(lambda part: part[at], everything))
        return jax.tree.map(lambda a, b: jnp.where(reached, a, b), new, before)

    return lax.fori_loop(0, count, step, start)


def rms_scale(values):
    return values * lax.rsqrt(jnp.mean(values * values, axis=-1, keepdims=True) + NORM_EPS)


def gelu_tanh(values):
    return jax.nn.gelu(values, approximate=True)


def link(earlier, later):
    return (earlier[0] * later[0], later[0] * earlier[1] + later[1])


def block_product(values, weight):
    count, channels = values.shape
    block_size = weight.shape[1]
    shaped = values.reshape(count, channels // block_size, block_size)
    result = jnp.einsum(
        "lni,nij->lnj",
        shaped,
        weight.reshape(channels // block_size, block_size, block_size),
        preferred_element_type=jnp.float32,
    )
    return result.reshape(count, channels)


def block_back(grads, weight):
    count, channels = grads.shape
    block_size = weight.shape[1]
    shaped = grads.reshape(count, channels // block_size, block_size)
    result = jnp.einsum(
        "lnj,nij->lni",
        shaped,
        weight.reshape(channels // block_size, block_size, block_size),
        preferred_element_type=jnp.float32,
    )
    return result.reshape(count, channels)


def block_weight_grad(values, grads, block_size):
    count, channels = values.shape
    left = values.reshape(count, channels // block_size, block_size)
    right = grads.reshape(count, channels // block_size, block_size)
    return jnp.einsum("lni,lnj->nij", left, right, preferred_element_type=jnp.float32).reshape(
        channels, block_size
    )


def recurrence_terms(conv_in, r_in, i_in, lam_in, restart):
    log_a = -DECAY_SCALE * jax.nn.sigmoid(r_in) * jax.nn.softplus(-lam_in)
    decays = jnp.exp(log_a)
    factor = jnp.where(restart[:, None] > 0, 1.0, jnp.sqrt(-jnp.expm1(2.0 * log_a)))
    return (decays * (1.0 - restart[:, None]), factor * jax.nn.sigmoid(i_in) * conv_in, decays)


def shards(
    inputs,
    out_grad,
    row_lengths,
    norm_gain,
    w_gate,
    w_in,
    conv_w,
    conv_b,
    w_rgate,
    b_rgate,
    w_igate,
    b_igate,
    lam,
    w_out,
    mlp_gain,
    w_mlp_gate,
    w_mlp_up,
    w_mlp_down,
):
    gathered = (
        lax.all_gather(norm_gain, "seq", axis=0, tiled=True),
        lax.all_gather(w_gate, "seq", axis=0, tiled=True),
        lax.all_gather(w_in, "seq", axis=0, tiled=True),
        lax.all_gather(conv_w, "seq", axis=1, tiled=True),
        lax.all_gather(conv_b, "seq", axis=0, tiled=True),
        lax.all_gather(w_rgate, "seq", axis=0, tiled=True),
        lax.all_gather(b_rgate, "seq", axis=0, tiled=True),
        lax.all_gather(w_igate, "seq", axis=0, tiled=True),
        lax.all_gather(b_igate, "seq", axis=0, tiled=True),
        lax.all_gather(lam, "seq", axis=0, tiled=True),
        lax.all_gather(w_out, "seq", axis=0, tiled=True),
        lax.all_gather(mlp_gain, "seq", axis=0, tiled=True),
        lax.all_gather(w_mlp_gate, "seq", axis=0, tiled=True),
        lax.all_gather(w_mlp_up, "seq", axis=0, tiled=True),
        lax.all_gather(w_mlp_down, "seq", axis=0, tiled=True),
    )
    gain_first = gathered[0].astype(jnp.float32)
    conv_taps = gathered[3].astype(jnp.float32)
    conv_bias = gathered[4].astype(jnp.float32)
    lam_value = gathered[9].astype(jnp.float32)
    gain_second = gathered[11].astype(jnp.float32)
    tokens = inputs[0].astype(jnp.float32)
    local_len = tokens.shape[0]
    channels = gathered[2].shape[1]
    block_size = gathered[5].shape[1]
    kernel_taps = conv_taps.shape[0]
    lengths = row_lengths[0]
    row_ends = jnp.cumsum(lengths)
    row_starts = row_ends - lengths
    positions = lax.axis_index("seq") * local_len + jnp.arange(local_len, dtype=jnp.int32)
    started = positions[:, None] >= row_starts[None, :]
    row_index = jnp.sum(started.astype(jnp.int32), axis=1) - 1
    row_first = jnp.max(jnp.where(started, row_starts[None, :], 0), axis=1)
    offset = positions - row_first
    restart = (offset == 0).astype(jnp.float32)
    members = (row_index[:, None] == jnp.arange(lengths.shape[0], dtype=jnp.int32)[None, :]).astype(
        jnp.float32
    )
    tap_masks = [(offset >= tap).astype(jnp.float32)[:, None] for tap in range(kernel_taps)]
    scaled, norm_pull = jax.vjp(rms_scale, tokens)
    normed = (scaled * gain_first).astype(jnp.bfloat16)
    gate_pre = jnp.dot(normed, gathered[1], preferred_element_type=jnp.float32)
    gate_branch, gate_pull = jax.vjp(gelu_tanh, gate_pre)
    inner = jnp.dot(normed, gathered[2], preferred_element_type=jnp.float32).astype(jnp.bfloat16)
    edge_rows = shifted(inner[local_len - kernel_taps + 1 :], "seq", 1)
    extended = jnp.concatenate([edge_rows, inner], axis=0).astype(jnp.float32)
    conv_sum = conv_bias + jnp.zeros((local_len, channels), jnp.float32)
    for tap in range(kernel_taps):
        start_row = kernel_taps - 1 - tap
        conv_sum = (
            conv_sum + conv_taps[tap] * extended[start_row : start_row + local_len] * tap_masks[tap]
        )
    conv_low = conv_sum.astype(jnp.bfloat16)
    conv_value = conv_low.astype(jnp.float32)
    r_pre = block_product(conv_low, gathered[5]) + gathered[6].astype(jnp.float32)
    i_pre = block_product(conv_low, gathered[7]) + gathered[8].astype(jnp.float32)

    def local_terms(conv_in, r_in, i_in, lam_in):
        return recurrence_terms(conv_in, r_in, i_in, lam_in, restart)

    (carried, drive_term, decays), recur_pull = jax.vjp(
        local_terms, conv_value, r_pre, i_pre, lam_value
    )
    prefix_decay, local_state = lax.associative_scan(link, (carried, drive_term), axis=0)
    identity = (jnp.ones((channels,), jnp.float32), jnp.zeros((channels,), jnp.float32))
    incoming = entering((prefix_decay[-1], local_state[-1]), "seq", link, identity, False)[1]
    states = local_state + prefix_decay * incoming
    mixed_low = (states * gate_branch).astype(jnp.bfloat16)
    residual = tokens + jnp.dot(mixed_low, gathered[10], preferred_element_type=jnp.float32)
    scaled_two, norm_pull_two = jax.vjp(rms_scale, residual)
    normed_two = (scaled_two * gain_second).astype(jnp.bfloat16)
    up_gate = jnp.dot(normed_two, gathered[12], preferred_element_type=jnp.float32)
    up_lin = jnp.dot(normed_two, gathered[13], preferred_element_type=jnp.float32)
    gelu_up, up_pull = jax.vjp(gelu_tanh, up_gate)
    hidden = (gelu_up * up_lin).astype(jnp.bfloat16)
    block_out = (
        residual + jnp.dot(hidden, gathered[14], preferred_element_type=jnp.float32)
    ).astype(jnp.bfloat16)
    row_sums = lax.psum(jnp.dot(members.T, decays, precision=lax.Precision.HIGHEST), "seq")
    gate_mean = row_sums / lengths.astype(jnp.float32)[:, None]
    grad_top = out_grad[0]
    grad_mdown = jnp.einsum("tf,td->fd", hidden, grad_top, preferred_element_type=jnp.float32)
    d_hidden = jnp.einsum("td,fd->tf", grad_top, gathered[14], preferred_element_type=jnp.float32)
    d_upgate = up_pull(d_hidden * up_lin)[0].astype(jnp.bfloat16)
    d_uplin = (d_hidden * gelu_up).astype(jnp.bfloat16)
    grad_mgate = jnp.einsum("td,tf->df", normed_two, d_upgate, preferred_element_type=jnp.float32)
    grad_mup = jnp.einsum("td,tf->df", normed_two, d_uplin, preferred_element_type=jnp.float32)
    d_normed_two = jnp.einsum(
        "tf,df->td", d_upgate, gathered[12], preferred_element_type=jnp.float32
    )
    d_normed_two = d_normed_two + jnp.einsum(
        "tf,df->td", d_uplin, gathered[13], preferred_element_type=jnp.float32
    )
    grad_mgain = jnp.sum(d_normed_two * scaled_two, axis=0)
    d_residual = grad_top.astype(jnp.float32) + norm_pull_two(d_normed_two * gain_second)[0]
    d_outlow = d_residual.astype(jnp.bfloat16)
    grad_outw = jnp.einsum("tr,td->rd", mixed_low, d_outlow, preferred_element_type=jnp.float32)
    d_mixed = jnp.einsum("td,rd->tr", d_outlow, gathered[10], preferred_element_type=jnp.float32)
    direct = d_mixed * gate_branch
    d_gatelow = gate_pull(d_mixed * states)[0].astype(jnp.bfloat16)
    grad_gatew = jnp.einsum("td,tr->dr", normed, d_gatelow, preferred_element_type=jnp.float32)
    next_decay = jnp.concatenate([carried[1:], jnp.ones((1, channels), jnp.float32)], axis=0)
    suffix_decay, local_grad = lax.associative_scan(
        link, (next_decay, direct), axis=0, reverse=True
    )
    arriving = entering(
        (carried[0] * suffix_decay[0], carried[0] * local_grad[0]), "seq", link, identity, True
    )[1]
    d_states = local_grad + suffix_decay * arriving
    previous = jnp.concatenate([incoming[None, :], states[:-1]], axis=0)
    grad_convval, d_rpre, d_ipre, grad_lambda = recur_pull(
        (d_states * previous, d_states, jnp.zeros_like(decays))
    )
    d_rlow = d_rpre.astype(jnp.bfloat16)
    d_ilow = d_ipre.astype(jnp.bfloat16)
    grad_rw = block_weight_grad(conv_low, d_rlow, block_size)
    grad_rb = jnp.sum(d_rlow.astype(jnp.float32), axis=0)
    grad_iw = block_weight_grad(conv_low, d_ilow, block_size)
    grad_ib = jnp.sum(d_ilow.astype(jnp.float32), axis=0)
    grad_convsum = grad_convval + block_back(d_rlow, gathered[5]) + block_back(d_ilow, gathered[7])
    grad_cb = jnp.sum(grad_convsum, axis=0)
    conv_again = gathered[3].astype(jnp.float32)
    grad_extended = jnp.zeros((local_len + kernel_taps - 1, channels), jnp.float32)
    tap_grads = []
    for tap in range(kernel_taps):
        start_row = kernel_taps - 1 - tap
        masked = grad_convsum * tap_masks[tap]
        tap_grads.append(jnp.sum(masked * extended[start_row : start_row + local_len], axis=0))
        grad_extended = grad_extended + jnp.pad(
            masked * conv_again[tap], ((start_row, tap), (0, 0))
        )
    grad_cw = jnp.stack(tap_grads)
    edge_grads = shifted(grad_extended[: kernel_taps - 1], "seq", -1)
    d_inner = (
        grad_extended[kernel_taps - 1 :]
        + jnp.pad(edge_grads, ((local_len - kernel_taps + 1, 0), (0, 0)))
    ).astype(jnp.bfloat16)
    grad_inw = jnp.einsum("td,tr->dr", normed, d_inner, preferred_element_type=jnp.float32)
    d_normed = jnp.einsum("tr,dr->td", d_gatelow, gathered[1], preferred_element_type=jnp.float32)
    d_normed = d_normed + jnp.einsum(
        "tr,dr->td", d_inner, gathered[2], preferred_element_type=jnp.float32
    )
    grad_gain = jnp.sum(d_normed * scaled, axis=0)
    d_tokens = d_residual + norm_pull(d_normed * gain_first)[0]
    shares = (
        lax.psum_scatter(grad_gain, "seq", scatter_dimension=0, tiled=True),
        lax.psum_scatter(grad_gatew, "seq", scatter_dimension=0, tiled=True),
        lax.psum_scatter(grad_inw, "seq", scatter_dimension=0, tiled=True),
        lax.psum_scatter(grad_cw, "seq", scatter_dimension=1, tiled=True),
        lax.psum_scatter(grad_cb, "seq", scatter_dimension=0, tiled=True),
        lax.psum_scatter(grad_rw, "seq", scatter_dimension=0, tiled=True),
        lax.psum_scatter(grad_rb, "seq", scatter_dimension=0, tiled=True),
        lax.psum_scatter(grad_iw, "seq", scatter_dimension=0, tiled=True),
        lax.psum_scatter(grad_ib, "seq", scatter_dimension=0, tiled=True),
        lax.psum_scatter(grad_lambda, "seq", scatter_dimension=0, tiled=True),
        lax.psum_scatter(grad_outw, "seq", scatter_dimension=0, tiled=True),
        lax.psum_scatter(grad_mgain, "seq", scatter_dimension=0, tiled=True),
        lax.psum_scatter(grad_mgate, "seq", scatter_dimension=0, tiled=True),
        lax.psum_scatter(grad_mup, "seq", scatter_dimension=0, tiled=True),
        lax.psum_scatter(grad_mdown, "seq", scatter_dimension=0, tiled=True),
    )
    totals = (
        lax.psum(shares[0].astype(jnp.bfloat16), "batch").astype(jnp.float32),
        lax.psum(shares[1].astype(jnp.bfloat16), "batch").astype(jnp.float32),
        lax.psum(shares[2].astype(jnp.bfloat16), "batch").astype(jnp.float32),
        lax.psum(shares[3].astype(jnp.bfloat16), "batch").astype(jnp.float32),
        lax.psum(shares[4].astype(jnp.bfloat16), "batch").astype(jnp.float32),
        lax.psum(shares[5].astype(jnp.bfloat16), "batch").astype(jnp.float32),
        lax.psum(shares[6].astype(jnp.bfloat16), "batch").astype(jnp.float32),
        lax.psum(shares[7].astype(jnp.bfloat16), "batch").astype(jnp.float32),
        lax.psum(shares[8].astype(jnp.bfloat16), "batch").astype(jnp.float32),
        lax.psum(shares[9].astype(jnp.bfloat16), "batch").astype(jnp.float32),
        lax.psum(shares[10].astype(jnp.bfloat16), "batch").astype(jnp.float32),
        lax.psum(shares[11].astype(jnp.bfloat16), "batch").astype(jnp.float32),
        lax.psum(shares[12].astype(jnp.bfloat16), "batch").astype(jnp.float32),
        lax.psum(shares[13].astype(jnp.bfloat16), "batch").astype(jnp.float32),
        lax.psum(shares[14].astype(jnp.bfloat16), "batch").astype(jnp.float32),
    )
    return (
        block_out[None],
        d_tokens[None],
        totals[0],
        totals[1],
        totals[2],
        totals[3],
        totals[4],
        totals[5],
        totals[6],
        totals[7],
        totals[8],
        totals[9],
        totals[10],
        totals[11],
        totals[12],
        totals[13],
        totals[14],
        gate_mean[None],
    )


def planes(
    inputs,
    out_grad,
    row_lengths,
    norm_gain,
    w_gate,
    w_in,
    conv_w,
    conv_b,
    w_rgate,
    b_rgate,
    w_igate,
    b_igate,
    lam,
    w_out,
    mlp_gain,
    w_mlp_gate,
    w_mlp_up,
    w_mlp_down,
):
    vmem = pltpu.VMEM
    done = kernel_call(
        layer,
        dict(
            x_in=inputs[0], cw=conv_w, cb=conv_b, br=b_rgate, bi=b_igate, lam=lam, ngain=norm_gain, mgain=mlp_gain,
            lens=row_lengths, g=out_grad[0], wg=w_gate, wi=w_in, wr=w_rgate, wv=w_igate, wout=w_out,
            wmg=w_mlp_gate, wmu=w_mlp_up, wmd=w_mlp_down,
        ),
        dict(
            block_out=array(256, 1024, dtype=BF),
            d_in=array(256, 1024),
            fm=array(4, 256, 768, dtype=BF),
            fm_x=array(4, 128, 768, dtype=BF),
            fd=array(4, 96, 1024, dtype=BF),
            fa=array(4, 256, 256, dtype=BF),
            fa_x=array(4, 128, 256, dtype=BF),
            fb=array(4, 128, 256, dtype=BF),
            fo=array(4, 48, 1280, dtype=BF),
            fr=array(8, 2, 8, 128),
            vec_out=array(8, 256),
            gain_out=array(8, 128),
            normed_far=array(8, 256, 1024, dtype=BF),
        ),
        dict(
            x=vmem((256, 1024), BF),
            x_all=vmem((8, 256, 1024), BF),
            normed=vmem((8, 256, 1024), BF),
            g_all=vmem((8, 256, 1024), BF),
            small_rows=vmem((16, 256), F32),
            small=vmem((16, 256), BF),
            small_all=vmem((2, 4, 16, 256), BF),
            lens_out=vmem((8, 128), F32),
            lens_all=vmem((4, 8, 128), F32),
            off=vmem((4, 520, 128), F32),
            starts_all=vmem((4, 8, 128), F32),
            chan=vmem((2, 16, 128), F32),
            gain=vmem((8, 1024), F32),
            wgi3=vmem((4, 256, 768), BF),
            w2=vmem((1024, 512), BF),
            gq=vmem((4, 48, 256), BF),
            g3=vmem((2, 192, 256), BF),
            wq=vmem((4, 48, 1024), BF),
            wri=vmem((2, 128, 256), BF),
            w3=vmem((2, 192, 1024), BF),
            wo=vmem((256, 1024), BF),
            wgu_out=vmem((2, 128, 768), BF),
            wgu_all=vmem((8, 128, 768), BF),
            wmd_all=vmem((4, 96, 1024), BF),
            gp=vmem((8, 512, 128), F32),
            gb=vmem((8, 520, 128), F32),
            inner=vmem((8, 520, 128), F32),
            conv=vmem((8, 512, 128), BF),
            sr=vmem((8, 512, 128), F32),
            si=vmem((8, 512, 128), F32),
            dec=vmem((8, 512, 128), F32),
            drv=vmem((8, 512, 128), F32),
            states=vmem((8, 520, 128), F32),
            mixed=vmem((8, 256, 256), BF),
            tot=vmem((2, 4, 2, 8, 128), F32),
            inc=vmem((8, 128), F32),
            rs_all=vmem((4, 8, 8, 128), F32),
            rows_sum=vmem((8, 8, 128), F32),
            residual=vmem((256, 1024), F32),
            d_res=vmem((256, 1024), F32),
            hid=vmem((8, 256, 384), BF),
            dgu=vmem((8, 256, 768), BF),
            gm=vmem((4, 256, 768), BF),
            gm_sum=vmem((256, 768), BF),
            gd=vmem((4, 96, 1024), BF),
            gd_in=vmem((3, 96, 1024), BF),
            gd_sum=vmem((96, 1024), BF),
            go=vmem((256, 1280), BF),
            go_q=vmem((4, 48, 1280), BF),
            go_l=vmem((3, 48, 1280), BF),
            go_sum=vmem((48, 1280), BF),
            ga_sum=vmem((256, 256), BF),
            gb2_sum=vmem((128, 256), BF),
            gain2_sum=vmem((8, 1024), F32),
            vec=vmem((2, 8, 8, 128), F32),
            vsum=vmem((4, 8, 256), F32),
            vout=vmem((4, 8, 256), F32),
            gsum=vmem((8, 8, 128), F32),
            gline=vmem((8, 8, 128), F32),
            gplane=vmem((4, 8, 128), F32),
            free=pltpu.SemaphoreType.REGULAR,
            **reduce_scratch(256, 1024),
        ),
        154,
        37,
        (
            "x_in", "g", "wg", "wi", "wr", "wv", "wout", "wmg", "wmu", "wmd", "d_in", "block_out", "fm", "fm_x", "fd", "fa", "fa_x", "fb", "fo",
            "fr", "normed_far",
        ),
    )
    out = kernel_call(
        assemble,
        dict(
            {name: done[name] for name in ("d_in", "block_out", "fm", "fm_x", "fd", "fa", "fa_x", "fb", "fo", "fr")},
            vec_in=done["vec_out"], gains=done["gain_out"], lens=row_lengths,
        ),
        dict(
            o_din=array(256, 1024),
            o_block=array(256, 1024, dtype=BF),
            o_gate=array(128, 1536),
            o_in=array(128, 1536),
            o_mgate=array(128, 3072),
            o_mup=array(128, 3072),
            o_mdown=array(384, 1024),
            o_out=array(192, 1024),
            o_r=array(192, 128),
            o_i=array(192, 128),
            o_cw=array(4, 192),
            o_cb=array(1, 192),
            o_rb=array(1, 192),
            o_ib=array(1, 192),
            o_lam=array(1, 192),
            o_ngain=array(1, 128),
            o_mgain=array(1, 128),
            o_mean=array(5, 1, 1536),
        ),
        dict(
            v_din=vmem((256, 1024), F32),
            v_block=vmem((256, 1024), BF),
            vm=vmem((2, 4, 128, 768), BF),
            va=vmem((2, 4, 128, 256), BF),
            vb=vmem((4, 128, 256), BF),
            vd=vmem((4, 96, 1024), BF),
            vo=vmem((4, 48, 1280), BF),
            s_mgate=vmem((128, 3072), F32),
            s_mup=vmem((128, 3072), F32),
            s_gate=vmem((128, 1536), F32),
            s_in=vmem((128, 1536), F32),
            s_down=vmem((384, 1024), F32),
            s_out=vmem((192, 1024), F32),
            s_r=vmem((192, 128), F32),
            s_i=vmem((192, 128), F32),
            s_cw=vmem((4, 192), F32),
            s_cb=vmem((1, 192), F32),
            s_rb=vmem((1, 192), F32),
            s_ib=vmem((1, 192), F32),
            s_lam=vmem((1, 192), F32),
            s_ngain=vmem((1, 128), F32),
            s_mgain=vmem((1, 128), F32),
            s_mean=vmem((5, 1, 1536), F32),
            v_vec=vmem((8, 256), F32),
            v_gains=vmem((8, 128), F32),
            v_fr=vmem((8, 2, 8, 128), F32),
            v_lens=vmem((1, 5), jnp.int32),
        ),
        0,
        37,
        None,
    )
    return (
        out["o_block"][None],
        out["o_din"][None],
        out["o_ngain"][0],
        out["o_gate"],
        out["o_in"],
        out["o_cw"],
        out["o_cb"][0],
        out["o_r"],
        out["o_rb"][0],
        out["o_i"],
        out["o_ib"][0],
        out["o_lam"][0],
        out["o_out"],
        out["o_mgain"][0],
        out["o_mgate"],
        out["o_mup"],
        out["o_mdown"],
        jnp.transpose(out["o_mean"], (1, 0, 2)),
    )


def solution(mesh):
    in_specs = (
        P("batch", "seq", None),
        P("batch", "seq", None),
        P("batch", None),
        P("seq"),
        P("seq", None),
        P("seq", None),
        P(None, "seq"),
        P("seq"),
        P("seq", None),
        P("seq"),
        P("seq", None),
        P("seq"),
        P("seq"),
        P("seq", None),
        P("seq"),
        P("seq", None),
        P("seq", None),
        P("seq", None),
    )
    out_specs = (
        P("batch", "seq", None),
        P("batch", "seq", None),
        P("seq"),
        P("seq", None),
        P("seq", None),
        P(None, "seq"),
        P("seq"),
        P("seq", None),
        P("seq"),
        P("seq", None),
        P("seq"),
        P("seq"),
        P("seq", None),
        P("seq"),
        P("seq", None),
        P("seq", None),
        P("seq", None),
        P("batch", None, None),
    )
    in_planes = mesh.shape["batch"] == 4 and mesh.shape["seq"] == 8
    body = planes if in_planes else shards
    return jax.shard_map(body, mesh=mesh, in_specs=in_specs, out_specs=out_specs, check_vma=False)
```
